32 devices in a mesh: rep: 2 (over x), grp: 4 (over z), tp: 4 (over y, core).
Axes of the slice: x: 2, y: 2, z: 4, core: 2. Of those that a mesh axis runs over, the one named last changes fastest.
Arguments:
- x_in: bfloat16 [4, 8, 128, 1280], P(None, ('rep', 'grp'), None, 'tp'), parts along dimension 1, may hold values from -6 to 6
- taps: bfloat16 [4, 8, 128, 6400], P(None, ('rep', 'grp'), None, 'tp'), parts along dimension 1, may hold values from -6 to 6
- ln_gain: float32 [1280], replicated, may hold values from 0.1 to 1.9
- ln_bias: float32 [1280], replicated, may hold values from -3 to 3
- w_up: bfloat16 [1280, 5120], P(None, 'tp'), may hold values from -0.15625 to 0.15625
- b_up: float32 [5120], P('tp'), may hold values from -3 to 3
- w_down: bfloat16 [5120, 1280], P('tp'), may hold values from -0.078125 to 0.078125
- b_down: float32 [1280], P('tp'), may hold values from -3 to 3
- kv_w_out: bfloat16 [1280, 2048], P('tp'), may hold values from -0.0625 to 0.0625
- kv_w_taps: bfloat16 [6400, 2048], P('tp'), may hold values from -0.09375 to 0.09375
- k_gain: float32 [128], replicated, may hold values from 1 to 2.5
- q_gain: float32 [128], replicated, may hold values from 1 to 2.5
- queries: bfloat16 [4096, 8192], P(('rep', 'grp'), 'tp'), parts along dimension 0, may hold values from -6 to 6
- tiles_per_request: int32 [16], P('rep'), parts along dimension 0, may hold values from 1 to 4, as said below
- owner: int32 [16], P('rep'), parts along dimension 0, may hold values from 0 to 3, as said below
- text_per_request: int32 [16], P('rep'), parts along dimension 0, may hold values from 64 to 256, as said below
Outputs:
- attended: bfloat16 [4096, 8192], P(('rep', 'grp'), 'tp'), parts along dimension 0
The draws below stay inside these ranges and needn't reach their ends.
There are 2 independent parts, one for each index of `rep`. The reference program is written for one: setup_inputs(seed, part) draws one part's arguments, and reference() takes and returns one part's arrays. A program takes and returns all parts, laid end to end along the dimension named above; an argument that names none is the same for every part. Nothing has to cross between parts.
Inputs may be any that keep to these rules, and one draw needn't show every extreme that they name: `owner`: each group owns exactly 2 requests. `tiles_per_request`: the tiles of all requests sum to 16; the tiles of one group's requests sum to at most 8, and some group has exactly 8. `text_per_request`: the text tokens of one group's requests sum to at most 512, and some group has exactly 512.
All inputs are finite; a program needn't handle non-finite values.
Results may differ from the reference program's by a relative error of at most 0.04.
Values may be sent and summed in bfloat16 or wider, within the bound.
No kernel may reach another device: no remote copies, remote signals or barrier semaphores. Data moves between devices by JAX's collectives and lax.ppermute only.
A program may use at most 128 MiB of HBM per device.

```python
import math
import jax
import jax.numpy as jnp
from jax import lax

DV = 1280
MLPV = 5120
TAPS = 5
QH = 64
KVH = 8
HD = 128
TILE_ROWS = 128
TEXT_G = 512
TILES_ENC = 4
MAXT = 4
REQ_G = 2
FEAT = 7680
KVW = 2048
QW = 8192
TILES = 16
NREQ = 8
CAP = 8
N_GRP = 4
N_TP = 4


def owner_table(key):
    shuffled = jax.random.permutation(jax.random.fold_in(key, 101), NREQ)
    return (shuffled // REQ_G).astype(jnp.int32)


def chosen_group(key, salt):
    return jax.random.randint(jax.random.fold_in(key, salt), (), 0, N_GRP).astype(jnp.int32)


def draw_owner(key, part):
    return owner_table(key)


def draw_tiles_per_request(key, part):
    owners = owner_table(key)
    forced = owners == chosen_group(key, 202)
    extra_total = TILES - CAP - (NREQ - REQ_G)
    priority = jax.random.randint(jax.random.fold_in(key, 303), (max(extra_total, 1), NREQ), 0, 1 << 20)
    request_ids = jnp.arange(NREQ, dtype=jnp.int32)

    def add_one(step_index, extra):
        eligible = jnp.logical_not(forced) & (extra < MAXT - 1)
        ranked = jnp.where(eligible, priority[step_index], -1)
        picked = jnp.argmax(ranked).astype(jnp.int32)
        return extra + (request_ids == picked).astype(jnp.int32)
    extra = lax.fori_loop(0, extra_total, add_one, jnp.zeros((NREQ,), jnp.int32))
    return jnp.where(forced, MAXT, 1 + extra).astype(jnp.int32)


def draw_text_per_request(key, part):
    owners = owner_table(key)
    forced = owners == chosen_group(key, 404)
    base_counts = jax.random.randint(jax.random.fold_in(key, 505), (NREQ,), TEXT_G // 8, TEXT_G // 2 + 1)
    return jnp.where(forced, TEXT_G // 2, base_counts).astype(jnp.int32)


def with_spikes(values, rng, source, target, shards_of, factor):
    def block_of(dim):
        return (jnp.arange(values.shape[dim]) // (values.shape[dim] // shards_of)).reshape((-1,) + (1,) * (values.ndim - 1 - dim))

    near = jax.random.permutation(rng, shards_of)[block_of(target)]
    other_side = (block_of(target) + shards_of // 2) % shards_of
    return jnp.where((block_of(source) == near) | (block_of(source) == other_side), factor * values, values)


def steps_of(key, shape, split, least, high):
    def one(dim, parts):
        steps = jax.random.uniform(jax.random.fold_in(jax.random.fold_in(key, 6), dim), (parts,), jnp.float32, least / len(split), high / len(split))
        return jnp.repeat(jnp.exp(steps), shape[dim] // parts).reshape((-1,) + (1,) * (len(shape) - dim - 1))

    loudness = one(*split[0])
    for cut in split[1:]:
        loudness = loudness * one(*cut)
    return loudness


def gaussian(rng, shape, deviation, limit, split=(), kind=jnp.bfloat16):
    values = deviation * jax.random.normal(rng, shape, jnp.float32)
    if split:
        values = values * steps_of(rng, shape, split, -0.22, 0.18)
    return jnp.clip(values, -limit, limit).astype(kind)


def bell_draw_with(rng, dims, width, limit, shards, heavy, kind=jnp.bfloat16):
    values = width * jax.random.normal(rng, dims, jnp.float32)
    if shards:
        values = values * steps_of(rng, dims, shards, -0.22, 0.18)
    return jnp.clip(with_spikes(values, jax.random.fold_in(rng, 3), *heavy), -limit, limit).astype(kind)


def setup_inputs(seed: int = 0, part: int = 0) -> dict:
    keys = jax.random.split(jax.random.key(seed), 17)
    part_splits = jax.random.split(jax.random.fold_in(keys[16], part), 17)
    return {
        "x_in": gaussian(part_splits[0], (TILES_ENC, N_GRP, TILE_ROWS, DV), 1.0, 6.0, ((1, 4), (3, 4))),
        "taps": gaussian(part_splits[1], (TILES_ENC, N_GRP, TILE_ROWS, DV * TAPS), 1.0, 6.0, ((1, 4), (3, 4))),
        "ln_gain": jnp.clip(1.0 + 0.18 * jax.random.normal(keys[2], (DV,), jnp.float32), 0.1, 1.9),
        "ln_bias": gaussian(keys[3], (DV,), 0.5, 3.0, (), jnp.float32),
        "w_up": gaussian(keys[4], (DV, MLPV), DV ** -0.5, 0.15625, ((1, 4),)),
        "b_up": gaussian(keys[5], (MLPV,), 0.5, 3.0, ((0, 4),), jnp.float32),
        "w_down": gaussian(keys[6], (MLPV, DV), MLPV ** -0.5, 0.078125, ((0, 4),)),
        "b_down": gaussian(keys[7], (DV,), 0.5, 3.0, ((0, 4),), jnp.float32),
        "kv_w_out": gaussian(keys[8], (DV, KVW), FEAT ** -0.5, 0.0625, ((0, 4),)),
        "kv_w_taps": bell_draw_with(keys[9], (DV * TAPS, KVW), FEAT ** -0.5, 0.09375, ((0, 4),), (0, 1, 4, 2.0)),
        "k_gain": jnp.clip(jnp.exp(jax.random.uniform(keys[10], (HD,), jnp.float32, math.log(1.0), math.log(2.5))), 1.0, 2.5),
        "q_gain": jnp.clip(jnp.exp(jax.random.uniform(keys[11], (HD,), jnp.float32, math.log(1.0), math.log(2.5))), 1.0, 2.5),
        "queries": gaussian(part_splits[12], (N_GRP * TEXT_G, QW), 1.0, 6.0, ((0, 4), (1, 4))),
        "tiles_per_request": draw_tiles_per_request(jax.random.fold_in(jax.random.fold_in(keys[16], part), 71), part),
        "owner": draw_owner(jax.random.fold_in(jax.random.fold_in(keys[16], part), 71), part),
        "text_per_request": draw_text_per_request(jax.random.fold_in(jax.random.fold_in(keys[16], part), 71), part),
    }


epsilon = 1e-05

def layer_norm(row_block, ln_gain, ln_bias):
    values = row_block.astype(jnp.float32)
    average = lax.optimization_barrier(jnp.mean(values, axis=-1, keepdims=True))
    centered = values - average
    variance = lax.optimization_barrier(jnp.mean(centered * centered, axis=-1, keepdims=True))
    return (centered * lax.rsqrt(variance + epsilon) * ln_gain + ln_bias).astype(jnp.bfloat16)

def head_norm(values, head_gain):
    square = lax.optimization_barrier(jnp.mean(values * values, axis=-1, keepdims=True))
    return values * lax.rsqrt(square + epsilon) * head_gain

def group_layout(tiles_per_request, owner, text_per_request, group_count):
    request_count = owner.shape[0]
    request_ids = jnp.arange(request_count, dtype=jnp.int32)
    group_ids = jnp.arange(group_count, dtype=jnp.int32)
    member = owner[None, :] == group_ids[:, None]
    first_req = lax.optimization_barrier(jnp.min(jnp.where(member, request_ids[None, :], request_count), axis=1))
    second_req = lax.optimization_barrier(jnp.max(jnp.where(member, request_ids[None, :], -1), axis=1))
    pick_first = request_ids[None, :] == first_req[:, None]
    pick_second = request_ids[None, :] == second_req[:, None]
    tiles_first = lax.optimization_barrier(jnp.sum(jnp.where(pick_first, tiles_per_request[None, :], 0), axis=1)).astype(jnp.int32)
    tiles_second = lax.optimization_barrier(jnp.sum(jnp.where(pick_second, tiles_per_request[None, :], 0), axis=1)).astype(jnp.int32)
    text_first = lax.optimization_barrier(jnp.sum(jnp.where(pick_first, text_per_request[None, :], 0), axis=1)).astype(jnp.int32)
    text_second = lax.optimization_barrier(jnp.sum(jnp.where(pick_second, text_per_request[None, :], 0), axis=1)).astype(jnp.int32)
    tiles_both = (tiles_first + tiles_second).astype(jnp.int32)
    text_both = (text_first + text_second).astype(jnp.int32)
    offsets = (jnp.cumsum(tiles_both) - tiles_both).astype(jnp.int32)
    return (tiles_first, tiles_both, offsets, text_first, text_both)

def slot_label(position, first_count, both_count):
    return jnp.where(position < first_count, 0, jnp.where(position < both_count, 1, -1)).astype(jnp.int32)

def reference(x_in, taps, ln_gain, ln_bias, w_up, b_up, w_down, b_down, kv_w_out, kv_w_taps, k_gain, q_gain, queries, tiles_per_request, owner, text_per_request):
    token_count = TILES * TILE_ROWS
    token_rows = x_in.reshape(token_count, DV)
    normed = layer_norm(token_rows, ln_gain, ln_bias)
    hidden = jax.nn.gelu(jnp.dot(normed, w_up, preferred_element_type=jnp.float32) + b_up, approximate=False).astype(jnp.bfloat16)
    encoded = (token_rows.astype(jnp.float32) + jnp.dot(hidden, w_down, preferred_element_type=jnp.float32) + b_down).astype(jnp.bfloat16)
    tap_rows = taps.reshape(token_count, DV * TAPS)
    out_block = DV // N_TP
    tap_block = DV * TAPS // N_TP
    kv_total = jnp.zeros((token_count, KVW), jnp.float32)
    for block_index in range(N_TP):
        part_out = jnp.dot(encoded[:, block_index * out_block:(block_index + 1) * out_block], kv_w_out[block_index * out_block:(block_index + 1) * out_block], preferred_element_type=jnp.float32)
        part_tap = jnp.dot(tap_rows[:, block_index * tap_block:(block_index + 1) * tap_block], kv_w_taps[block_index * tap_block:(block_index + 1) * tap_block], preferred_element_type=jnp.float32)
        rounded = lax.optimization_barrier((part_out + part_tap).astype(jnp.bfloat16))
        kv_total = kv_total + rounded.astype(jnp.float32)
    kv_total = kv_total.reshape(TILES, TILE_ROWS, KVH, 2, HD)
    key_rows = head_norm(kv_total[:, :, :, 0, :], k_gain).astype(jnp.bfloat16)
    value_rows = kv_total[:, :, :, 1, :].astype(jnp.bfloat16)
    tiles_first, tiles_both, offsets, text_first, text_both = group_layout(tiles_per_request, owner, text_per_request, N_GRP)
    group_size = QH // KVH
    query_view = queries.reshape(N_GRP, TEXT_G, KVH, group_size, HD).astype(jnp.float32)
    query_rows = head_norm(query_view, q_gain).astype(jnp.bfloat16)
    slot_ids = jnp.arange(CAP, dtype=jnp.int32)
    text_ids = jnp.arange(TEXT_G, dtype=jnp.int32)
    scale = 1.0 / math_sqrt(HD)

    def per_group(item):
        query_group, first_count, both_count, offset, text_one, text_two = item
        tile_index = jnp.clip(offset + slot_ids, 0, TILES - 1).astype(jnp.int32)
        key_group = jnp.take(key_rows, tile_index, axis=0).reshape(CAP * TILE_ROWS, KVH, HD)
        value_group = jnp.take(value_rows, tile_index, axis=0).reshape(CAP * TILE_ROWS, KVH, HD)
        key_label = jnp.repeat(slot_label(slot_ids, first_count, both_count), TILE_ROWS)
        text_label = slot_label(text_ids, text_one, text_two)
        allowed = (text_label[:, None] == key_label[None, :]) & (text_label[:, None] >= 0)
        live_rows = text_label >= 0

        def per_head(head_item):
            query_head, key_head, value_head = head_item
            scores = jnp.einsum('tgd,sd->tgs', query_head.astype(jnp.float32), key_head.astype(jnp.float32)) * scale
            weights = jnp.where(allowed[:, None, :], jnp.exp(scores), 0.0)
            total = lax.optimization_barrier(jnp.sum(weights, axis=-1, keepdims=True))
            total = jnp.where(live_rows[:, None, None], total, 1.0)
            probs = jnp.where(live_rows[:, None, None], weights / total, 0.0).astype(jnp.bfloat16)
            result = jnp.einsum('tgs,sd->tgd', probs.astype(jnp.float32), value_head.astype(jnp.float32))
            return result.astype(jnp.bfloat16)
        head_out = lax.map(per_head, (jnp.transpose(query_group, (1, 0, 2, 3)), jnp.transpose(key_group, (1, 0, 2)), jnp.transpose(value_group, (1, 0, 2))))
        return jnp.transpose(head_out, (1, 0, 2, 3)).reshape(TEXT_G, QH * HD)
    attended = lax.map(per_group, (query_rows, tiles_first, tiles_both, offsets, text_first, text_both))
    return attended.reshape(N_GRP * TEXT_G, QH * HD)

def math_sqrt(number):
    return float(number) ** 0.5
```

```python
import functools
import math

import jax
import jax.numpy as jnp
from jax import lax
from jax.experimental import pallas as pl
from jax.experimental.pallas import tpu as pltpu
from jax.sharding import PartitionSpec as P

KVH = 8
HD = 128
MAXT = 4
REQ_G = 2
LANES = 128
ROW_BLOCK = 128
HIDDEN_BLOCK = 256
VALUE_SHIFT = 2.0**-24
epsilon = 1e-05

F32 = jnp.float32
BF16 = jnp.bfloat16
VMEM = pl.BlockSpec(memory_space=pltpu.VMEM)
SMEM = pl.BlockSpec(memory_space=pltpu.SMEM)
MIB = 1024 * 1024


def bits_of(count):
    bits = count.bit_length() - 1
    assert 1 << bits == count
    return bits


def xor_order(blocks, index):
    blocks = list(blocks)
    for b in range(bits_of(len(blocks))):
        swap = ((index >> b) & 1) == 1
        for k in range(len(blocks)):
            if not (k >> b) & 1:
                low, high = blocks[k], blocks[k | (1 << b)]
                blocks[k] = lax.select(swap, high, low)
                blocks[k | (1 << b)] = lax.select(swap, low, high)
    return blocks


def xor_pairs(count, mask):
    return [(i, i ^ mask) for i in range(count)]


def tail_plan(rows, width):
    whole = width // LANES * LANES
    tail = width - whole
    packed = tail > 0 and rows // ROW_BLOCK * tail == whole
    return whole, tail, packed


def layout_kernel(group_count, tiles_local, where_ref, tiles_ref, owner_ref, text_ref, meta_ref):
    group = where_ref[0]
    zero = jnp.int32(0)
    firsts, counts, offsets, texts_first, texts_both = [], [], [], [], []
    offset = zero
    for p in range(group_count):
        first, count, text_first, text_both, seen = zero, zero, zero, zero, zero
        for r in range(owner_ref.shape[0]):
            mine = owner_ref[r] == p
            tiles = jnp.where(mine, tiles_ref[r], 0)
            text = jnp.where(mine, text_ref[r], 0)
            first = first + jnp.where(seen == 0, tiles, 0)
            text_first = text_first + jnp.where(seen == 0, text, 0)
            count = count + tiles
            text_both = text_both + text
            seen = seen + jnp.where(mine, 1, 0)
        firsts.append(first)
        counts.append(count)
        offsets.append(offset)
        texts_first.append(text_first)
        texts_both.append(text_both)
        offset = offset + count

    def pick(values, index):
        out = values[0]
        for p in range(1, group_count):
            out = jnp.where(index == p, values[p], out)
        return out

    slots = slot_count_of(group_count)
    star, most = zero, counts[0]
    for p in range(1, group_count):
        larger = counts[p] > most
        star = jnp.where(larger, p, star)
        most = jnp.where(larger, counts[p], most)

    def local_tile(offset, slot):
        lane = lax.rem(group - offset + group_count * REQ_G * MAXT * group_count, group_count)
        tile = lax.div(offset + slot * group_count + lane, group_count)
        return jnp.minimum(tile, tiles_local - 1)

    my_first, my_count = pick(firsts, group), pick(counts, group)
    my_offset = pick(offsets, group)
    place = meta_places(group_count)
    meta_ref[place["first"]] = my_first
    meta_ref[place["second"]] = my_count - my_first
    meta_ref[place["text_first"]] = pick(texts_first, group)
    meta_ref[place["text_both"]] = pick(texts_both, group)
    meta_ref[place["star"]] = local_tile(pick(offsets, star), 1)
    for slot in range(slots):
        for d in range(group_count):
            other = group ^ d
            meta_ref[place["send"] + slot * group_count + d] = local_tile(pick(offsets, other), slot)
            lane = lax.rem(other - my_offset + group_count * REQ_G * MAXT * group_count, group_count)
            position = slot * group_count + lane
            goes = jnp.where(
                position < my_first,
                position,
                jnp.where(position < my_count, MAXT + position - my_first, -1),
            )
            meta_ref[place["goes"] + slot * group_count + d] = goes


def slot_count_of(group_count):
    return (REQ_G * MAXT + group_count - 1) // group_count


def meta_places(group_count):
    table = slot_count_of(group_count) * group_count
    return {
        "first": 0,
        "second": 1,
        "text_first": 2,
        "text_both": 3,
        "star": 4,
        "send": 8,
        "goes": 8 + table,
        "size": 8 + 2 * table,
    }


def request_layout(group_count, tiles_local, where, tiles_per_request, owner, text_per_request):
    size = meta_places(group_count)["size"]
    return pl.pallas_call(
        functools.partial(layout_kernel, group_count, tiles_local),
        out_shape=jax.ShapeDtypeStruct((size,), jnp.int32),
        in_specs=[SMEM] * 4,
        out_specs=SMEM,
        cost_estimate=pl.CostEstimate(flops=1000, bytes_accessed=4000, transcendentals=0),
        name="request_layout",
    )(where, tiles_per_request, owner, text_per_request)


def mlp_kernel(piece_count, where_ref, *refs):
    pieces = refs[:piece_count]
    gain_ref, bias_ref, up_ref, up_bias_ref, down_ref = refs[piece_count : piece_count + 5]
    outs = refs[piece_count + 5 : 2 * piece_count + 5]
    normed_ref, hidden_ref, total_ref = refs[2 * piece_count + 5 :]
    index = where_ref[1]
    rows, width = pieces[0].shape
    channels = width * piece_count
    for row in range(0, rows, ROW_BLOCK):
        take = pl.ds(row, ROW_BLOCK)
        blocks = xor_order([piece[take, :].astype(F32) for piece in pieces], index)
        values = jnp.concatenate(blocks, axis=1)
        average = jnp.sum(values, axis=1, keepdims=True) * (1.0 / channels)
        centered = values - average
        variance = jnp.sum(centered * centered, axis=1, keepdims=True) * (1.0 / channels)
        normed = centered * lax.rsqrt(variance + epsilon) * gain_ref[...] + bias_ref[...]
        normed_ref[take, :] = normed.astype(BF16)
    hidden_width = up_ref.shape[1]
    step = math.gcd(hidden_width, HIDDEN_BLOCK)
    for col in range(0, hidden_width, step):
        take = pl.ds(col, step)
        value = jnp.dot(normed_ref[...], up_ref[:, take], preferred_element_type=F32)
        value = value + up_bias_ref[:, take]
        value = 0.5 * value * (1.0 + lax.erf(value * (1.0 / math.sqrt(2.0))))
        hidden_ref[:, take] = value.astype(BF16)
    step = math.gcd(channels, HIDDEN_BLOCK)
    for col in range(0, channels, step):
        take = pl.ds(col, step)
        total_ref[:, take] = jnp.dot(
            hidden_ref[...], down_ref[:, take], preferred_element_type=F32
        )
    whole, tail, packed = tail_plan(rows, width)
    for row in range(0, rows, ROW_BLOCK):
        take = pl.ds(row, ROW_BLOCK)
        blocks = [total_ref[take, j * width : (j + 1) * width] for j in range(piece_count)]
        for out, block in zip(outs, xor_order(blocks, index)):
            block = block.astype(BF16)
            if packed:
                out[take, :] = block[:, :whole]
                out[rows : rows + ROW_BLOCK, row // ROW_BLOCK * tail : (row // ROW_BLOCK + 1) * tail] = block[:, whole:]
            else:
                out[take, :] = block


def encoder_mlp(where, pieces, ln_gain, ln_bias, w_up, b_up, w_down):
    rows, width = pieces[0].shape
    count = len(pieces)
    channels, hidden_width = w_up.shape
    whole, _, packed = tail_plan(rows, width)
    shape = (rows + ROW_BLOCK, whole) if packed else (rows, width)
    return pl.pallas_call(
        functools.partial(mlp_kernel, count),
        out_shape=[jax.ShapeDtypeStruct(shape, BF16)] * count,
        in_specs=[SMEM] + [VMEM] * (count + 5),
        out_specs=[VMEM] * count,
        scratch_shapes=[
            pltpu.VMEM((rows, channels), BF16),
            pltpu.VMEM((rows, hidden_width), BF16),
            pltpu.VMEM((rows, channels), F32),
        ],
        compiler_params=pltpu.CompilerParams(vmem_limit_bytes=32 * MIB),
        cost_estimate=pl.CostEstimate(
            flops=4 * rows * channels * hidden_width,
            bytes_accessed=4 * channels * hidden_width + 4 * rows * channels,
            transcendentals=rows * hidden_width,
        ),
        name="encoder_mlp",
    )(
        where,
        *pieces,
        ln_gain.reshape(1, channels),
        ln_bias.reshape(1, channels),
        w_up,
        b_up.reshape(1, hidden_width),
        w_down,
    )


def tap_kernel(where_ref, tap_ref, weight_ref, out_ref):
    out_ref[...] = jnp.dot(
        tap_ref[...], weight_ref[...], preferred_element_type=F32
    ).astype(BF16)[None, None]


def tap_projection(where, tap_rows, weights, head_count, dest_count, dup):
    rows, depth = tap_rows.shape
    block = 2 * HD

    def head_of(n, where_ref):
        dest = lax.div(where_ref[1], jnp.int32(dup)) ^ lax.rem(n, dest_count)
        return dest * head_count + lax.div(n, dest_count)

    return pl.pallas_call(
        tap_kernel,
        out_shape=jax.ShapeDtypeStruct((head_count, dest_count, rows, block), BF16),
        grid_spec=pltpu.PrefetchScalarGridSpec(
            num_scalar_prefetch=1,
            grid=(head_count * dest_count,),
            in_specs=[
                pl.BlockSpec((rows, depth), lambda n, w: (0, 0)),
                pl.BlockSpec((depth, block), lambda n, w: (0, head_of(n, w))),
            ],
            out_specs=pl.BlockSpec(
                (1, 1, rows, block),
                lambda n, w: (lax.div(n, dest_count), lax.rem(n, dest_count), 0, 0),
            ),
        ),
        compiler_params=pltpu.CompilerParams(vmem_limit_bytes=16 * MIB),
        cost_estimate=pl.CostEstimate(
            flops=2 * rows * depth * weights.shape[1],
            bytes_accessed=2 * depth * weights.shape[1],
            transcendentals=0,
        ),
        name="tap_projection",
    )(where, tap_rows, weights)


def kv_kernel(head_count, dest_count, dup, term_count, where_ref, *refs):
    x_ref, bias_ref, weight_ref, tap_ref = refs[:4]
    terms = refs[4 : 4 + term_count]
    outs = refs[4 + term_count : -1]
    encoded_ref = refs[-1]
    rows, width = x_ref.shape
    whole, tail, packed = tail_plan(rows, width)
    for row in range(0, rows, ROW_BLOCK):
        take = pl.ds(row, ROW_BLOCK)

        def summed(part, lanes):
            out = terms[0][part, lanes].astype(F32)
            for term in terms[1:]:
                out = out + term[part, lanes].astype(F32)
            return out

        if packed:
            start = row // ROW_BLOCK * tail
            main = summed(take, slice(None))
            rest = summed(pl.ds(rows, ROW_BLOCK), slice(start, start + tail))
            total = jnp.concatenate([main, rest], axis=1)
        else:
            total = summed(take, slice(None))
        encoded_ref[take, :] = (x_ref[take, :].astype(F32) + total + bias_ref[...]).astype(BF16)
    block = 2 * HD
    mine = lax.div(where_ref[1], jnp.int32(dup))
    for head in range(head_count):
        for k in range(dest_count):
            column = ((mine ^ k) * head_count + head) * block
            weights = weight_ref[:, pl.ds(pl.multiple_of(column, block), block)]
            value = jnp.dot(encoded_ref[...], weights, preferred_element_type=F32)
            value = value + tap_ref[head, k].astype(F32)
            outs[head * dest_count + k][...] = value.astype(BF16)


def kv_projection(where, x_rows, b_down, weights, tap_part, terms, dup):
    rows, width = x_rows.shape
    head_count, dest_count = tap_part.shape[:2]
    block = 2 * HD
    outs = pl.pallas_call(
        functools.partial(kv_kernel, head_count, dest_count, dup, len(terms)),
        out_shape=[jax.ShapeDtypeStruct((rows, block), BF16)] * (head_count * dest_count),
        in_specs=[SMEM] + [VMEM] * (4 + len(terms)),
        out_specs=[VMEM] * (head_count * dest_count),
        scratch_shapes=[pltpu.VMEM((rows, width), BF16)],
        compiler_params=pltpu.CompilerParams(vmem_limit_bytes=24 * MIB),
        cost_estimate=pl.CostEstimate(
            flops=2 * rows * width * weights.shape[1],
            bytes_accessed=2 * width * weights.shape[1] + 4 * rows * weights.shape[1],
            transcendentals=0,
        ),
        name="kv_projection",
    )(where, x_rows, b_down.reshape(1, width), weights, tap_part, *terms)
    return [outs[h * dest_count : (h + 1) * dest_count] for h in range(head_count)]


def finish_kernel(term_count, picks, meta_ref, gain_ref, *refs):
    terms = refs[:term_count]
    outs = refs[term_count : term_count + len(picks)]
    done_ref = refs[-1]
    rows = terms[0].shape[0]
    for row in range(0, rows, ROW_BLOCK):
        take = pl.ds(row, ROW_BLOCK)
        total = terms[0][take, :].astype(F32)
        for term in terms[1:]:
            total = total + term[take, :].astype(F32)
        keys = total[:, :HD]
        square = jnp.sum(keys * keys, axis=1, keepdims=True) * (1.0 / HD)
        keys = keys * lax.rsqrt(square + epsilon) * gain_ref[...]
        done_ref[take, :HD] = keys.astype(BF16)
        done_ref[take, HD:] = (total[:, HD:] * VALUE_SHIFT).astype(BF16)
    for out, places in zip(outs, picks):
        for n, place in enumerate(places):
            start = pl.multiple_of(meta_ref[place] * ROW_BLOCK, ROW_BLOCK)
            out[n] = done_ref[pl.ds(start, ROW_BLOCK), :]


def finish_tiles(meta, k_gain, terms, picks):
    rows, block = terms[0].shape
    return pl.pallas_call(
        functools.partial(finish_kernel, len(terms), picks),
        out_shape=[jax.ShapeDtypeStruct((len(p), ROW_BLOCK, block), BF16) for p in picks],
        in_specs=[SMEM] + [VMEM] * (1 + len(terms)),
        out_specs=[VMEM] * len(picks),
        scratch_shapes=[pltpu.VMEM((rows, block), BF16)],
        compiler_params=pltpu.CompilerParams(vmem_limit_bytes=8 * MIB),
        cost_estimate=pl.CostEstimate(
            flops=10 * rows * block, bytes_accessed=10 * rows * block, transcendentals=rows
        ),
        name="finish_tiles",
    )(meta, k_gain.reshape(1, HD), *terms)


def query_kernel(gain_ref, query_ref, out_ref):
    gain = gain_ref[...] * (math.log2(math.e) / math.sqrt(HD))
    for col in range(0, query_ref.shape[1], HD):
        values = query_ref[:, col : col + HD].astype(F32)
        square = jnp.sum(values * values, axis=1, keepdims=True) * (1.0 / HD)
        out_ref[:, col : col + HD] = (values * lax.rsqrt(square + epsilon) * gain).astype(BF16)


def query_norm(queries, q_gain):
    rows, width = queries.shape
    step = math.gcd(rows, 128)
    return pl.pallas_call(
        query_kernel,
        out_shape=jax.ShapeDtypeStruct((rows, width), BF16),
        grid=(rows // step,),
        in_specs=[
            pl.BlockSpec((1, HD), lambda i: (0, 0)),
            pl.BlockSpec((step, width), lambda i: (i, 0)),
        ],
        out_specs=pl.BlockSpec((step, width), lambda i: (i, 0)),
        compiler_params=pltpu.CompilerParams(vmem_limit_bytes=16 * MIB),
        cost_estimate=pl.CostEstimate(
            flops=8 * rows * width, bytes_accessed=4 * rows * width, transcendentals=rows * width // HD
        ),
        name="query_norm",
    )(q_gain.reshape(1, HD), queries)


def attend_kernel(group_count, sources, has_base, meta_ref, query_ref, *refs):
    tile_refs = refs[: len(sources)]
    out_ref, key_ref, value_ref = refs[len(sources) + has_base :]
    place = meta_places(group_count)
    counts = (meta_ref[place["first"]], meta_ref[place["second"]])
    text_first, text_both = meta_ref[place["text_first"]], meta_ref[place["text_both"]]
    span = MAXT * ROW_BLOCK
    key_ref[...] = jnp.zeros_like(key_ref)
    value_ref[...] = jnp.zeros_like(value_ref)
    out_ref[...] = jnp.zeros_like(out_ref)
    for tile_ref, places in zip(tile_refs, sources):
        for n, slot in enumerate(places):
            goes = meta_ref[place["goes"] + slot]

            @pl.when(goes >= 0)
            def _(tile_ref=tile_ref, n=n, goes=goes):
                take = pl.ds(pl.multiple_of(goes * ROW_BLOCK, ROW_BLOCK), ROW_BLOCK)
                key_ref[take, :] = tile_ref[n, :, :HD]
                value_ref[take, :HD] = tile_ref[n, :, HD:]
                value_ref[take, HD:] = jnp.ones((ROW_BLOCK, HD), BF16)

    text_rows, width = query_ref.shape
    heads = width // HD
    for block in range(text_rows // ROW_BLOCK):
        start = block * ROW_BLOCK
        take = pl.ds(start, ROW_BLOCK)
        for label, (low, high) in enumerate(((0, text_first), (text_first, text_both))):
            meets = jnp.maximum(low, start) < jnp.minimum(high, start + ROW_BLOCK)

            def attend(key_rows, label=label, start=start, take=take, low=low, high=high):
                part = pl.ds(label * span, key_rows)
                slots = start + lax.broadcasted_iota(jnp.int32, (ROW_BLOCK, HD), 0)
                owned = (slots >= low) & (slots < high)
                for head in range(heads):
                    lanes = slice(head * HD, (head + 1) * HD)
                    scores = lax.dot_general(
                        query_ref[take, lanes],
                        key_ref[part, :],
                        (((1,), (1,)), ((), ())),
                        preferred_element_type=F32,
                    )
                    weights = jnp.exp2(scores).astype(BF16)
                    sums = jnp.dot(weights, value_ref[part, :], preferred_element_type=F32)
                    result = sums[:, :HD] / sums[:, HD:] * (1.0 / VALUE_SHIFT)
                    kept = out_ref[take, lanes].astype(F32)
                    out_ref[take, lanes] = jnp.where(owned, result, kept).astype(BF16)

            half = span // 2
            few = counts[label] * ROW_BLOCK <= half

            @pl.when(meets & few)
            def _(attend=attend):
                attend(half)

            @pl.when(meets & jnp.logical_not(few))
            def _(attend=attend):
                attend(span)


def attend_head(group_count, meta, queries, tiles, sources, base, head, head_count):
    rows, width = queries.shape
    head_width = width // head_count
    group_rows = REQ_G * MAXT * ROW_BLOCK
    whole_tile = pl.BlockSpec(memory_space=pltpu.VMEM)
    extra = [] if base is None else [base]
    return pl.pallas_call(
        functools.partial(attend_kernel, group_count, sources, len(extra)),
        out_shape=jax.ShapeDtypeStruct((rows, width), BF16),
        grid=(1,),
        in_specs=[
            SMEM,
            pl.BlockSpec((rows, head_width), lambda i: (0, head)),
        ]
        + [whole_tile] * len(tiles)
        + [pl.BlockSpec(memory_space=pl.ANY)] * len(extra),
        out_specs=pl.BlockSpec((rows, head_width), lambda i: (0, head)),
        scratch_shapes=[
            pltpu.VMEM((group_rows, HD), BF16),
            pltpu.VMEM((group_rows, 2 * HD), BF16),
        ],
        input_output_aliases={2 + len(tiles): 0} if extra else {},
        compiler_params=pltpu.CompilerParams(vmem_limit_bytes=24 * MIB),
        cost_estimate=pl.CostEstimate(
            flops=4 * rows * head_width * group_rows,
            bytes_accessed=4 * rows * head_width,
            transcendentals=rows * head_width // HD * group_rows // 2,
        ),
        name="attend_head",
    )(meta, queries, *tiles, *extra)


def add_rounded(a, b):
    return (a.astype(F32) + b.astype(F32)).astype(BF16)


def scatter_sum(blocks, count, first_bit):
    blocks = dict(enumerate(blocks))
    bits = bits_of(len(blocks))
    for b in range(bits):
        pairs = xor_pairs(count, 1 << (b + first_bit))
        got = {}
        for k in sorted((k for k in blocks if (k >> b) & 1), reverse=True):
            got[k ^ (1 << b)] = lax.ppermute(blocks[k], "tp", pairs)
        if b == bits - 1:
            return [blocks[0], got[0]]
        blocks = {
            k: add_rounded(blocks[k], got[k]) for k in got
        }
    return [blocks[0]]


def gather_pieces(own, count):
    pieces = {0: own}
    for b in reversed(range(bits_of(count))):
        pairs = xor_pairs(count, 1 << b)
        for k in list(pieces):
            pieces[k | (1 << b)] = lax.ppermute(pieces[k], "tp", pairs)
    return [pieces[k] for k in range(count)]


def local(
    x_in,
    taps,
    ln_gain,
    ln_bias,
    w_up,
    b_up,
    w_down,
    b_down,
    kv_w_out,
    kv_w_taps,
    k_gain,
    q_gain,
    queries,
    tiles_per_request,
    owner,
    text_per_request,
):
    group_count = lax.axis_size("grp")
    tp_count = lax.axis_size("tp")
    where = jnp.stack([lax.axis_index("grp"), lax.axis_index("tp")]).astype(jnp.int32)
    tiles_local, _, tile_rows, channel_share = x_in.shape
    local_rows = tiles_local * tile_rows
    x_rows = x_in.reshape(local_rows, channel_share)
    tap_rows = taps.reshape(local_rows, taps.shape[3])

    head_count = max(1, KVH // tp_count)
    dup = max(1, tp_count // KVH)
    dest_count = tp_count // dup

    pieces = gather_pieces(x_rows, tp_count)
    tap_part = tap_projection(where, tap_rows, kv_w_taps, head_count, dest_count, dup)
    query_rows = query_norm(queries, q_gain)
    meta = request_layout(
        group_count, tiles_local, where, tiles_per_request, owner, text_per_request
    )

    mlp_blocks = encoder_mlp(where, pieces, ln_gain, ln_bias, w_up, b_up, w_down)
    mlp_terms = scatter_sum(mlp_blocks, tp_count, 0)
    kv_blocks = kv_projection(where, x_rows, b_down, kv_w_out, tap_part, mlp_terms, dup)

    place = meta_places(group_count)
    slots = slot_count_of(group_count)
    total_tiles = group_count * tiles_local
    most_other = total_tiles - REQ_G * MAXT - REQ_G * (group_count - 2)
    one_large = group_count == 4 and slots == 2 and most_other <= group_count
    out = None
    for head in range(head_count):
        blocks = kv_blocks[head]
        for b in range(bits_of(dup)):
            pairs = xor_pairs(tp_count, 1 << b)
            blocks = [add_rounded(v, lax.ppermute(v, "tp", pairs)) for v in blocks]
        terms = scatter_sum(blocks, tp_count, bits_of(dup))
        send = place["send"]

        def move(value, mask):
            return lax.ppermute(value, "grp", xor_pairs(group_count, mask))

        if one_large:
            star = place["star"]
            picks = ((send, star), (send + 1, star), (send + 2,), (send + 3, star))
            own, near, middle, far = finish_tiles(meta, k_gain, terms, picks)
            far_got = move(far, 3)
            middle_got = move(middle, 2)
            near_got = move(near, 1)
            passed = move(far_got[1:], 1)
            tiles = (own, near_got, middle_got, far_got, passed)
            sources = ((0, 4), (1, 5), (2,), (3, 7), (6,))
        else:
            picks = tuple(
                tuple(send + s * group_count + d for s in range(slots)) for d in range(group_count)
            )
            made = finish_tiles(meta, k_gain, terms, picks)
            tiles = tuple(made[:1]) + tuple(move(made[d], d) for d in range(1, group_count))
            sources = tuple(
                tuple(s * group_count + d for s in range(slots)) for d in range(group_count)
            )
        out = attend_head(
            group_count, meta, query_rows, tiles, sources, out, head, head_count
        )
    return out


def solution(mesh):
    in_specs = (
        P(None, ("rep", "grp"), None, "tp"),
        P(None, ("rep", "grp"), None, "tp"),
        P(),
        P(),
        P(None, "tp"),
        P("tp"),
        P("tp", None),
        P("tp"),
        P("tp", None),
        P("tp", None),
        P(),
        P(),
        P(("rep", "grp"), "tp"),
        P("rep"),
        P("rep"),
        P("rep"),
    )
    out_specs = P(("rep", "grp"), "tp")
    return jax.shard_map(local, mesh=mesh, in_specs=in_specs, out_specs=out_specs, check_vma=False)
```

```python
import functools
import math

import jax
import jax.numpy as jnp
from jax import lax
from jax.experimental import pallas as pl
from jax.experimental.pallas import tpu as pltpu
from jax.sharding import PartitionSpec as P

KVH = 8
HD = 128
MAXT = 4
REQ_G = 2
LANES = 128
ROW_BLOCK = 128
HIDDEN_BLOCK = 256
VALUE_SHIFT = 2.0**-24
epsilon = 1e-05

F32 = jnp.float32
BF16 = jnp.bfloat16
VMEM = pl.BlockSpec(memory_space=pltpu.VMEM)
HBM = pl.BlockSpec(memory_space=pl.ANY)
SMEM = pl.BlockSpec(memory_space=pltpu.SMEM)
MIB = 1024 * 1024


def bits_of(count):
    bits = count.bit_length() - 1
    assert 1 << bits == count
    return bits


def xor_order(blocks, index):
    blocks = list(blocks)
    for b in range(bits_of(len(blocks))):
        swap = ((index >> b) & 1) == 1
        for k in range(len(blocks)):
            if not (k >> b) & 1:
                low, high = blocks[k], blocks[k | (1 << b)]
                blocks[k] = lax.select(swap, high, low)
                blocks[k | (1 << b)] = lax.select(swap, low, high)
    return blocks


def xor_pairs(count, mask):
    return [(i, i ^ mask) for i in range(count)]


def lane_rows(vector):
    return jnp.pad(vector, (0, -vector.shape[0] % LANES)).reshape(-1, LANES)


def one_row(ref, width):
    rows = [ref[n : n + 1, :] for n in range(ref.shape[0])]
    return (rows[0] if len(rows) == 1 else jnp.concatenate(rows, axis=1))[:, :width]


def column_step(width):
    return HIDDEN_BLOCK if width % HIDDEN_BLOCK == 0 else width


def tail_plan(rows, width):
    whole = width // LANES * LANES
    tail = width - whole
    packed = tail > 0 and rows // ROW_BLOCK * tail == whole
    return whole, tail, packed


def layout_kernel(group_count, tiles_local, where_ref, tiles_ref, owner_ref, text_ref, meta_ref):
    group = where_ref[0]
    zero = jnp.int32(0)
    firsts, counts, offsets, texts_first, texts_both = [], [], [], [], []
    offset = zero
    for p in range(group_count):
        first, count, text_first, text_both, seen = zero, zero, zero, zero, zero
        for r in range(owner_ref.shape[0]):
            mine = owner_ref[r] == p
            tiles = jnp.where(mine, tiles_ref[r], 0)
            text = jnp.where(mine, text_ref[r], 0)
            first = first + jnp.where(seen == 0, tiles, 0)
            text_first = text_first + jnp.where(seen == 0, text, 0)
            count = count + tiles
            text_both = text_both + text
            seen = seen + jnp.where(mine, 1, 0)
        firsts.append(first)
        counts.append(count)
        offsets.append(offset)
        texts_first.append(text_first)
        texts_both.append(text_both)
        offset = offset + count

    def pick(values, index):
        out = values[0]
        for p in range(1, group_count):
            out = jnp.where(index == p, values[p], out)
        return out

    slots = slot_count_of(group_count)
    star, most = zero, counts[0]
    for p in range(1, group_count):
        larger = counts[p] > most
        star = jnp.where(larger, p, star)
        most = jnp.where(larger, counts[p], most)

    def local_tile(offset, slot):
        lane = lax.rem(group - offset + group_count * REQ_G * MAXT * group_count, group_count)
        tile = lax.div(offset + slot * group_count + lane, group_count)
        return jnp.minimum(tile, tiles_local - 1)

    my_first, my_count = pick(firsts, group), pick(counts, group)
    my_offset = pick(offsets, group)
    place = meta_places(group_count)
    meta_ref[place["tp"]] = where_ref[1]
    meta_ref[place["first"]] = my_first
    meta_ref[place["second"]] = my_count - my_first
    meta_ref[place["text_first"]] = pick(texts_first, group)
    meta_ref[place["text_both"]] = pick(texts_both, group)
    meta_ref[place["star"]] = local_tile(pick(offsets, star), 1)
    for slot in range(slots):
        for d in range(group_count):
            other = group ^ d
            meta_ref[place["send"] + slot * group_count + d] = local_tile(pick(offsets, other), slot)
            lane = lax.rem(other - my_offset + group_count * REQ_G * MAXT * group_count, group_count)
            position = slot * group_count + lane
            goes = jnp.where(
                position < my_first,
                position,
                jnp.where(position < my_count, MAXT + position - my_first, -1),
            )
            meta_ref[place["goes"] + slot * group_count + d] = goes


def slot_count_of(group_count):
    return (REQ_G * MAXT + group_count - 1) // group_count


def meta_places(group_count):
    table = slot_count_of(group_count) * group_count
    return {
        "first": 0,
        "second": 1,
        "text_first": 2,
        "text_both": 3,
        "star": 4,
        "tp": 5,
        "send": 8,
        "goes": 8 + table,
        "size": 8 + 2 * table,
    }


def mlp_kernel(piece_count, place, meta_ref, *refs):
    pieces = refs[:piece_count]
    gain_ref, bias_ref, up_bias_ref, up_ref, down_ref = refs[piece_count : piece_count + 5]
    outs = refs[piece_count + 5 : 2 * piece_count + 5]
    cat_ref, normed_ref, hidden_ref, total_ref = refs[2 * piece_count + 5 :]
    index = meta_ref[place]
    tiles, width, tile_rows = pieces[0].shape
    rows = tiles * tile_rows
    channels, hidden_width = up_ref.shape
    up_step = column_step(hidden_width)
    down_step = column_step(channels)

    gain, bias = one_row(gain_ref, channels), one_row(bias_ref, channels)
    up_bias = one_row(up_bias_ref, hidden_width)
    for tile in range(tiles):
        for k, piece in enumerate(pieces):
            start = pl.multiple_of((index ^ k) * width, math.gcd(width, LANES))
            cat_ref[pl.ds(start, width), :] = piece[tile]
        values = cat_ref[...].T.astype(F32)
        average = jnp.sum(values, axis=1, keepdims=True) * (1.0 / channels)
        centered = values - average
        variance = jnp.sum(centered * centered, axis=1, keepdims=True) * (1.0 / channels)
        normed = centered * lax.rsqrt(variance + epsilon)
        normed = normed * gain + bias
        normed_ref[tile * tile_rows : (tile + 1) * tile_rows, :] = normed.astype(BF16)
    for n in range(hidden_width // up_step):
        take = slice(n * up_step, (n + 1) * up_step)
        value = jnp.dot(normed_ref[...], up_ref[:, take], preferred_element_type=F32)
        value = value + up_bias[:, take]
        value = 0.5 * value * (1.0 + lax.erf(value * (1.0 / math.sqrt(2.0))))
        hidden_ref[:, take] = value.astype(BF16)
    for n in range(channels // down_step):
        take = slice(n * down_step, (n + 1) * down_step)
        total_ref[:, take] = jnp.dot(
            hidden_ref[...], down_ref[:, take], preferred_element_type=F32
        )
    whole, tail, packed = tail_plan(rows, width)
    for row in range(0, rows, ROW_BLOCK):
        take = pl.ds(row, ROW_BLOCK)
        blocks = [total_ref[take, j * width : (j + 1) * width] for j in range(piece_count)]
        for out, block in zip(outs, xor_order(blocks, index)):
            block = block.astype(BF16)
            if packed:
                part = row // ROW_BLOCK
                out[take, :] = block[:, :whole]
                out[rows : rows + ROW_BLOCK, part * tail : (part + 1) * tail] = block[:, whole:]
            else:
                out[take, :] = block


def encoder_mlp(meta, place, pieces, ln_gain, ln_bias, w_up, b_up, w_down):
    tiles, width, tile_rows = pieces[0].shape
    rows = tiles * tile_rows
    count = len(pieces)
    channels, hidden_width = w_up.shape
    whole, _, packed = tail_plan(rows, width)
    shape = (rows + ROW_BLOCK, whole) if packed else (rows, width)
    return pl.pallas_call(
        functools.partial(mlp_kernel, count, place),
        out_shape=[jax.ShapeDtypeStruct(shape, BF16)] * count,
        in_specs=[SMEM] + [VMEM] * (count + 5),
        out_specs=[VMEM] * count,
        scratch_shapes=[
            pltpu.VMEM((channels, tile_rows), BF16),
            pltpu.VMEM((rows, channels), BF16),
            pltpu.VMEM((rows, hidden_width), BF16),
            pltpu.VMEM((rows, channels), F32),
        ],
        compiler_params=pltpu.CompilerParams(vmem_limit_bytes=44 * MIB),
        cost_estimate=pl.CostEstimate(
            flops=4 * rows * channels * hidden_width,
            bytes_accessed=4 * channels * hidden_width + 4 * rows * channels,
            transcendentals=rows * hidden_width,
        ),
        name="encoder_mlp",
    )(
        meta,
        *pieces,
        lane_rows(ln_gain),
        lane_rows(ln_bias),
        lane_rows(b_up),
        w_up,
        w_down,
    )


def prepare_kernel(
    group_count,
    tiles_local,
    where_ref,
    tiles_ref,
    owner_ref,
    text_ref,
    gain_ref,
    tap_ref,
    weight_ref,
    query_ref,
    out_ref,
    normed_ref,
    meta_ref,
    row_ref,
):
    @pl.when(pl.program_id(0) == 0)
    def _():
        layout_kernel(
            group_count, tiles_local, where_ref, tiles_ref, owner_ref, text_ref, meta_ref
        )
        tiles, _, tile_rows = tap_ref.shape
        for tile in range(tiles):
            row_ref[tile * tile_rows : (tile + 1) * tile_rows, :] = tap_ref[tile].T

    out_ref[...] = jnp.dot(
        row_ref[...], weight_ref[...], preferred_element_type=F32
    ).astype(BF16)[None, None]
    gain = gain_ref[...] * (math.log2(math.e) / math.sqrt(HD))
    for col in range(0, query_ref.shape[1], HD):
        values = query_ref[:, col : col + HD].astype(F32)
        square = jnp.sum(values * values, axis=1, keepdims=True) * (1.0 / HD)
        normed_ref[:, col : col + HD] = (values * lax.rsqrt(square + epsilon) * gain).astype(BF16)


def prepare(
    where, requests, q_gain, tap_tiles, weights, queries, group_count, head_count, dest_count, dup
):
    tiles, depth, tile_rows = tap_tiles.shape
    rows = tiles * tile_rows
    block = 2 * HD
    steps = head_count * dest_count
    text_rows, width = queries.shape
    query_step = text_rows // steps
    meta_size = meta_places(group_count)["size"]

    def head_of(n, where_ref):
        dest = lax.div(where_ref[1], jnp.int32(dup)) ^ lax.rem(n, dest_count)
        return dest * head_count + lax.div(n, dest_count)

    return pl.pallas_call(
        functools.partial(prepare_kernel, group_count, tiles),
        out_shape=[
            jax.ShapeDtypeStruct((head_count, dest_count, rows, block), BF16),
            jax.ShapeDtypeStruct((text_rows, width), BF16),
            jax.ShapeDtypeStruct((meta_size,), jnp.int32),
        ],
        grid_spec=pltpu.PrefetchScalarGridSpec(
            num_scalar_prefetch=1,
            grid=(steps,),
            in_specs=[
                SMEM,
                SMEM,
                SMEM,
                pl.BlockSpec((1, HD), lambda n, w: (0, 0)),
                pl.BlockSpec(tap_tiles.shape, lambda n, w: (0, 0, 0)),
                pl.BlockSpec((depth, block), lambda n, w: (0, head_of(n, w))),
                pl.BlockSpec((query_step, width), lambda n, w: (n, 0)),
            ],
            out_specs=[
                pl.BlockSpec(
                    (1, 1, rows, block),
                    lambda n, w: (lax.div(n, dest_count), lax.rem(n, dest_count), 0, 0),
                ),
                pl.BlockSpec((query_step, width), lambda n, w: (n, 0)),
                SMEM,
            ],
            scratch_shapes=[pltpu.VMEM((rows, depth), BF16)],
        ),
        compiler_params=pltpu.CompilerParams(vmem_limit_bytes=44 * MIB),
        cost_estimate=pl.CostEstimate(
            flops=2 * rows * depth * weights.shape[1],
            bytes_accessed=2 * depth * weights.shape[1],
            transcendentals=0,
        ),
        name="prepare",
    )(where, *requests, lane_rows(q_gain), tap_tiles, weights, queries)


def kv_kernel(head_count, dest_count, dup, place, term_count, meta_ref, *refs):
    x_ref, bias_ref, weight_ref, tap_ref = refs[:4]
    terms = refs[4 : 4 + term_count]
    outs = refs[4 + term_count : -1]
    encoded_ref = refs[-1]
    tiles, width, tile_rows = x_ref.shape
    rows = tiles * tile_rows
    whole, tail, packed = tail_plan(rows, width)
    bias = one_row(bias_ref, width)
    for row in range(0, rows, ROW_BLOCK):
        take = pl.ds(row, ROW_BLOCK)

        def summed(part, lanes):
            out = terms[0][part, lanes].astype(F32)
            for term in terms[1:]:
                out = out + term[part, lanes].astype(F32)
            return out

        if packed:
            start = row // ROW_BLOCK * tail
            main = summed(take, slice(None))
            rest = summed(pl.ds(rows, ROW_BLOCK), slice(start, start + tail))
            total = jnp.concatenate([main, rest], axis=1)
        else:
            total = summed(take, slice(None))
        total = total + x_ref[row // ROW_BLOCK].T.astype(F32)
        total = total + bias
        encoded_ref[take, :] = total.astype(BF16)
    block = 2 * HD
    mine = lax.div(meta_ref[place], jnp.int32(dup))
    for head in range(head_count):
        for k in range(dest_count):
            column = ((mine ^ k) * head_count + head) * block
            weights = weight_ref[:, pl.ds(pl.multiple_of(column, block), block)]
            value = jnp.dot(encoded_ref[...], weights, preferred_element_type=F32)
            value = value + tap_ref[head, k].astype(F32)
            outs[head * dest_count + k][...] = value.astype(BF16)


def kv_projection(meta, place, x_tiles, b_down, weights, tap_part, terms, dup):
    tiles, width, tile_rows = x_tiles.shape
    rows = tiles * tile_rows
    head_count, dest_count = tap_part.shape[:2]
    block = 2 * HD
    outs = pl.pallas_call(
        functools.partial(kv_kernel, head_count, dest_count, dup, place, len(terms)),
        out_shape=[jax.ShapeDtypeStruct((rows, block), BF16)] * (head_count * dest_count),
        in_specs=[SMEM] + [VMEM] * (4 + len(terms)),
        out_specs=[VMEM] * (head_count * dest_count),
        scratch_shapes=[pltpu.VMEM((rows, width), BF16)],
        compiler_params=pltpu.CompilerParams(vmem_limit_bytes=24 * MIB),
        cost_estimate=pl.CostEstimate(
            flops=2 * rows * width * weights.shape[1],
            bytes_accessed=2 * width * weights.shape[1] + 4 * rows * weights.shape[1],
            transcendentals=0,
        ),
        name="kv_projection",
    )(meta, x_tiles, lane_rows(b_down), weights, tap_part, *terms)
    return [outs[h * dest_count : (h + 1) * dest_count] for h in range(head_count)]


def finish_kernel(term_count, picks, meta_ref, gain_ref, *refs):
    terms = refs[:term_count]
    outs = refs[term_count : term_count + len(picks)]
    done_ref = refs[-1]
    rows = terms[0].shape[0]
    for row in range(0, rows, ROW_BLOCK):
        take = pl.ds(row, ROW_BLOCK)
        total = terms[0][take, :].astype(F32)
        for term in terms[1:]:
            total = total + term[take, :].astype(F32)
        keys = total[:, :HD]
        square = jnp.sum(keys * keys, axis=1, keepdims=True) * (1.0 / HD)
        keys = keys * lax.rsqrt(square + epsilon) * gain_ref[...]
        done_ref[take, :HD] = keys.astype(BF16)
        done_ref[take, HD:] = (total[:, HD:] * VALUE_SHIFT).astype(BF16)
    for out, places in zip(outs, picks):
        for n, place in enumerate(places):
            start = pl.multiple_of(meta_ref[place] * ROW_BLOCK, ROW_BLOCK)
            out[n] = done_ref[pl.ds(start, ROW_BLOCK), :]


def finish_tiles(meta, k_gain, terms, picks):
    rows, block = terms[0].shape
    return pl.pallas_call(
        functools.partial(finish_kernel, len(terms), picks),
        out_shape=[jax.ShapeDtypeStruct((len(p), ROW_BLOCK, block), BF16) for p in picks],
        in_specs=[SMEM] + [VMEM] * (1 + len(terms)),
        out_specs=[VMEM] * len(picks),
        scratch_shapes=[pltpu.VMEM((rows, block), BF16)],
        compiler_params=pltpu.CompilerParams(vmem_limit_bytes=8 * MIB),
        cost_estimate=pl.CostEstimate(
            flops=10 * rows * block, bytes_accessed=10 * rows * block, transcendentals=rows
        ),
        name="finish_tiles",
    )(meta, lane_rows(k_gain), *terms)


def attend_kernel(group_count, sources, has_base, meta_ref, query_ref, *refs):
    tile_refs = refs[: len(sources)]
    out_ref, key_ref, value_ref = refs[len(sources) + has_base :]
    place = meta_places(group_count)
    counts = (meta_ref[place["first"]], meta_ref[place["second"]])
    text_first, text_both = meta_ref[place["text_first"]], meta_ref[place["text_both"]]
    span = MAXT * ROW_BLOCK
    key_ref[...] = jnp.zeros_like(key_ref)
    value_ref[...] = jnp.zeros_like(value_ref)
    out_ref[...] = jnp.zeros_like(out_ref)
    for tile_ref, places in zip(tile_refs, sources):
        for n, slot in enumerate(places):
            goes = meta_ref[place["goes"] + slot]

            @pl.when(goes >= 0)
            def _(tile_ref=tile_ref, n=n, goes=goes):
                take = pl.ds(pl.multiple_of(goes * ROW_BLOCK, ROW_BLOCK), ROW_BLOCK)
                key_ref[take, :] = tile_ref[n, :, :HD]
                value_ref[take, :HD] = tile_ref[n, :, HD:]
                value_ref[take, HD:] = jnp.ones((ROW_BLOCK, HD), BF16)

    text_rows, width = query_ref.shape
    heads = width // HD
    for block in range(text_rows // ROW_BLOCK):
        start = block * ROW_BLOCK
        take = pl.ds(start, ROW_BLOCK)
        for label, (low, high) in enumerate(((0, text_first), (text_first, text_both))):
            meets = jnp.maximum(low, start) < jnp.minimum(high, start + ROW_BLOCK)

            def attend(key_rows, label=label, start=start, take=take, low=low, high=high):
                part = pl.ds(label * span, key_rows)
                slots = start + lax.broadcasted_iota(jnp.int32, (ROW_BLOCK, HD), 0)
                owned = (slots >= low) & (slots < high)
                for head in range(heads):
                    lanes = slice(head * HD, (head + 1) * HD)
                    scores = lax.dot_general(
                        query_ref[take, lanes],
                        key_ref[part, :],
                        (((1,), (1,)), ((), ())),
                        preferred_element_type=F32,
                    )
                    weights = jnp.exp2(scores).astype(BF16)
                    sums = jnp.dot(weights, value_ref[part, :], preferred_element_type=F32)
                    result = sums[:, :HD] / sums[:, HD:] * (1.0 / VALUE_SHIFT)
                    kept = out_ref[take, lanes].astype(F32)
                    out_ref[take, lanes] = jnp.where(owned, result, kept).astype(BF16)

            half = span // 2
            few = counts[label] * ROW_BLOCK <= half

            @pl.when(meets & few)
            def _(attend=attend):
                attend(half)

            @pl.when(meets & jnp.logical_not(few))
            def _(attend=attend):
                attend(span)


def attend_head(group_count, meta, queries, tiles, sources, base, head, head_count):
    rows, width = queries.shape
    head_width = width // head_count
    group_rows = REQ_G * MAXT * ROW_BLOCK
    whole_tile = pl.BlockSpec(memory_space=pltpu.VMEM)
    extra = [] if base is None else [base]
    return pl.pallas_call(
        functools.partial(attend_kernel, group_count, sources, len(extra)),
        out_shape=jax.ShapeDtypeStruct((rows, width), BF16),
        grid=(1,),
        in_specs=[
            SMEM,
            pl.BlockSpec((rows, head_width), lambda i: (0, head)),
        ]
        + [whole_tile] * len(tiles)
        + [pl.BlockSpec(memory_space=pl.ANY)] * len(extra),
        out_specs=pl.BlockSpec((rows, head_width), lambda i: (0, head)),
        scratch_shapes=[
            pltpu.VMEM((group_rows, HD), BF16),
            pltpu.VMEM((group_rows, 2 * HD), BF16),
        ],
        input_output_aliases={2 + len(tiles): 0} if extra else {},
        compiler_params=pltpu.CompilerParams(vmem_limit_bytes=24 * MIB),
        cost_estimate=pl.CostEstimate(
            flops=4 * rows * head_width * group_rows,
            bytes_accessed=4 * rows * head_width,
            transcendentals=rows * head_width // HD * group_rows // 2,
        ),
        name="attend_head",
    )(meta, queries, *tiles, *extra)


def add_rounded(a, b):
    return (a.astype(F32) + b.astype(F32)).astype(BF16)


def scatter_sum(blocks, count, first_bit):
    blocks = dict(enumerate(blocks))
    bits = bits_of(len(blocks))
    for b in range(bits):
        pairs = xor_pairs(count, 1 << (b + first_bit))
        got = {}
        for k in sorted((k for k in blocks if (k >> b) & 1), reverse=True):
            got[k ^ (1 << b)] = lax.ppermute(blocks[k], "tp", pairs)
        if b == bits - 1:
            return [blocks[0], got[0]]
        blocks = {
            k: add_rounded(blocks[k], got[k]) for k in got
        }
    return [blocks[0]]


def gather_pieces(own, count, ready):
    bits = bits_of(count)
    pieces = {0: own}
    for b in reversed(range(bits)):
        pairs = xor_pairs(count, 1 << b)
        for k in sorted(pieces):
            block = pieces[k]
            if b == 0 and k:
                block, ready = lax.optimization_barrier((block, ready))
            pieces[k | (1 << b)] = lax.ppermute(block, "tp", pairs)
    return [pieces[k] for k in range(count)], ready


def local(
    x_in,
    taps,
    ln_gain,
    ln_bias,
    w_up,
    b_up,
    w_down,
    b_down,
    kv_w_out,
    kv_w_taps,
    k_gain,
    q_gain,
    queries,
    tiles_per_request,
    owner,
    text_per_request,
):
    group_count = lax.axis_size("grp")
    tp_count = lax.axis_size("tp")
    where = jnp.stack([lax.axis_index("grp"), lax.axis_index("tp")]).astype(jnp.int32)
    tiles_local = x_in.shape[0]
    x_tiles = jnp.swapaxes(x_in, 2, 3)[:, 0]
    tap_tiles = jnp.swapaxes(taps, 2, 3)[:, 0]
    head_count = max(1, KVH // tp_count)
    dup = max(1, tp_count // KVH)
    dest_count = tp_count // dup
    place = meta_places(group_count)

    tap_part, query_rows, meta = prepare(
        where,
        (tiles_per_request, owner, text_per_request),
        q_gain,
        tap_tiles,
        kv_w_taps,
        queries,
        group_count,
        head_count,
        dest_count,
        dup,
    )
    pieces, meta = gather_pieces(x_tiles, tp_count, meta)
    mlp_blocks = encoder_mlp(
        meta, place["tp"], pieces, ln_gain, ln_bias, w_up, b_up, w_down
    )
    mlp_terms = scatter_sum(mlp_blocks, tp_count, 0)
    kv_blocks = kv_projection(
        meta, place["tp"], x_tiles, b_down, kv_w_out, tap_part, mlp_terms, dup
    )

    slots = slot_count_of(group_count)
    total_tiles = group_count * tiles_local
    most_other = total_tiles - REQ_G * MAXT - REQ_G * (group_count - 2)
    one_large = group_count == 4 and slots == 2 and most_other <= group_count
    out = None
    for head in range(head_count):
        blocks = kv_blocks[head]
        for b in range(bits_of(dup)):
            pairs = xor_pairs(tp_count, 1 << b)
            blocks = [add_rounded(v, lax.ppermute(v, "tp", pairs)) for v in blocks]
        terms = scatter_sum(blocks, tp_count, bits_of(dup))
        send = place["send"]

        def move(value, mask):
            return lax.ppermute(value, "grp", xor_pairs(group_count, mask))

        if one_large:
            star = place["star"]
            picks = ((send, star), (send + 1, star), (send + 2,), (send + 3, star))
            own, near, middle, far = finish_tiles(meta, k_gain, terms, picks)
            far_got = move(far, 3)
            middle_got = move(middle, 2)
            near_got = move(near, 1)
            passed = move(far_got[1:], 1)
            tiles = (own, near_got, middle_got, far_got, passed)
            sources = ((0, 4), (1, 5), (2,), (3, 7), (6,))
        else:
            picks = tuple(
                tuple(send + s * group_count + d for s in range(slots)) for d in range(group_count)
            )
            made = finish_tiles(meta, k_gain, terms, picks)
            tiles = tuple(made[:1]) + tuple(move(made[d], d) for d in range(1, group_count))
            sources = tuple(
                tuple(s * group_count + d for s in range(slots)) for d in range(group_count)
            )
        out = attend_head(
            group_count, meta, query_rows, tiles, sources, out, head, head_count
        )
    return out


def solution(mesh):
    in_specs = (
        P(None, ("rep", "grp"), None, "tp"),
        P(None, ("rep", "grp"), None, "tp"),
        P(),
        P(),
        P(None, "tp"),
        P("tp"),
        P("tp", None),
        P("tp"),
        P("tp", None),
        P("tp", None),
        P(),
        P(),
        P(("rep", "grp"), "tp"),
        P("rep"),
        P("rep"),
        P("rep"),
    )
    out_specs = P(("rep", "grp"), "tp")
    return jax.shard_map(local, mesh=mesh, in_specs=in_specs, out_specs=out_specs, check_vma=False)
```

```python
import functools
import math

import jax
import jax.numpy as jnp
from jax import lax
from jax.experimental import pallas as pl
from jax.experimental.pallas import tpu as pltpu
from jax.sharding import PartitionSpec as P

KVH = 8
HD = 128
MAXT = 4
REQ_G = 2
LANES = 128
ROW_BLOCK = 128
HIDDEN_BLOCK = 256
VALUE_SHIFT = 2.0**-24
epsilon = 1e-05

F32 = jnp.float32
BF16 = jnp.bfloat16
VMEM = pl.BlockSpec(memory_space=pltpu.VMEM)
HBM = pl.BlockSpec(memory_space=pl.ANY)
SMEM = pl.BlockSpec(memory_space=pltpu.SMEM)
MIB = 1024 * 1024
LIGHT = pl.CostEstimate(flops=1024, bytes_accessed=1024, transcendentals=0)


def bits_of(count):
    bits = count.bit_length() - 1
    assert 1 << bits == count
    return bits


def xor_order(blocks, index):
    blocks = list(blocks)
    for b in range(bits_of(len(blocks))):
        swap = ((index >> b) & 1) == 1
        for k in range(len(blocks)):
            if not (k >> b) & 1:
                low, high = blocks[k], blocks[k | (1 << b)]
                blocks[k] = lax.select(swap, high, low)
                blocks[k | (1 << b)] = lax.select(swap, low, high)
    return blocks


def xor_pairs(count, mask):
    return [(i, i ^ mask) for i in range(count)]


def lane_rows(vector):
    return jnp.pad(vector, (0, -vector.shape[0] % LANES)).reshape(-1, LANES)


def one_row(ref, width):
    rows = [ref[n : n + 1, :] for n in range(ref.shape[0])]
    return (rows[0] if len(rows) == 1 else jnp.concatenate(rows, axis=1))[:, :width]


def column_step(width):
    return HIDDEN_BLOCK if width % HIDDEN_BLOCK == 0 else width


def tail_plan(rows, width):
    whole = width // LANES * LANES
    tail = width - whole
    packed = tail > 0 and whole > 0 and whole % tail == 0 and rows * tail % whole == 0
    extra = rows * tail // whole if packed else 0
    packed = packed and extra % 16 == 0 and ROW_BLOCK % extra == 0
    return whole, tail, extra if packed else 0


def sent_shape(rows, width):
    whole, _, extra = tail_plan(rows, width)
    return (rows + extra, whole) if extra else (rows, width)


def layout_kernel(group_count, tiles_local, where_ref, tiles_ref, owner_ref, text_ref, meta_ref):
    group = where_ref[0]
    zero = jnp.int32(0)
    firsts, counts, offsets, texts_first, texts_both = [], [], [], [], []
    offset = zero
    for p in range(group_count):
        first, count, text_first, text_both, seen = zero, zero, zero, zero, zero
        for r in range(owner_ref.shape[0]):
            mine = owner_ref[r] == p
            tiles = jnp.where(mine, tiles_ref[r], 0)
            text = jnp.where(mine, text_ref[r], 0)
            first = first + jnp.where(seen == 0, tiles, 0)
            text_first = text_first + jnp.where(seen == 0, text, 0)
            count = count + tiles
            text_both = text_both + text
            seen = seen + jnp.where(mine, 1, 0)
        firsts.append(first)
        counts.append(count)
        offsets.append(offset)
        texts_first.append(text_first)
        texts_both.append(text_both)
        offset = offset + count

    def pick(values, index):
        out = values[0]
        for p in range(1, group_count):
            out = jnp.where(index == p, values[p], out)
        return out

    slots = slot_count_of(group_count)
    star, most = zero, counts[0]
    for p in range(1, group_count):
        larger = counts[p] > most
        star = jnp.where(larger, p, star)
        most = jnp.where(larger, counts[p], most)

    def local_tile(offset, slot):
        lane = lax.rem(group - offset + group_count * REQ_G * MAXT * group_count, group_count)
        tile = lax.div(offset + slot * group_count + lane, group_count)
        return jnp.minimum(tile, tiles_local - 1)

    my_first, my_count = pick(firsts, group), pick(counts, group)
    my_offset = pick(offsets, group)
    place = meta_places(group_count)
    meta_ref[place["tp"]] = where_ref[1]
    meta_ref[place["first"]] = my_first
    meta_ref[place["second"]] = my_count - my_first
    meta_ref[place["text_first"]] = pick(texts_first, group)
    meta_ref[place["text_both"]] = pick(texts_both, group)
    meta_ref[place["star"]] = local_tile(pick(offsets, star), 1)
    for slot in range(slots):
        for d in range(group_count):
            other = group ^ d
            meta_ref[place["send"] + slot * group_count + d] = local_tile(pick(offsets, other), slot)
            lane = lax.rem(other - my_offset + group_count * REQ_G * MAXT * group_count, group_count)
            position = slot * group_count + lane
            goes = jnp.where(
                position < my_first,
                position,
                jnp.where(position < my_count, MAXT + position - my_first, -1),
            )
            meta_ref[place["goes"] + slot * group_count + d] = goes


def slot_count_of(group_count):
    return (REQ_G * MAXT + group_count - 1) // group_count


def meta_places(group_count):
    table = slot_count_of(group_count) * group_count
    return {
        "first": 0,
        "second": 1,
        "text_first": 2,
        "text_both": 3,
        "star": 4,
        "tp": 5,
        "send": 8,
        "goes": 8 + table,
        "size": 8 + 2 * table,
    }


def mlp_kernel(piece_count, bases, tiles, place, meta_ref, *refs):
    pieces = refs[:piece_count]
    gain_ref, bias_ref, up_bias_ref, up_ref, down_ref = refs[piece_count : piece_count + 5]
    outs = refs[piece_count + 5 : 2 * piece_count + 5]
    cat_ref, normed_ref, hidden_ref, total_ref = refs[2 * piece_count + 5 :]
    index = meta_ref[place]
    _, width, tile_rows = pieces[0].shape
    rows = tiles * tile_rows
    channels, hidden_width = up_ref.shape
    up_step = column_step(hidden_width)
    down_step = column_step(channels)

    gain, bias = one_row(gain_ref, channels), one_row(bias_ref, channels)
    up_bias = one_row(up_bias_ref, hidden_width)
    for tile in range(tiles):
        for k, piece in enumerate(pieces):
            start = pl.multiple_of((index ^ k) * width, math.gcd(width, LANES))
            cat_ref[pl.ds(start, width), :] = piece[bases[k] + tile]
        values = cat_ref[...].T.astype(F32)
        average = jnp.sum(values, axis=1, keepdims=True) * (1.0 / channels)
        centered = values - average
        variance = jnp.sum(centered * centered, axis=1, keepdims=True) * (1.0 / channels)
        normed = centered * lax.rsqrt(variance + epsilon)
        normed = normed * gain + bias
        normed_ref[tile * tile_rows : (tile + 1) * tile_rows, :] = normed.astype(BF16)
    for n in range(hidden_width // up_step):
        take = slice(n * up_step, (n + 1) * up_step)
        value = jnp.dot(normed_ref[...], up_ref[:, take], preferred_element_type=F32)
        value = value + up_bias[:, take]
        value = 0.5 * value * (1.0 + lax.erf(value * (1.0 / math.sqrt(2.0))))
        hidden_ref[:, take] = value.astype(BF16)
    for n in range(channels // down_step):
        take = slice(n * down_step, (n + 1) * down_step)
        total_ref[:, take] = jnp.dot(
            hidden_ref[...], down_ref[:, take], preferred_element_type=F32
        )
    whole, tail, extra = tail_plan(rows, width)
    step = extra or ROW_BLOCK
    for part in range(rows // step):
        take = pl.ds(part * step, step)
        blocks = [total_ref[take, j * width : (j + 1) * width] for j in range(piece_count)]
        for out, block in zip(outs, xor_order(blocks, index)):
            block = block.astype(BF16)
            if extra:
                out[take, :] = block[:, :whole]
                out[rows : rows + extra, part * tail : (part + 1) * tail] = block[:, whole:]
            else:
                out[take, :] = block


def encoder_mlp(meta, place, pieces, bases, tiles, ln_gain, ln_bias, w_up, b_up, w_down):
    _, width, tile_rows = pieces[0].shape
    rows = tiles * tile_rows
    count = len(pieces)
    channels, hidden_width = w_up.shape
    shape = sent_shape(rows, width)
    return pl.pallas_call(
        functools.partial(mlp_kernel, count, bases, tiles, place),
        out_shape=[jax.ShapeDtypeStruct(shape, BF16)] * count,
        in_specs=[SMEM] + [VMEM] * (count + 5),
        out_specs=[VMEM] * count,
        scratch_shapes=[
            pltpu.VMEM((channels, tile_rows), BF16),
            pltpu.VMEM((rows, channels), BF16),
            pltpu.VMEM((rows, hidden_width), BF16),
            pltpu.VMEM((rows, channels), F32),
        ],
        compiler_params=pltpu.CompilerParams(vmem_limit_bytes=44 * MIB),
        cost_estimate=LIGHT,
        name="encoder_mlp",
    )(
        meta,
        *pieces,
        lane_rows(ln_gain),
        lane_rows(ln_bias),
        lane_rows(b_up),
        w_up,
        w_down,
    )


def prepare_kernel(
    group_count,
    tiles_local,
    where_ref,
    tiles_ref,
    owner_ref,
    text_ref,
    gain_ref,
    query_ref,
    normed_ref,
    meta_ref,
):
    @pl.when(pl.program_id(0) == 0)
    def _():
        layout_kernel(
            group_count, tiles_local, where_ref, tiles_ref, owner_ref, text_ref, meta_ref
        )

    gain = gain_ref[...] * (math.log2(math.e) / math.sqrt(HD))
    for col in range(0, query_ref.shape[1], HD):
        values = query_ref[:, col : col + HD].astype(F32)
        square = jnp.sum(values * values, axis=1, keepdims=True) * (1.0 / HD)
        normed_ref[:, col : col + HD] = (values * lax.rsqrt(square + epsilon) * gain).astype(BF16)


def prepare(where, requests, q_gain, queries, group_count, tiles_local):
    text_rows, width = queries.shape
    step = ROW_BLOCK
    return pl.pallas_call(
        functools.partial(prepare_kernel, group_count, tiles_local),
        out_shape=[
            jax.ShapeDtypeStruct((text_rows, width), BF16),
            jax.ShapeDtypeStruct((meta_places(group_count)["size"],), jnp.int32),
        ],
        grid=(text_rows // step,),
        in_specs=[
            SMEM,
            SMEM,
            SMEM,
            SMEM,
            pl.BlockSpec((1, HD), lambda n: (0, 0)),
            pl.BlockSpec((step, width), lambda n: (n, 0)),
        ],
        out_specs=[pl.BlockSpec((step, width), lambda n: (n, 0)), SMEM],
        compiler_params=pltpu.CompilerParams(vmem_limit_bytes=16 * MIB),
        cost_estimate=LIGHT,
        name="prepare",
    )(where, *requests, lane_rows(q_gain), queries)


def tap_kernel(meta_ref, tap_ref, weight_ref, out_ref, row_ref):
    @pl.when(pl.program_id(0) == 0)
    def _():
        tiles, _, tile_rows = tap_ref.shape
        for tile in range(tiles):
            row_ref[tile * tile_rows : (tile + 1) * tile_rows, :] = tap_ref[tile].T

    out_ref[...] = jnp.dot(
        row_ref[...], weight_ref[...], preferred_element_type=F32
    ).astype(BF16)[None, None]


def tap_projection(meta, place, tap_tiles, weights, head_count, dest_count, dup):
    tiles, depth, tile_rows = tap_tiles.shape
    rows = tiles * tile_rows
    block = 2 * HD

    def head_of(n, meta_ref):
        dest = lax.div(meta_ref[place], jnp.int32(dup)) ^ lax.rem(n, dest_count)
        return dest * head_count + lax.div(n, dest_count)

    return pl.pallas_call(
        tap_kernel,
        out_shape=jax.ShapeDtypeStruct((head_count, dest_count, rows, block), BF16),
        grid_spec=pltpu.PrefetchScalarGridSpec(
            num_scalar_prefetch=1,
            grid=(head_count * dest_count,),
            in_specs=[
                pl.BlockSpec(tap_tiles.shape, lambda n, w: (0, 0, 0)),
                pl.BlockSpec((depth, block), lambda n, w: (0, head_of(n, w))),
            ],
            out_specs=pl.BlockSpec(
                (1, 1, rows, block),
                lambda n, w: (lax.div(n, dest_count), lax.rem(n, dest_count), 0, 0),
            ),
            scratch_shapes=[pltpu.VMEM((rows, depth), BF16)],
        ),
        compiler_params=pltpu.CompilerParams(vmem_limit_bytes=16 * MIB),
        cost_estimate=LIGHT,
        name="tap_projection",
    )(meta, tap_tiles, weights)


def kv_kernel(head_count, dest_count, dup, place, term_counts, meta_ref, *refs):
    x_ref, bias_ref, weight_ref, tap_ref = refs[:4]
    terms = refs[4 : 4 + sum(term_counts)]
    outs = refs[4 + sum(term_counts) : -1]
    encoded_ref = refs[-1]
    tiles, width, tile_rows = x_ref.shape
    half_tiles = tiles // len(term_counts)
    whole, tail, extra = tail_plan(half_tiles * tile_rows, width)
    bias = one_row(bias_ref, width)
    for tile in range(tiles):
        half, row = tile // half_tiles, tile % half_tiles * tile_rows
        mine = terms[sum(term_counts[:half]) : sum(term_counts[: half + 1])]

        def summed(part, lanes):
            out = mine[0][part, lanes].astype(F32)
            for term in mine[1:]:
                out = out + term[part, lanes].astype(F32)
            return out

        total = summed(pl.ds(row, tile_rows), slice(None))
        if extra:
            chunks = range(row // extra, (row + tile_rows) // extra)
            rest = [
                summed(pl.ds(half_tiles * tile_rows, extra), slice(c * tail, (c + 1) * tail))
                for c in chunks
            ]
            rest = rest[0] if len(rest) == 1 else jnp.concatenate(rest, axis=0)
            total = jnp.concatenate([total, rest], axis=1)
        total = total + x_ref[tile].T.astype(F32) + bias
        encoded_ref[tile * tile_rows : (tile + 1) * tile_rows, :] = total.astype(BF16)
    block = 2 * HD
    mine = lax.div(meta_ref[place], jnp.int32(dup))
    for head in range(head_count):
        for k in range(dest_count):
            column = ((mine ^ k) * head_count + head) * block
            weights = weight_ref[:, pl.ds(pl.multiple_of(column, block), block)]
            value = jnp.dot(encoded_ref[...], weights, preferred_element_type=F32)
            value = value + tap_ref[head, k].astype(F32)
            outs[head * dest_count + k][...] = value.astype(BF16)


def kv_projection(meta, place, x_tiles, b_down, weights, tap_part, halves, dup):
    terms = [term for half in halves for term in half]
    tiles, width, tile_rows = x_tiles.shape
    rows = tiles * tile_rows
    head_count, dest_count = tap_part.shape[:2]
    block = 2 * HD
    outs = pl.pallas_call(
        functools.partial(
            kv_kernel, head_count, dest_count, dup, place, tuple(len(half) for half in halves)
        ),
        out_shape=[jax.ShapeDtypeStruct((rows, block), BF16)] * (head_count * dest_count),
        in_specs=[SMEM] + [VMEM] * (4 + len(terms)),
        out_specs=[VMEM] * (head_count * dest_count),
        scratch_shapes=[pltpu.VMEM((rows, width), BF16)],
        compiler_params=pltpu.CompilerParams(vmem_limit_bytes=24 * MIB),
        cost_estimate=LIGHT,
        name="kv_projection",
    )(meta, x_tiles, lane_rows(b_down), weights, tap_part, *terms)
    return [outs[h * dest_count : (h + 1) * dest_count] for h in range(head_count)]


def finish_kernel(term_count, picks, meta_ref, gain_ref, *refs):
    terms = refs[:term_count]
    outs = refs[term_count : term_count + len(picks)]
    done_ref = refs[-1]
    rows = terms[0].shape[0]
    for row in range(0, rows, ROW_BLOCK):
        take = pl.ds(row, ROW_BLOCK)
        total = terms[0][take, :].astype(F32)
        for term in terms[1:]:
            total = total + term[take, :].astype(F32)
        keys = total[:, :HD]
        square = jnp.sum(keys * keys, axis=1, keepdims=True) * (1.0 / HD)
        keys = keys * lax.rsqrt(square + epsilon) * gain_ref[...]
        done_ref[take, :HD] = keys.astype(BF16)
        done_ref[take, HD:] = (total[:, HD:] * VALUE_SHIFT).astype(BF16)
    for out, places in zip(outs, picks):
        for n, place in enumerate(places):
            start = pl.multiple_of(meta_ref[place] * ROW_BLOCK, ROW_BLOCK)
            out[n] = done_ref[pl.ds(start, ROW_BLOCK), :]


def finish_tiles(meta, k_gain, terms, picks):
    rows, block = terms[0].shape
    return pl.pallas_call(
        functools.partial(finish_kernel, len(terms), picks),
        out_shape=[jax.ShapeDtypeStruct((len(p), ROW_BLOCK, block), BF16) for p in picks],
        in_specs=[SMEM] + [VMEM] * (1 + len(terms)),
        out_specs=[VMEM] * len(picks),
        scratch_shapes=[pltpu.VMEM((rows, block), BF16)],
        compiler_params=pltpu.CompilerParams(vmem_limit_bytes=8 * MIB),
        cost_estimate=LIGHT,
        name="finish_tiles",
    )(meta, lane_rows(k_gain), *terms)


def attend_kernel(group_count, sources, has_base, meta_ref, query_ref, *refs):
    tile_refs = refs[: len(sources)]
    out_ref, key_ref, value_ref = refs[len(sources) + has_base :]
    place = meta_places(group_count)
    counts = (meta_ref[place["first"]], meta_ref[place["second"]])
    text_first, text_both = meta_ref[place["text_first"]], meta_ref[place["text_both"]]
    span = MAXT * ROW_BLOCK
    key_ref[...] = jnp.zeros_like(key_ref)
    value_ref[...] = jnp.zeros_like(value_ref)
    out_ref[...] = jnp.zeros_like(out_ref)
    for tile_ref, places in zip(tile_refs, sources):
        for n, slot in enumerate(places):
            goes = meta_ref[place["goes"] + slot]

            @pl.when(goes >= 0)
            def _(tile_ref=tile_ref, n=n, goes=goes):
                take = pl.ds(pl.multiple_of(goes * ROW_BLOCK, ROW_BLOCK), ROW_BLOCK)
                key_ref[take, :] = tile_ref[n, :, :HD]
                value_ref[take, :HD] = tile_ref[n, :, HD:]
                value_ref[take, HD:] = jnp.ones((ROW_BLOCK, HD), BF16)

    text_rows, width = query_ref.shape
    heads = width // HD
    for block in range(text_rows // ROW_BLOCK):
        start = block * ROW_BLOCK
        take = pl.ds(start, ROW_BLOCK)
        for label, (low, high) in enumerate(((0, text_first), (text_first, text_both))):
            meets = jnp.maximum(low, start) < jnp.minimum(high, start + ROW_BLOCK)

            def attend(key_rows, label=label, start=start, take=take, low=low, high=high):
                part = pl.ds(label * span, key_rows)
                slots = start + lax.broadcasted_iota(jnp.int32, (ROW_BLOCK, HD), 0)
                owned = (slots >= low) & (slots < high)
                for head in range(heads):
                    lanes = slice(head * HD, (head + 1) * HD)
                    scores = lax.dot_general(
                        query_ref[take, lanes],
                        key_ref[part, :],
                        (((1,), (1,)), ((), ())),
                        preferred_element_type=F32,
                    )
                    weights = jnp.exp2(scores).astype(BF16)
                    sums = jnp.dot(weights, value_ref[part, :], preferred_element_type=F32)
                    result = sums[:, :HD] / sums[:, HD:] * (1.0 / VALUE_SHIFT)
                    kept = out_ref[take, lanes].astype(F32)
                    out_ref[take, lanes] = jnp.where(owned, result, kept).astype(BF16)

            half = span // 2
            few = counts[label] * ROW_BLOCK <= half

            @pl.when(meets & few)
            def _(attend=attend):
                attend(half)

            @pl.when(meets & jnp.logical_not(few))
            def _(attend=attend):
                attend(span)


def attend_head(group_count, meta, queries, tiles, sources, base, head, head_count):
    rows, width = queries.shape
    head_width = width // head_count
    group_rows = REQ_G * MAXT * ROW_BLOCK
    whole_tile = pl.BlockSpec(memory_space=pltpu.VMEM)
    extra = [] if base is None else [base]
    return pl.pallas_call(
        functools.partial(attend_kernel, group_count, sources, len(extra)),
        out_shape=jax.ShapeDtypeStruct((rows, width), BF16),
        grid=(1,),
        in_specs=[
            SMEM,
            pl.BlockSpec((rows, head_width), lambda i: (0, head)),
        ]
        + [whole_tile] * len(tiles)
        + [pl.BlockSpec(memory_space=pl.ANY)] * len(extra),
        out_specs=pl.BlockSpec((rows, head_width), lambda i: (0, head)),
        scratch_shapes=[
            pltpu.VMEM((group_rows, HD), BF16),
            pltpu.VMEM((group_rows, 2 * HD), BF16),
        ],
        input_output_aliases={2 + len(tiles): 0} if extra else {},
        compiler_params=pltpu.CompilerParams(vmem_limit_bytes=24 * MIB),
        cost_estimate=LIGHT,
        name="attend_head",
    )(meta, queries, *tiles, *extra)


def add_rounded(a, b):
    return (a.astype(F32) + b.astype(F32)).astype(BF16)


def scatter_sum(blocks, count, first_bit):
    blocks = dict(enumerate(blocks))
    bits = bits_of(len(blocks))
    for b in range(bits):
        pairs = xor_pairs(count, 1 << (b + first_bit))
        got, sent = {}, None
        for k in sorted((k for k in blocks if (k >> b) & 1), reverse=True):
            sent = blocks[k]
            got[k ^ (1 << b)] = lax.ppermute(sent, "tp", pairs)
        if b == bits - 1:
            return [blocks[0], got[0]], sent
        blocks = {k: add_rounded(blocks[k], got[k]) for k in got}
    return [blocks[0]], blocks[0]


def gather_half(whole, tiles, half, count, ready):
    bits = bits_of(count)
    first = half * tiles
    pieces = {0: whole[0][first : first + tiles]}
    for b in reversed(range(1, bits)):
        pairs = xor_pairs(count, 1 << b)
        for k in sorted(pieces):
            pieces[k | (1 << b)] = lax.ppermute(pieces[k], "tp", pairs)
    pairs = xor_pairs(count, 1)
    for k in sorted(pieces):
        if k:
            block, ready = lax.optimization_barrier((pieces[k], ready))
            pieces[k | 1] = lax.ppermute(block, "tp", pairs)
    pieces[0], pieces[1] = whole
    bases = tuple(first if k < 2 else 0 for k in range(count))
    return [pieces[k] for k in range(count)], bases, ready


def local(
    x_in,
    taps,
    ln_gain,
    ln_bias,
    w_up,
    b_up,
    w_down,
    b_down,
    kv_w_out,
    kv_w_taps,
    k_gain,
    q_gain,
    queries,
    tiles_per_request,
    owner,
    text_per_request,
):
    group_count = lax.axis_size("grp")
    tp_count = lax.axis_size("tp")
    where = jnp.stack([lax.axis_index("grp"), lax.axis_index("tp")]).astype(jnp.int32)
    tiles_local = x_in.shape[0]
    x_tiles = jnp.swapaxes(x_in, 2, 3)[:, 0]
    tap_tiles = jnp.swapaxes(taps, 2, 3)[:, 0]
    head_count = max(1, KVH // tp_count)
    dup = max(1, tp_count // KVH)
    dest_count = tp_count // dup
    place = meta_places(group_count)

    query_rows, meta = prepare(
        where,
        (tiles_per_request, owner, text_per_request),
        q_gain,
        queries,
        group_count,
        tiles_local,
    )
    halves = 2 if tiles_local % 2 == 0 else 1
    tiles = tiles_local // halves
    whole = [x_tiles, lax.ppermute(x_tiles, "tp", xor_pairs(tp_count, 1))]
    mlp_terms = []
    ready = meta
    for half in range(halves):
        pieces, bases, ready = gather_half(whole, tiles, half, tp_count, ready)
        if half == 0:
            meta = ready
        mlp_blocks = encoder_mlp(
            meta, place["tp"], pieces, bases, tiles, ln_gain, ln_bias, w_up, b_up, w_down
        )
        terms, sent = scatter_sum(mlp_blocks, tp_count, 0)
        mlp_terms.append(terms)
        ready, _ = lax.optimization_barrier((meta, mlp_blocks[0]))
        meta, _ = lax.optimization_barrier((meta, sent))
    tap_part = tap_projection(
        meta, place["tp"], tap_tiles, kv_w_taps, head_count, dest_count, dup
    )
    kv_blocks = kv_projection(
        meta, place["tp"], x_tiles, b_down, kv_w_out, tap_part, mlp_terms, dup
    )

    slots = slot_count_of(group_count)
    total_tiles = group_count * tiles_local
    most_other = total_tiles - REQ_G * MAXT - REQ_G * (group_count - 2)
    one_large = group_count == 4 and slots == 2 and most_other <= group_count
    out = None
    before = {}
    for head in range(head_count):
        blocks = kv_blocks[head]
        for b in range(bits_of(dup)):
            pairs = xor_pairs(tp_count, 1 << b)
            blocks = [add_rounded(v, lax.ppermute(v, "tp", pairs)) for v in blocks]
        terms, _ = scatter_sum(blocks, tp_count, bits_of(dup))
        send = place["send"]

        def move(value, mask, name):
            if name in before:
                value, _ = lax.optimization_barrier((value, before[name]))
            got = lax.ppermute(value, "grp", xor_pairs(group_count, mask))
            if name is not None:
                before[name] = got
            return got

        if one_large:
            star = place["star"]
            picks = ((send, star), (send + 1, star), (send + 2,), (send + 3, star))
            own, near, middle, far = finish_tiles(meta, k_gain, terms, picks)
            far_got = move(far, 3, None)
            middle_got = move(middle, 2, "middle")
            near_got = move(near, 1, "near")
            after = middle_got if out is None else out
            far_got, _ = lax.optimization_barrier((far_got, after))
            passed = move(far_got[1:], 1, None)
            tiles = (own, near_got, middle_got, far_got, passed)
            sources = ((0, 4), (1, 5), (2,), (3, 7), (6,))
        else:
            picks = tuple(
                tuple(send + s * group_count + d for s in range(slots)) for d in range(group_count)
            )
            made = finish_tiles(meta, k_gain, terms, picks)
            tiles = tuple(made[:1]) + tuple(move(made[d], d, d) for d in range(1, group_count))
            sources = tuple(
                tuple(s * group_count + d for s in range(slots)) for d in range(group_count)
            )
        out = attend_head(
            group_count, meta, query_rows, tiles, sources, out, head, head_count
        )
    return out


def solution(mesh):
    in_specs = (
        P(None, ("rep", "grp"), None, "tp"),
        P(None, ("rep", "grp"), None, "tp"),
        P(),
        P(),
        P(None, "tp"),
        P("tp"),
        P("tp", None),
        P("tp"),
        P("tp", None),
        P("tp", None),
        P(),
        P(),
        P(("rep", "grp"), "tp"),
        P("rep"),
        P("rep"),
        P("rep"),
    )
    out_specs = P(("rep", "grp"), "tp")
    return jax.shard_map(local, mesh=mesh, in_specs=in_specs, out_specs=out_specs, check_vma=False)
```

```python
import functools
import math

import jax
import jax.numpy as jnp
from jax import lax
from jax.experimental import pallas as pl
from jax.experimental.pallas import tpu as pltpu
from jax.sharding import PartitionSpec as P

KVH = 8
HD = 128
MAXT = 4
REQ_G = 2
LANES = 128
ROW_BLOCK = 128
HIDDEN_BLOCK = 256
HEAD_GROUP = 8
VALUE_SHIFT = 2.0**-24
epsilon = 1e-05

F32 = jnp.float32
BF16 = jnp.bfloat16
VMEM = pl.BlockSpec(memory_space=pltpu.VMEM)
HBM = pl.BlockSpec(memory_space=pl.ANY)
SMEM = pl.BlockSpec(memory_space=pltpu.SMEM)
MIB = 1024 * 1024
LIGHT = pl.CostEstimate(flops=1024, bytes_accessed=1024, transcendentals=0)


def bits_of(count):
    bits = count.bit_length() - 1
    assert 1 << bits == count
    return bits


def xor_order(blocks, index):
    blocks = list(blocks)
    for b in range(bits_of(len(blocks))):
        swap = ((index >> b) & 1) == 1
        for k in range(len(blocks)):
            if not (k >> b) & 1:
                low, high = blocks[k], blocks[k | (1 << b)]
                blocks[k] = lax.select(swap, high, low)
                blocks[k | (1 << b)] = lax.select(swap, low, high)
    return blocks


def xor_pairs(count, mask):
    return [(i, i ^ mask) for i in range(count)]


def lane_rows(vector):
    return jnp.pad(vector, (0, -vector.shape[0] % LANES)).reshape(-1, LANES)


def one_row(ref, width):
    rows = [ref[n : n + 1, :] for n in range(ref.shape[0])]
    return (rows[0] if len(rows) == 1 else jnp.concatenate(rows, axis=1))[:, :width]


def column_step(width):
    return HIDDEN_BLOCK if width % HIDDEN_BLOCK == 0 else width


def tail_plan(rows, width):
    whole = width // LANES * LANES
    tail = width - whole
    packed = tail > 0 and whole > 0 and whole % tail == 0 and rows * tail % whole == 0
    extra = rows * tail // whole if packed else 0
    packed = packed and extra % 16 == 0 and ROW_BLOCK % extra == 0
    return whole, tail, extra if packed else 0


def sent_shape(rows, width):
    whole, _, extra = tail_plan(rows, width)
    return (rows + extra, whole) if extra else (rows, width)


def layout_kernel(group_count, tiles_local, where_ref, meta_ref):
    group = where_ref[0]
    requests = (where_ref.shape[0] - 2) // 3
    tiles_of, owner_of, text_of = ([where_ref[2 + n * requests + r] for r in range(requests)] for n in range(3))
    zero = jnp.int32(0)
    firsts, counts, offsets, texts_first, texts_both = [], [], [], [], []
    offset = zero
    for p in range(group_count):
        first, count, text_first, text_both, seen = zero, zero, zero, zero, zero
        for r in range(requests):
            mine = owner_of[r] == p
            tiles = jnp.where(mine, tiles_of[r], 0)
            text = jnp.where(mine, text_of[r], 0)
            first = first + jnp.where(seen == 0, tiles, 0)
            text_first = text_first + jnp.where(seen == 0, text, 0)
            count = count + tiles
            text_both = text_both + text
            seen = seen + jnp.where(mine, 1, 0)
        firsts.append(first)
        counts.append(count)
        offsets.append(offset)
        texts_first.append(text_first)
        texts_both.append(text_both)
        offset = offset + count

    def pick(values, index):
        out = values[0]
        for p in range(1, group_count):
            out = jnp.where(index == p, values[p], out)
        return out

    slots = slot_count_of(group_count)
    star, most = zero, counts[0]
    for p in range(1, group_count):
        larger = counts[p] > most
        star = jnp.where(larger, p, star)
        most = jnp.where(larger, counts[p], most)

    def local_tile(offset, slot):
        lane = lax.rem(group - offset + group_count * REQ_G * MAXT * group_count, group_count)
        tile = lax.div(offset + slot * group_count + lane, group_count)
        return jnp.minimum(tile, tiles_local - 1)

    my_first, my_count = pick(firsts, group), pick(counts, group)
    my_offset = pick(offsets, group)
    place = meta_places(group_count)
    meta_ref[place["first"]] = my_first
    meta_ref[place["second"]] = my_count - my_first
    meta_ref[place["text_first"]] = pick(texts_first, group)
    meta_ref[place["text_both"]] = pick(texts_both, group)
    meta_ref[place["star"]] = local_tile(pick(offsets, star), 1)
    for slot in range(slots):
        for d in range(group_count):
            other = group ^ d
            meta_ref[place["send"] + slot * group_count + d] = local_tile(pick(offsets, other), slot)
            lane = lax.rem(other - my_offset + group_count * REQ_G * MAXT * group_count, group_count)
            position = slot * group_count + lane
            goes = jnp.where(
                position < my_first,
                position,
                jnp.where(position < my_count, MAXT + position - my_first, -1),
            )
            meta_ref[place["goes"] + slot * group_count + d] = goes


def slot_count_of(group_count):
    return (REQ_G * MAXT + group_count - 1) // group_count


def meta_places(group_count):
    table = slot_count_of(group_count) * group_count
    return {
        "first": 0,
        "second": 1,
        "text_first": 2,
        "text_both": 3,
        "star": 4,
        "send": 8,
        "goes": 8 + table,
        "size": 8 + 2 * table,
    }


def mlp_kernel(piece_count, bases, tiles, where_ref, *refs):
    pieces = refs[:piece_count]
    gain_ref, bias_ref, up_bias_ref, up_ref, down_ref = refs[piece_count : piece_count + 5]
    outs = refs[piece_count + 5 : 2 * piece_count + 5]
    cat_ref, normed_ref, hidden_ref, total_ref = refs[2 * piece_count + 5 :]
    index = where_ref[1]
    _, width, tile_rows = pieces[0].shape
    rows = tiles * tile_rows
    channels, hidden_width = up_ref.shape
    up_step = column_step(hidden_width)
    down_step = column_step(channels)

    gain, bias = one_row(gain_ref, channels), one_row(bias_ref, channels)
    up_bias = one_row(up_bias_ref, hidden_width)
    for tile in range(tiles):
        for k, piece in enumerate(pieces):
            start = pl.multiple_of((index ^ k) * width, math.gcd(width, LANES))
            cat_ref[pl.ds(start, width), :] = piece[bases[k] + tile]
        values = cat_ref[...].T.astype(F32)
        average = jnp.sum(values, axis=1, keepdims=True) * (1.0 / channels)
        centered = values - average
        variance = jnp.sum(centered * centered, axis=1, keepdims=True) * (1.0 / channels)
        normed = centered * lax.rsqrt(variance + epsilon)
        normed = normed * gain + bias
        normed_ref[tile * tile_rows : (tile + 1) * tile_rows, :] = normed.astype(BF16)
    for n in range(hidden_width // up_step):
        take = slice(n * up_step, (n + 1) * up_step)
        value = jnp.dot(normed_ref[...], up_ref[:, take], preferred_element_type=F32)
        value = value + up_bias[:, take]
        value = 0.5 * value * (1.0 + lax.erf(value * (1.0 / math.sqrt(2.0))))
        hidden_ref[:, take] = value.astype(BF16)
    for n in range(channels // down_step):
        take = slice(n * down_step, (n + 1) * down_step)
        total_ref[:, take] = jnp.dot(
            hidden_ref[...], down_ref[:, take], preferred_element_type=F32
        )
    whole, tail, extra = tail_plan(rows, width)
    step = extra or ROW_BLOCK
    for part in range(rows // step):
        take = pl.ds(part * step, step)
        blocks = [total_ref[take, j * width : (j + 1) * width] for j in range(piece_count)]
        for out, block in zip(outs, xor_order(blocks, index)):
            block = block.astype(BF16)
            if extra:
                out[take, :] = block[:, :whole]
                out[rows : rows + extra, part * tail : (part + 1) * tail] = block[:, whole:]
            else:
                out[take, :] = block


def encoder_mlp(where, pieces, bases, tiles, ln_gain, ln_bias, w_up, b_up, w_down):
    _, width, tile_rows = pieces[0].shape
    rows = tiles * tile_rows
    count = len(pieces)
    channels, hidden_width = w_up.shape
    shape = sent_shape(rows, width)
    return pl.pallas_call(
        functools.partial(mlp_kernel, count, bases, tiles),
        out_shape=[jax.ShapeDtypeStruct(shape, BF16)] * count,
        in_specs=[SMEM] + [VMEM] * (count + 5),
        out_specs=[VMEM] * count,
        scratch_shapes=[
            pltpu.VMEM((channels, tile_rows), BF16),
            pltpu.VMEM((rows, channels), BF16),
            pltpu.VMEM((rows, hidden_width), BF16),
            pltpu.VMEM((rows, channels), F32),
        ],
        compiler_params=pltpu.CompilerParams(vmem_limit_bytes=44 * MIB),
        cost_estimate=LIGHT,
        name="encoder_mlp",
    )(
        where,
        *pieces,
        lane_rows(ln_gain),
        lane_rows(ln_bias),
        lane_rows(b_up),
        w_up,
        w_down,
    )


def prepare_kernel(
    group_count,
    tiles_local,
    where_ref,
    gain_ref,
    query_ref,
    normed_ref,
    meta_ref,
):
    @pl.when(pl.program_id(0) == 0)
    def _():
        layout_kernel(group_count, tiles_local, where_ref, meta_ref)

    gain = gain_ref[...] * (math.log2(math.e) / math.sqrt(HD))
    for col in range(0, query_ref.shape[1], HD):
        values = query_ref[:, col : col + HD].astype(F32)
        square = jnp.sum(values * values, axis=1, keepdims=True) * (1.0 / HD)
        normed_ref[:, col : col + HD] = (values * lax.rsqrt(square + epsilon) * gain).astype(BF16)


def prepare(where, q_gain, queries, group_count, tiles_local):
    text_rows, width = queries.shape
    step = ROW_BLOCK
    return pl.pallas_call(
        functools.partial(prepare_kernel, group_count, tiles_local),
        out_shape=[
            jax.ShapeDtypeStruct((text_rows, width), BF16),
            jax.ShapeDtypeStruct((meta_places(group_count)["size"],), jnp.int32),
        ],
        grid=(text_rows // step,),
        in_specs=[
            SMEM,
            pl.BlockSpec((1, HD), lambda n: (0, 0)),
            pl.BlockSpec((step, width), lambda n: (n, 0)),
        ],
        out_specs=[pl.BlockSpec((step, width), lambda n: (n, 0)), SMEM],
        compiler_params=pltpu.CompilerParams(vmem_limit_bytes=16 * MIB),
        cost_estimate=LIGHT,
        name="prepare",
    )(where, lane_rows(q_gain), queries)


def tap_kernel(staged, first, where_ref, tap_ref, weight_ref, *refs):
    sources, out_ref = refs[:staged], refs[staged]
    targets, scratch = refs[staged + 1 : 2 * staged + 1], refs[2 * staged + 1 :]
    step, last = pl.program_id(0), pl.num_programs(0) - 1

    def copies():
        return [
            pltpu.make_async_copy(source, target, scratch[1].at[n])
            for n, (source, target) in enumerate(zip(sources, targets))
        ]

    if first:
        row_ref = scratch[0]

        @pl.when(step == 0)
        def _():
            for copy in copies():
                copy.start()
            tiles, _, tile_rows = tap_ref.shape
            for tile in range(tiles):
                row_ref[tile * tile_rows : (tile + 1) * tile_rows, :] = tap_ref[tile].T

    else:
        row_ref = tap_ref
    out_ref[...] = jnp.dot(
        row_ref[...], weight_ref[...], preferred_element_type=F32
    ).astype(BF16)[None]
    if first:

        @pl.when(step == last)
        def _():
            for copy in copies():
                copy.wait()


def tap_projection(where, taps, weights, head, head_count, dest_count, dup, staged):
    first = head == 0
    if first:
        tiles, depth, tile_rows = taps.shape
        rows = tiles * tile_rows
    else:
        rows, depth = taps.shape
    block = 2 * HD

    def head_of(n, where_ref):
        return (lax.div(where_ref[1], jnp.int32(dup)) ^ n) * head_count + head

    row_shape = jax.ShapeDtypeStruct((rows, depth), BF16)
    return pl.pallas_call(
        functools.partial(tap_kernel, len(staged), first),
        out_shape=[jax.ShapeDtypeStruct((dest_count, rows, block), BF16)]
        + [jax.ShapeDtypeStruct(w.shape, w.dtype) for w in staged]
        + ([row_shape] if first else []),
        grid_spec=pltpu.PrefetchScalarGridSpec(
            num_scalar_prefetch=1,
            grid=(dest_count,),
            in_specs=[
                VMEM,
                pl.BlockSpec((depth, block), lambda n, w: (0, head_of(n, w))),
            ]
            + [HBM] * len(staged),
            out_specs=[pl.BlockSpec((1, rows, block), lambda n, w: (n, 0, 0))]
            + [VMEM] * (len(staged) + first),
            scratch_shapes=[pltpu.SemaphoreType.DMA((max(1, len(staged)),))] if first else [],
        ),
        compiler_params=pltpu.CompilerParams(vmem_limit_bytes=(42 if first else 50) * MIB),
        cost_estimate=LIGHT,
        name="tap_projection",
    )(where, taps, weights, *staged)


def kv_kernel(head_count, dest_count, dup, term_counts, where_ref, *refs):
    x_ref, bias_ref, weight_ref = refs[:3]
    tap_refs = refs[3 : 3 + head_count]
    terms = refs[3 + head_count : 3 + head_count + sum(term_counts)]
    outs = refs[3 + head_count + sum(term_counts) : -1]
    encoded_ref = refs[-1]
    tiles, width, tile_rows = x_ref.shape
    half_tiles = tiles // len(term_counts)
    whole, tail, extra = tail_plan(half_tiles * tile_rows, width)
    bias = one_row(bias_ref, width)
    for tile in range(tiles):
        half, row = tile // half_tiles, tile % half_tiles * tile_rows
        mine = terms[sum(term_counts[:half]) : sum(term_counts[: half + 1])]

        def summed(part, lanes):
            out = mine[0][part, lanes].astype(F32)
            for term in mine[1:]:
                out = out + term[part, lanes].astype(F32)
            return out

        total = summed(pl.ds(row, tile_rows), slice(None))
        if extra:
            chunks = range(row // extra, (row + tile_rows) // extra)
            rest = [
                summed(pl.ds(half_tiles * tile_rows, extra), slice(c * tail, (c + 1) * tail))
                for c in chunks
            ]
            rest = rest[0] if len(rest) == 1 else jnp.concatenate(rest, axis=0)
            total = jnp.concatenate([total, rest], axis=1)
        total = total + x_ref[tile].T.astype(F32) + bias
        encoded_ref[tile * tile_rows : (tile + 1) * tile_rows, :] = total.astype(BF16)
    block = 2 * HD
    mine = lax.div(where_ref[1], jnp.int32(dup))
    for head in range(head_count):
        for k in range(dest_count):
            column = ((mine ^ k) * head_count + head) * block
            weights = weight_ref[:, pl.ds(pl.multiple_of(column, block), block)]
            value = jnp.dot(encoded_ref[...], weights, preferred_element_type=F32)
            value = value + tap_refs[head][k].astype(F32)
            outs[head * dest_count + k][...] = value.astype(BF16)


def kv_projection(where, x_tiles, b_down, weights, tap_parts, halves, dup):
    terms = [term for half in halves for term in half]
    tiles, width, tile_rows = x_tiles.shape
    rows = tiles * tile_rows
    head_count, dest_count = len(tap_parts), tap_parts[0].shape[0]
    block = 2 * HD
    outs = pl.pallas_call(
        functools.partial(
            kv_kernel, head_count, dest_count, dup, tuple(len(half) for half in halves)
        ),
        out_shape=[jax.ShapeDtypeStruct((rows, block), BF16)] * (head_count * dest_count),
        in_specs=[SMEM] + [VMEM] * (3 + head_count + len(terms)),
        out_specs=[VMEM] * (head_count * dest_count),
        scratch_shapes=[pltpu.VMEM((rows, width), BF16)],
        compiler_params=pltpu.CompilerParams(vmem_limit_bytes=24 * MIB),
        cost_estimate=LIGHT,
        name="kv_projection",
    )(where, x_tiles, lane_rows(b_down), weights, *tap_parts, *terms)
    return [outs[h * dest_count : (h + 1) * dest_count] for h in range(head_count)]


def finish_kernel(term_count, picks, meta_ref, gain_ref, *refs):
    terms = refs[:term_count]
    outs = refs[term_count : term_count + len(picks)]
    done_ref = refs[-1]
    rows = terms[0].shape[0]
    for row in range(0, rows, ROW_BLOCK):
        take = pl.ds(row, ROW_BLOCK)
        total = terms[0][take, :].astype(F32)
        for term in terms[1:]:
            total = total + term[take, :].astype(F32)
        keys = total[:, :HD]
        square = jnp.sum(keys * keys, axis=1, keepdims=True) * (1.0 / HD)
        keys = keys * lax.rsqrt(square + epsilon) * gain_ref[...]
        done_ref[take, :HD] = keys.astype(BF16)
        done_ref[take, HD:] = (total[:, HD:] * VALUE_SHIFT).astype(BF16)
    for out, places in zip(outs, picks):
        for n, place in enumerate(places):
            start = pl.multiple_of(meta_ref[place] * ROW_BLOCK, ROW_BLOCK)
            out[n] = done_ref[pl.ds(start, ROW_BLOCK), :]


def finish_tiles(meta, k_gain, terms, picks):
    rows, block = terms[0].shape
    return pl.pallas_call(
        functools.partial(finish_kernel, len(terms), picks),
        out_shape=[jax.ShapeDtypeStruct((len(p), ROW_BLOCK, block), BF16) for p in picks],
        in_specs=[SMEM] + [VMEM] * (1 + len(terms)),
        out_specs=[VMEM] * len(picks),
        scratch_shapes=[pltpu.VMEM((rows, block), BF16)],
        compiler_params=pltpu.CompilerParams(vmem_limit_bytes=8 * MIB),
        cost_estimate=LIGHT,
        name="finish_tiles",
    )(meta, lane_rows(k_gain), *terms)


def attend_kernel(group_count, sources, has_base, meta_ref, query_ref, *refs):
    tile_refs = refs[: len(sources)]
    out_ref, key_ref, value_ref = refs[len(sources) + has_base :]
    place = meta_places(group_count)
    counts = (meta_ref[place["first"]], meta_ref[place["second"]])
    text_first, text_both = meta_ref[place["text_first"]], meta_ref[place["text_both"]]
    span = MAXT * ROW_BLOCK
    key_ref[...] = jnp.zeros_like(key_ref)
    value_ref[...] = jnp.zeros_like(value_ref)
    out_ref[...] = jnp.zeros_like(out_ref)
    for tile_ref, places in zip(tile_refs, sources):
        for n, slot in enumerate(places):
            goes = meta_ref[place["goes"] + slot]

            @pl.when(goes >= 0)
            def _(tile_ref=tile_ref, n=n, goes=goes):
                take = pl.ds(pl.multiple_of(goes * ROW_BLOCK, ROW_BLOCK), ROW_BLOCK)
                key_ref[take, :] = tile_ref[n, :, :HD]
                value_ref[take, :HD] = tile_ref[n, :, HD:]
                value_ref[take, HD:] = jnp.ones((ROW_BLOCK, HD), BF16)

    text_rows, width = query_ref.shape
    heads = width // HD
    for block in range(text_rows // ROW_BLOCK):
        start = block * ROW_BLOCK
        take = pl.ds(start, ROW_BLOCK)
        for label, (low, high) in enumerate(((0, text_first), (text_first, text_both))):
            meets = jnp.maximum(low, start) < jnp.minimum(high, start + ROW_BLOCK)

            def attend(key_rows, label=label, start=start, take=take, low=low, high=high):
                part = pl.ds(label * span, key_rows)
                slots = start + lax.broadcasted_iota(jnp.int32, (ROW_BLOCK, HD), 0)
                owned = (slots >= low) & (slots < high)
                for first in range(0, heads, HEAD_GROUP):
                    group = range(first, min(first + HEAD_GROUP, heads))
                    stacked = jnp.concatenate(
                        [query_ref[take, h * HD : (h + 1) * HD] for h in group], axis=0
                    )
                    scores = lax.dot_general(
                        stacked,
                        key_ref[part, :],
                        (((1,), (1,)), ((), ())),
                        preferred_element_type=F32,
                    )
                    weights = jnp.exp2(scores).astype(BF16)
                    sums = jnp.dot(weights, value_ref[part, :], preferred_element_type=F32)
                    result = sums[:, :HD] / sums[:, HD:] * (1.0 / VALUE_SHIFT)
                    for n, h in enumerate(group):
                        lanes = slice(h * HD, (h + 1) * HD)
                        own = result[n * ROW_BLOCK : (n + 1) * ROW_BLOCK]
                        kept = out_ref[take, lanes].astype(F32)
                        out_ref[take, lanes] = jnp.where(owned, own, kept).astype(BF16)

            half = span // 2
            few = counts[label] * ROW_BLOCK <= half

            @pl.when(meets & few)
            def _(attend=attend):
                attend(half)

            @pl.when(meets & jnp.logical_not(few))
            def _(attend=attend):
                attend(span)


def attend_head(group_count, meta, queries, tiles, sources, base, head, head_count):
    rows, width = queries.shape
    head_width = width // head_count
    group_rows = REQ_G * MAXT * ROW_BLOCK
    whole_tile = pl.BlockSpec(memory_space=pltpu.VMEM)
    extra = [] if base is None else [base]
    return pl.pallas_call(
        functools.partial(attend_kernel, group_count, sources, len(extra)),
        out_shape=jax.ShapeDtypeStruct((rows, width), BF16),
        grid=(1,),
        in_specs=[
            SMEM,
            pl.BlockSpec((rows, head_width), lambda i: (0, head)),
        ]
        + [whole_tile] * len(tiles)
        + [pl.BlockSpec(memory_space=pl.ANY)] * len(extra),
        out_specs=pl.BlockSpec((rows, head_width), lambda i: (0, head)),
        scratch_shapes=[
            pltpu.VMEM((group_rows, HD), BF16),
            pltpu.VMEM((group_rows, 2 * HD), BF16),
        ],
        input_output_aliases={2 + len(tiles): 0} if extra else {},
        compiler_params=pltpu.CompilerParams(vmem_limit_bytes=24 * MIB),
        cost_estimate=LIGHT,
        name="attend_head",
    )(meta, queries, *tiles, *extra)


def add_rounded(a, b):
    return (a.astype(F32) + b.astype(F32)).astype(BF16)


def after(value, *others):
    others = [v for v in others if v is not None]
    return lax.optimization_barrier((value, others))[0]


def scatter_sum(blocks, count, first_bit, earlier=None):
    blocks = dict(enumerate(blocks))
    bits = bits_of(len(blocks))
    for b in range(bits):
        pairs = xor_pairs(count, 1 << (b + first_bit))
        got, sent = {}, None
        for k in sorted((k for k in blocks if (k >> b) & 1), reverse=True):
            sent = blocks[k]
            if b == bits - 1 and earlier is not None:
                sent = after(sent, earlier)
            got[k ^ (1 << b)] = lax.ppermute(sent, "tp", pairs)
        if b == bits - 1:
            return [blocks[0], got[0]], sent
        blocks = {k: add_rounded(blocks[k], got[k]) for k in got}
    return [blocks[0]], blocks[0]


def gather_half(whole, own, first, count, ready):
    bits = bits_of(count)
    pieces = {0: own}
    for b in reversed(range(1, bits)):
        pairs = xor_pairs(count, 1 << b)
        for k in sorted(pieces):
            pieces[k | (1 << b)] = lax.ppermute(pieces[k], "tp", pairs)
    pairs = xor_pairs(count, 1)
    for k in sorted(pieces):
        if k:
            pieces[k | 1] = lax.ppermute(after(pieces[k], ready), "tp", pairs)
    pieces[0], pieces[1] = whole
    bases = tuple(first if k < 2 else 0 for k in range(count))
    return [pieces[k] for k in range(count)], bases


def local(
    x_in,
    taps,
    ln_gain,
    ln_bias,
    w_up,
    b_up,
    w_down,
    b_down,
    kv_w_out,
    kv_w_taps,
    k_gain,
    q_gain,
    queries,
    tiles_per_request,
    owner,
    text_per_request,
):
    group_count = lax.axis_size("grp")
    tp_count = lax.axis_size("tp")
    position = jnp.stack([lax.axis_index("grp"), lax.axis_index("tp")]).astype(jnp.int32)
    where = jnp.concatenate([position, tiles_per_request, owner, text_per_request])
    tiles_local = x_in.shape[0]
    x_tiles = jnp.swapaxes(x_in, 2, 3)[:, 0]
    tap_tiles = jnp.swapaxes(taps, 2, 3)[:, 0]
    head_count = max(1, KVH // tp_count)
    dup = max(1, tp_count // KVH)
    dest_count = tp_count // dup
    place = meta_places(group_count)

    halves = 2 if tiles_local % 2 == 0 else 1
    tiles = tiles_local // halves
    own_halves = [x_tiles[:tiles]] + [
        after(x_tiles, where)[h * tiles : (h + 1) * tiles] for h in range(1, halves)
    ]
    whole = [x_tiles, lax.ppermute(x_tiles, "tp", xor_pairs(tp_count, 1))]

    first_taps, w_up, w_down, tap_rows = tap_projection(
        where, tap_tiles, kv_w_taps, 0, head_count, dest_count, dup, (w_up, w_down)
    )
    tap_parts = [first_taps]
    mlp_terms = []
    ready, begun = first_taps, where
    for half in range(halves):
        pieces, bases = gather_half(whole, own_halves[half], half * tiles, tp_count, ready)
        mlp_blocks = encoder_mlp(
            begun, pieces, bases, tiles, ln_gain, ln_bias, w_up, b_up, w_down
        )
        terms, sent = scatter_sum(mlp_blocks, tp_count, 0)
        mlp_terms.append(terms)
        ready, begun = mlp_blocks[0], after(where, sent)
    for head in range(1, head_count):
        tap_parts += tap_projection(
            begun, tap_rows, kv_w_taps, head, head_count, dest_count, dup, ()
        )
    kv_blocks = kv_projection(
        where, x_tiles, b_down, kv_w_out, tap_parts, mlp_terms, dup
    )
    kv_terms, arrived = [], None
    for head in range(head_count):
        blocks = kv_blocks[head]
        for b in range(bits_of(dup)):
            pairs = xor_pairs(tp_count, 1 << b)
            blocks = [add_rounded(v, lax.ppermute(v, "tp", pairs)) for v in blocks]
        terms, sent = scatter_sum(blocks, tp_count, bits_of(dup), arrived)
        kv_terms.append(terms)
        if head == 0:
            query_rows, meta = prepare(
                after(where, sent), q_gain, queries, group_count, tiles_local
            )
        arrived = (terms[-1], meta)

    slots = slot_count_of(group_count)
    total_tiles = group_count * tiles_local
    most_other = total_tiles - REQ_G * MAXT - REQ_G * (group_count - 2)
    one_large = group_count == 4 and slots == 2 and most_other <= group_count
    send = place["send"]
    out, before = None, ()

    def move(value, mask):
        return lax.ppermute(value, "grp", xor_pairs(group_count, mask))

    for head in range(head_count):
        terms = kv_terms[head]
        if one_large:
            star = place["star"]
            picks = ((send, star), (send + 1, star), (send + 2,), (send + 3, star))
            own, near, middle, far = finish_tiles(meta, k_gain, terms, picks)
            if before:
                near, middle, far = (after(v, w) for v, w in zip((near, middle, far), before))
            far_got, middle_got, near_got = move(far, 3), move(middle, 2), move(near, 1)
            before = (near_got, far_got, middle_got)
            passed = move(after(far_got[1:], middle_got, out), 1)
            tiles = (own, near_got, middle_got, far_got, passed)
            sources = ((0, 4), (1, 5), (2,), (3, 7), (6,))
        else:
            picks = tuple(
                tuple(send + s * group_count + d for s in range(slots)) for d in range(group_count)
            )
            made = finish_tiles(meta, k_gain, terms, picks)
            tiles = tuple(made[:1]) + tuple(move(made[d], d) for d in range(1, group_count))
            sources = tuple(
                tuple(s * group_count + d for s in range(slots)) for d in range(group_count)
            )
        out = attend_head(
            group_count, meta, query_rows, tiles, sources, out, head, head_count
        )
    return out


def solution(mesh):
    in_specs = (
        P(None, ("rep", "grp"), None, "tp"),
        P(None, ("rep", "grp"), None, "tp"),
        P(),
        P(),
        P(None, "tp"),
        P("tp"),
        P("tp", None),
        P("tp"),
        P("tp", None),
        P("tp", None),
        P(),
        P(),
        P(("rep", "grp"), "tp"),
        P("rep"),
        P("rep"),
        P("rep"),
    )
    out_specs = P(("rep", "grp"), "tp")
    return jax.shard_map(local, mesh=mesh, in_specs=in_specs, out_specs=out_specs, check_vma=False)
```

```python
import functools
import math

import jax
import jax.numpy as jnp
from jax import lax
from jax.experimental import pallas as pl
from jax.experimental.pallas import tpu as pltpu
from jax.sharding import PartitionSpec as P

KVH = 8
HD = 128
MAXT = 4
REQ_G = 2
LANES = 128
ROW_BLOCK = 128
HIDDEN_BLOCK = 256
HEAD_GROUP = 8
VALUE_SHIFT = 2.0**-24
epsilon = 1e-05

F32 = jnp.float32
BF16 = jnp.bfloat16
VMEM = pl.BlockSpec(memory_space=pltpu.VMEM)
HBM = pl.BlockSpec(memory_space=pltpu.HBM)
SMEM = pl.BlockSpec(memory_space=pltpu.SMEM)
MIB = 1024 * 1024
LIGHT = pl.CostEstimate(flops=1024, bytes_accessed=1024, transcendentals=0)


def bits_of(count):
    bits = count.bit_length() - 1
    assert 1 << bits == count
    return bits


def xor_order(blocks, index):
    blocks = list(blocks)
    for b in range(bits_of(len(blocks))):
        swap = ((index >> b) & 1) == 1
        for k in range(len(blocks)):
            if not (k >> b) & 1:
                low, high = blocks[k], blocks[k | (1 << b)]
                blocks[k] = lax.select(swap, high, low)
                blocks[k | (1 << b)] = lax.select(swap, low, high)
    return blocks


def xor_pairs(count, mask):
    return [(i, i ^ mask) for i in range(count)]


def lane_rows(vector):
    return jnp.pad(vector, (0, -vector.shape[0] % LANES)).reshape(-1, LANES)


def one_row(ref, width):
    rows = [ref[n : n + 1, :] for n in range(ref.shape[0])]
    return (rows[0] if len(rows) == 1 else jnp.concatenate(rows, axis=1))[:, :width]


def column_step(width):
    return HIDDEN_BLOCK if width % HIDDEN_BLOCK == 0 else width


def tail_plan(rows, width):
    whole = width // LANES * LANES
    tail = width - whole
    packed = tail > 0 and whole > 0 and whole % tail == 0 and rows * tail % whole == 0
    extra = rows * tail // whole if packed else 0
    packed = packed and extra % 16 == 0 and ROW_BLOCK % extra == 0
    return whole, tail, extra if packed else 0


def sent_shape(rows, width):
    whole, _, extra = tail_plan(rows, width)
    return (rows + extra, whole) if extra else (rows, width)


def layout_kernel(group_count, tiles_local, where_ref, meta_ref):
    group = where_ref[0]
    requests = (where_ref.shape[0] - 2) // 3
    tiles_of, owner_of, text_of = ([where_ref[2 + n * requests + r] for r in range(requests)] for n in range(3))
    zero = jnp.int32(0)
    firsts, counts, offsets, texts_first, texts_both = [], [], [], [], []
    offset = zero
    for p in range(group_count):
        first, count, text_first, text_both, seen = zero, zero, zero, zero, zero
        for r in range(requests):
            mine = owner_of[r] == p
            tiles = jnp.where(mine, tiles_of[r], 0)
            text = jnp.where(mine, text_of[r], 0)
            first = first + jnp.where(seen == 0, tiles, 0)
            text_first = text_first + jnp.where(seen == 0, text, 0)
            count = count + tiles
            text_both = text_both + text
            seen = seen + jnp.where(mine, 1, 0)
        firsts.append(first)
        counts.append(count)
        offsets.append(offset)
        texts_first.append(text_first)
        texts_both.append(text_both)
        offset = offset + count

    def pick(values, index):
        out = values[0]
        for p in range(1, group_count):
            out = jnp.where(index == p, values[p], out)
        return out

    slots = slot_count_of(group_count)
    star, most = zero, counts[0]
    for p in range(1, group_count):
        larger = counts[p] > most
        star = jnp.where(larger, p, star)
        most = jnp.where(larger, counts[p], most)

    def local_tile(offset, slot):
        lane = lax.rem(group - offset + group_count * REQ_G * MAXT * group_count, group_count)
        tile = lax.div(offset + slot * group_count + lane, group_count)
        return jnp.minimum(tile, tiles_local - 1)

    my_first, my_count = pick(firsts, group), pick(counts, group)
    my_offset = pick(offsets, group)
    place = meta_places(group_count)
    meta_ref[place["first"]] = my_first
    meta_ref[place["second"]] = my_count - my_first
    meta_ref[place["text_first"]] = pick(texts_first, group)
    meta_ref[place["text_both"]] = pick(texts_both, group)
    meta_ref[place["star"]] = local_tile(pick(offsets, star), 1)
    for slot in range(slots):
        for d in range(group_count):
            other = group ^ d
            meta_ref[place["send"] + slot * group_count + d] = local_tile(pick(offsets, other), slot)
            lane = lax.rem(other - my_offset + group_count * REQ_G * MAXT * group_count, group_count)
            position = slot * group_count + lane
            goes = jnp.where(
                position < my_first,
                position,
                jnp.where(position < my_count, MAXT + position - my_first, -1),
            )
            meta_ref[place["goes"] + slot * group_count + d] = goes


def slot_count_of(group_count):
    return (REQ_G * MAXT + group_count - 1) // group_count


def meta_places(group_count):
    table = slot_count_of(group_count) * group_count
    return {
        "first": 0,
        "second": 1,
        "text_first": 2,
        "text_both": 3,
        "star": 4,
        "send": 8,
        "goes": 8 + table,
        "size": 8 + 2 * table,
    }


def mlp_kernel(piece_count, bases, tiles, where_ref, *refs):
    pieces = refs[:piece_count]
    gain_ref, bias_ref, up_bias_ref, up_ref, down_ref = refs[piece_count : piece_count + 5]
    outs = refs[piece_count + 5 : 2 * piece_count + 5]
    cat_ref, normed_ref, hidden_ref, total_ref = refs[2 * piece_count + 5 :]
    index = where_ref[1]
    _, width, tile_rows = pieces[0].shape
    rows = tiles * tile_rows
    channels, hidden_width = up_ref.shape
    up_step = column_step(hidden_width)
    down_step = column_step(channels)

    gain, bias = one_row(gain_ref, channels), one_row(bias_ref, channels)
    up_bias = one_row(up_bias_ref, hidden_width)
    for tile in range(tiles):
        for k, piece in enumerate(pieces):
            start = pl.multiple_of((index ^ k) * width, math.gcd(width, LANES))
            cat_ref[pl.ds(start, width), :] = piece[bases[k] + tile]
        values = cat_ref[...].T.astype(F32)
        average = jnp.sum(values, axis=1, keepdims=True) * (1.0 / channels)
        centered = values - average
        variance = jnp.sum(centered * centered, axis=1, keepdims=True) * (1.0 / channels)
        normed = centered * lax.rsqrt(variance + epsilon)
        normed = normed * gain + bias
        normed_ref[tile * tile_rows : (tile + 1) * tile_rows, :] = normed.astype(BF16)
    for n in range(hidden_width // up_step):
        take = slice(n * up_step, (n + 1) * up_step)
        value = jnp.dot(normed_ref[...], up_ref[:, take], preferred_element_type=F32)
        value = value + up_bias[:, take]
        value = 0.5 * value * (1.0 + lax.erf(value * (1.0 / math.sqrt(2.0))))
        hidden_ref[:, take] = value.astype(BF16)
    for n in range(channels // down_step):
        take = slice(n * down_step, (n + 1) * down_step)
        total_ref[:, take] = jnp.dot(
            hidden_ref[...], down_ref[:, take], preferred_element_type=F32
        )
    whole, tail, extra = tail_plan(rows, width)
    step = extra or ROW_BLOCK
    for part in range(rows // step):
        take = pl.ds(part * step, step)
        blocks = [total_ref[take, j * width : (j + 1) * width] for j in range(piece_count)]
        for out, block in zip(outs, xor_order(blocks, index)):
            block = block.astype(BF16)
            if extra:
                out[take, :] = block[:, :whole]
                out[rows : rows + extra, part * tail : (part + 1) * tail] = block[:, whole:]
            else:
                out[take, :] = block


def encoder_mlp(where, pieces, bases, tiles, ln_gain, ln_bias, w_up, b_up, w_down):
    _, width, tile_rows = pieces[0].shape
    rows = tiles * tile_rows
    count = len(pieces)
    channels, hidden_width = w_up.shape
    shape = sent_shape(rows, width)
    return pl.pallas_call(
        functools.partial(mlp_kernel, count, bases, tiles),
        out_shape=[jax.ShapeDtypeStruct(shape, BF16)] * count,
        in_specs=[SMEM] + [VMEM] * (count + 5),
        out_specs=[VMEM] * count,
        scratch_shapes=[
            pltpu.VMEM((channels, tile_rows), BF16),
            pltpu.VMEM((rows, channels), BF16),
            pltpu.VMEM((rows, hidden_width), BF16),
            pltpu.VMEM((rows, channels), F32),
        ],
        compiler_params=pltpu.CompilerParams(vmem_limit_bytes=44 * MIB),
        cost_estimate=LIGHT,
        name="encoder_mlp",
    )(
        where,
        *pieces,
        lane_rows(ln_gain),
        lane_rows(ln_bias),
        lane_rows(b_up),
        w_up,
        w_down,
    )


def prepare_kernel(
    group_count,
    tiles_local,
    where_ref,
    gain_ref,
    query_ref,
    normed_ref,
    meta_ref,
):
    @pl.when(pl.program_id(0) == 0)
    def _():
        layout_kernel(group_count, tiles_local, where_ref, meta_ref)

    gain = gain_ref[...] * (math.log2(math.e) / math.sqrt(HD))
    for col in range(0, query_ref.shape[1], HD):
        values = query_ref[:, col : col + HD].astype(F32)
        square = jnp.sum(values * values, axis=1, keepdims=True) * (1.0 / HD)
        normed_ref[:, col : col + HD] = (values * lax.rsqrt(square + epsilon) * gain).astype(BF16)


def prepare(where, q_gain, queries, group_count, tiles_local):
    text_rows, width = queries.shape
    step = ROW_BLOCK
    return pl.pallas_call(
        functools.partial(prepare_kernel, group_count, tiles_local),
        out_shape=[
            jax.ShapeDtypeStruct((text_rows, width), BF16),
            jax.ShapeDtypeStruct((meta_places(group_count)["size"],), jnp.int32),
        ],
        grid=(text_rows // step,),
        in_specs=[
            SMEM,
            pl.BlockSpec((1, HD), lambda n: (0, 0)),
            pl.BlockSpec((step, width), lambda n: (n, 0)),
        ],
        out_specs=[pl.BlockSpec((step, width), lambda n: (n, 0)), SMEM],
        compiler_params=pltpu.CompilerParams(vmem_limit_bytes=16 * MIB),
        cost_estimate=LIGHT,
        name="prepare",
    )(where, lane_rows(q_gain), queries)


def tap_kernel(head, head_count, dup, staged, where_ref, tap_hbm, weight_hbm, *refs):
    sources, out_ref = refs[:staged], refs[staged]
    targets = refs[staged + 1 : 2 * staged + 1]
    if staged:
        tap_ref, weight_ref, tap_sem, weight_sem, staged_sem = refs[2 * staged + 1 :]
    else:
        tap_ref, (weight_ref, weight_sem) = tap_hbm, refs[1:]
    tiles, _, tile_rows = tap_ref.shape
    dest_count, _, block = weight_ref.shape
    mine = lax.div(where_ref[1], jnp.int32(dup))
    taps = [
        pltpu.make_async_copy(tap_hbm.at[n], tap_ref.at[n], tap_sem.at[n])
        for n in range(tiles if staged else 0)
    ]
    weights = []
    for k in range(dest_count):
        column = pl.multiple_of(((mine ^ k) * head_count + head) * block, block)
        weights.append(
            pltpu.make_async_copy(
                weight_hbm.at[:, pl.ds(column, block)], weight_ref.at[k], weight_sem.at[k]
            )
        )
    others = [
        pltpu.make_async_copy(source, target, staged_sem.at[n])
        for n, (source, target) in enumerate(zip(sources, targets))
    ]
    for copy in weights[:1] + taps + weights[1:] + others:
        copy.start()
    for k in range(dest_count):
        weights[k].wait()
        for tile in range(tiles):
            if k == 0 and staged:
                taps[tile].wait()
            value = lax.dot_general(
                tap_ref[tile],
                weight_ref[k],
                (((0,), (0,)), ((), ())),
                preferred_element_type=F32,
            )
            out_ref[k, tile * tile_rows : (tile + 1) * tile_rows, :] = value.astype(BF16)
    for copy in others:
        copy.wait()


def tap_projection(where, tap_tiles, weights, head, head_count, dest_count, dup, staged):
    tiles, depth, tile_rows = tap_tiles.shape
    block = 2 * HD
    return pl.pallas_call(
        functools.partial(tap_kernel, head, head_count, dup, len(staged)),
        out_shape=[jax.ShapeDtypeStruct((dest_count, tiles * tile_rows, block), BF16)]
        + [jax.ShapeDtypeStruct(w.shape, w.dtype) for w in staged]
        + ([jax.ShapeDtypeStruct(tap_tiles.shape, BF16)] if staged else []),
        in_specs=[SMEM, HBM if staged else VMEM, HBM] + [HBM] * len(staged),
        out_specs=[VMEM] * (1 + len(staged) + bool(staged)),
        scratch_shapes=[pltpu.VMEM((dest_count, depth, block), BF16)]
        + ([pltpu.SemaphoreType.DMA((tiles,))] if staged else [])
        + [pltpu.SemaphoreType.DMA((dest_count,))]
        + ([pltpu.SemaphoreType.DMA((len(staged),))] if staged else []),
        compiler_params=pltpu.CompilerParams(vmem_limit_bytes=(42 if staged else 50) * MIB),
        cost_estimate=LIGHT,
        name="tap_projection",
    )(where, tap_tiles, weights, *staged)


def kv_kernel(head_count, dest_count, dup, term_counts, where_ref, *refs):
    x_ref, bias_ref, weight_ref = refs[:3]
    tap_refs = refs[3 : 3 + head_count]
    terms = refs[3 + head_count : 3 + head_count + sum(term_counts)]
    outs = refs[3 + head_count + sum(term_counts) : -1]
    encoded_ref = refs[-1]
    tiles, width, tile_rows = x_ref.shape
    half_tiles = tiles // len(term_counts)
    whole, tail, extra = tail_plan(half_tiles * tile_rows, width)
    bias = one_row(bias_ref, width)
    for tile in range(tiles):
        half, row = tile // half_tiles, tile % half_tiles * tile_rows
        mine = terms[sum(term_counts[:half]) : sum(term_counts[: half + 1])]

        def summed(part, lanes):
            out = mine[0][part, lanes].astype(F32)
            for term in mine[1:]:
                out = out + term[part, lanes].astype(F32)
            return out

        total = summed(pl.ds(row, tile_rows), slice(None))
        if extra:
            chunks = range(row // extra, (row + tile_rows) // extra)
            rest = [
                summed(pl.ds(half_tiles * tile_rows, extra), slice(c * tail, (c + 1) * tail))
                for c in chunks
            ]
            rest = rest[0] if len(rest) == 1 else jnp.concatenate(rest, axis=0)
            total = jnp.concatenate([total, rest], axis=1)
        total = total + x_ref[tile].T.astype(F32) + bias
        encoded_ref[tile * tile_rows : (tile + 1) * tile_rows, :] = total.astype(BF16)
    block = 2 * HD
    mine = lax.div(where_ref[1], jnp.int32(dup))
    for head in range(head_count):
        for k in range(dest_count):
            column = ((mine ^ k) * head_count + head) * block
            weights = weight_ref[:, pl.ds(pl.multiple_of(column, block), block)]
            value = jnp.dot(encoded_ref[...], weights, preferred_element_type=F32)
            value = value + tap_refs[head][k].astype(F32)
            outs[head * dest_count + k][...] = value.astype(BF16)


def kv_projection(where, x_tiles, b_down, weights, tap_parts, halves, dup):
    terms = [term for half in halves for term in half]
    tiles, width, tile_rows = x_tiles.shape
    rows = tiles * tile_rows
    head_count, dest_count = len(tap_parts), tap_parts[0].shape[0]
    block = 2 * HD
    outs = pl.pallas_call(
        functools.partial(
            kv_kernel, head_count, dest_count, dup, tuple(len(half) for half in halves)
        ),
        out_shape=[jax.ShapeDtypeStruct((rows, block), BF16)] * (head_count * dest_count),
        in_specs=[SMEM] + [VMEM] * (3 + head_count + len(terms)),
        out_specs=[VMEM] * (head_count * dest_count),
        scratch_shapes=[pltpu.VMEM((rows, width), BF16)],
        compiler_params=pltpu.CompilerParams(vmem_limit_bytes=24 * MIB),
        cost_estimate=LIGHT,
        name="kv_projection",
    )(where, x_tiles, lane_rows(b_down), weights, *tap_parts, *terms)
    return [outs[h * dest_count : (h + 1) * dest_count] for h in range(head_count)]


def finish_kernel(term_count, picks, meta_ref, gain_ref, *refs):
    terms = refs[:term_count]
    outs = refs[term_count : term_count + len(picks)]
    done_ref = refs[-1]
    rows = terms[0].shape[0]
    for row in range(0, rows, ROW_BLOCK):
        take = pl.ds(row, ROW_BLOCK)
        total = terms[0][take, :].astype(F32)
        for term in terms[1:]:
            total = total + term[take, :].astype(F32)
        keys = total[:, :HD]
        square = jnp.sum(keys * keys, axis=1, keepdims=True) * (1.0 / HD)
        keys = keys * lax.rsqrt(square + epsilon) * gain_ref[...]
        done_ref[take, :HD] = keys.astype(BF16)
        done_ref[take, HD:] = (total[:, HD:] * VALUE_SHIFT).astype(BF16)
    for out, places in zip(outs, picks):
        for n, place in enumerate(places):
            start = pl.multiple_of(meta_ref[place] * ROW_BLOCK, ROW_BLOCK)
            out[n] = done_ref[pl.ds(start, ROW_BLOCK), :]


def finish_tiles(meta, k_gain, terms, picks):
    rows, block = terms[0].shape
    return pl.pallas_call(
        functools.partial(finish_kernel, len(terms), picks),
        out_shape=[jax.ShapeDtypeStruct((len(p), ROW_BLOCK, block), BF16) for p in picks],
        in_specs=[SMEM] + [VMEM] * (1 + len(terms)),
        out_specs=[VMEM] * len(picks),
        scratch_shapes=[pltpu.VMEM((rows, block), BF16)],
        compiler_params=pltpu.CompilerParams(vmem_limit_bytes=8 * MIB),
        cost_estimate=LIGHT,
        name="finish_tiles",
    )(meta, lane_rows(k_gain), *terms)


def attend_kernel(group_count, sources, has_base, meta_ref, query_ref, *refs):
    tile_refs = refs[: len(sources)]
    out_ref, key_ref, value_ref = refs[len(sources) + has_base :]
    place = meta_places(group_count)
    counts = (meta_ref[place["first"]], meta_ref[place["second"]])
    text_first, text_both = meta_ref[place["text_first"]], meta_ref[place["text_both"]]
    span = MAXT * ROW_BLOCK
    key_ref[...] = jnp.zeros_like(key_ref)
    value_ref[...] = jnp.zeros_like(value_ref)
    out_ref[...] = jnp.zeros_like(out_ref)
    for tile_ref, places in zip(tile_refs, sources):
        for n, slot in enumerate(places):
            if slot is None:
                continue
            goes = meta_ref[place["goes"] + slot]

            @pl.when(goes >= 0)
            def _(tile_ref=tile_ref, n=n, goes=goes):
                take = pl.ds(pl.multiple_of(goes * ROW_BLOCK, ROW_BLOCK), ROW_BLOCK)
                key_ref[take, :] = tile_ref[n, :, :HD]
                value_ref[take, :HD] = tile_ref[n, :, HD:]
                value_ref[take, HD:] = jnp.ones((ROW_BLOCK, HD), BF16)

    text_rows, width = query_ref.shape
    heads = width // HD
    for block in range(text_rows // ROW_BLOCK):
        start = block * ROW_BLOCK
        take = pl.ds(start, ROW_BLOCK)
        for label, (low, high) in enumerate(((0, text_first), (text_first, text_both))):
            meets = jnp.maximum(low, start) < jnp.minimum(high, start + ROW_BLOCK)

            def attend(key_rows, label=label, start=start, take=take, low=low, high=high):
                part = pl.ds(label * span, key_rows)
                slots = start + lax.broadcasted_iota(jnp.int32, (ROW_BLOCK, HD), 0)
                owned = (slots >= low) & (slots < high)
                for first in range(0, heads, HEAD_GROUP):
                    group = range(first, min(first + HEAD_GROUP, heads))
                    stacked = jnp.concatenate(
                        [query_ref[take, h * HD : (h + 1) * HD] for h in group], axis=0
                    )
                    scores = lax.dot_general(
                        stacked,
                        key_ref[part, :],
                        (((1,), (1,)), ((), ())),
                        preferred_element_type=F32,
                    )
                    weights = jnp.exp2(scores).astype(BF16)
                    sums = jnp.dot(weights, value_ref[part, :], preferred_element_type=F32)
                    result = sums[:, :HD] / sums[:, HD:] * (1.0 / VALUE_SHIFT)
                    for n, h in enumerate(group):
                        lanes = slice(h * HD, (h + 1) * HD)
                        own = result[n * ROW_BLOCK : (n + 1) * ROW_BLOCK]
                        kept = out_ref[take, lanes].astype(F32)
                        out_ref[take, lanes] = jnp.where(owned, own, kept).astype(BF16)

            half = span // 2
            few = counts[label] * ROW_BLOCK <= half

            @pl.when(meets & few)
            def _(attend=attend):
                attend(half)

            @pl.when(meets & jnp.logical_not(few))
            def _(attend=attend):
                attend(span)


def attend_head(group_count, meta, queries, tiles, sources, base, head, head_count):
    rows, width = queries.shape
    head_width = width // head_count
    group_rows = REQ_G * MAXT * ROW_BLOCK
    whole_tile = pl.BlockSpec(memory_space=pltpu.VMEM)
    extra = [] if base is None else [base]
    return pl.pallas_call(
        functools.partial(attend_kernel, group_count, sources, len(extra)),
        out_shape=jax.ShapeDtypeStruct((rows, width), BF16),
        grid=(1,),
        in_specs=[
            SMEM,
            pl.BlockSpec((rows, head_width), lambda i: (0, head)),
        ]
        + [whole_tile] * len(tiles)
        + [pl.BlockSpec(memory_space=pl.ANY)] * len(extra),
        out_specs=pl.BlockSpec((rows, head_width), lambda i: (0, head)),
        scratch_shapes=[
            pltpu.VMEM((group_rows, HD), BF16),
            pltpu.VMEM((group_rows, 2 * HD), BF16),
        ],
        input_output_aliases={2 + len(tiles): 0} if extra else {},
        compiler_params=pltpu.CompilerParams(vmem_limit_bytes=24 * MIB),
        cost_estimate=LIGHT,
        name="attend_head",
    )(meta, queries, *tiles, *extra)


def add_rounded(a, b):
    return (a.astype(F32) + b.astype(F32)).astype(BF16)


def after(value, *others):
    others = [v for v in others if v is not None]
    return lax.optimization_barrier((value, others))[0]


def scatter_sum(blocks, count, first_bit, earlier=None):
    blocks = dict(enumerate(blocks))
    bits = bits_of(len(blocks))
    for b in range(bits):
        pairs = xor_pairs(count, 1 << (b + first_bit))
        got, sent = {}, None
        for k in sorted((k for k in blocks if (k >> b) & 1), reverse=True):
            sent = blocks[k]
            if b == bits - 1 and earlier is not None:
                sent = after(sent, earlier)
            got[k ^ (1 << b)] = lax.ppermute(sent, "tp", pairs)
        if b == bits - 1:
            return [blocks[0], got[0]], sent
        blocks = {k: add_rounded(blocks[k], got[k]) for k in got}
    return [blocks[0]], blocks[0]


def gather_half(whole, own, first, count, ready):
    bits = bits_of(count)
    pieces = {0: own}
    for b in reversed(range(1, bits)):
        pairs = xor_pairs(count, 1 << b)
        for k in sorted(pieces):
            pieces[k | (1 << b)] = lax.ppermute(pieces[k], "tp", pairs)
    pairs = xor_pairs(count, 1)
    for k in sorted(pieces):
        if k:
            pieces[k | 1] = lax.ppermute(after(pieces[k], ready), "tp", pairs)
    pieces[0], pieces[1] = whole
    bases = tuple(first if k < 2 else 0 for k in range(count))
    return [pieces[k] for k in range(count)], bases


def local(
    x_in,
    taps,
    ln_gain,
    ln_bias,
    w_up,
    b_up,
    w_down,
    b_down,
    kv_w_out,
    kv_w_taps,
    k_gain,
    q_gain,
    queries,
    tiles_per_request,
    owner,
    text_per_request,
):
    group_count = lax.axis_size("grp")
    tp_count = lax.axis_size("tp")
    position = jnp.stack([lax.axis_index("grp"), lax.axis_index("tp")]).astype(jnp.int32)
    where = jnp.concatenate([position, tiles_per_request, owner, text_per_request])
    tiles_local = x_in.shape[0]
    x_tiles = jnp.swapaxes(x_in, 2, 3)[:, 0]
    tap_tiles = jnp.swapaxes(taps, 2, 3)[:, 0]
    head_count = max(1, KVH // tp_count)
    dup = max(1, tp_count // KVH)
    dest_count = tp_count // dup
    place = meta_places(group_count)

    halves = 2 if tiles_local % 2 == 0 else 1
    tiles = tiles_local // halves
    own_halves = [x_tiles[:tiles]] + [
        after(x_tiles, where)[h * tiles : (h + 1) * tiles] for h in range(1, halves)
    ]
    whole = [x_tiles, lax.ppermute(x_tiles, "tp", xor_pairs(tp_count, 1))]

    first_taps, w_up, w_down, tap_tiles = tap_projection(
        where, tap_tiles, kv_w_taps, 0, head_count, dest_count, dup, (w_up, w_down)
    )
    tap_parts = [first_taps]
    mlp_terms = []
    ready, begun = first_taps, where
    for half in range(halves):
        pieces, bases = gather_half(whole, own_halves[half], half * tiles, tp_count, ready)
        mlp_blocks = encoder_mlp(
            begun, pieces, bases, tiles, ln_gain, ln_bias, w_up, b_up, w_down
        )
        terms, sent = scatter_sum(mlp_blocks, tp_count, 0)
        mlp_terms.append(terms)
        ready, begun = mlp_blocks[0], after(where, sent)
    for head in range(1, head_count):
        tap_parts += tap_projection(
            begun, tap_tiles, kv_w_taps, head, head_count, dest_count, dup, ()
        )
    kv_blocks = kv_projection(
        where, x_tiles, b_down, kv_w_out, tap_parts, mlp_terms, dup
    )
    kv_terms, arrived = [], None
    for head in range(head_count):
        blocks = kv_blocks[head]
        for b in range(bits_of(dup)):
            pairs = xor_pairs(tp_count, 1 << b)
            blocks = [add_rounded(v, lax.ppermute(v, "tp", pairs)) for v in blocks]
        terms, sent = scatter_sum(blocks, tp_count, bits_of(dup), arrived)
        kv_terms.append(terms)
        if head == 0:
            query_rows, meta = prepare(
                after(where, sent), q_gain, queries, group_count, tiles_local
            )
        arrived = (terms[-1], meta)

    slots = slot_count_of(group_count)
    total_tiles = group_count * tiles_local
    most_other = total_tiles - REQ_G * MAXT - REQ_G * (group_count - 2)
    one_large = group_count == 4 and slots == 2 and most_other <= group_count
    send = place["send"]
    out = None

    def move(value, mask):
        return lax.ppermute(value, "grp", xor_pairs(group_count, mask))

    for head in range(head_count):
        terms = kv_terms[head]
        if one_large:
            star = place["star"]
            picks = ((send, star), (send + 1, star), (send + 2, send + 3, star))
            own, near, across = finish_tiles(meta, k_gain, terms, picks)
            across_got = move(across, 2)
            near_got = move(near, 1)
            passed = move(across_got[1:], 1)
            tiles = (own, near_got, across_got, passed)
            sources = ((0, 4), (1, 5), (2, None, 6), (3, 7))
        else:
            picks = tuple(
                tuple(send + s * group_count + d for s in range(slots)) for d in range(group_count)
            )
            made = finish_tiles(meta, k_gain, terms, picks)
            tiles = tuple(made[:1]) + tuple(move(made[d], d) for d in range(1, group_count))
            sources = tuple(
                tuple(s * group_count + d for s in range(slots)) for d in range(group_count)
            )
        out = attend_head(
            group_count, meta, query_rows, tiles, sources, out, head, head_count
        )
    return out


def solution(mesh):
    in_specs = (
        P(None, ("rep", "grp"), None, "tp"),
        P(None, ("rep", "grp"), None, "tp"),
        P(),
        P(),
        P(None, "tp"),
        P("tp"),
        P("tp", None),
        P("tp"),
        P("tp", None),
        P("tp", None),
        P(),
        P(),
        P(("rep", "grp"), "tp"),
        P("rep"),
        P("rep"),
        P("rep"),
    )
    out_specs = P(("rep", "grp"), "tp")
    return jax.shard_map(local, mesh=mesh, in_specs=in_specs, out_specs=out_specs, check_vma=False)
```

```python
import functools
import math

import jax
import jax.numpy as jnp
from jax import lax
from jax.experimental import pallas as pl
from jax.experimental.pallas import tpu as pltpu
from jax.sharding import PartitionSpec as P

KVH = 8
HD = 128
MAXT = 4
REQ_G = 2
LANES = 128
ROW_BLOCK = 128
HIDDEN_BLOCK = 256
HEAD_GROUP = 8
HALVES = 1
TAPS_EARLY = 3
VALUE_SHIFT = 2.0**-24
epsilon = 1e-05

F32 = jnp.float32
BF16 = jnp.bfloat16
VMEM = pl.BlockSpec(memory_space=pltpu.VMEM)
HBM = pl.BlockSpec(memory_space=pltpu.HBM)
SMEM = pl.BlockSpec(memory_space=pltpu.SMEM)
MIB = 1024 * 1024
LIGHT = pl.CostEstimate(flops=1024, bytes_accessed=1024, transcendentals=0)


def bits_of(count):
    bits = count.bit_length() - 1
    assert 1 << bits == count
    return bits


def xor_order(blocks, index):
    blocks = list(blocks)
    for b in range(bits_of(len(blocks))):
        swap = ((index >> b) & 1) == 1
        for k in range(len(blocks)):
            if not (k >> b) & 1:
                low, high = blocks[k], blocks[k | (1 << b)]
                blocks[k] = lax.select(swap, high, low)
                blocks[k | (1 << b)] = lax.select(swap, low, high)
    return blocks


def xor_pairs(count, mask):
    return [(i, i ^ mask) for i in range(count)]


def lane_rows(vector):
    return jnp.pad(vector, (0, -vector.shape[0] % LANES)).reshape(-1, LANES)


def one_row(ref, width):
    rows = [ref[n : n + 1, :] for n in range(ref.shape[0])]
    return (rows[0] if len(rows) == 1 else jnp.concatenate(rows, axis=1))[:, :width]


def column_step(width):
    return HIDDEN_BLOCK if width % HIDDEN_BLOCK == 0 else width


def tail_plan(rows, width):
    whole = width // LANES * LANES
    tail = width - whole
    packed = tail > 0 and whole > 0 and whole % tail == 0 and rows * tail % whole == 0
    extra = rows * tail // whole if packed else 0
    packed = packed and extra % 16 == 0 and ROW_BLOCK % extra == 0
    return whole, tail, extra if packed else 0


def sent_shape(rows, width):
    whole, _, extra = tail_plan(rows, width)
    return (rows + extra, whole) if extra else (rows, width)


def layout_kernel(group_count, tiles_local, where_ref, meta_ref):
    group = where_ref[0]
    requests = (where_ref.shape[0] - 2) // 3
    tiles_of, owner_of, text_of = ([where_ref[2 + n * requests + r] for r in range(requests)] for n in range(3))
    zero = jnp.int32(0)
    firsts, counts, offsets, texts_first, texts_both = [], [], [], [], []
    offset = zero
    for p in range(group_count):
        first, count, text_first, text_both, seen = zero, zero, zero, zero, zero
        for r in range(requests):
            mine = owner_of[r] == p
            tiles = jnp.where(mine, tiles_of[r], 0)
            text = jnp.where(mine, text_of[r], 0)
            first = first + jnp.where(seen == 0, tiles, 0)
            text_first = text_first + jnp.where(seen == 0, text, 0)
            count = count + tiles
            text_both = text_both + text
            seen = seen + jnp.where(mine, 1, 0)
        firsts.append(first)
        counts.append(count)
        offsets.append(offset)
        texts_first.append(text_first)
        texts_both.append(text_both)
        offset = offset + count

    def pick(values, index):
        out = values[0]
        for p in range(1, group_count):
            out = jnp.where(index == p, values[p], out)
        return out

    slots = slot_count_of(group_count)
    star, most = zero, counts[0]
    for p in range(1, group_count):
        larger = counts[p] > most
        star = jnp.where(larger, p, star)
        most = jnp.where(larger, counts[p], most)

    def local_tile(offset, slot):
        lane = lax.rem(group - offset + group_count * REQ_G * MAXT * group_count, group_count)
        tile = lax.div(offset + slot * group_count + lane, group_count)
        return jnp.minimum(tile, tiles_local - 1)

    my_first, my_count = pick(firsts, group), pick(counts, group)
    my_offset = pick(offsets, group)
    place = meta_places(group_count)
    meta_ref[place["first"]] = my_first
    meta_ref[place["second"]] = my_count - my_first
    meta_ref[place["text_first"]] = pick(texts_first, group)
    meta_ref[place["text_both"]] = pick(texts_both, group)
    meta_ref[place["star"]] = local_tile(pick(offsets, star), 1)
    for slot in range(slots):
        for d in range(group_count):
            other = group ^ d
            meta_ref[place["send"] + slot * group_count + d] = local_tile(pick(offsets, other), slot)
            lane = lax.rem(other - my_offset + group_count * REQ_G * MAXT * group_count, group_count)
            position = slot * group_count + lane
            goes = jnp.where(
                position < my_first,
                position,
                jnp.where(position < my_count, MAXT + position - my_first, -1),
            )
            meta_ref[place["goes"] + slot * group_count + d] = goes


def slot_count_of(group_count):
    return (REQ_G * MAXT + group_count - 1) // group_count


def meta_places(group_count):
    table = slot_count_of(group_count) * group_count
    return {
        "first": 0,
        "second": 1,
        "text_first": 2,
        "text_both": 3,
        "star": 4,
        "send": 8,
        "goes": 8 + table,
        "size": 8 + 2 * table,
    }


def mlp_kernel(piece_count, bases, tiles, where_ref, *refs):
    pieces = refs[:piece_count]
    gain_ref, bias_ref, up_bias_ref, up_ref, down_ref = refs[piece_count : piece_count + 5]
    outs = refs[piece_count + 5 : 2 * piece_count + 5]
    cat_ref, normed_ref, hidden_ref, total_ref = refs[2 * piece_count + 5 :]
    index = where_ref[1]
    _, width, tile_rows = pieces[0].shape
    rows = tiles * tile_rows
    channels, hidden_width = up_ref.shape
    up_step = column_step(hidden_width)
    down_step = column_step(channels)

    gain, bias = one_row(gain_ref, channels), one_row(bias_ref, channels)
    up_bias = one_row(up_bias_ref, hidden_width)
    for tile in range(tiles):
        for k, piece in enumerate(pieces):
            start = pl.multiple_of((index ^ k) * width, math.gcd(width, LANES))
            cat_ref[pl.ds(start, width), :] = piece[bases[k] + tile]
        values = cat_ref[...].T.astype(F32)
        average = jnp.sum(values, axis=1, keepdims=True) * (1.0 / channels)
        centered = values - average
        variance = jnp.sum(centered * centered, axis=1, keepdims=True) * (1.0 / channels)
        normed = centered * lax.rsqrt(variance + epsilon)
        normed = normed * gain + bias
        normed_ref[tile * tile_rows : (tile + 1) * tile_rows, :] = normed.astype(BF16)
    for n in range(hidden_width // up_step):
        take = slice(n * up_step, (n + 1) * up_step)
        value = jnp.dot(normed_ref[...], up_ref[:, take], preferred_element_type=F32)
        value = value + up_bias[:, take]
        value = 0.5 * value * (1.0 + lax.erf(value * (1.0 / math.sqrt(2.0))))
        hidden_ref[:, take] = value.astype(BF16)
    for n in range(channels // down_step):
        take = slice(n * down_step, (n + 1) * down_step)
        total_ref[:, take] = jnp.dot(
            hidden_ref[...], down_ref[:, take], preferred_element_type=F32
        )
    whole, tail, extra = tail_plan(rows, width)
    step = extra or ROW_BLOCK
    for part in range(rows // step):
        take = pl.ds(part * step, step)
        blocks = [total_ref[take, j * width : (j + 1) * width] for j in range(piece_count)]
        for out, block in zip(outs, xor_order(blocks, index)):
            block = block.astype(BF16)
            if extra:
                out[take, :] = block[:, :whole]
                out[rows : rows + extra, part * tail : (part + 1) * tail] = block[:, whole:]
            else:
                out[take, :] = block


def encoder_mlp(where, pieces, bases, tiles, ln_gain, ln_bias, w_up, b_up, w_down):
    _, width, tile_rows = pieces[0].shape
    rows = tiles * tile_rows
    count = len(pieces)
    channels, hidden_width = w_up.shape
    shape = sent_shape(rows, width)
    return pl.pallas_call(
        functools.partial(mlp_kernel, count, bases, tiles),
        out_shape=[jax.ShapeDtypeStruct(shape, BF16)] * count,
        in_specs=[SMEM] + [VMEM] * (count + 5),
        out_specs=[VMEM] * count,
        scratch_shapes=[
            pltpu.VMEM((channels, tile_rows), BF16),
            pltpu.VMEM((rows, channels), BF16),
            pltpu.VMEM((rows, hidden_width), BF16),
            pltpu.VMEM((rows, channels), F32),
        ],
        compiler_params=pltpu.CompilerParams(vmem_limit_bytes=44 * MIB),
        cost_estimate=LIGHT,
        name="encoder_mlp",
    )(
        where,
        *pieces,
        lane_rows(ln_gain),
        lane_rows(ln_bias),
        lane_rows(b_up),
        w_up,
        w_down,
    )


def prepare_kernel(
    group_count,
    tiles_local,
    where_ref,
    gain_ref,
    query_ref,
    normed_ref,
    meta_ref,
):
    @pl.when(pl.program_id(0) == 0)
    def _():
        layout_kernel(group_count, tiles_local, where_ref, meta_ref)

    gain = gain_ref[...] * (math.log2(math.e) / math.sqrt(HD))
    for col in range(0, query_ref.shape[1], HD):
        values = query_ref[:, col : col + HD].astype(F32)
        square = jnp.sum(values * values, axis=1, keepdims=True) * (1.0 / HD)
        normed_ref[:, col : col + HD] = (values * lax.rsqrt(square + epsilon) * gain).astype(BF16)


def prepare(where, q_gain, queries, group_count, tiles_local):
    text_rows, width = queries.shape
    step = ROW_BLOCK
    return pl.pallas_call(
        functools.partial(prepare_kernel, group_count, tiles_local),
        out_shape=[
            jax.ShapeDtypeStruct((text_rows, width), BF16),
            jax.ShapeDtypeStruct((meta_places(group_count)["size"],), jnp.int32),
        ],
        grid=(text_rows // step,),
        in_specs=[
            SMEM,
            pl.BlockSpec((1, HD), lambda n: (0, 0)),
            pl.BlockSpec((step, width), lambda n: (n, 0)),
        ],
        out_specs=[pl.BlockSpec((step, width), lambda n: (n, 0)), SMEM],
        compiler_params=pltpu.CompilerParams(vmem_limit_bytes=16 * MIB),
        cost_estimate=LIGHT,
        name="prepare",
    )(where, lane_rows(q_gain), queries)


def tap_kernel(blocks, head_count, dup, staged, where_ref, tap_hbm, weight_hbm, *refs):
    sources, out_ref = refs[:staged], refs[staged]
    targets = refs[staged + 1 : 2 * staged + 1]
    if staged:
        tap_ref, weight_ref, tap_sem, weight_sem, staged_sem = refs[2 * staged + 1 :]
    else:
        tap_ref, (weight_ref, weight_sem) = tap_hbm, refs[1:]
    tiles, _, tile_rows = tap_ref.shape
    block = weight_ref.shape[2]
    mine = lax.div(where_ref[1], jnp.int32(dup))
    taps = [
        pltpu.make_async_copy(tap_hbm.at[n], tap_ref.at[n], tap_sem.at[n])
        for n in range(tiles if staged else 0)
    ]
    weights = []
    for n, (head, k) in enumerate(blocks):
        column = pl.multiple_of(((mine ^ k) * head_count + head) * block, block)
        weights.append(
            pltpu.make_async_copy(
                weight_hbm.at[:, pl.ds(column, block)], weight_ref.at[n], weight_sem.at[n]
            )
        )
    others = [
        pltpu.make_async_copy(source, target, staged_sem.at[n])
        for n, (source, target) in enumerate(zip(sources, targets))
    ]
    for copy in weights[:1] + taps + weights[1:] + others:
        copy.start()
    for n in range(len(blocks)):
        weights[n].wait()
        for tile in range(tiles):
            if n == 0 and staged:
                taps[tile].wait()
            value = lax.dot_general(
                tap_ref[tile],
                weight_ref[n],
                (((0,), (0,)), ((), ())),
                preferred_element_type=F32,
            )
            out_ref[n, tile * tile_rows : (tile + 1) * tile_rows, :] = value.astype(BF16)
    for copy in others:
        copy.wait()


def tap_projection(where, tap_tiles, weights, blocks, head_count, dup, staged):
    tiles, depth, tile_rows = tap_tiles.shape
    block = 2 * HD
    return pl.pallas_call(
        functools.partial(tap_kernel, blocks, head_count, dup, len(staged)),
        out_shape=[jax.ShapeDtypeStruct((len(blocks), tiles * tile_rows, block), BF16)]
        + [jax.ShapeDtypeStruct(w.shape, w.dtype) for w in staged]
        + ([jax.ShapeDtypeStruct(tap_tiles.shape, BF16)] if staged else []),
        in_specs=[SMEM, HBM if staged else VMEM, HBM] + [HBM] * len(staged),
        out_specs=[VMEM] * (1 + len(staged) + bool(staged)),
        scratch_shapes=[pltpu.VMEM((len(blocks), depth, block), BF16)]
        + ([pltpu.SemaphoreType.DMA((tiles,))] if staged else [])
        + [pltpu.SemaphoreType.DMA((len(blocks),))]
        + ([pltpu.SemaphoreType.DMA((len(staged),))] if staged else []),
        compiler_params=pltpu.CompilerParams(vmem_limit_bytes=(42 if staged else 50) * MIB),
        cost_estimate=LIGHT,
        name="tap_projection",
    )(where, tap_tiles, weights, *staged)


def kv_kernel(head_count, dest_count, dup, part_count, term_counts, where_ref, *refs):
    x_ref, bias_ref, weight_ref = refs[:3]
    tap_blocks = [ref.at[n] for ref in refs[3 : 3 + part_count] for n in range(ref.shape[0])]
    terms = refs[3 + part_count : 3 + part_count + sum(term_counts)]
    outs = refs[3 + part_count + sum(term_counts) : -1]
    encoded_ref = refs[-1]
    tiles, width, tile_rows = x_ref.shape
    half_tiles = tiles // len(term_counts)
    whole, tail, extra = tail_plan(half_tiles * tile_rows, width)
    bias = one_row(bias_ref, width)
    for tile in range(tiles):
        half, row = tile // half_tiles, tile % half_tiles * tile_rows
        mine = terms[sum(term_counts[:half]) : sum(term_counts[: half + 1])]

        def summed(part, lanes):
            out = mine[0][part, lanes].astype(F32)
            for term in mine[1:]:
                out = out + term[part, lanes].astype(F32)
            return out

        total = summed(pl.ds(row, tile_rows), slice(None))
        if extra:
            chunks = range(row // extra, (row + tile_rows) // extra)
            rest = [
                summed(pl.ds(half_tiles * tile_rows, extra), slice(c * tail, (c + 1) * tail))
                for c in chunks
            ]
            rest = rest[0] if len(rest) == 1 else jnp.concatenate(rest, axis=0)
            total = jnp.concatenate([total, rest], axis=1)
        total = total + x_ref[tile].T.astype(F32) + bias
        encoded_ref[tile * tile_rows : (tile + 1) * tile_rows, :] = total.astype(BF16)
    block = 2 * HD
    mine = lax.div(where_ref[1], jnp.int32(dup))
    for head in range(head_count):
        for k in range(dest_count):
            column = ((mine ^ k) * head_count + head) * block
            weights = weight_ref[:, pl.ds(pl.multiple_of(column, block), block)]
            value = jnp.dot(encoded_ref[...], weights, preferred_element_type=F32)
            value = value + tap_blocks[head * dest_count + k][...].astype(F32)
            outs[head * dest_count + k][...] = value.astype(BF16)


def kv_projection(
    where, x_tiles, b_down, weights, tap_parts, halves, head_count, dest_count, dup
):
    terms = [term for half in halves for term in half]
    tiles, width, tile_rows = x_tiles.shape
    rows = tiles * tile_rows
    block = 2 * HD
    outs = pl.pallas_call(
        functools.partial(
            kv_kernel,
            head_count,
            dest_count,
            dup,
            len(tap_parts),
            tuple(len(half) for half in halves),
        ),
        out_shape=[jax.ShapeDtypeStruct((rows, block), BF16)] * (head_count * dest_count),
        in_specs=[SMEM] + [VMEM] * (3 + len(tap_parts) + len(terms)),
        out_specs=[VMEM] * (head_count * dest_count),
        scratch_shapes=[pltpu.VMEM((rows, width), BF16)],
        compiler_params=pltpu.CompilerParams(vmem_limit_bytes=24 * MIB),
        cost_estimate=LIGHT,
        name="kv_projection",
    )(where, x_tiles, lane_rows(b_down), weights, *tap_parts, *terms)
    return [outs[h * dest_count : (h + 1) * dest_count] for h in range(head_count)]


def finish_kernel(term_count, picks, meta_ref, gain_ref, *refs):
    terms = refs[:term_count]
    outs = refs[term_count : term_count + len(picks)]
    done_ref = refs[-1]
    rows = terms[0].shape[0]
    for row in range(0, rows, ROW_BLOCK):
        take = pl.ds(row, ROW_BLOCK)
        total = terms[0][take, :].astype(F32)
        for term in terms[1:]:
            total = total + term[take, :].astype(F32)
        keys = total[:, :HD]
        square = jnp.sum(keys * keys, axis=1, keepdims=True) * (1.0 / HD)
        keys = keys * lax.rsqrt(square + epsilon) * gain_ref[...]
        done_ref[take, :HD] = keys.astype(BF16).T
        done_ref[take, HD:] = (total[:, HD:] * VALUE_SHIFT).astype(BF16)
    for out, places in zip(outs, picks):
        for n, place in enumerate(places):
            start = pl.multiple_of(meta_ref[place] * ROW_BLOCK, ROW_BLOCK)
            out[n] = done_ref[pl.ds(start, ROW_BLOCK), :]


def finish_tiles(meta, k_gain, terms, picks):
    rows, block = terms[0].shape
    return pl.pallas_call(
        functools.partial(finish_kernel, len(terms), picks),
        out_shape=[jax.ShapeDtypeStruct((len(p), ROW_BLOCK, block), BF16) for p in picks],
        in_specs=[SMEM] + [VMEM] * (1 + len(terms)),
        out_specs=[VMEM] * len(picks),
        scratch_shapes=[pltpu.VMEM((rows, block), BF16)],
        compiler_params=pltpu.CompilerParams(vmem_limit_bytes=8 * MIB),
        cost_estimate=LIGHT,
        name="finish_tiles",
    )(meta, lane_rows(k_gain), *terms)


def attend_kernel(group_count, sources, head, has_base, meta_ref, query_ref, *refs):
    tile_refs = refs[: len(sources)]
    out_hbm, out_ref, key_ref, value_ref, out_sem = refs[len(sources) + has_base :]
    place = meta_places(group_count)
    counts = (meta_ref[place["first"]], meta_ref[place["second"]])
    text_first, text_both = meta_ref[place["text_first"]], meta_ref[place["text_both"]]
    span = MAXT * ROW_BLOCK
    text_rows, width = out_ref.shape
    heads = width // HD
    for label in range(REQ_G):
        for tile in range(1, MAXT):

            @pl.when(counts[label] <= tile)
            def _(tile=label * MAXT + tile):
                take = slice(tile * ROW_BLOCK, (tile + 1) * ROW_BLOCK)
                key_ref[:, take] = jnp.zeros((HD, ROW_BLOCK), BF16)
                value_ref[take, :] = jnp.zeros((ROW_BLOCK, 2 * HD), BF16)

    for tile_ref, places in zip(tile_refs, sources):
        for n, slot in enumerate(places):
            if slot is None:
                continue
            goes = meta_ref[place["goes"] + slot]

            @pl.when(goes >= 0)
            def _(tile_ref=tile_ref, n=n, goes=goes):
                take = pl.ds(pl.multiple_of(goes * ROW_BLOCK, ROW_BLOCK), ROW_BLOCK)
                key_ref[:, take] = tile_ref[n, :, :HD]
                value_ref[take, :HD] = tile_ref[n, :, HD:]
                value_ref[take, HD:] = jnp.ones((ROW_BLOCK, HD), BF16)

    copies = []
    for block in range(text_rows // ROW_BLOCK):
        start = block * ROW_BLOCK
        take = pl.ds(start, ROW_BLOCK)
        for label, (low, high) in enumerate(((0, text_first), (text_first, text_both))):
            meets = jnp.maximum(low, start) < jnp.minimum(high, start + ROW_BLOCK)

            def attend(key_rows, label=label, start=start, take=take, low=low, high=high):
                part = pl.ds(label * span, key_rows)
                slots = start + lax.broadcasted_iota(jnp.int32, (ROW_BLOCK, HD), 0)
                owned = (slots >= low) & (slots < high)
                for first in range(0, heads, HEAD_GROUP):
                    group = range(first, min(first + HEAD_GROUP, heads))
                    column = head * width
                    stacked = jnp.concatenate(
                        [
                            query_ref[take, column + h * HD : column + (h + 1) * HD]
                            for h in group
                        ],
                        axis=0,
                    )
                    scores = jnp.dot(stacked, key_ref[:, part], preferred_element_type=F32)
                    weights = jnp.exp2(scores).astype(BF16)
                    sums = jnp.dot(weights, value_ref[part, :], preferred_element_type=F32)
                    result = sums[:, :HD] / sums[:, HD:] * (1.0 / VALUE_SHIFT)
                    for n, h in enumerate(group):
                        lanes = slice(h * HD, (h + 1) * HD)
                        own = result[n * ROW_BLOCK : (n + 1) * ROW_BLOCK]
                        kept = 0.0 if label == 0 else out_ref[take, lanes].astype(F32)
                        out_ref[take, lanes] = jnp.where(owned, own, kept).astype(BF16)

            half = span // 2
            few = counts[label] * ROW_BLOCK <= half

            @pl.when(meets & few)
            def _(attend=attend):
                attend(half)

            @pl.when(meets & jnp.logical_not(few))
            def _(attend=attend):
                attend(span)

            if label == 0:

                @pl.when(jnp.logical_not(meets))
                def _(take=take):
                    out_ref[take, :] = jnp.zeros((ROW_BLOCK, width), BF16)

        copies.append(
            pltpu.make_async_copy(
                out_ref.at[take, :],
                out_hbm.at[take, pl.ds(head * width, width)],
                out_sem.at[block],
            )
        )
        copies[-1].start()
    for copy in copies:
        copy.wait()


def attend_head(group_count, meta, queries, tiles, sources, base, head, head_count):
    rows, width = queries.shape
    head_width = width // head_count
    group_rows = REQ_G * MAXT * ROW_BLOCK
    extra = [] if base is None else [base]
    return pl.pallas_call(
        functools.partial(attend_kernel, group_count, sources, head, len(extra)),
        out_shape=jax.ShapeDtypeStruct((rows, width), BF16),
        in_specs=[SMEM] + [VMEM] * (1 + len(tiles)) + [HBM] * len(extra),
        out_specs=HBM,
        scratch_shapes=[
            pltpu.VMEM((rows, head_width), BF16),
            pltpu.VMEM((HD, group_rows), BF16),
            pltpu.VMEM((group_rows, 2 * HD), BF16),
            pltpu.SemaphoreType.DMA((rows // ROW_BLOCK,)),
        ],
        input_output_aliases={2 + len(tiles): 0} if extra else {},
        compiler_params=pltpu.CompilerParams(vmem_limit_bytes=24 * MIB),
        cost_estimate=LIGHT,
        name="attend_head",
    )(meta, queries, *tiles, *extra)


def add_rounded(a, b):
    return (a.astype(F32) + b.astype(F32)).astype(BF16)


def after(value, *others):
    others = [v for v in others if v is not None]
    return lax.optimization_barrier((value, others))[0]


def scatter_sum(blocks, count, first_bit, earlier=None):
    blocks = dict(enumerate(blocks))
    bits = bits_of(len(blocks))
    for b in range(bits):
        pairs = xor_pairs(count, 1 << (b + first_bit))
        got, sent = {}, None
        for k in sorted((k for k in blocks if (k >> b) & 1), reverse=True):
            sent = blocks[k]
            if b == bits - 1 and earlier is not None:
                sent = after(sent, earlier)
            got[k ^ (1 << b)] = lax.ppermute(sent, "tp", pairs)
        if b == bits - 1:
            return [blocks[0], got[0]], sent
        blocks = {k: add_rounded(blocks[k], got[k]) for k in got}
    return [blocks[0]], blocks[0]


def gather_half(whole, own, first, count, ready):
    bits = bits_of(count)
    pieces = {0: own}
    for b in reversed(range(1, bits)):
        pairs = xor_pairs(count, 1 << b)
        for k in sorted(pieces):
            pieces[k | (1 << b)] = lax.ppermute(pieces[k], "tp", pairs)
    pairs = xor_pairs(count, 1)
    for k in sorted(pieces):
        if k:
            pieces[k | 1] = lax.ppermute(after(pieces[k], ready), "tp", pairs)
    pieces[0], pieces[1] = whole
    bases = tuple(first if k < 2 else 0 for k in range(count))
    return [pieces[k] for k in range(count)], bases


def local(
    x_in,
    taps,
    ln_gain,
    ln_bias,
    w_up,
    b_up,
    w_down,
    b_down,
    kv_w_out,
    kv_w_taps,
    k_gain,
    q_gain,
    queries,
    tiles_per_request,
    owner,
    text_per_request,
):
    group_count = lax.axis_size("grp")
    tp_count = lax.axis_size("tp")
    position = jnp.stack([lax.axis_index("grp"), lax.axis_index("tp")]).astype(jnp.int32)
    where = jnp.concatenate([position, tiles_per_request, owner, text_per_request])
    tiles_local = x_in.shape[0]
    x_tiles = jnp.swapaxes(x_in, 2, 3)[:, 0]
    tap_tiles = jnp.swapaxes(taps, 2, 3)[:, 0]
    head_count = max(1, KVH // tp_count)
    dup = max(1, tp_count // KVH)
    dest_count = tp_count // dup
    place = meta_places(group_count)

    halves = HALVES if tiles_local % HALVES == 0 else 1
    tiles = tiles_local // halves
    own_halves = [x_tiles[:tiles]] + [
        after(x_tiles, where)[h * tiles : (h + 1) * tiles] for h in range(1, halves)
    ]
    whole = [x_tiles, lax.ppermute(x_tiles, "tp", xor_pairs(tp_count, 1))]

    tap_blocks = [(h, k) for h in range(head_count) for k in range(dest_count)]
    early = len(tap_blocks) * TAPS_EARLY // 8
    first_taps, w_up, w_down, tap_tiles = tap_projection(
        where, tap_tiles, kv_w_taps, tap_blocks[:early], head_count, dup, (w_up, w_down)
    )
    mlp_terms = []
    ready, begun = first_taps, where
    for half in range(halves):
        pieces, bases = gather_half(whole, own_halves[half], half * tiles, tp_count, ready)
        mlp_blocks = encoder_mlp(
            begun, pieces, bases, tiles, ln_gain, ln_bias, w_up, b_up, w_down
        )
        terms, sent = scatter_sum(mlp_blocks, tp_count, 0)
        mlp_terms.append(terms)
        ready, begun = mlp_blocks[0], after(where, sent)
    (last_taps,) = tap_projection(
        begun, tap_tiles, kv_w_taps, tap_blocks[early:], head_count, dup, ()
    )
    kv_blocks = kv_projection(
        where,
        x_tiles,
        b_down,
        kv_w_out,
        (first_taps, last_taps),
        mlp_terms,
        head_count,
        dest_count,
        dup,
    )
    kv_terms, arrived = [], None
    for head in range(head_count):
        blocks = kv_blocks[head]
        for b in range(bits_of(dup)):
            pairs = xor_pairs(tp_count, 1 << b)
            blocks = [add_rounded(v, lax.ppermute(v, "tp", pairs)) for v in blocks]
        terms, sent = scatter_sum(blocks, tp_count, bits_of(dup), arrived)
        kv_terms.append(terms)
        if head == 0:
            query_rows, meta = prepare(
                after(where, sent), q_gain, queries, group_count, tiles_local
            )
        arrived = (terms[-1], meta)

    slots = slot_count_of(group_count)
    total_tiles = group_count * tiles_local
    most_other = total_tiles - REQ_G * MAXT - REQ_G * (group_count - 2)
    one_large = group_count == 4 and slots == 2 and most_other <= group_count
    send = place["send"]
    out = None

    def move(value, mask):
        return lax.ppermute(value, "grp", xor_pairs(group_count, mask))

    for head in range(head_count):
        terms = kv_terms[head]
        if one_large:
            star = place["star"]
            picks = ((send, star), (send + 1, star), (send + 2, star), (send + 3,))
            own, near, middle, far = finish_tiles(meta, k_gain, terms, picks)
            middle_got, far_got, near_got = move(middle, 2), move(far, 3), move(near, 1)
            passed = move(middle_got[1:], 1)
            tiles = (own, near_got, middle_got, far_got, passed)
            sources = ((0, 4), (1, 5), (2, 6), (3,), (7,))
        else:
            picks = tuple(
                tuple(send + s * group_count + d for s in range(slots)) for d in range(group_count)
            )
            made = finish_tiles(meta, k_gain, terms, picks)
            tiles = tuple(made[:1]) + tuple(move(made[d], d) for d in range(1, group_count))
            sources = tuple(
                tuple(s * group_count + d for s in range(slots)) for d in range(group_count)
            )
        out = attend_head(
            group_count, meta, query_rows, tiles, sources, out, head, head_count
        )
    return out


def solution(mesh):
    in_specs = (
        P(None, ("rep", "grp"), None, "tp"),
        P(None, ("rep", "grp"), None, "tp"),
        P(),
        P(),
        P(None, "tp"),
        P("tp"),
        P("tp", None),
        P("tp"),
        P("tp", None),
        P("tp", None),
        P(),
        P(),
        P(("rep", "grp"), "tp"),
        P("rep"),
        P("rep"),
        P("rep"),
    )
    out_specs = P(("rep", "grp"), "tp")
    return jax.shard_map(local, mesh=mesh, in_specs=in_specs, out_specs=out_specs, check_vma=False)
```

```python
import functools
import math

import jax
import jax.numpy as jnp
from jax import lax
from jax.experimental import pallas as pl
from jax.experimental.pallas import tpu as pltpu
from jax.sharding import PartitionSpec as P

KVH = 8
HD = 128
MAXT = 4
REQ_G = 2
LANES = 128
ROW_BLOCK = 128
HIDDEN_BLOCK = 256
HEAD_GROUP = 8
HALVES = 1
TAPS_EARLY = 3
VALUE_SHIFT = 2.0**-24
epsilon = 1e-05

F32 = jnp.float32
BF16 = jnp.bfloat16
VMEM = pl.BlockSpec(memory_space=pltpu.VMEM)
HBM = pl.BlockSpec(memory_space=pltpu.HBM)
SMEM = pl.BlockSpec(memory_space=pltpu.SMEM)
MIB = 1024 * 1024
LIGHT = pl.CostEstimate(flops=1024, bytes_accessed=1024, transcendentals=0)


def bits_of(count):
    bits = count.bit_length() - 1
    assert 1 << bits == count
    return bits


def xor_order(blocks, index):
    blocks = list(blocks)
    for b in range(bits_of(len(blocks))):
        swap = ((index >> b) & 1) == 1
        for k in range(len(blocks)):
            if not (k >> b) & 1:
                low, high = blocks[k], blocks[k | (1 << b)]
                blocks[k] = lax.select(swap, high, low)
                blocks[k | (1 << b)] = lax.select(swap, low, high)
    return blocks


def xor_pairs(count, mask):
    return [(i, i ^ mask) for i in range(count)]


def lane_rows(vector):
    return jnp.pad(vector, (0, -vector.shape[0] % LANES)).reshape(-1, LANES)


def one_row(ref, width):
    rows = [ref[n : n + 1, :] for n in range(ref.shape[0])]
    return (rows[0] if len(rows) == 1 else jnp.concatenate(rows, axis=1))[:, :width]


def column_step(width):
    return HIDDEN_BLOCK if width % HIDDEN_BLOCK == 0 else width


def tail_plan(rows, width):
    whole = width // LANES * LANES
    tail = width - whole
    packed = tail > 0 and whole > 0 and whole % tail == 0 and rows * tail % whole == 0
    extra = rows * tail // whole if packed else 0
    packed = packed and extra % 16 == 0 and ROW_BLOCK % extra == 0
    return whole, tail, extra if packed else 0


def sent_shape(rows, width):
    whole, _, extra = tail_plan(rows, width)
    return (rows + extra, whole) if extra else (rows, width)


def layout_kernel(group_count, tiles_local, where_ref, meta_ref):
    group = where_ref[0]
    requests = (where_ref.shape[0] - 2) // 3
    tiles_of, owner_of, text_of = ([where_ref[2 + n * requests + r] for r in range(requests)] for n in range(3))
    zero = jnp.int32(0)
    firsts, counts, offsets, texts_first, texts_both = [], [], [], [], []
    offset = zero
    for p in range(group_count):
        first, count, text_first, text_both, seen = zero, zero, zero, zero, zero
        for r in range(requests):
            mine = owner_of[r] == p
            tiles = jnp.where(mine, tiles_of[r], 0)
            text = jnp.where(mine, text_of[r], 0)
            first = first + jnp.where(seen == 0, tiles, 0)
            text_first = text_first + jnp.where(seen == 0, text, 0)
            count = count + tiles
            text_both = text_both + text
            seen = seen + jnp.where(mine, 1, 0)
        firsts.append(first)
        counts.append(count)
        offsets.append(offset)
        texts_first.append(text_first)
        texts_both.append(text_both)
        offset = offset + count

    def pick(values, index):
        out = values[0]
        for p in range(1, group_count):
            out = jnp.where(index == p, values[p], out)
        return out

    slots = slot_count_of(group_count)
    star, most = zero, counts[0]
    for p in range(1, group_count):
        larger = counts[p] > most
        star = jnp.where(larger, p, star)
        most = jnp.where(larger, counts[p], most)

    def local_tile(offset, slot):
        lane = lax.rem(group - offset + group_count * REQ_G * MAXT * group_count, group_count)
        tile = lax.div(offset + slot * group_count + lane, group_count)
        return jnp.minimum(tile, tiles_local - 1)

    my_first, my_count = pick(firsts, group), pick(counts, group)
    my_offset = pick(offsets, group)
    place = meta_places(group_count)
    meta_ref[place["first"]] = my_first
    meta_ref[place["second"]] = my_count - my_first
    meta_ref[place["text_first"]] = pick(texts_first, group)
    meta_ref[place["text_both"]] = pick(texts_both, group)
    meta_ref[place["star"]] = local_tile(pick(offsets, star), 1)
    for slot in range(slots):
        for d in range(group_count):
            other = group ^ d
            meta_ref[place["send"] + slot * group_count + d] = local_tile(pick(offsets, other), slot)
            lane = lax.rem(other - my_offset + group_count * REQ_G * MAXT * group_count, group_count)
            position = slot * group_count + lane
            goes = jnp.where(
                position < my_first,
                position,
                jnp.where(position < my_count, MAXT + position - my_first, -1),
            )
            meta_ref[place["goes"] + slot * group_count + d] = goes


def slot_count_of(group_count):
    return (REQ_G * MAXT + group_count - 1) // group_count


def meta_places(group_count):
    table = slot_count_of(group_count) * group_count
    return {
        "first": 0,
        "second": 1,
        "text_first": 2,
        "text_both": 3,
        "star": 4,
        "send": 8,
        "goes": 8 + table,
        "size": 8 + 2 * table,
    }


def mlp_kernel(piece_count, bases, tiles, where_ref, *refs):
    pieces = refs[:piece_count]
    gain_ref, bias_ref, up_bias_ref, up_ref, down_ref = refs[piece_count : piece_count + 5]
    outs = refs[piece_count + 5 : 2 * piece_count + 5]
    cat_ref, normed_ref, hidden_ref, total_ref = refs[2 * piece_count + 5 :]
    index = where_ref[1]
    _, width, tile_rows = pieces[0].shape
    rows = tiles * tile_rows
    channels, hidden_width = up_ref.shape
    up_step = column_step(hidden_width)
    down_step = column_step(channels)

    gain, bias = one_row(gain_ref, channels), one_row(bias_ref, channels)
    up_bias = one_row(up_bias_ref, hidden_width)
    for tile in range(tiles):
        for k, piece in enumerate(pieces):
            start = pl.multiple_of((index ^ k) * width, math.gcd(width, LANES))
            cat_ref[pl.ds(start, width), :] = piece[bases[k] + tile]
        values = cat_ref[...].T.astype(F32)
        average = jnp.sum(values, axis=1, keepdims=True) * (1.0 / channels)
        centered = values - average
        variance = jnp.sum(centered * centered, axis=1, keepdims=True) * (1.0 / channels)
        normed = centered * lax.rsqrt(variance + epsilon)
        normed = normed * gain + bias
        normed_ref[tile * tile_rows : (tile + 1) * tile_rows, :] = normed.astype(BF16)
    for n in range(hidden_width // up_step):
        take = slice(n * up_step, (n + 1) * up_step)
        value = jnp.dot(normed_ref[...], up_ref[:, take], preferred_element_type=F32)
        value = value + up_bias[:, take]
        value = 0.5 * value * (1.0 + lax.erf(value * (1.0 / math.sqrt(2.0))))
        hidden_ref[:, take] = value.astype(BF16)
    for n in range(channels // down_step):
        take = slice(n * down_step, (n + 1) * down_step)
        total_ref[:, take] = jnp.dot(
            hidden_ref[...], down_ref[:, take], preferred_element_type=F32
        )
    whole, tail, extra = tail_plan(rows, width)
    step = extra or ROW_BLOCK
    for part in range(rows // step):
        take = pl.ds(part * step, step)
        blocks = [total_ref[take, j * width : (j + 1) * width] for j in range(piece_count)]
        for out, block in zip(outs, xor_order(blocks, index)):
            block = block.astype(BF16)
            if extra:
                out[take, :] = block[:, :whole]
                out[rows : rows + extra, part * tail : (part + 1) * tail] = block[:, whole:]
            else:
                out[take, :] = block


def encoder_mlp(where, pieces, bases, tiles, ln_gain, ln_bias, w_up, b_up, w_down):
    _, width, tile_rows = pieces[0].shape
    rows = tiles * tile_rows
    count = len(pieces)
    channels, hidden_width = w_up.shape
    shape = sent_shape(rows, width)
    return pl.pallas_call(
        functools.partial(mlp_kernel, count, bases, tiles),
        out_shape=[jax.ShapeDtypeStruct(shape, BF16)] * count,
        in_specs=[SMEM] + [VMEM] * (count + 5),
        out_specs=[VMEM] * count,
        scratch_shapes=[
            pltpu.VMEM((channels, tile_rows), BF16),
            pltpu.VMEM((rows, channels), BF16),
            pltpu.VMEM((rows, hidden_width), BF16),
            pltpu.VMEM((rows, channels), F32),
        ],
        compiler_params=pltpu.CompilerParams(vmem_limit_bytes=44 * MIB),
        cost_estimate=LIGHT,
        name="encoder_mlp",
    )(
        where,
        *pieces,
        lane_rows(ln_gain),
        lane_rows(ln_bias),
        lane_rows(b_up),
        w_up,
        w_down,
    )


def prepare_kernel(
    group_count,
    tiles_local,
    where_ref,
    gain_ref,
    query_ref,
    normed_ref,
    meta_ref,
):
    @pl.when(pl.program_id(0) == 0)
    def _():
        layout_kernel(group_count, tiles_local, where_ref, meta_ref)

    gain = gain_ref[...] * (math.log2(math.e) / math.sqrt(HD))
    for col in range(0, query_ref.shape[1], HD):
        values = query_ref[:, col : col + HD].astype(F32)
        square = jnp.sum(values * values, axis=1, keepdims=True) * (1.0 / HD)
        normed_ref[:, col : col + HD] = (values * lax.rsqrt(square + epsilon) * gain).astype(BF16)


def prepare(where, q_gain, queries, group_count, tiles_local):
    text_rows, width = queries.shape
    step = ROW_BLOCK
    return pl.pallas_call(
        functools.partial(prepare_kernel, group_count, tiles_local),
        out_shape=[
            jax.ShapeDtypeStruct((text_rows, width), BF16),
            jax.ShapeDtypeStruct((meta_places(group_count)["size"],), jnp.int32),
        ],
        grid=(text_rows // step,),
        in_specs=[
            SMEM,
            pl.BlockSpec((1, HD), lambda n: (0, 0)),
            pl.BlockSpec((step, width), lambda n: (n, 0)),
        ],
        out_specs=[pl.BlockSpec((step, width), lambda n: (n, 0)), SMEM],
        compiler_params=pltpu.CompilerParams(vmem_limit_bytes=16 * MIB),
        cost_estimate=LIGHT,
        name="prepare",
    )(where, lane_rows(q_gain), queries)


def tap_kernel(blocks, head_count, dup, staged, where_ref, tap_hbm, weight_hbm, *refs):
    sources, out_ref = refs[:staged], refs[staged]
    targets = refs[staged + 1 : 2 * staged + 1]
    if staged:
        tap_ref, weight_ref, tap_sem, weight_sem, staged_sem = refs[2 * staged + 1 :]
    else:
        tap_ref, (weight_ref, weight_sem) = tap_hbm, refs[1:]
    tiles, _, tile_rows = tap_ref.shape
    block = weight_ref.shape[2]
    mine = lax.div(where_ref[1], jnp.int32(dup))
    taps = [
        pltpu.make_async_copy(tap_hbm.at[n], tap_ref.at[n], tap_sem.at[n])
        for n in range(tiles if staged else 0)
    ]
    weights = []
    for n, (head, k) in enumerate(blocks):
        column = pl.multiple_of(((mine ^ k) * head_count + head) * block, block)
        weights.append(
            pltpu.make_async_copy(
                weight_hbm.at[:, pl.ds(column, block)], weight_ref.at[n], weight_sem.at[n]
            )
        )
    others = [
        pltpu.make_async_copy(source, target, staged_sem.at[n])
        for n, (source, target) in enumerate(zip(sources, targets))
    ]
    for copy in weights[:1] + taps + weights[1:] + others:
        copy.start()
    for n in range(len(blocks)):
        weights[n].wait()
        for tile in range(tiles):
            if n == 0 and staged:
                taps[tile].wait()
            value = lax.dot_general(
                tap_ref[tile],
                weight_ref[n],
                (((0,), (0,)), ((), ())),
                preferred_element_type=F32,
            )
            out_ref[n, tile * tile_rows : (tile + 1) * tile_rows, :] = value.astype(BF16)
    for copy in others:
        copy.wait()


def tap_projection(where, tap_tiles, weights, blocks, head_count, dup, staged):
    tiles, depth, tile_rows = tap_tiles.shape
    block = 2 * HD
    return pl.pallas_call(
        functools.partial(tap_kernel, blocks, head_count, dup, len(staged)),
        out_shape=[jax.ShapeDtypeStruct((len(blocks), tiles * tile_rows, block), BF16)]
        + [jax.ShapeDtypeStruct(w.shape, w.dtype) for w in staged]
        + ([jax.ShapeDtypeStruct(tap_tiles.shape, BF16)] if staged else []),
        in_specs=[SMEM, HBM if staged else VMEM, HBM] + [HBM] * len(staged),
        out_specs=[VMEM] * (1 + len(staged) + bool(staged)),
        scratch_shapes=[pltpu.VMEM((len(blocks), depth, block), BF16)]
        + ([pltpu.SemaphoreType.DMA((tiles,))] if staged else [])
        + [pltpu.SemaphoreType.DMA((len(blocks),))]
        + ([pltpu.SemaphoreType.DMA((len(staged),))] if staged else []),
        compiler_params=pltpu.CompilerParams(vmem_limit_bytes=(42 if staged else 50) * MIB),
        cost_estimate=LIGHT,
        name="tap_projection",
    )(where, tap_tiles, weights, *staged)


def kv_kernel(head_count, dest_count, dup, part_count, term_counts, where_ref, *refs):
    x_ref, bias_ref, weight_ref = refs[:3]
    tap_blocks = [ref.at[n] for ref in refs[3 : 3 + part_count] for n in range(ref.shape[0])]
    terms = refs[3 + part_count : 3 + part_count + sum(term_counts)]
    outs = refs[3 + part_count + sum(term_counts) : -1]
    encoded_ref = refs[-1]
    tiles, width, tile_rows = x_ref.shape
    half_tiles = tiles // len(term_counts)
    whole, tail, extra = tail_plan(half_tiles * tile_rows, width)
    bias = one_row(bias_ref, width)
    for tile in range(tiles):
        half, row = tile // half_tiles, tile % half_tiles * tile_rows
        mine = terms[sum(term_counts[:half]) : sum(term_counts[: half + 1])]

        def summed(part, lanes):
            out = mine[0][part, lanes].astype(F32)
            for term in mine[1:]:
                out = out + term[part, lanes].astype(F32)
            return out

        total = summed(pl.ds(row, tile_rows), slice(None))
        if extra:
            chunks = range(row // extra, (row + tile_rows) // extra)
            rest = [
                summed(pl.ds(half_tiles * tile_rows, extra), slice(c * tail, (c + 1) * tail))
                for c in chunks
            ]
            rest = rest[0] if len(rest) == 1 else jnp.concatenate(rest, axis=0)
            total = jnp.concatenate([total, rest], axis=1)
        total = total + x_ref[tile].T.astype(F32) + bias
        encoded_ref[tile * tile_rows : (tile + 1) * tile_rows, :] = total.astype(BF16)
    block = 2 * HD
    mine = lax.div(where_ref[1], jnp.int32(dup))
    for head in range(head_count):
        for k in range(dest_count):
            column = ((mine ^ k) * head_count + head) * block
            weights = weight_ref[:, pl.ds(pl.multiple_of(column, block), block)]
            value = jnp.dot(encoded_ref[...], weights, preferred_element_type=F32)
            value = value + tap_blocks[head * dest_count + k][...].astype(F32)
            outs[head * dest_count + k][...] = value.astype(BF16)


def kv_projection(
    where, x_tiles, b_down, weights, tap_parts, halves, head_count, dest_count, dup
):
    terms = [term for half in halves for term in half]
    tiles, width, tile_rows = x_tiles.shape
    rows = tiles * tile_rows
    block = 2 * HD
    outs = pl.pallas_call(
        functools.partial(
            kv_kernel,
            head_count,
            dest_count,
            dup,
            len(tap_parts),
            tuple(len(half) for half in halves),
        ),
        out_shape=[jax.ShapeDtypeStruct((rows, block), BF16)] * (head_count * dest_count),
        in_specs=[SMEM] + [VMEM] * (3 + len(tap_parts) + len(terms)),
        out_specs=[VMEM] * (head_count * dest_count),
        scratch_shapes=[pltpu.VMEM((rows, width), BF16)],
        compiler_params=pltpu.CompilerParams(vmem_limit_bytes=24 * MIB),
        cost_estimate=LIGHT,
        name="kv_projection",
    )(where, x_tiles, lane_rows(b_down), weights, *tap_parts, *terms)
    return [outs[h * dest_count : (h + 1) * dest_count] for h in range(head_count)]


def finish_kernel(term_count, picks, meta_ref, gain_ref, *refs):
    terms = refs[:term_count]
    outs = refs[term_count : term_count + len(picks)]
    done_ref = refs[-1]
    rows = terms[0].shape[0]
    for row in range(0, rows, ROW_BLOCK):
        take = pl.ds(row, ROW_BLOCK)
        total = terms[0][take, :].astype(F32)
        for term in terms[1:]:
            total = total + term[take, :].astype(F32)
        keys = total[:, :HD]
        square = jnp.sum(keys * keys, axis=1, keepdims=True) * (1.0 / HD)
        keys = keys * lax.rsqrt(square + epsilon) * gain_ref[...]
        done_ref[take, :HD] = keys.astype(BF16).T
        done_ref[take, HD:] = (total[:, HD:] * VALUE_SHIFT).astype(BF16)
    for out, places in zip(outs, picks):
        for n, place in enumerate(places):
            start = pl.multiple_of(meta_ref[place] * ROW_BLOCK, ROW_BLOCK)
            out[n] = done_ref[pl.ds(start, ROW_BLOCK), :]


def finish_tiles(meta, k_gain, terms, picks):
    rows, block = terms[0].shape
    return pl.pallas_call(
        functools.partial(finish_kernel, len(terms), picks),
        out_shape=[jax.ShapeDtypeStruct((len(p), ROW_BLOCK, block), BF16) for p in picks],
        in_specs=[SMEM] + [VMEM] * (1 + len(terms)),
        out_specs=[VMEM] * len(picks),
        scratch_shapes=[pltpu.VMEM((rows, block), BF16)],
        compiler_params=pltpu.CompilerParams(vmem_limit_bytes=8 * MIB),
        cost_estimate=LIGHT,
        name="finish_tiles",
    )(meta, lane_rows(k_gain), *terms)


def attend_kernel(group_count, sources, head, has_base, meta_ref, query_ref, *refs):
    tile_refs = refs[: len(sources)]
    out_hbm, out_ref, key_ref, value_ref, out_sem = refs[len(sources) + has_base :]
    place = meta_places(group_count)
    counts = (meta_ref[place["first"]], meta_ref[place["second"]])
    text_first, text_both = meta_ref[place["text_first"]], meta_ref[place["text_both"]]
    span = MAXT * ROW_BLOCK
    text_rows, width = out_ref.shape
    heads = width // HD
    for label in range(REQ_G):
        for tile in range(1, MAXT):

            @pl.when(counts[label] <= tile)
            def _(tile=label * MAXT + tile):
                take = slice(tile * ROW_BLOCK, (tile + 1) * ROW_BLOCK)
                key_ref[:, take] = jnp.zeros((HD, ROW_BLOCK), BF16)
                value_ref[take, :] = jnp.zeros((ROW_BLOCK, 2 * HD), BF16)

    for tile_ref, places in zip(tile_refs, sources):
        for n, slot in enumerate(places):
            if slot is None:
                continue
            goes = meta_ref[place["goes"] + slot]

            @pl.when(goes >= 0)
            def _(tile_ref=tile_ref, n=n, goes=goes):
                take = pl.ds(pl.multiple_of(goes * ROW_BLOCK, ROW_BLOCK), ROW_BLOCK)
                key_ref[:, take] = tile_ref[n, :, :HD]
                value_ref[take, :HD] = tile_ref[n, :, HD:]
                value_ref[take, HD:] = jnp.ones((ROW_BLOCK, HD), BF16)

    copies = []
    for block in range(text_rows // ROW_BLOCK):
        start = block * ROW_BLOCK
        take = pl.ds(start, ROW_BLOCK)
        for label, (low, high) in enumerate(((0, text_first), (text_first, text_both))):
            meets = jnp.maximum(low, start) < jnp.minimum(high, start + ROW_BLOCK)

            def attend(key_rows, label=label, start=start, take=take, low=low, high=high):
                part = pl.ds(label * span, key_rows)
                slots = start + lax.broadcasted_iota(jnp.int32, (ROW_BLOCK, HD), 0)
                owned = (slots >= low) & (slots < high)
                for first in range(0, heads, HEAD_GROUP):
                    group = range(first, min(first + HEAD_GROUP, heads))
                    column = head * width
                    stacked = jnp.concatenate(
                        [
                            query_ref[take, column + h * HD : column + (h + 1) * HD]
                            for h in group
                        ],
                        axis=0,
                    )
                    scores = jnp.dot(stacked, key_ref[:, part], preferred_element_type=F32)
                    weights = jnp.exp2(scores).astype(BF16)
                    sums = jnp.dot(weights, value_ref[part, :], preferred_element_type=F32)
                    result = sums[:, :HD] / sums[:, HD:] * (1.0 / VALUE_SHIFT)
                    for n, h in enumerate(group):
                        lanes = slice(h * HD, (h + 1) * HD)
                        own = result[n * ROW_BLOCK : (n + 1) * ROW_BLOCK]
                        kept = 0.0 if label == 0 else out_ref[take, lanes].astype(F32)
                        out_ref[take, lanes] = jnp.where(owned, own, kept).astype(BF16)

            half = span // 2
            few = counts[label] * ROW_BLOCK <= half

            @pl.when(meets & few)
            def _(attend=attend):
                attend(half)

            @pl.when(meets & jnp.logical_not(few))
            def _(attend=attend):
                attend(span)

            if label == 0:

                @pl.when(jnp.logical_not(meets))
                def _(take=take):
                    out_ref[take, :] = jnp.zeros((ROW_BLOCK, width), BF16)

        copies.append(
            pltpu.make_async_copy(
                out_ref.at[take, :],
                out_hbm.at[take, pl.ds(head * width, width)],
                out_sem.at[block],
            )
        )
        copies[-1].start()
    for copy in copies:
        copy.wait()


def attend_head(group_count, meta, queries, tiles, sources, base, head, head_count):
    rows, width = queries.shape
    head_width = width // head_count
    group_rows = REQ_G * MAXT * ROW_BLOCK
    extra = [] if base is None else [base]
    return pl.pallas_call(
        functools.partial(attend_kernel, group_count, sources, head, len(extra)),
        out_shape=jax.ShapeDtypeStruct((rows, width), BF16),
        in_specs=[SMEM] + [VMEM] * (1 + len(tiles)) + [HBM] * len(extra),
        out_specs=HBM,
        scratch_shapes=[
            pltpu.VMEM((rows, head_width), BF16),
            pltpu.VMEM((HD, group_rows), BF16),
            pltpu.VMEM((group_rows, 2 * HD), BF16),
            pltpu.SemaphoreType.DMA((rows // ROW_BLOCK,)),
        ],
        input_output_aliases={2 + len(tiles): 0} if extra else {},
        compiler_params=pltpu.CompilerParams(vmem_limit_bytes=24 * MIB),
        cost_estimate=LIGHT,
        name="attend_head",
    )(meta, queries, *tiles, *extra)


def add_rounded(a, b):
    return (a.astype(F32) + b.astype(F32)).astype(BF16)


def after(value, *others):
    others = [v for v in others if v is not None]
    return lax.optimization_barrier((value, others))[0]


def scatter_sum(blocks, count, first_bit, earlier=None):
    blocks = dict(enumerate(blocks))
    bits = bits_of(len(blocks))
    for b in range(bits):
        pairs = xor_pairs(count, 1 << (b + first_bit))
        got, sent = {}, None
        for k in sorted((k for k in blocks if (k >> b) & 1), reverse=True):
            sent = blocks[k]
            if b == bits - 1 and earlier is not None:
                sent = after(sent, earlier)
            got[k ^ (1 << b)] = lax.ppermute(sent, "tp", pairs)
        if b == bits - 1:
            return [blocks[0], got[0]], sent
        blocks = {k: add_rounded(blocks[k], got[k]) for k in got}
    return [blocks[0]], blocks[0]


def gather_half(whole, own, first, count, ready):
    bits = bits_of(count)
    pieces = {0: own}
    for b in reversed(range(1, bits)):
        pairs = xor_pairs(count, 1 << b)
        for k in sorted(pieces):
            pieces[k | (1 << b)] = lax.ppermute(pieces[k], "tp", pairs)
    pairs = xor_pairs(count, 1)
    for k in sorted(pieces):
        if k:
            pieces[k | 1] = lax.ppermute(after(pieces[k], ready), "tp", pairs)
    pieces[0], pieces[1] = whole
    bases = tuple(first if k < 2 else 0 for k in range(count))
    return [pieces[k] for k in range(count)], bases


def local(
    x_in,
    taps,
    ln_gain,
    ln_bias,
    w_up,
    b_up,
    w_down,
    b_down,
    kv_w_out,
    kv_w_taps,
    k_gain,
    q_gain,
    queries,
    tiles_per_request,
    owner,
    text_per_request,
):
    group_count = lax.axis_size("grp")
    tp_count = lax.axis_size("tp")
    position = jnp.stack([lax.axis_index("grp"), lax.axis_index("tp")]).astype(jnp.int32)
    where = jnp.concatenate([position, tiles_per_request, owner, text_per_request])
    tiles_local = x_in.shape[0]
    x_tiles = jnp.swapaxes(x_in, 2, 3)[:, 0]
    tap_tiles = jnp.swapaxes(taps, 2, 3)[:, 0]
    head_count = max(1, KVH // tp_count)
    dup = max(1, tp_count // KVH)
    dest_count = tp_count // dup
    place = meta_places(group_count)

    halves = HALVES if tiles_local % HALVES == 0 else 1
    tiles = tiles_local // halves
    own_halves = [x_tiles[:tiles]] + [
        after(x_tiles, where)[h * tiles : (h + 1) * tiles] for h in range(1, halves)
    ]
    whole = [x_tiles, lax.ppermute(x_tiles, "tp", xor_pairs(tp_count, 1))]

    tap_blocks = [(h, k) for h in range(head_count) for k in range(dest_count)]
    early = len(tap_blocks) * TAPS_EARLY // 8
    first_taps, w_up, w_down, tap_tiles = tap_projection(
        where, tap_tiles, kv_w_taps, tap_blocks[:early], head_count, dup, (w_up, w_down)
    )
    mlp_terms = []
    ready, begun = first_taps, where
    for half in range(halves):
        pieces, bases = gather_half(whole, own_halves[half], half * tiles, tp_count, ready)
        mlp_blocks = encoder_mlp(
            begun, pieces, bases, tiles, ln_gain, ln_bias, w_up, b_up, w_down
        )
        terms, sent = scatter_sum(mlp_blocks, tp_count, 0)
        mlp_terms.append(terms)
        ready, begun = mlp_blocks[0], after(where, sent)
    (last_taps,) = tap_projection(
        begun, tap_tiles, kv_w_taps, tap_blocks[early:], head_count, dup, ()
    )
    kv_blocks = kv_projection(
        where,
        x_tiles,
        b_down,
        kv_w_out,
        (first_taps, last_taps),
        mlp_terms,
        head_count,
        dest_count,
        dup,
    )
    kv_terms, arrived = [], None
    for head in range(head_count):
        blocks = kv_blocks[head]
        for b in range(bits_of(dup)):
            pairs = xor_pairs(tp_count, 1 << b)
            blocks = [add_rounded(v, lax.ppermute(v, "tp", pairs)) for v in blocks]
        terms, sent = scatter_sum(blocks, tp_count, bits_of(dup), arrived)
        kv_terms.append(terms)
        if head == 0:
            query_rows, meta = prepare(
                after(where, sent), q_gain, queries, group_count, tiles_local
            )
        arrived = (terms[-1], meta)

    slots = slot_count_of(group_count)
    total_tiles = group_count * tiles_local
    most_other = total_tiles - REQ_G * MAXT - REQ_G * (group_count - 2)
    one_large = group_count == 4 and slots == 2 and most_other <= group_count
    send = place["send"]
    out = None

    def move(value, mask):
        return lax.ppermute(value, "grp", xor_pairs(group_count, mask))

    for head in range(head_count):
        terms = kv_terms[head]
        if one_large:
            star = place["star"]
            picks = ((send, star), (send + 1, star), (send + 2, star), (send + 3,))
            own, near, middle, far = finish_tiles(meta, k_gain, terms, picks)
            middle_got, far_got, near_got = move(middle, 2), move(far, 3), move(near, 1)
            passed = move(after(middle_got[1:], far_got, out), 1)
            tiles = (own, near_got, middle_got, far_got, passed)
            sources = ((0, 4), (1, 5), (2, 6), (3,), (7,))
        else:
            picks = tuple(
                tuple(send + s * group_count + d for s in range(slots)) for d in range(group_count)
            )
            made = finish_tiles(meta, k_gain, terms, picks)
            tiles = tuple(made[:1]) + tuple(move(made[d], d) for d in range(1, group_count))
            sources = tuple(
                tuple(s * group_count + d for s in range(slots)) for d in range(group_count)
            )
        out = attend_head(
            group_count, meta, query_rows, tiles, sources, out, head, head_count
        )
    return out


def solution(mesh):
    in_specs = (
        P(None, ("rep", "grp"), None, "tp"),
        P(None, ("rep", "grp"), None, "tp"),
        P(),
        P(),
        P(None, "tp"),
        P("tp"),
        P("tp", None),
        P("tp"),
        P("tp", None),
        P("tp", None),
        P(),
        P(),
        P(("rep", "grp"), "tp"),
        P("rep"),
        P("rep"),
        P("rep"),
    )
    out_specs = P(("rep", "grp"), "tp")
    return jax.shard_map(local, mesh=mesh, in_specs=in_specs, out_specs=out_specs, check_vma=False)
```

```python
import functools
import math

import jax
import jax.numpy as jnp
from jax import lax
from jax.experimental import pallas as pl
from jax.experimental.pallas import tpu as pltpu
from jax.sharding import PartitionSpec as P

KVH = 8
HD = 128
MAXT = 4
REQ_G = 2
LANES = 128
ROW_BLOCK = 128
HIDDEN_BLOCK = 256
HEAD_GROUP = 8
HALVES = 1
TAPS_EARLY = 3
VALUE_SHIFT = 2.0**-24
epsilon = 1e-05

F32 = jnp.float32
BF16 = jnp.bfloat16
VMEM = pl.BlockSpec(memory_space=pltpu.VMEM)
HBM = pl.BlockSpec(memory_space=pltpu.HBM)
SMEM = pl.BlockSpec(memory_space=pltpu.SMEM)
MIB = 1024 * 1024
LIGHT = pl.CostEstimate(flops=1024, bytes_accessed=1024, transcendentals=0)


def bits_of(count):
    bits = count.bit_length() - 1
    assert 1 << bits == count
    return bits


def xor_order(blocks, index):
    blocks = list(blocks)
    for b in range(bits_of(len(blocks))):
        swap = ((index >> b) & 1) == 1
        for k in range(len(blocks)):
            if not (k >> b) & 1:
                low, high = blocks[k], blocks[k | (1 << b)]
                blocks[k] = lax.select(swap, high, low)
                blocks[k | (1 << b)] = lax.select(swap, low, high)
    return blocks


def xor_pairs(count, mask):
    return [(i, i ^ mask) for i in range(count)]


def lane_rows(vector):
    return jnp.pad(vector, (0, -vector.shape[0] % LANES)).reshape(-1, LANES)


def one_row(ref, width):
    rows = [ref[n : n + 1, :] for n in range(ref.shape[0])]
    return (rows[0] if len(rows) == 1 else jnp.concatenate(rows, axis=1))[:, :width]


def column_step(width):
    return HIDDEN_BLOCK if width % HIDDEN_BLOCK == 0 else width


def tail_plan(rows, width):
    whole = width // LANES * LANES
    tail = width - whole
    packed = tail > 0 and whole > 0 and whole % tail == 0 and rows * tail % whole == 0
    extra = rows * tail // whole if packed else 0
    packed = packed and extra % 16 == 0 and ROW_BLOCK % extra == 0
    return whole, tail, extra if packed else 0


def sent_shape(rows, width):
    whole, _, extra = tail_plan(rows, width)
    return (rows + extra, whole) if extra else (rows, width)


def layout_kernel(group_count, tiles_local, where_ref, meta_ref):
    group = where_ref[0]
    requests = (where_ref.shape[0] - 2) // 3
    tiles_of, owner_of, text_of = ([where_ref[2 + n * requests + r] for r in range(requests)] for n in range(3))
    zero = jnp.int32(0)
    firsts, counts, offsets, texts_first, texts_both = [], [], [], [], []
    offset = zero
    for p in range(group_count):
        first, count, text_first, text_both, seen = zero, zero, zero, zero, zero
        for r in range(requests):
            mine = owner_of[r] == p
            tiles = jnp.where(mine, tiles_of[r], 0)
            text = jnp.where(mine, text_of[r], 0)
            first = first + jnp.where(seen == 0, tiles, 0)
            text_first = text_first + jnp.where(seen == 0, text, 0)
            count = count + tiles
            text_both = text_both + text
            seen = seen + jnp.where(mine, 1, 0)
        firsts.append(first)
        counts.append(count)
        offsets.append(offset)
        texts_first.append(text_first)
        texts_both.append(text_both)
        offset = offset + count

    def pick(values, index):
        out = values[0]
        for p in range(1, group_count):
            out = jnp.where(index == p, values[p], out)
        return out

    slots = slot_count_of(group_count)
    star, most = zero, counts[0]
    for p in range(1, group_count):
        larger = counts[p] > most
        star = jnp.where(larger, p, star)
        most = jnp.where(larger, counts[p], most)

    def local_tile(offset, slot):
        lane = lax.rem(group - offset + group_count * REQ_G * MAXT * group_count, group_count)
        tile = lax.div(offset + slot * group_count + lane, group_count)
        return jnp.minimum(tile, tiles_local - 1)

    my_first, my_count = pick(firsts, group), pick(counts, group)
    my_offset = pick(offsets, group)
    place = meta_places(group_count)
    meta_ref[place["first"]] = my_first
    meta_ref[place["second"]] = my_count - my_first
    meta_ref[place["text_first"]] = pick(texts_first, group)
    meta_ref[place["text_both"]] = pick(texts_both, group)
    meta_ref[place["star"]] = local_tile(pick(offsets, star), 1)
    for slot in range(slots):
        for d in range(group_count):
            other = group ^ d
            meta_ref[place["send"] + slot * group_count + d] = local_tile(pick(offsets, other), slot)
            lane = lax.rem(other - my_offset + group_count * REQ_G * MAXT * group_count, group_count)
            position = slot * group_count + lane
            goes = jnp.where(
                position < my_first,
                position,
                jnp.where(position < my_count, MAXT + position - my_first, -1),
            )
            meta_ref[place["goes"] + slot * group_count + d] = goes


def slot_count_of(group_count):
    return (REQ_G * MAXT + group_count - 1) // group_count


def meta_places(group_count):
    table = slot_count_of(group_count) * group_count
    return {
        "first": 0,
        "second": 1,
        "text_first": 2,
        "text_both": 3,
        "star": 4,
        "send": 8,
        "goes": 8 + table,
        "size": 8 + 2 * table,
    }


def mlp_kernel(piece_count, bases, tiles, where_ref, *refs):
    pieces = refs[:piece_count]
    gain_ref, bias_ref, up_bias_ref, up_ref, down_ref = refs[piece_count : piece_count + 5]
    outs = refs[piece_count + 5 : 2 * piece_count + 5]
    cat_ref, normed_ref, hidden_ref, total_ref = refs[2 * piece_count + 5 :]
    index = where_ref[1]
    _, width, tile_rows = pieces[0].shape
    rows = tiles * tile_rows
    channels, hidden_width = up_ref.shape
    up_step = column_step(hidden_width)
    down_step = column_step(channels)

    gain, bias = one_row(gain_ref, channels), one_row(bias_ref, channels)
    up_bias = one_row(up_bias_ref, hidden_width)
    for tile in range(tiles):
        for k, piece in enumerate(pieces):
            start = pl.multiple_of((index ^ k) * width, math.gcd(width, LANES))
            cat_ref[pl.ds(start, width), :] = piece[bases[k] + tile]
        values = cat_ref[...].T.astype(F32)
        average = jnp.sum(values, axis=1, keepdims=True) * (1.0 / channels)
        centered = values - average
        variance = jnp.sum(centered * centered, axis=1, keepdims=True) * (1.0 / channels)
        normed = centered * lax.rsqrt(variance + epsilon)
        normed = normed * gain + bias
        normed_ref[tile * tile_rows : (tile + 1) * tile_rows, :] = normed.astype(BF16)
    for n in range(hidden_width // up_step):
        take = slice(n * up_step, (n + 1) * up_step)
        value = jnp.dot(normed_ref[...], up_ref[:, take], preferred_element_type=F32)
        value = value + up_bias[:, take]
        value = 0.5 * value * (1.0 + lax.erf(value * (1.0 / math.sqrt(2.0))))
        hidden_ref[:, take] = value.astype(BF16)
    for n in range(channels // down_step):
        take = slice(n * down_step, (n + 1) * down_step)
        total_ref[:, take] = jnp.dot(
            hidden_ref[...], down_ref[:, take], preferred_element_type=F32
        )
    whole, tail, extra = tail_plan(rows, width)
    step = extra or ROW_BLOCK
    for part in range(rows // step):
        take = pl.ds(part * step, step)
        blocks = [total_ref[take, j * width : (j + 1) * width] for j in range(piece_count)]
        for out, block in zip(outs, xor_order(blocks, index)):
            block = block.astype(BF16)
            if extra:
                out[take, :] = block[:, :whole]
                out[rows : rows + extra, part * tail : (part + 1) * tail] = block[:, whole:]
            else:
                out[take, :] = block


def encoder_mlp(where, pieces, bases, tiles, ln_gain, ln_bias, w_up, b_up, w_down):
    _, width, tile_rows = pieces[0].shape
    rows = tiles * tile_rows
    count = len(pieces)
    channels, hidden_width = w_up.shape
    shape = sent_shape(rows, width)
    return pl.pallas_call(
        functools.partial(mlp_kernel, count, bases, tiles),
        out_shape=[jax.ShapeDtypeStruct(shape, BF16)] * count,
        in_specs=[SMEM] + [VMEM] * (count + 5),
        out_specs=[VMEM] * count,
        scratch_shapes=[
            pltpu.VMEM((channels, tile_rows), BF16),
            pltpu.VMEM((rows, channels), BF16),
            pltpu.VMEM((rows, hidden_width), BF16),
            pltpu.VMEM((rows, channels), F32),
        ],
        compiler_params=pltpu.CompilerParams(vmem_limit_bytes=44 * MIB),
        cost_estimate=LIGHT,
        name="encoder_mlp",
    )(
        where,
        *pieces,
        lane_rows(ln_gain),
        lane_rows(ln_bias),
        lane_rows(b_up),
        w_up,
        w_down,
    )


def prepare_kernel(
    group_count,
    tiles_local,
    where_ref,
    gain_ref,
    query_ref,
    normed_ref,
    meta_ref,
):
    @pl.when(pl.program_id(0) == 0)
    def _():
        layout_kernel(group_count, tiles_local, where_ref, meta_ref)

    gain = gain_ref[...] * (math.log2(math.e) / math.sqrt(HD))
    for col in range(0, query_ref.shape[1], HD):
        values = query_ref[:, col : col + HD].astype(F32)
        square = jnp.sum(values * values, axis=1, keepdims=True) * (1.0 / HD)
        normed_ref[:, col : col + HD] = (values * lax.rsqrt(square + epsilon) * gain).astype(BF16)


def prepare(where, q_gain, queries, group_count, tiles_local):
    text_rows, width = queries.shape
    step = ROW_BLOCK
    return pl.pallas_call(
        functools.partial(prepare_kernel, group_count, tiles_local),
        out_shape=[
            jax.ShapeDtypeStruct((text_rows, width), BF16),
            jax.ShapeDtypeStruct((meta_places(group_count)["size"],), jnp.int32),
        ],
        grid=(text_rows // step,),
        in_specs=[
            SMEM,
            pl.BlockSpec((1, HD), lambda n: (0, 0)),
            pl.BlockSpec((step, width), lambda n: (n, 0)),
        ],
        out_specs=[pl.BlockSpec((step, width), lambda n: (n, 0)), SMEM],
        compiler_params=pltpu.CompilerParams(vmem_limit_bytes=16 * MIB),
        cost_estimate=LIGHT,
        name="prepare",
    )(where, lane_rows(q_gain), queries)


def tap_kernel(blocks, head_count, dup, staged, where_ref, tap_hbm, weight_hbm, *refs):
    sources, out_ref = refs[:staged], refs[staged]
    targets = refs[staged + 1 : 2 * staged + 1]
    if staged:
        tap_ref, weight_ref, tap_sem, weight_sem, staged_sem = refs[2 * staged + 1 :]
    else:
        tap_ref, (weight_ref, weight_sem) = tap_hbm, refs[1:]
    tiles, _, tile_rows = tap_ref.shape
    block = weight_ref.shape[2]
    mine = lax.div(where_ref[1], jnp.int32(dup))
    taps = [
        pltpu.make_async_copy(tap_hbm.at[n], tap_ref.at[n], tap_sem.at[n])
        for n in range(tiles if staged else 0)
    ]
    weights = []
    for n, (head, k) in enumerate(blocks):
        column = pl.multiple_of(((mine ^ k) * head_count + head) * block, block)
        weights.append(
            pltpu.make_async_copy(
                weight_hbm.at[:, pl.ds(column, block)], weight_ref.at[n], weight_sem.at[n]
            )
        )
    others = [
        pltpu.make_async_copy(source, target, staged_sem.at[n])
        for n, (source, target) in enumerate(zip(sources, targets))
    ]
    for copy in weights[:1] + taps + weights[1:] + others:
        copy.start()
    for n in range(len(blocks)):
        weights[n].wait()
        for tile in range(tiles):
            if n == 0 and staged:
                taps[tile].wait()
            value = lax.dot_general(
                tap_ref[tile],
                weight_ref[n],
                (((0,), (0,)), ((), ())),
                preferred_element_type=F32,
            )
            out_ref[n, tile * tile_rows : (tile + 1) * tile_rows, :] = value.astype(BF16)
    for copy in others:
        copy.wait()


def tap_projection(where, tap_tiles, weights, blocks, head_count, dup, staged):
    tiles, depth, tile_rows = tap_tiles.shape
    block = 2 * HD
    return pl.pallas_call(
        functools.partial(tap_kernel, blocks, head_count, dup, len(staged)),
        out_shape=[jax.ShapeDtypeStruct((len(blocks), tiles * tile_rows, block), BF16)]
        + [jax.ShapeDtypeStruct(w.shape, w.dtype) for w in staged]
        + ([jax.ShapeDtypeStruct(tap_tiles.shape, BF16)] if staged else []),
        in_specs=[SMEM, HBM if staged else VMEM, HBM] + [HBM] * len(staged),
        out_specs=[VMEM] * (1 + len(staged) + bool(staged)),
        scratch_shapes=[pltpu.VMEM((len(blocks), depth, block), BF16)]
        + ([pltpu.SemaphoreType.DMA((tiles,))] if staged else [])
        + [pltpu.SemaphoreType.DMA((len(blocks),))]
        + ([pltpu.SemaphoreType.DMA((len(staged),))] if staged else []),
        compiler_params=pltpu.CompilerParams(vmem_limit_bytes=(42 if staged else 50) * MIB),
        cost_estimate=LIGHT,
        name="tap_projection",
    )(where, tap_tiles, weights, *staged)


def kv_kernel(head_count, dest_count, dup, part_count, term_counts, where_ref, *refs):
    x_ref, bias_ref, weight_ref = refs[:3]
    tap_blocks = [ref.at[n] for ref in refs[3 : 3 + part_count] for n in range(ref.shape[0])]
    terms = refs[3 + part_count : 3 + part_count + sum(term_counts)]
    outs = refs[3 + part_count + sum(term_counts) : -1]
    encoded_ref = refs[-1]
    tiles, width, tile_rows = x_ref.shape
    half_tiles = tiles // len(term_counts)
    whole, tail, extra = tail_plan(half_tiles * tile_rows, width)
    bias = one_row(bias_ref, width)
    for tile in range(tiles):
        half, row = tile // half_tiles, tile % half_tiles * tile_rows
        mine = terms[sum(term_counts[:half]) : sum(term_counts[: half + 1])]

        def summed(part, lanes):
            out = mine[0][part, lanes].astype(F32)
            for term in mine[1:]:
                out = out + term[part, lanes].astype(F32)
            return out

        total = summed(pl.ds(row, tile_rows), slice(None))
        if extra:
            chunks = range(row // extra, (row + tile_rows) // extra)
            rest = [
                summed(pl.ds(half_tiles * tile_rows, extra), slice(c * tail, (c + 1) * tail))
                for c in chunks
            ]
            rest = rest[0] if len(rest) == 1 else jnp.concatenate(rest, axis=0)
            total = jnp.concatenate([total, rest], axis=1)
        total = total + x_ref[tile].T.astype(F32) + bias
        encoded_ref[tile * tile_rows : (tile + 1) * tile_rows, :] = total.astype(BF16)
    block = 2 * HD
    mine = lax.div(where_ref[1], jnp.int32(dup))
    for head in range(head_count):
        for k in range(dest_count):
            column = ((mine ^ k) * head_count + head) * block
            weights = weight_ref[:, pl.ds(pl.multiple_of(column, block), block)]
            value = jnp.dot(encoded_ref[...], weights, preferred_element_type=F32)
            value = value + tap_blocks[head * dest_count + k][...].astype(F32)
            outs[head * dest_count + k][...] = value.astype(BF16)


def kv_projection(
    where, x_tiles, b_down, weights, tap_parts, halves, head_count, dest_count, dup
):
    terms = [term for half in halves for term in half]
    tiles, width, tile_rows = x_tiles.shape
    rows = tiles * tile_rows
    block = 2 * HD
    outs = pl.pallas_call(
        functools.partial(
            kv_kernel,
            head_count,
            dest_count,
            dup,
            len(tap_parts),
            tuple(len(half) for half in halves),
        ),
        out_shape=[jax.ShapeDtypeStruct((rows, block), BF16)] * (head_count * dest_count),
        in_specs=[SMEM] + [VMEM] * (3 + len(tap_parts) + len(terms)),
        out_specs=[VMEM] * (head_count * dest_count),
        scratch_shapes=[pltpu.VMEM((rows, width), BF16)],
        compiler_params=pltpu.CompilerParams(vmem_limit_bytes=24 * MIB),
        cost_estimate=LIGHT,
        name="kv_projection",
    )(where, x_tiles, lane_rows(b_down), weights, *tap_parts, *terms)
    return [outs[h * dest_count : (h + 1) * dest_count] for h in range(head_count)]


def finish_kernel(term_count, picks, meta_ref, gain_ref, *refs):
    terms = refs[:term_count]
    outs = refs[term_count : term_count + len(picks)]
    done_ref = refs[-1]
    rows = terms[0].shape[0]
    for row in range(0, rows, ROW_BLOCK):
        take = pl.ds(row, ROW_BLOCK)
        total = terms[0][take, :].astype(F32)
        for term in terms[1:]:
            total = total + term[take, :].astype(F32)
        keys = total[:, :HD]
        square = jnp.sum(keys * keys, axis=1, keepdims=True) * (1.0 / HD)
        keys = keys * lax.rsqrt(square + epsilon) * gain_ref[...]
        done_ref[take, :HD] = keys.astype(BF16).T
        done_ref[take, HD:] = (total[:, HD:] * VALUE_SHIFT).astype(BF16)
    for out, places in zip(outs, picks):
        for n, place in enumerate(places):
            start = pl.multiple_of(meta_ref[place] * ROW_BLOCK, ROW_BLOCK)
            out[n] = done_ref[pl.ds(start, ROW_BLOCK), :]


def finish_tiles(meta, k_gain, terms, picks):
    rows, block = terms[0].shape
    return pl.pallas_call(
        functools.partial(finish_kernel, len(terms), picks),
        out_shape=[jax.ShapeDtypeStruct((len(p), ROW_BLOCK, block), BF16) for p in picks],
        in_specs=[SMEM] + [VMEM] * (1 + len(terms)),
        out_specs=[VMEM] * len(picks),
        scratch_shapes=[pltpu.VMEM((rows, block), BF16)],
        compiler_params=pltpu.CompilerParams(vmem_limit_bytes=8 * MIB),
        cost_estimate=LIGHT,
        name="finish_tiles",
    )(meta, lane_rows(k_gain), *terms)


def attend_kernel(group_count, sources, head, has_base, meta_ref, query_ref, *refs):
    tile_refs = refs[: len(sources)]
    out_hbm, out_ref, key_ref, value_ref, out_sem = refs[len(sources) + has_base :]
    place = meta_places(group_count)
    counts = (meta_ref[place["first"]], meta_ref[place["second"]])
    text_first, text_both = meta_ref[place["text_first"]], meta_ref[place["text_both"]]
    span = MAXT * ROW_BLOCK
    text_rows, width = out_ref.shape
    heads = width // HD
    for label in range(REQ_G):
        for tile in range(1, MAXT):

            @pl.when(counts[label] <= tile)
            def _(tile=label * MAXT + tile):
                take = slice(tile * ROW_BLOCK, (tile + 1) * ROW_BLOCK)
                key_ref[:, take] = jnp.zeros((HD, ROW_BLOCK), BF16)
                value_ref[take, :] = jnp.zeros((ROW_BLOCK, 2 * HD), BF16)

    for tile_ref, places in zip(tile_refs, sources):
        for n, slot in enumerate(places):
            if slot is None:
                continue
            goes = meta_ref[place["goes"] + slot]

            @pl.when(goes >= 0)
            def _(tile_ref=tile_ref, n=n, goes=goes):
                take = pl.ds(pl.multiple_of(goes * ROW_BLOCK, ROW_BLOCK), ROW_BLOCK)
                key_ref[:, take] = tile_ref[n, :, :HD]
                value_ref[take, :HD] = tile_ref[n, :, HD:]
                value_ref[take, HD:] = jnp.ones((ROW_BLOCK, HD), BF16)

    copies = []
    for block in range(text_rows // ROW_BLOCK):
        start = block * ROW_BLOCK
        take = pl.ds(start, ROW_BLOCK)
        for label, (low, high) in enumerate(((0, text_first), (text_first, text_both))):
            meets = jnp.maximum(low, start) < jnp.minimum(high, start + ROW_BLOCK)

            def attend(key_rows, label=label, start=start, take=take, low=low, high=high):
                part = pl.ds(label * span, key_rows)
                slots = start + lax.broadcasted_iota(jnp.int32, (ROW_BLOCK, HD), 0)
                owned = (slots >= low) & (slots < high)
                for first in range(0, heads, HEAD_GROUP):
                    group = range(first, min(first + HEAD_GROUP, heads))
                    column = head * width
                    stacked = jnp.concatenate(
                        [
                            query_ref[take, column + h * HD : column + (h + 1) * HD]
                            for h in group
                        ],
                        axis=0,
                    )
                    scores = jnp.dot(stacked, key_ref[:, part], preferred_element_type=F32)
                    weights = jnp.exp2(scores).astype(BF16)
                    sums = jnp.dot(weights, value_ref[part, :], preferred_element_type=F32)
                    result = sums[:, :HD] / sums[:, HD:] * (1.0 / VALUE_SHIFT)
                    for n, h in enumerate(group):
                        lanes = slice(h * HD, (h + 1) * HD)
                        own = result[n * ROW_BLOCK : (n + 1) * ROW_BLOCK]
                        kept = 0.0 if label == 0 else out_ref[take, lanes].astype(F32)
                        out_ref[take, lanes] = jnp.where(owned, own, kept).astype(BF16)

            half = span // 2
            few = counts[label] * ROW_BLOCK <= half

            @pl.when(meets & few)
            def _(attend=attend):
                attend(half)

            @pl.when(meets & jnp.logical_not(few))
            def _(attend=attend):
                attend(span)

            if label == 0:

                @pl.when(jnp.logical_not(meets))
                def _(take=take):
                    out_ref[take, :] = jnp.zeros((ROW_BLOCK, width), BF16)

        copies.append(
            pltpu.make_async_copy(
                out_ref.at[take, :],
                out_hbm.at[take, pl.ds(head * width, width)],
                out_sem.at[block],
            )
        )
        copies[-1].start()
    for copy in copies:
        copy.wait()


def attend_head(group_count, meta, queries, tiles, sources, base, head, head_count):
    rows, width = queries.shape
    head_width = width // head_count
    group_rows = REQ_G * MAXT * ROW_BLOCK
    extra = [] if base is None else [base]
    return pl.pallas_call(
        functools.partial(attend_kernel, group_count, sources, head, len(extra)),
        out_shape=jax.ShapeDtypeStruct((rows, width), BF16),
        in_specs=[SMEM] + [VMEM] * (1 + len(tiles)) + [HBM] * len(extra),
        out_specs=HBM,
        scratch_shapes=[
            pltpu.VMEM((rows, head_width), BF16),
            pltpu.VMEM((HD, group_rows), BF16),
            pltpu.VMEM((group_rows, 2 * HD), BF16),
            pltpu.SemaphoreType.DMA((rows // ROW_BLOCK,)),
        ],
        input_output_aliases={2 + len(tiles): 0} if extra else {},
        compiler_params=pltpu.CompilerParams(vmem_limit_bytes=24 * MIB),
        cost_estimate=LIGHT,
        name="attend_head",
    )(meta, queries, *tiles, *extra)


def add_rounded(a, b):
    return (a.astype(F32) + b.astype(F32)).astype(BF16)


def after(value, *others):
    others = [v for v in others if v is not None]
    return lax.optimization_barrier((value, others))[0]


def scatter_sum(blocks, count, first_bit, earlier=None):
    blocks = dict(enumerate(blocks))
    bits = bits_of(len(blocks))
    for b in range(bits):
        pairs = xor_pairs(count, 1 << (b + first_bit))
        got, sent = {}, None
        for k in sorted((k for k in blocks if (k >> b) & 1), reverse=True):
            sent = blocks[k]
            if b == bits - 1 and earlier is not None:
                sent = after(sent, earlier)
            got[k ^ (1 << b)] = lax.ppermute(sent, "tp", pairs)
        if b == bits - 1:
            return [blocks[0], got[0]], sent
        blocks = {k: add_rounded(blocks[k], got[k]) for k in got}
    return [blocks[0]], blocks[0]


def gather_half(whole, own, first, count, ready):
    bits = bits_of(count)
    pieces = {0: own}
    for b in reversed(range(1, bits)):
        pairs = xor_pairs(count, 1 << b)
        for k in sorted(pieces):
            pieces[k | (1 << b)] = lax.ppermute(pieces[k], "tp", pairs)
    pairs = xor_pairs(count, 1)
    for k in sorted(pieces):
        if k:
            pieces[k | 1] = lax.ppermute(after(pieces[k], ready), "tp", pairs)
    pieces[0], pieces[1] = whole
    bases = tuple(first if k < 2 else 0 for k in range(count))
    return [pieces[k] for k in range(count)], bases


def local(
    x_in,
    taps,
    ln_gain,
    ln_bias,
    w_up,
    b_up,
    w_down,
    b_down,
    kv_w_out,
    kv_w_taps,
    k_gain,
    q_gain,
    queries,
    tiles_per_request,
    owner,
    text_per_request,
):
    group_count = lax.axis_size("grp")
    tp_count = lax.axis_size("tp")
    position = jnp.stack([lax.axis_index("grp"), lax.axis_index("tp")]).astype(jnp.int32)
    where = jnp.concatenate([position, tiles_per_request, owner, text_per_request])
    tiles_local = x_in.shape[0]
    x_tiles = jnp.swapaxes(x_in, 2, 3)[:, 0]
    tap_tiles = jnp.swapaxes(taps, 2, 3)[:, 0]
    head_count = max(1, KVH // tp_count)
    dup = max(1, tp_count // KVH)
    dest_count = tp_count // dup
    place = meta_places(group_count)

    halves = HALVES if tiles_local % HALVES == 0 else 1
    tiles = tiles_local // halves
    own_halves = [x_tiles[:tiles]] + [
        after(x_tiles, where)[h * tiles : (h + 1) * tiles] for h in range(1, halves)
    ]
    whole = [x_tiles, lax.ppermute(x_tiles, "tp", xor_pairs(tp_count, 1))]

    tap_blocks = [(h, k) for h in range(head_count) for k in range(dest_count)]
    early = len(tap_blocks) * TAPS_EARLY // 8
    first_taps, w_up, w_down, tap_tiles = tap_projection(
        where, tap_tiles, kv_w_taps, tap_blocks[:early], head_count, dup, (w_up, w_down)
    )
    mlp_terms = []
    ready, begun = first_taps, where
    for half in range(halves):
        pieces, bases = gather_half(whole, own_halves[half], half * tiles, tp_count, ready)
        mlp_blocks = encoder_mlp(
            begun, pieces, bases, tiles, ln_gain, ln_bias, w_up, b_up, w_down
        )
        terms, sent = scatter_sum(mlp_blocks, tp_count, 0)
        mlp_terms.append(terms)
        ready, begun = mlp_blocks[0], after(where, sent)
    (last_taps,) = tap_projection(
        begun, tap_tiles, kv_w_taps, tap_blocks[early:], head_count, dup, ()
    )
    kv_blocks = kv_projection(
        where,
        x_tiles,
        b_down,
        kv_w_out,
        (first_taps, last_taps),
        mlp_terms,
        head_count,
        dest_count,
        dup,
    )
    kv_terms, arrived = [], None
    for head in range(head_count):
        blocks = kv_blocks[head]
        for b in range(bits_of(dup)):
            pairs = xor_pairs(tp_count, 1 << b)
            blocks = [add_rounded(v, lax.ppermute(v, "tp", pairs)) for v in blocks]
        terms, sent = scatter_sum(blocks, tp_count, bits_of(dup), arrived)
        kv_terms.append(terms)
        if head == 0:
            query_rows, meta = prepare(
                after(where, sent), q_gain, queries, group_count, tiles_local
            )
        arrived = (terms[-1], meta)

    slots = slot_count_of(group_count)
    total_tiles = group_count * tiles_local
    most_other = total_tiles - REQ_G * MAXT - REQ_G * (group_count - 2)
    one_large = group_count == 4 and slots == 2 and most_other <= group_count
    send = place["send"]
    out = None

    def move(value, mask):
        return lax.ppermute(value, "grp", xor_pairs(group_count, mask))

    for head in range(head_count):
        terms = kv_terms[head]
        if one_large:
            star = place["star"]
            direct = head == head_count - 1
            picks = ((send, star), (send + 1, star), (send + 2, star))
            picks += ((send + 3, star) if direct else (send + 3,),)
            own, near, middle, far = finish_tiles(meta, k_gain, terms, picks)
            middle_got, far_got, near_got = move(middle, 2), move(far, 3), move(near, 1)
            tiles = (own, near_got, middle_got, far_got)
            sources = ((0, 4), (1, 5), (2, 6), (3, 7) if direct else (3,))
            if not direct:
                tiles += (move(after(middle_got[1:], far_got, out), 1),)
                sources += ((7,),)
        else:
            picks = tuple(
                tuple(send + s * group_count + d for s in range(slots)) for d in range(group_count)
            )
            made = finish_tiles(meta, k_gain, terms, picks)
            tiles = tuple(made[:1]) + tuple(move(made[d], d) for d in range(1, group_count))
            sources = tuple(
                tuple(s * group_count + d for s in range(slots)) for d in range(group_count)
            )
        out = attend_head(
            group_count, meta, query_rows, tiles, sources, out, head, head_count
        )
    return out


def solution(mesh):
    in_specs = (
        P(None, ("rep", "grp"), None, "tp"),
        P(None, ("rep", "grp"), None, "tp"),
        P(),
        P(),
        P(None, "tp"),
        P("tp"),
        P("tp", None),
        P("tp"),
        P("tp", None),
        P("tp", None),
        P(),
        P(),
        P(("rep", "grp"), "tp"),
        P("rep"),
        P("rep"),
        P("rep"),
    )
    out_specs = P(("rep", "grp"), "tp")
    return jax.shard_map(local, mesh=mesh, in_specs=in_specs, out_specs=out_specs, check_vma=False)
```

```python
import functools
import math

import jax
import jax.numpy as jnp
from jax import lax
from jax.experimental import pallas as pl
from jax.experimental.pallas import tpu as pltpu
from jax.sharding import PartitionSpec as P

KVH = 8
HD = 128
MAXT = 4
REQ_G = 2
LANES = 128
ROW_BLOCK = 128
HIDDEN_BLOCK = 256
HEAD_GROUP = 8
HALVES = 1
TAPS_EARLY = 3
VALUE_SHIFT = 2.0**-24
epsilon = 1e-05

F32 = jnp.float32
BF16 = jnp.bfloat16
VMEM = pl.BlockSpec(memory_space=pltpu.VMEM)
HBM = pl.BlockSpec(memory_space=pltpu.HBM)
SMEM = pl.BlockSpec(memory_space=pltpu.SMEM)
MIB = 1024 * 1024
LIGHT = pl.CostEstimate(flops=1024, bytes_accessed=1024, transcendentals=0)


def bits_of(count):
    bits = count.bit_length() - 1
    assert 1 << bits == count
    return bits


def xor_order(blocks, index):
    blocks = list(blocks)
    for b in range(bits_of(len(blocks))):
        swap = ((index >> b) & 1) == 1
        for k in range(len(blocks)):
            if not (k >> b) & 1:
                low, high = blocks[k], blocks[k | (1 << b)]
                blocks[k] = lax.select(swap, high, low)
                blocks[k | (1 << b)] = lax.select(swap, low, high)
    return blocks


def xor_pairs(count, mask):
    return [(i, i ^ mask) for i in range(count)]


def lane_rows(vector):
    return jnp.pad(vector, (0, -vector.shape[0] % LANES)).reshape(-1, LANES)


def one_row(ref, width):
    rows = [ref[n : n + 1, :] for n in range(ref.shape[0])]
    return (rows[0] if len(rows) == 1 else jnp.concatenate(rows, axis=1))[:, :width]


def column_step(width):
    return HIDDEN_BLOCK if width % HIDDEN_BLOCK == 0 else width


def tail_plan(rows, width):
    whole = width // LANES * LANES
    tail = width - whole
    packed = tail > 0 and whole > 0 and whole % tail == 0 and rows * tail % whole == 0
    extra = rows * tail // whole if packed else 0
    packed = packed and extra % 16 == 0 and ROW_BLOCK % extra == 0
    return whole, tail, extra if packed else 0


def sent_shape(rows, width):
    whole, _, extra = tail_plan(rows, width)
    return (rows + extra, whole) if extra else (rows, width)


def layout_kernel(group_count, tiles_local, where_ref, meta_ref):
    group = where_ref[0]
    requests = (where_ref.shape[0] - 2) // 3
    tiles_of, owner_of, text_of = ([where_ref[2 + n * requests + r] for r in range(requests)] for n in range(3))
    zero = jnp.int32(0)
    firsts, counts, offsets, texts_first, texts_both = [], [], [], [], []
    offset = zero
    for p in range(group_count):
        first, count, text_first, text_both, seen = zero, zero, zero, zero, zero
        for r in range(requests):
            mine = owner_of[r] == p
            tiles = jnp.where(mine, tiles_of[r], 0)
            text = jnp.where(mine, text_of[r], 0)
            first = first + jnp.where(seen == 0, tiles, 0)
            text_first = text_first + jnp.where(seen == 0, text, 0)
            count = count + tiles
            text_both = text_both + text
            seen = seen + jnp.where(mine, 1, 0)
        firsts.append(first)
        counts.append(count)
        offsets.append(offset)
        texts_first.append(text_first)
        texts_both.append(text_both)
        offset = offset + count

    def pick(values, index):
        out = values[0]
        for p in range(1, group_count):
            out = jnp.where(index == p, values[p], out)
        return out

    slots = slot_count_of(group_count)
    star, most = zero, counts[0]
    for p in range(1, group_count):
        larger = counts[p] > most
        star = jnp.where(larger, p, star)
        most = jnp.where(larger, counts[p], most)

    def local_tile(offset, slot):
        lane = lax.rem(group - offset + group_count * REQ_G * MAXT * group_count, group_count)
        tile = lax.div(offset + slot * group_count + lane, group_count)
        return jnp.minimum(tile, tiles_local - 1)

    my_first, my_count = pick(firsts, group), pick(counts, group)
    my_offset = pick(offsets, group)
    place = meta_places(group_count)
    meta_ref[place["first"]] = my_first
    meta_ref[place["second"]] = my_count - my_first
    meta_ref[place["text_first"]] = pick(texts_first, group)
    meta_ref[place["text_both"]] = pick(texts_both, group)
    meta_ref[place["star"]] = local_tile(pick(offsets, star), 1)
    for slot in range(slots):
        for d in range(group_count):
            other = group ^ d
            meta_ref[place["send"] + slot * group_count + d] = local_tile(pick(offsets, other), slot)
            lane = lax.rem(other - my_offset + group_count * REQ_G * MAXT * group_count, group_count)
            position = slot * group_count + lane
            goes = jnp.where(
                position < my_first,
                position,
                jnp.where(position < my_count, MAXT + position - my_first, -1),
            )
            meta_ref[place["goes"] + slot * group_count + d] = goes


def slot_count_of(group_count):
    return (REQ_G * MAXT + group_count - 1) // group_count


def meta_places(group_count):
    table = slot_count_of(group_count) * group_count
    return {
        "first": 0,
        "second": 1,
        "text_first": 2,
        "text_both": 3,
        "star": 4,
        "send": 8,
        "goes": 8 + table,
        "size": 8 + 2 * table,
    }


def mlp_kernel(piece_count, bases, tiles, where_ref, *refs):
    pieces = refs[:piece_count]
    gain_ref, bias_ref, up_bias_ref, up_ref, down_ref = refs[piece_count : piece_count + 5]
    outs = refs[piece_count + 5 : 2 * piece_count + 5]
    cat_ref, normed_ref, hidden_ref, total_ref = refs[2 * piece_count + 5 :]
    index = where_ref[1]
    _, width, tile_rows = pieces[0].shape
    rows = tiles * tile_rows
    channels, hidden_width = up_ref.shape
    up_step = column_step(hidden_width)
    down_step = column_step(channels)

    gain, bias = one_row(gain_ref, channels), one_row(bias_ref, channels)
    up_bias = one_row(up_bias_ref, hidden_width)
    for tile in range(tiles):
        for k, piece in enumerate(pieces):
            start = pl.multiple_of((index ^ k) * width, math.gcd(width, LANES))
            cat_ref[pl.ds(start, width), :] = piece[bases[k] + tile]
        values = cat_ref[...].T.astype(F32)
        average = jnp.sum(values, axis=1, keepdims=True) * (1.0 / channels)
        centered = values - average
        variance = jnp.sum(centered * centered, axis=1, keepdims=True) * (1.0 / channels)
        normed = centered * lax.rsqrt(variance + epsilon)
        normed = normed * gain + bias
        normed_ref[tile * tile_rows : (tile + 1) * tile_rows, :] = normed.astype(BF16)
    for n in range(hidden_width // up_step):
        take = slice(n * up_step, (n + 1) * up_step)
        value = jnp.dot(normed_ref[...], up_ref[:, take], preferred_element_type=F32)
        value = value + up_bias[:, take]
        value = 0.5 * value * (1.0 + lax.erf(value * (1.0 / math.sqrt(2.0))))
        hidden_ref[:, take] = value.astype(BF16)
    for n in range(channels // down_step):
        take = slice(n * down_step, (n + 1) * down_step)
        total_ref[:, take] = jnp.dot(
            hidden_ref[...], down_ref[:, take], preferred_element_type=F32
        )
    whole, tail, extra = tail_plan(rows, width)
    step = extra or ROW_BLOCK
    for part in range(rows // step):
        take = pl.ds(part * step, step)
        blocks = [total_ref[take, j * width : (j + 1) * width] for j in range(piece_count)]
        for out, block in zip(outs, xor_order(blocks, index)):
            block = block.astype(BF16)
            if extra:
                out[take, :] = block[:, :whole]
                out[rows : rows + extra, part * tail : (part + 1) * tail] = block[:, whole:]
            else:
                out[take, :] = block


def encoder_mlp(where, pieces, bases, tiles, ln_gain, ln_bias, w_up, b_up, w_down):
    _, width, tile_rows = pieces[0].shape
    rows = tiles * tile_rows
    count = len(pieces)
    channels, hidden_width = w_up.shape
    shape = sent_shape(rows, width)
    return pl.pallas_call(
        functools.partial(mlp_kernel, count, bases, tiles),
        out_shape=[jax.ShapeDtypeStruct(shape, BF16)] * count,
        in_specs=[SMEM] + [VMEM] * (count + 5),
        out_specs=[VMEM] * count,
        scratch_shapes=[
            pltpu.VMEM((channels, tile_rows), BF16),
            pltpu.VMEM((rows, channels), BF16),
            pltpu.VMEM((rows, hidden_width), BF16),
            pltpu.VMEM((rows, channels), F32),
        ],
        compiler_params=pltpu.CompilerParams(vmem_limit_bytes=44 * MIB),
        cost_estimate=LIGHT,
        name="encoder_mlp",
    )(
        where,
        *pieces,
        lane_rows(ln_gain),
        lane_rows(ln_bias),
        lane_rows(b_up),
        w_up,
        w_down,
    )


def prepare_kernel(
    group_count,
    tiles_local,
    where_ref,
    gain_ref,
    query_ref,
    normed_ref,
    meta_ref,
):
    @pl.when(pl.program_id(0) == 0)
    def _():
        layout_kernel(group_count, tiles_local, where_ref, meta_ref)

    gain = gain_ref[...] * (math.log2(math.e) / math.sqrt(HD))
    for col in range(0, query_ref.shape[1], HD):
        values = query_ref[:, col : col + HD].astype(F32)
        square = jnp.sum(values * values, axis=1, keepdims=True) * (1.0 / HD)
        normed_ref[:, col : col + HD] = (values * lax.rsqrt(square + epsilon) * gain).astype(BF16)


def prepare(where, q_gain, queries, group_count, tiles_local):
    text_rows, width = queries.shape
    step = ROW_BLOCK
    return pl.pallas_call(
        functools.partial(prepare_kernel, group_count, tiles_local),
        out_shape=[
            jax.ShapeDtypeStruct((text_rows, width), BF16),
            jax.ShapeDtypeStruct((meta_places(group_count)["size"],), jnp.int32),
        ],
        grid=(text_rows // step,),
        in_specs=[
            SMEM,
            pl.BlockSpec((1, HD), lambda n: (0, 0)),
            pl.BlockSpec((step, width), lambda n: (n, 0)),
        ],
        out_specs=[pl.BlockSpec((step, width), lambda n: (n, 0)), SMEM],
        compiler_params=pltpu.CompilerParams(vmem_limit_bytes=16 * MIB),
        cost_estimate=LIGHT,
        name="prepare",
    )(where, lane_rows(q_gain), queries)


def tap_kernel(blocks, head_count, dup, staged, where_ref, tap_hbm, weight_hbm, *refs):
    sources, out_ref = refs[:staged], refs[staged]
    targets = refs[staged + 1 : 2 * staged + 1]
    if staged:
        tap_ref, weight_ref, tap_sem, weight_sem, staged_sem = refs[2 * staged + 1 :]
    else:
        tap_ref, (weight_ref, weight_sem) = tap_hbm, refs[1:]
    tiles, _, tile_rows = tap_ref.shape
    block = weight_ref.shape[2]
    mine = lax.div(where_ref[1], jnp.int32(dup))
    taps = [
        pltpu.make_async_copy(tap_hbm.at[n], tap_ref.at[n], tap_sem.at[n])
        for n in range(tiles if staged else 0)
    ]
    weights = []
    for n, (head, k) in enumerate(blocks):
        column = pl.multiple_of(((mine ^ k) * head_count + head) * block, block)
        weights.append(
            pltpu.make_async_copy(
                weight_hbm.at[:, pl.ds(column, block)], weight_ref.at[n], weight_sem.at[n]
            )
        )
    others = [
        pltpu.make_async_copy(source, target, staged_sem.at[n])
        for n, (source, target) in enumerate(zip(sources, targets))
    ]
    for copy in weights[:1] + taps + weights[1:] + others:
        copy.start()
    for n in range(len(blocks)):
        weights[n].wait()
        for tile in range(tiles):
            if n == 0 and staged:
                taps[tile].wait()
            value = lax.dot_general(
                tap_ref[tile],
                weight_ref[n],
                (((0,), (0,)), ((), ())),
                preferred_element_type=F32,
            )
            out_ref[n, tile * tile_rows : (tile + 1) * tile_rows, :] = value.astype(BF16)
    for copy in others:
        copy.wait()


def tap_projection(where, tap_tiles, weights, blocks, head_count, dup, staged):
    tiles, depth, tile_rows = tap_tiles.shape
    block = 2 * HD
    return pl.pallas_call(
        functools.partial(tap_kernel, blocks, head_count, dup, len(staged)),
        out_shape=[jax.ShapeDtypeStruct((len(blocks), tiles * tile_rows, block), BF16)]
        + [jax.ShapeDtypeStruct(w.shape, w.dtype) for w in staged]
        + ([jax.ShapeDtypeStruct(tap_tiles.shape, BF16)] if staged else []),
        in_specs=[SMEM, HBM if staged else VMEM, HBM] + [HBM] * len(staged),
        out_specs=[VMEM] * (1 + len(staged) + bool(staged)),
        scratch_shapes=[pltpu.VMEM((len(blocks), depth, block), BF16)]
        + ([pltpu.SemaphoreType.DMA((tiles,))] if staged else [])
        + [pltpu.SemaphoreType.DMA((len(blocks),))]
        + ([pltpu.SemaphoreType.DMA((len(staged),))] if staged else []),
        compiler_params=pltpu.CompilerParams(vmem_limit_bytes=(42 if staged else 50) * MIB),
        cost_estimate=LIGHT,
        name="tap_projection",
    )(where, tap_tiles, weights, *staged)


def kv_kernel(head_count, dest_count, dup, part_count, term_counts, where_ref, *refs):
    x_ref, bias_ref, weight_ref = refs[:3]
    tap_blocks = [ref.at[n] for ref in refs[3 : 3 + part_count] for n in range(ref.shape[0])]
    terms = refs[3 + part_count : 3 + part_count + sum(term_counts)]
    outs = refs[3 + part_count + sum(term_counts) : -1]
    encoded_ref = refs[-1]
    tiles, width, tile_rows = x_ref.shape
    half_tiles = tiles // len(term_counts)
    whole, tail, extra = tail_plan(half_tiles * tile_rows, width)
    bias = one_row(bias_ref, width)
    for tile in range(tiles):
        half, row = tile // half_tiles, tile % half_tiles * tile_rows
        mine = terms[sum(term_counts[:half]) : sum(term_counts[: half + 1])]

        def summed(part, lanes):
            out = mine[0][part, lanes].astype(F32)
            for term in mine[1:]:
                out = out + term[part, lanes].astype(F32)
            return out

        total = summed(pl.ds(row, tile_rows), slice(None))
        if extra:
            chunks = range(row // extra, (row + tile_rows) // extra)
            rest = [
                summed(pl.ds(half_tiles * tile_rows, extra), slice(c * tail, (c + 1) * tail))
                for c in chunks
            ]
            rest = rest[0] if len(rest) == 1 else jnp.concatenate(rest, axis=0)
            total = jnp.concatenate([total, rest], axis=1)
        total = total + x_ref[tile].T.astype(F32) + bias
        encoded_ref[tile * tile_rows : (tile + 1) * tile_rows, :] = total.astype(BF16)
    block = 2 * HD
    mine = lax.div(where_ref[1], jnp.int32(dup))
    for head in range(head_count):
        for k in range(dest_count):
            column = ((mine ^ k) * head_count + head) * block
            weights = weight_ref[:, pl.ds(pl.multiple_of(column, block), block)]
            value = jnp.dot(encoded_ref[...], weights, preferred_element_type=F32)
            value = value + tap_blocks[head * dest_count + k][...].astype(F32)
            outs[head * dest_count + k][...] = value.astype(BF16)


def kv_projection(
    where, x_tiles, b_down, weights, tap_parts, halves, head_count, dest_count, dup
):
    terms = [term for half in halves for term in half]
    tiles, width, tile_rows = x_tiles.shape
    rows = tiles * tile_rows
    block = 2 * HD
    outs = pl.pallas_call(
        functools.partial(
            kv_kernel,
            head_count,
            dest_count,
            dup,
            len(tap_parts),
            tuple(len(half) for half in halves),
        ),
        out_shape=[jax.ShapeDtypeStruct((rows, block), BF16)] * (head_count * dest_count),
        in_specs=[SMEM] + [VMEM] * (3 + len(tap_parts) + len(terms)),
        out_specs=[VMEM] * (head_count * dest_count),
        scratch_shapes=[pltpu.VMEM((rows, width), BF16)],
        compiler_params=pltpu.CompilerParams(vmem_limit_bytes=24 * MIB),
        cost_estimate=LIGHT,
        name="kv_projection",
    )(where, x_tiles, lane_rows(b_down), weights, *tap_parts, *terms)
    return [outs[h * dest_count : (h + 1) * dest_count] for h in range(head_count)]


def finish_kernel(term_count, picks, meta_ref, gain_ref, *refs):
    terms = refs[:term_count]
    outs = refs[term_count : term_count + len(picks)]
    done_ref = refs[-1]
    rows = terms[0].shape[0]
    for row in range(0, rows, ROW_BLOCK):
        take = pl.ds(row, ROW_BLOCK)
        total = terms[0][take, :].astype(F32)
        for term in terms[1:]:
            total = total + term[take, :].astype(F32)
        keys = total[:, :HD]
        square = jnp.sum(keys * keys, axis=1, keepdims=True) * (1.0 / HD)
        keys = keys * lax.rsqrt(square + epsilon) * gain_ref[...]
        done_ref[take, :HD] = keys.astype(BF16).T
        done_ref[take, HD:] = (total[:, HD:] * VALUE_SHIFT).astype(BF16)
    for out, places in zip(outs, picks):
        for n, place in enumerate(places):
            start = pl.multiple_of(meta_ref[place] * ROW_BLOCK, ROW_BLOCK)
            out[n] = done_ref[pl.ds(start, ROW_BLOCK), :]


def finish_tiles(meta, k_gain, terms, picks):
    rows, block = terms[0].shape
    return pl.pallas_call(
        functools.partial(finish_kernel, len(terms), picks),
        out_shape=[jax.ShapeDtypeStruct((len(p), ROW_BLOCK, block), BF16) for p in picks],
        in_specs=[SMEM] + [VMEM] * (1 + len(terms)),
        out_specs=[VMEM] * len(picks),
        scratch_shapes=[pltpu.VMEM((rows, block), BF16)],
        compiler_params=pltpu.CompilerParams(vmem_limit_bytes=8 * MIB),
        cost_estimate=LIGHT,
        name="finish_tiles",
    )(meta, lane_rows(k_gain), *terms)


def attend_kernel(group_count, sources, head, has_base, meta_ref, query_ref, *refs):
    tile_refs = refs[: len(sources)]
    out_hbm, out_ref, key_ref, value_ref, out_sem = refs[len(sources) + has_base :]
    place = meta_places(group_count)
    counts = (meta_ref[place["first"]], meta_ref[place["second"]])
    text_first, text_both = meta_ref[place["text_first"]], meta_ref[place["text_both"]]
    span = MAXT * ROW_BLOCK
    text_rows, width = out_ref.shape
    heads = width // HD
    for label in range(REQ_G):
        for tile in range(1, MAXT):

            @pl.when(counts[label] <= tile)
            def _(tile=label * MAXT + tile):
                take = slice(tile * ROW_BLOCK, (tile + 1) * ROW_BLOCK)
                key_ref[:, take] = jnp.zeros((HD, ROW_BLOCK), BF16)
                value_ref[take, :] = jnp.zeros((ROW_BLOCK, 2 * HD), BF16)

    for tile_ref, places in zip(tile_refs, sources):
        for n, slot in enumerate(places):
            if slot is None:
                continue
            goes = meta_ref[place["goes"] + slot]

            @pl.when(goes >= 0)
            def _(tile_ref=tile_ref, n=n, goes=goes):
                take = pl.ds(pl.multiple_of(goes * ROW_BLOCK, ROW_BLOCK), ROW_BLOCK)
                key_ref[:, take] = tile_ref[n, :, :HD]
                value_ref[take, :HD] = tile_ref[n, :, HD:]
                value_ref[take, HD:] = jnp.ones((ROW_BLOCK, HD), BF16)

    copies = []
    for block in range(text_rows // ROW_BLOCK):
        start = block * ROW_BLOCK
        take = pl.ds(start, ROW_BLOCK)
        for label, (low, high) in enumerate(((0, text_first), (text_first, text_both))):
            meets = jnp.maximum(low, start) < jnp.minimum(high, start + ROW_BLOCK)

            def attend(key_rows, label=label, start=start, take=take, low=low, high=high):
                part = pl.ds(label * span, key_rows)
                slots = start + lax.broadcasted_iota(jnp.int32, (ROW_BLOCK, HD), 0)
                owned = (slots >= low) & (slots < high)
                for first in range(0, heads, HEAD_GROUP):
                    group = range(first, min(first + HEAD_GROUP, heads))
                    column = head * width
                    stacked = jnp.concatenate(
                        [
                            query_ref[take, column + h * HD : column + (h + 1) * HD]
                            for h in group
                        ],
                        axis=0,
                    )
                    scores = jnp.dot(stacked, key_ref[:, part], preferred_element_type=F32)
                    weights = jnp.exp2(scores).astype(BF16)
                    sums = jnp.dot(weights, value_ref[part, :], preferred_element_type=F32)
                    result = sums[:, :HD] / sums[:, HD:] * (1.0 / VALUE_SHIFT)
                    for n, h in enumerate(group):
                        lanes = slice(h * HD, (h + 1) * HD)
                        own = result[n * ROW_BLOCK : (n + 1) * ROW_BLOCK]
                        kept = 0.0 if label == 0 else out_ref[take, lanes].astype(F32)
                        out_ref[take, lanes] = jnp.where(owned, own, kept).astype(BF16)

            half = span // 2
            few = counts[label] * ROW_BLOCK <= half

            @pl.when(meets & few)
            def _(attend=attend):
                attend(half)

            @pl.when(meets & jnp.logical_not(few))
            def _(attend=attend):
                attend(span)

            if label == 0:

                @pl.when(jnp.logical_not(meets))
                def _(take=take):
                    out_ref[take, :] = jnp.zeros((ROW_BLOCK, width), BF16)

        copies.append(
            pltpu.make_async_copy(
                out_ref.at[take, :],
                out_hbm.at[take, pl.ds(head * width, width)],
                out_sem.at[block],
            )
        )
        copies[-1].start()
    for copy in copies:
        copy.wait()


def attend_head(group_count, meta, queries, tiles, sources, base, head, head_count):
    rows, width = queries.shape
    head_width = width // head_count
    group_rows = REQ_G * MAXT * ROW_BLOCK
    extra = [] if base is None else [base]
    return pl.pallas_call(
        functools.partial(attend_kernel, group_count, sources, head, len(extra)),
        out_shape=jax.ShapeDtypeStruct((rows, width), BF16),
        in_specs=[SMEM] + [VMEM] * (1 + len(tiles)) + [HBM] * len(extra),
        out_specs=HBM,
        scratch_shapes=[
            pltpu.VMEM((rows, head_width), BF16),
            pltpu.VMEM((HD, group_rows), BF16),
            pltpu.VMEM((group_rows, 2 * HD), BF16),
            pltpu.SemaphoreType.DMA((rows // ROW_BLOCK,)),
        ],
        input_output_aliases={2 + len(tiles): 0} if extra else {},
        compiler_params=pltpu.CompilerParams(vmem_limit_bytes=24 * MIB),
        cost_estimate=LIGHT,
        name="attend_head",
    )(meta, queries, *tiles, *extra)


def add_rounded(a, b):
    return (a.astype(F32) + b.astype(F32)).astype(BF16)


def after(value, *others):
    others = [v for v in others if v is not None]
    return lax.optimization_barrier((value, others))[0]


def scatter_sum(blocks, count, first_bit, earlier=None):
    blocks = dict(enumerate(blocks))
    bits = bits_of(len(blocks))
    for b in range(bits):
        pairs = xor_pairs(count, 1 << (b + first_bit))
        got, sent = {}, None
        for k in sorted((k for k in blocks if (k >> b) & 1), reverse=True):
            sent = blocks[k]
            if b == bits - 1 and earlier is not None:
                sent = after(sent, earlier)
            got[k ^ (1 << b)] = lax.ppermute(sent, "tp", pairs)
        if b == bits - 1:
            return [blocks[0], got[0]], sent
        blocks = {k: add_rounded(blocks[k], got[k]) for k in got}
    return [blocks[0]], blocks[0]


def gather_half(whole, own, first, count, ready):
    bits = bits_of(count)
    pieces = {0: own}
    for b in reversed(range(1, bits)):
        pairs = xor_pairs(count, 1 << b)
        for k in sorted(pieces):
            pieces[k | (1 << b)] = lax.ppermute(pieces[k], "tp", pairs)
    pairs = xor_pairs(count, 1)
    for k in sorted(pieces):
        if k:
            pieces[k | 1] = lax.ppermute(after(pieces[k], ready), "tp", pairs)
    pieces[0], pieces[1] = whole
    bases = tuple(first if k < 2 else 0 for k in range(count))
    return [pieces[k] for k in range(count)], bases


def local(
    x_in,
    taps,
    ln_gain,
    ln_bias,
    w_up,
    b_up,
    w_down,
    b_down,
    kv_w_out,
    kv_w_taps,
    k_gain,
    q_gain,
    queries,
    tiles_per_request,
    owner,
    text_per_request,
):
    group_count = lax.axis_size("grp")
    tp_count = lax.axis_size("tp")
    position = jnp.stack([lax.axis_index("grp"), lax.axis_index("tp")]).astype(jnp.int32)
    where = jnp.concatenate([position, tiles_per_request, owner, text_per_request])
    tiles_local = x_in.shape[0]
    x_tiles = jnp.swapaxes(x_in, 2, 3)[:, 0]
    tap_tiles = jnp.swapaxes(taps, 2, 3)[:, 0]
    head_count = max(1, KVH // tp_count)
    dup = max(1, tp_count // KVH)
    dest_count = tp_count // dup
    place = meta_places(group_count)

    halves = HALVES if tiles_local % HALVES == 0 else 1
    tiles = tiles_local // halves
    own_halves = [x_tiles[:tiles]] + [
        after(x_tiles, where)[h * tiles : (h + 1) * tiles] for h in range(1, halves)
    ]
    whole = [x_tiles, lax.ppermute(x_tiles, "tp", xor_pairs(tp_count, 1))]

    tap_blocks = [(h, k) for h in range(head_count) for k in range(dest_count)]
    early = len(tap_blocks) * TAPS_EARLY // 8
    first_taps, w_up, w_down, tap_tiles = tap_projection(
        where, tap_tiles, kv_w_taps, tap_blocks[:early], head_count, dup, (w_up, w_down)
    )
    mlp_terms = []
    ready, begun = first_taps, where
    for half in range(halves):
        pieces, bases = gather_half(whole, own_halves[half], half * tiles, tp_count, ready)
        mlp_blocks = encoder_mlp(
            begun, pieces, bases, tiles, ln_gain, ln_bias, w_up, b_up, w_down
        )
        terms, sent = scatter_sum(mlp_blocks, tp_count, 0)
        mlp_terms.append(terms)
        ready, begun = mlp_blocks[0], after(where, sent)
    (last_taps,) = tap_projection(
        begun, tap_tiles, kv_w_taps, tap_blocks[early:], head_count, dup, ()
    )
    kv_blocks = kv_projection(
        where,
        x_tiles,
        b_down,
        kv_w_out,
        (first_taps, last_taps),
        mlp_terms,
        head_count,
        dest_count,
        dup,
    )
    kv_terms, arrived = [], None
    for head in range(head_count):
        blocks = kv_blocks[head]
        for b in range(bits_of(dup)):
            pairs = xor_pairs(tp_count, 1 << b)
            blocks = [add_rounded(v, lax.ppermute(v, "tp", pairs)) for v in blocks]
        terms, sent = scatter_sum(blocks, tp_count, bits_of(dup), arrived)
        kv_terms.append(terms)
        if head == 0:
            query_rows, meta = prepare(
                after(where, sent), q_gain, queries, group_count, tiles_local
            )
        arrived = (terms[-1], meta)

    slots = slot_count_of(group_count)
    total_tiles = group_count * tiles_local
    most_other = total_tiles - REQ_G * MAXT - REQ_G * (group_count - 2)
    one_large = group_count == 4 and slots == 2 and most_other <= group_count
    send = place["send"]
    out = None

    def move(value, mask):
        return lax.ppermute(value, "grp", xor_pairs(group_count, mask))

    for head in range(head_count):
        terms = kv_terms[head]
        if one_large:
            star = place["star"]
            picks = tuple((send + d, star) for d in range(group_count))
            made = finish_tiles(meta, k_gain, terms, picks)
            moved = {d: move(made[d], d) for d in (2, 3, 1)}
            tiles = (made[0],) + tuple(moved[d] for d in (1, 2, 3))
            sources = tuple((d, group_count + d) for d in range(group_count))
        else:
            picks = tuple(
                tuple(send + s * group_count + d for s in range(slots)) for d in range(group_count)
            )
            made = finish_tiles(meta, k_gain, terms, picks)
            tiles = tuple(made[:1]) + tuple(move(made[d], d) for d in range(1, group_count))
            sources = tuple(
                tuple(s * group_count + d for s in range(slots)) for d in range(group_count)
            )
        out = attend_head(
            group_count, meta, query_rows, tiles, sources, out, head, head_count
        )
    return out


def solution(mesh):
    in_specs = (
        P(None, ("rep", "grp"), None, "tp"),
        P(None, ("rep", "grp"), None, "tp"),
        P(),
        P(),
        P(None, "tp"),
        P("tp"),
        P("tp", None),
        P("tp"),
        P("tp", None),
        P("tp", None),
        P(),
        P(),
        P(("rep", "grp"), "tp"),
        P("rep"),
        P("rep"),
        P("rep"),
    )
    out_specs = P(("rep", "grp"), "tp")
    return jax.shard_map(local, mesh=mesh, in_specs=in_specs, out_specs=out_specs, check_vma=False)
```

```python
import functools
import math

import jax
import jax.numpy as jnp
from jax import lax
from jax.experimental import pallas as pl
from jax.experimental.pallas import tpu as pltpu
from jax.sharding import PartitionSpec as P

KVH = 8
HD = 128
MAXT = 4
REQ_G = 2
LANES = 128
ROW_BLOCK = 128
HIDDEN_BLOCK = 256
HEAD_GROUP = 8
HALVES = 1
TAPS_EARLY = 3
VALUE_SHIFT = 2.0**-24
epsilon = 1e-05

F32 = jnp.float32
BF16 = jnp.bfloat16
VMEM = pl.BlockSpec(memory_space=pltpu.VMEM)
HBM = pl.BlockSpec(memory_space=pltpu.HBM)
SMEM = pl.BlockSpec(memory_space=pltpu.SMEM)
MIB = 1024 * 1024
LIGHT = pl.CostEstimate(flops=1024, bytes_accessed=1024, transcendentals=0)


def bits_of(count):
    bits = count.bit_length() - 1
    assert 1 << bits == count
    return bits


def xor_order(blocks, index):
    blocks = list(blocks)
    for b in range(bits_of(len(blocks))):
        swap = ((index >> b) & 1) == 1
        for k in range(len(blocks)):
            if not (k >> b) & 1:
                low, high = blocks[k], blocks[k | (1 << b)]
                blocks[k] = lax.select(swap, high, low)
                blocks[k | (1 << b)] = lax.select(swap, low, high)
    return blocks


def xor_pairs(count, mask):
    return [(i, i ^ mask) for i in range(count)]


def lane_rows(vector):
    return jnp.pad(vector, (0, -vector.shape[0] % LANES)).reshape(-1, LANES)


def one_row(ref, width):
    rows = [ref[n : n + 1, :] for n in range(ref.shape[0])]
    return (rows[0] if len(rows) == 1 else jnp.concatenate(rows, axis=1))[:, :width]


def column_step(width):
    return HIDDEN_BLOCK if width % HIDDEN_BLOCK == 0 else width


def tail_plan(rows, width):
    whole = width // LANES * LANES
    tail = width - whole
    packed = tail > 0 and whole > 0 and whole % tail == 0 and rows * tail % whole == 0
    extra = rows * tail // whole if packed else 0
    packed = packed and extra % 16 == 0 and ROW_BLOCK % extra == 0
    return whole, tail, extra if packed else 0


def sent_shape(rows, width):
    whole, _, extra = tail_plan(rows, width)
    return (rows + extra, whole) if extra else (rows, width)


def layout_kernel(group_count, tiles_local, where_ref, meta_ref):
    group = where_ref[0]
    requests = (where_ref.shape[0] - 2) // 3
    tiles_of, owner_of, text_of = ([where_ref[2 + n * requests + r] for r in range(requests)] for n in range(3))
    zero = jnp.int32(0)
    firsts, counts, offsets, texts_first, texts_both = [], [], [], [], []
    offset = zero
    for p in range(group_count):
        first, count, text_first, text_both, seen = zero, zero, zero, zero, zero
        for r in range(requests):
            mine = owner_of[r] == p
            tiles = jnp.where(mine, tiles_of[r], 0)
            text = jnp.where(mine, text_of[r], 0)
            first = first + jnp.where(seen == 0, tiles, 0)
            text_first = text_first + jnp.where(seen == 0, text, 0)
            count = count + tiles
            text_both = text_both + text
            seen = seen + jnp.where(mine, 1, 0)
        firsts.append(first)
        counts.append(count)
        offsets.append(offset)
        texts_first.append(text_first)
        texts_both.append(text_both)
        offset = offset + count

    def pick(values, index):
        out = values[0]
        for p in range(1, group_count):
            out = jnp.where(index == p, values[p], out)
        return out

    slots = slot_count_of(group_count)
    star, most = zero, counts[0]
    for p in range(1, group_count):
        larger = counts[p] > most
        star = jnp.where(larger, p, star)
        most = jnp.where(larger, counts[p], most)

    def local_tile(offset, slot):
        lane = lax.rem(group - offset + group_count * REQ_G * MAXT * group_count, group_count)
        tile = lax.div(offset + slot * group_count + lane, group_count)
        return jnp.minimum(tile, tiles_local - 1)

    my_first, my_count = pick(firsts, group), pick(counts, group)
    my_offset = pick(offsets, group)
    place = meta_places(group_count)
    meta_ref[place["first"]] = my_first
    meta_ref[place["second"]] = my_count - my_first
    meta_ref[place["text_first"]] = pick(texts_first, group)
    meta_ref[place["text_both"]] = pick(texts_both, group)
    meta_ref[place["star"]] = local_tile(pick(offsets, star), 1)
    for slot in range(slots):
        for d in range(group_count):
            other = group ^ d
            meta_ref[place["send"] + slot * group_count + d] = local_tile(pick(offsets, other), slot)
            lane = lax.rem(other - my_offset + group_count * REQ_G * MAXT * group_count, group_count)
            position = slot * group_count + lane
            goes = jnp.where(
                position < my_first,
                position,
                jnp.where(position < my_count, MAXT + position - my_first, -1),
            )
            meta_ref[place["goes"] + slot * group_count + d] = goes


def slot_count_of(group_count):
    return (REQ_G * MAXT + group_count - 1) // group_count


def meta_places(group_count):
    table = slot_count_of(group_count) * group_count
    return {
        "first": 0,
        "second": 1,
        "text_first": 2,
        "text_both": 3,
        "star": 4,
        "send": 8,
        "goes": 8 + table,
        "size": 8 + 2 * table,
    }


def mlp_kernel(piece_count, bases, tiles, where_ref, *refs):
    pieces = refs[:piece_count]
    gain_ref, bias_ref, up_bias_ref, up_ref, down_ref = refs[piece_count : piece_count + 5]
    outs = refs[piece_count + 5 : 2 * piece_count + 5]
    cat_ref, normed_ref, hidden_ref, total_ref = refs[2 * piece_count + 5 :]
    index = where_ref[1]
    _, width, tile_rows = pieces[0].shape
    rows = tiles * tile_rows
    channels, hidden_width = up_ref.shape
    up_step = column_step(hidden_width)
    down_step = column_step(channels)

    gain, bias = one_row(gain_ref, channels), one_row(bias_ref, channels)
    up_bias = one_row(up_bias_ref, hidden_width)
    for tile in range(tiles):
        for k, piece in enumerate(pieces):
            start = pl.multiple_of((index ^ k) * width, math.gcd(width, LANES))
            cat_ref[pl.ds(start, width), :] = piece[bases[k] + tile]
        values = cat_ref[...].T.astype(F32)
        average = jnp.sum(values, axis=1, keepdims=True) * (1.0 / channels)
        centered = values - average
        variance = jnp.sum(centered * centered, axis=1, keepdims=True) * (1.0 / channels)
        normed = centered * lax.rsqrt(variance + epsilon)
        normed = normed * gain + bias
        normed_ref[tile * tile_rows : (tile + 1) * tile_rows, :] = normed.astype(BF16)
    for n in range(hidden_width // up_step):
        take = slice(n * up_step, (n + 1) * up_step)
        value = jnp.dot(normed_ref[...], up_ref[:, take], preferred_element_type=F32)
        value = value + up_bias[:, take]
        value = 0.5 * value * (1.0 + lax.erf(value * (1.0 / math.sqrt(2.0))))
        hidden_ref[:, take] = value.astype(BF16)
    for n in range(channels // down_step):
        take = slice(n * down_step, (n + 1) * down_step)
        total_ref[:, take] = jnp.dot(
            hidden_ref[...], down_ref[:, take], preferred_element_type=F32
        )
    whole, tail, extra = tail_plan(rows, width)
    step = extra or ROW_BLOCK
    for part in range(rows // step):
        take = pl.ds(part * step, step)
        blocks = [total_ref[take, j * width : (j + 1) * width] for j in range(piece_count)]
        for out, block in zip(outs, xor_order(blocks, index)):
            block = block.astype(BF16)
            if extra:
                out[take, :] = block[:, :whole]
                out[rows : rows + extra, part * tail : (part + 1) * tail] = block[:, whole:]
            else:
                out[take, :] = block


def encoder_mlp(where, pieces, bases, tiles, ln_gain, ln_bias, w_up, b_up, w_down):
    _, width, tile_rows = pieces[0].shape
    rows = tiles * tile_rows
    count = len(pieces)
    channels, hidden_width = w_up.shape
    shape = sent_shape(rows, width)
    return pl.pallas_call(
        functools.partial(mlp_kernel, count, bases, tiles),
        out_shape=[jax.ShapeDtypeStruct(shape, BF16)] * count,
        in_specs=[SMEM] + [VMEM] * (count + 5),
        out_specs=[VMEM] * count,
        scratch_shapes=[
            pltpu.VMEM((channels, tile_rows), BF16),
            pltpu.VMEM((rows, channels), BF16),
            pltpu.VMEM((rows, hidden_width), BF16),
            pltpu.VMEM((rows, channels), F32),
        ],
        compiler_params=pltpu.CompilerParams(vmem_limit_bytes=44 * MIB),
        cost_estimate=LIGHT,
        name="encoder_mlp",
    )(
        where,
        *pieces,
        lane_rows(ln_gain),
        lane_rows(ln_bias),
        lane_rows(b_up),
        w_up,
        w_down,
    )


def prepare_kernel(
    group_count,
    tiles_local,
    where_ref,
    gain_ref,
    query_ref,
    normed_ref,
    meta_ref,
):
    @pl.when(pl.program_id(0) == 0)
    def _():
        layout_kernel(group_count, tiles_local, where_ref, meta_ref)

    gain = gain_ref[...] * (math.log2(math.e) / math.sqrt(HD))
    for col in range(0, query_ref.shape[1], HD):
        values = query_ref[:, col : col + HD].astype(F32)
        square = jnp.sum(values * values, axis=1, keepdims=True) * (1.0 / HD)
        normed_ref[:, col : col + HD] = (values * lax.rsqrt(square + epsilon) * gain).astype(BF16)


def prepare(where, q_gain, queries, group_count, tiles_local):
    text_rows, width = queries.shape
    step = ROW_BLOCK
    return pl.pallas_call(
        functools.partial(prepare_kernel, group_count, tiles_local),
        out_shape=[
            jax.ShapeDtypeStruct((text_rows, width), BF16),
            jax.ShapeDtypeStruct((meta_places(group_count)["size"],), jnp.int32),
        ],
        grid=(text_rows // step,),
        in_specs=[
            SMEM,
            pl.BlockSpec((1, HD), lambda n: (0, 0)),
            pl.BlockSpec((step, width), lambda n: (n, 0)),
        ],
        out_specs=[pl.BlockSpec((step, width), lambda n: (n, 0)), SMEM],
        compiler_params=pltpu.CompilerParams(vmem_limit_bytes=16 * MIB),
        cost_estimate=LIGHT,
        name="prepare",
    )(where, lane_rows(q_gain), queries)


def tap_kernel(blocks, head_count, dup, staged, where_ref, tap_hbm, weight_hbm, *refs):
    sources, out_ref = refs[:staged], refs[staged]
    targets = refs[staged + 1 : 2 * staged + 1]
    if staged:
        tap_ref, weight_ref, tap_sem, weight_sem, staged_sem = refs[2 * staged + 1 :]
    else:
        tap_ref, (weight_ref, weight_sem) = tap_hbm, refs[1:]
    tiles, _, tile_rows = tap_ref.shape
    block = weight_ref.shape[2]
    mine = lax.div(where_ref[1], jnp.int32(dup))
    taps = [
        pltpu.make_async_copy(tap_hbm.at[n], tap_ref.at[n], tap_sem.at[n])
        for n in range(tiles if staged else 0)
    ]
    weights = []
    for n, (head, k) in enumerate(blocks):
        column = pl.multiple_of(((mine ^ k) * head_count + head) * block, block)
        weights.append(
            pltpu.make_async_copy(
                weight_hbm.at[:, pl.ds(column, block)], weight_ref.at[n], weight_sem.at[n]
            )
        )
    others = [
        pltpu.make_async_copy(source, target, staged_sem.at[n])
        for n, (source, target) in enumerate(zip(sources, targets))
    ]
    for copy in weights[:1] + taps + weights[1:] + others:
        copy.start()
    for n in range(len(blocks)):
        weights[n].wait()
        for tile in range(tiles):
            if n == 0 and staged:
                taps[tile].wait()
            value = lax.dot_general(
                tap_ref[tile],
                weight_ref[n],
                (((0,), (0,)), ((), ())),
                preferred_element_type=F32,
            )
            out_ref[n, tile * tile_rows : (tile + 1) * tile_rows, :] = value.astype(BF16)
    for copy in others:
        copy.wait()


def tap_projection(where, tap_tiles, weights, blocks, head_count, dup, staged):
    tiles, depth, tile_rows = tap_tiles.shape
    block = 2 * HD
    return pl.pallas_call(
        functools.partial(tap_kernel, blocks, head_count, dup, len(staged)),
        out_shape=[jax.ShapeDtypeStruct((len(blocks), tiles * tile_rows, block), BF16)]
        + [jax.ShapeDtypeStruct(w.shape, w.dtype) for w in staged]
        + ([jax.ShapeDtypeStruct(tap_tiles.shape, BF16)] if staged else []),
        in_specs=[SMEM, HBM if staged else VMEM, HBM] + [HBM] * len(staged),
        out_specs=[VMEM] * (1 + len(staged) + bool(staged)),
        scratch_shapes=[pltpu.VMEM((len(blocks), depth, block), BF16)]
        + ([pltpu.SemaphoreType.DMA((tiles,))] if staged else [])
        + [pltpu.SemaphoreType.DMA((len(blocks),))]
        + ([pltpu.SemaphoreType.DMA((len(staged),))] if staged else []),
        compiler_params=pltpu.CompilerParams(vmem_limit_bytes=(42 if staged else 50) * MIB),
        cost_estimate=LIGHT,
        name="tap_projection",
    )(where, tap_tiles, weights, *staged)


def encode(x_ref, bias_ref, term_counts, terms, encoded_ref):
    tiles, width, tile_rows = x_ref.shape
    half_tiles = tiles // len(term_counts)
    whole, tail, extra = tail_plan(half_tiles * tile_rows, width)
    bias = one_row(bias_ref, width)
    for tile in range(tiles):
        half, row = tile // half_tiles, tile % half_tiles * tile_rows
        mine = terms[sum(term_counts[:half]) : sum(term_counts[: half + 1])]

        def summed(part, lanes):
            out = mine[0][part, lanes].astype(F32)
            for term in mine[1:]:
                out = out + term[part, lanes].astype(F32)
            return out

        total = summed(pl.ds(row, tile_rows), slice(None))
        if extra:
            chunks = range(row // extra, (row + tile_rows) // extra)
            rest = [
                summed(pl.ds(half_tiles * tile_rows, extra), slice(c * tail, (c + 1) * tail))
                for c in chunks
            ]
            rest = rest[0] if len(rest) == 1 else jnp.concatenate(rest, axis=0)
            total = jnp.concatenate([total, rest], axis=1)
        total = total + x_ref[tile].T.astype(F32) + bias
        encoded_ref[tile * tile_rows : (tile + 1) * tile_rows, :] = total.astype(BF16)


def kv_kernel(head, head_count, dest_count, dup, taps_at, term_counts, where_ref, *refs):
    weight_ref, refs = refs[0], refs[1:]
    part_count = 1 + max(part for part, _ in taps_at)
    tap_refs, refs = refs[:part_count], refs[part_count:]
    outs = refs[-dest_count - 1 :] if head == 0 else refs[-dest_count:]
    if head == 0:
        encoded_ref = outs[-1]
        encode(refs[0], refs[1], term_counts, refs[2 : 2 + sum(term_counts)], encoded_ref)
    else:
        encoded_ref = refs[0]
    block = 2 * HD
    mine = lax.div(where_ref[1], jnp.int32(dup))
    for k in range(dest_count):
        column = ((mine ^ k) * head_count + head) * block
        weights = weight_ref[:, pl.ds(pl.multiple_of(column, block), block)]
        value = jnp.dot(encoded_ref[...], weights, preferred_element_type=F32)
        part, n = taps_at[k]
        value = value + tap_refs[part][n].astype(F32)
        outs[k][...] = value.astype(BF16)


def kv_projection(where, weights, tap_parts, taps_at, inputs, term_counts, head, head_count, dup):
    tap_parts = tap_parts[: 1 + max(part for part, _ in taps_at)]
    rows, dest_count, block = tap_parts[0].shape[1], len(taps_at), 2 * HD
    outs = [jax.ShapeDtypeStruct((rows, block), BF16)] * dest_count
    if head == 0:
        outs.append(jax.ShapeDtypeStruct((rows, weights.shape[0]), BF16))
    return pl.pallas_call(
        functools.partial(
            kv_kernel, head, head_count, dest_count, dup, tuple(taps_at), term_counts
        ),
        out_shape=outs,
        in_specs=[SMEM] + [VMEM] * (1 + len(tap_parts) + len(inputs)),
        out_specs=[VMEM] * len(outs),
        compiler_params=pltpu.CompilerParams(vmem_limit_bytes=24 * MIB),
        cost_estimate=LIGHT,
        name="kv_projection",
    )(where, weights, *tap_parts, *inputs)


def finish_kernel(term_count, picks, meta_ref, gain_ref, *refs):
    terms = refs[:term_count]
    outs = refs[term_count : term_count + len(picks)]
    done_ref = refs[-1]
    rows = terms[0].shape[0]
    for row in range(0, rows, ROW_BLOCK):
        take = pl.ds(row, ROW_BLOCK)
        total = terms[0][take, :].astype(F32)
        for term in terms[1:]:
            total = total + term[take, :].astype(F32)
        keys = total[:, :HD]
        square = jnp.sum(keys * keys, axis=1, keepdims=True) * (1.0 / HD)
        keys = keys * lax.rsqrt(square + epsilon) * gain_ref[...]
        done_ref[take, :HD] = keys.astype(BF16).T
        done_ref[take, HD:] = (total[:, HD:] * VALUE_SHIFT).astype(BF16)
    for out, places in zip(outs, picks):
        for n, place in enumerate(places):
            start = pl.multiple_of(meta_ref[place] * ROW_BLOCK, ROW_BLOCK)
            out[n] = done_ref[pl.ds(start, ROW_BLOCK), :]


def finish_tiles(meta, k_gain, terms, picks):
    rows, block = terms[0].shape
    return pl.pallas_call(
        functools.partial(finish_kernel, len(terms), picks),
        out_shape=[jax.ShapeDtypeStruct((len(p), ROW_BLOCK, block), BF16) for p in picks],
        in_specs=[SMEM] + [VMEM] * (1 + len(terms)),
        out_specs=[VMEM] * len(picks),
        scratch_shapes=[pltpu.VMEM((rows, block), BF16)],
        compiler_params=pltpu.CompilerParams(vmem_limit_bytes=8 * MIB),
        cost_estimate=LIGHT,
        name="finish_tiles",
    )(meta, lane_rows(k_gain), *terms)


def attend_kernel(group_count, sources, head, has_base, meta_ref, query_ref, *refs):
    tile_refs = refs[: len(sources)]
    out_hbm, out_ref, key_ref, value_ref, out_sem = refs[len(sources) + has_base :]
    place = meta_places(group_count)
    counts = (meta_ref[place["first"]], meta_ref[place["second"]])
    text_first, text_both = meta_ref[place["text_first"]], meta_ref[place["text_both"]]
    span = MAXT * ROW_BLOCK
    text_rows, width = out_ref.shape
    heads = width // HD
    for label in range(REQ_G):
        for tile in range(1, MAXT):

            @pl.when(counts[label] <= tile)
            def _(tile=label * MAXT + tile):
                take = slice(tile * ROW_BLOCK, (tile + 1) * ROW_BLOCK)
                key_ref[:, take] = jnp.zeros((HD, ROW_BLOCK), BF16)
                value_ref[take, :] = jnp.zeros((ROW_BLOCK, 2 * HD), BF16)

    for tile_ref, places in zip(tile_refs, sources):
        for n, slot in enumerate(places):
            if slot is None:
                continue
            goes = meta_ref[place["goes"] + slot]

            @pl.when(goes >= 0)
            def _(tile_ref=tile_ref, n=n, goes=goes):
                take = pl.ds(pl.multiple_of(goes * ROW_BLOCK, ROW_BLOCK), ROW_BLOCK)
                key_ref[:, take] = tile_ref[n, :, :HD]
                value_ref[take, :HD] = tile_ref[n, :, HD:]
                value_ref[take, HD:] = jnp.ones((ROW_BLOCK, HD), BF16)

    copies = []
    for block in range(text_rows // ROW_BLOCK):
        start = block * ROW_BLOCK
        take = pl.ds(start, ROW_BLOCK)
        for label, (low, high) in enumerate(((0, text_first), (text_first, text_both))):
            meets = jnp.maximum(low, start) < jnp.minimum(high, start + ROW_BLOCK)

            def attend(key_rows, label=label, start=start, take=take, low=low, high=high):
                part = pl.ds(label * span, key_rows)
                slots = start + lax.broadcasted_iota(jnp.int32, (ROW_BLOCK, HD), 0)
                owned = (slots >= low) & (slots < high)
                for first in range(0, heads, HEAD_GROUP):
                    group = range(first, min(first + HEAD_GROUP, heads))
                    column = head * width
                    stacked = jnp.concatenate(
                        [
                            query_ref[take, column + h * HD : column + (h + 1) * HD]
                            for h in group
                        ],
                        axis=0,
                    )
                    scores = jnp.dot(stacked, key_ref[:, part], preferred_element_type=F32)
                    weights = jnp.exp2(scores).astype(BF16)
                    sums = jnp.dot(weights, value_ref[part, :], preferred_element_type=F32)
                    result = sums[:, :HD] / sums[:, HD:] * (1.0 / VALUE_SHIFT)
                    for n, h in enumerate(group):
                        lanes = slice(h * HD, (h + 1) * HD)
                        own = result[n * ROW_BLOCK : (n + 1) * ROW_BLOCK]
                        kept = 0.0 if label == 0 else out_ref[take, lanes].astype(F32)
                        out_ref[take, lanes] = jnp.where(owned, own, kept).astype(BF16)

            half = span // 2
            few = counts[label] * ROW_BLOCK <= half

            @pl.when(meets & few)
            def _(attend=attend):
                attend(half)

            @pl.when(meets & jnp.logical_not(few))
            def _(attend=attend):
                attend(span)

            if label == 0:

                @pl.when(jnp.logical_not(meets))
                def _(take=take):
                    out_ref[take, :] = jnp.zeros((ROW_BLOCK, width), BF16)

        copies.append(
            pltpu.make_async_copy(
                out_ref.at[take, :],
                out_hbm.at[take, pl.ds(head * width, width)],
                out_sem.at[block],
            )
        )
        copies[-1].start()
    for copy in copies:
        copy.wait()


def attend_head(group_count, meta, queries, tiles, sources, base, head, head_count):
    rows, width = queries.shape
    head_width = width // head_count
    group_rows = REQ_G * MAXT * ROW_BLOCK
    extra = [] if base is None else [base]
    return pl.pallas_call(
        functools.partial(attend_kernel, group_count, sources, head, len(extra)),
        out_shape=jax.ShapeDtypeStruct((rows, width), BF16),
        in_specs=[SMEM] + [VMEM] * (1 + len(tiles)) + [HBM] * len(extra),
        out_specs=HBM,
        scratch_shapes=[
            pltpu.VMEM((rows, head_width), BF16),
            pltpu.VMEM((HD, group_rows), BF16),
            pltpu.VMEM((group_rows, 2 * HD), BF16),
            pltpu.SemaphoreType.DMA((rows // ROW_BLOCK,)),
        ],
        input_output_aliases={2 + len(tiles): 0} if extra else {},
        compiler_params=pltpu.CompilerParams(vmem_limit_bytes=24 * MIB),
        cost_estimate=LIGHT,
        name="attend_head",
    )(meta, queries, *tiles, *extra)


def add_rounded(a, b):
    return (a.astype(F32) + b.astype(F32)).astype(BF16)


def after(value, *others):
    others = [v for v in others if v is not None]
    return lax.optimization_barrier((value, others))[0]


def scatter_sum(blocks, count, first_bit, earlier=None):
    blocks = dict(enumerate(blocks))
    bits = bits_of(len(blocks))
    for b in range(bits):
        pairs = xor_pairs(count, 1 << (b + first_bit))
        got, sent = {}, None
        for k in sorted((k for k in blocks if (k >> b) & 1), reverse=True):
            sent = blocks[k]
            if b == bits - 1 and earlier is not None:
                sent = after(sent, earlier)
            got[k ^ (1 << b)] = lax.ppermute(sent, "tp", pairs)
        if b == bits - 1:
            return [blocks[0], got[0]], sent
        blocks = {k: add_rounded(blocks[k], got[k]) for k in got}
    return [blocks[0]], blocks[0]


def gather_half(whole, own, first, count, ready):
    bits = bits_of(count)
    pieces = {0: own}
    for b in reversed(range(1, bits)):
        pairs = xor_pairs(count, 1 << b)
        for k in sorted(pieces):
            pieces[k | (1 << b)] = lax.ppermute(pieces[k], "tp", pairs)
    pairs = xor_pairs(count, 1)
    for k in sorted(pieces):
        if k:
            pieces[k | 1] = lax.ppermute(after(pieces[k], ready), "tp", pairs)
    pieces[0], pieces[1] = whole
    bases = tuple(first if k < 2 else 0 for k in range(count))
    return [pieces[k] for k in range(count)], bases


def local(
    x_in,
    taps,
    ln_gain,
    ln_bias,
    w_up,
    b_up,
    w_down,
    b_down,
    kv_w_out,
    kv_w_taps,
    k_gain,
    q_gain,
    queries,
    tiles_per_request,
    owner,
    text_per_request,
):
    group_count = lax.axis_size("grp")
    tp_count = lax.axis_size("tp")
    position = jnp.stack([lax.axis_index("grp"), lax.axis_index("tp")]).astype(jnp.int32)
    where = jnp.concatenate([position, tiles_per_request, owner, text_per_request])
    tiles_local = x_in.shape[0]
    x_tiles = jnp.swapaxes(x_in, 2, 3)[:, 0]
    tap_tiles = jnp.swapaxes(taps, 2, 3)[:, 0]
    head_count = max(1, KVH // tp_count)
    dup = max(1, tp_count // KVH)
    dest_count = tp_count // dup
    place = meta_places(group_count)

    halves = HALVES if tiles_local % HALVES == 0 else 1
    tiles = tiles_local // halves
    own_halves = [x_tiles[:tiles]] + [
        after(x_tiles, where)[h * tiles : (h + 1) * tiles] for h in range(1, halves)
    ]
    whole = [x_tiles, lax.ppermute(x_tiles, "tp", xor_pairs(tp_count, 1))]

    tap_blocks = [(h, k) for h in range(head_count) for k in range(dest_count)]
    early = len(tap_blocks) * TAPS_EARLY // 8
    first_taps, w_up, w_down, tap_tiles = tap_projection(
        where, tap_tiles, kv_w_taps, tap_blocks[:early], head_count, dup, (w_up, w_down)
    )
    mlp_terms = []
    ready, begun = first_taps, where
    for half in range(halves):
        pieces, bases = gather_half(whole, own_halves[half], half * tiles, tp_count, ready)
        mlp_blocks = encoder_mlp(
            begun, pieces, bases, tiles, ln_gain, ln_bias, w_up, b_up, w_down
        )
        terms, sent = scatter_sum(mlp_blocks, tp_count, 0)
        mlp_terms.append(terms)
        ready, begun = mlp_blocks[0], after(where, sent)
    (last_taps,) = tap_projection(
        begun, tap_tiles, kv_w_taps, tap_blocks[early:], head_count, dup, ()
    )
    taps_at = [(0, n) for n in range(early)]
    taps_at += [(1, n) for n in range(len(tap_blocks) - early)]
    kv_blocks = []
    inputs = (x_tiles, lane_rows(b_down), *(term for half in mlp_terms for term in half))
    for head in range(head_count):
        made = kv_projection(
            where,
            kv_w_out,
            (first_taps, last_taps),
            taps_at[head * dest_count : (head + 1) * dest_count],
            inputs,
            tuple(len(half) for half in mlp_terms),
            head,
            head_count,
            dup,
        )
        kv_blocks.append(made[:dest_count])
        if head == 0:
            inputs = (made[-1],)
    kv_terms, arrived = [], None
    for head in range(head_count):
        blocks = kv_blocks[head]
        for b in range(bits_of(dup)):
            pairs = xor_pairs(tp_count, 1 << b)
            blocks = [add_rounded(v, lax.ppermute(v, "tp", pairs)) for v in blocks]
        terms, sent = scatter_sum(blocks, tp_count, bits_of(dup), arrived)
        kv_terms.append(terms)
        if head == 0:
            query_rows, meta = prepare(
                after(where, sent), q_gain, queries, group_count, tiles_local
            )
        arrived = (terms[-1], meta)

    slots = slot_count_of(group_count)
    total_tiles = group_count * tiles_local
    most_other = total_tiles - REQ_G * MAXT - REQ_G * (group_count - 2)
    one_large = group_count == 4 and slots == 2 and most_other <= group_count
    send = place["send"]
    out = None

    def move(value, mask):
        return lax.ppermute(value, "grp", xor_pairs(group_count, mask))

    for head in range(head_count):
        terms = kv_terms[head]
        if one_large:
            star = place["star"]
            picks = tuple((send + d, star) for d in range(group_count))
            made = finish_tiles(meta, k_gain, terms, picks)
            moved = {d: move(made[d], d) for d in (2, 3, 1)}
            tiles = (made[0],) + tuple(moved[d] for d in (1, 2, 3))
            sources = tuple((d, group_count + d) for d in range(group_count))
        else:
            picks = tuple(
                tuple(send + s * group_count + d for s in range(slots)) for d in range(group_count)
            )
            made = finish_tiles(meta, k_gain, terms, picks)
            tiles = tuple(made[:1]) + tuple(move(made[d], d) for d in range(1, group_count))
            sources = tuple(
                tuple(s * group_count + d for s in range(slots)) for d in range(group_count)
            )
        out = attend_head(
            group_count, meta, query_rows, tiles, sources, out, head, head_count
        )
    return out


def solution(mesh):
    in_specs = (
        P(None, ("rep", "grp"), None, "tp"),
        P(None, ("rep", "grp"), None, "tp"),
        P(),
        P(),
        P(None, "tp"),
        P("tp"),
        P("tp", None),
        P("tp"),
        P("tp", None),
        P("tp", None),
        P(),
        P(),
        P(("rep", "grp"), "tp"),
        P("rep"),
        P("rep"),
        P("rep"),
    )
    out_specs = P(("rep", "grp"), "tp")
    return jax.shard_map(local, mesh=mesh, in_specs=in_specs, out_specs=out_specs, check_vma=False)
```

```python
import functools
import math

import jax
import jax.numpy as jnp
from jax import lax
from jax.experimental import pallas as pl
from jax.experimental.pallas import tpu as pltpu
from jax.sharding import PartitionSpec as P

KVH = 8
HD = 128
MAXT = 4
REQ_G = 2
LANES = 128
ROW_BLOCK = 128
HIDDEN_BLOCK = 256
HEAD_GROUP = 8
HALVES = 1
TAPS_EARLY = 3
VALUE_SHIFT = 2.0**-24
epsilon = 1e-05

F32 = jnp.float32
BF16 = jnp.bfloat16
VMEM = pl.BlockSpec(memory_space=pltpu.VMEM)
HBM = pl.BlockSpec(memory_space=pltpu.HBM)
SMEM = pl.BlockSpec(memory_space=pltpu.SMEM)
MIB = 1024 * 1024
LIGHT = pl.CostEstimate(flops=1024, bytes_accessed=1024, transcendentals=0)


def bits_of(count):
    bits = count.bit_length() - 1
    assert 1 << bits == count
    return bits


def xor_order(blocks, index):
    blocks = list(blocks)
    for b in range(bits_of(len(blocks))):
        swap = ((index >> b) & 1) == 1
        for k in range(len(blocks)):
            if not (k >> b) & 1:
                low, high = blocks[k], blocks[k | (1 << b)]
                blocks[k] = lax.select(swap, high, low)
                blocks[k | (1 << b)] = lax.select(swap, low, high)
    return blocks


def xor_pairs(count, mask):
    return [(i, i ^ mask) for i in range(count)]


def lane_rows(vector):
    return jnp.pad(vector, (0, -vector.shape[0] % LANES)).reshape(-1, LANES)


def one_row(ref, width):
    rows = [ref[n : n + 1, :] for n in range(ref.shape[0])]
    return (rows[0] if len(rows) == 1 else jnp.concatenate(rows, axis=1))[:, :width]


def column_step(width):
    return HIDDEN_BLOCK if width % HIDDEN_BLOCK == 0 else width


def tail_plan(rows, width):
    whole = width // LANES * LANES
    tail = width - whole
    packed = tail > 0 and whole > 0 and whole % tail == 0 and rows * tail % whole == 0
    extra = rows * tail // whole if packed else 0
    packed = packed and extra % 16 == 0 and ROW_BLOCK % extra == 0
    return whole, tail, extra if packed else 0


def sent_shape(rows, width):
    whole, _, extra = tail_plan(rows, width)
    return (rows + extra, whole) if extra else (rows, width)


def layout_kernel(group_count, tiles_local, where_ref, meta_ref):
    group = where_ref[0]
    requests = (where_ref.shape[0] - 2) // 3
    tiles_of, owner_of, text_of = ([where_ref[2 + n * requests + r] for r in range(requests)] for n in range(3))
    zero = jnp.int32(0)
    firsts, counts, offsets, texts_first, texts_both = [], [], [], [], []
    offset = zero
    for p in range(group_count):
        first, count, text_first, text_both, seen = zero, zero, zero, zero, zero
        for r in range(requests):
            mine = owner_of[r] == p
            tiles = jnp.where(mine, tiles_of[r], 0)
            text = jnp.where(mine, text_of[r], 0)
            first = first + jnp.where(seen == 0, tiles, 0)
            text_first = text_first + jnp.where(seen == 0, text, 0)
            count = count + tiles
            text_both = text_both + text
            seen = seen + jnp.where(mine, 1, 0)
        firsts.append(first)
        counts.append(count)
        offsets.append(offset)
        texts_first.append(text_first)
        texts_both.append(text_both)
        offset = offset + count

    def pick(values, index):
        out = values[0]
        for p in range(1, group_count):
            out = jnp.where(index == p, values[p], out)
        return out

    slots = slot_count_of(group_count)
    star, most = zero, counts[0]
    for p in range(1, group_count):
        larger = counts[p] > most
        star = jnp.where(larger, p, star)
        most = jnp.where(larger, counts[p], most)

    def local_tile(offset, slot):
        lane = lax.rem(group - offset + group_count * REQ_G * MAXT * group_count, group_count)
        tile = lax.div(offset + slot * group_count + lane, group_count)
        return jnp.minimum(tile, tiles_local - 1)

    my_first, my_count = pick(firsts, group), pick(counts, group)
    my_offset = pick(offsets, group)
    place = meta_places(group_count)
    meta_ref[place["first"]] = my_first
    meta_ref[place["second"]] = my_count - my_first
    meta_ref[place["text_first"]] = pick(texts_first, group)
    meta_ref[place["text_both"]] = pick(texts_both, group)
    meta_ref[place["star"]] = local_tile(pick(offsets, star), 1)
    for slot in range(slots):
        for d in range(group_count):
            other = group ^ d
            meta_ref[place["send"] + slot * group_count + d] = local_tile(pick(offsets, other), slot)
            lane = lax.rem(other - my_offset + group_count * REQ_G * MAXT * group_count, group_count)
            position = slot * group_count + lane
            goes = jnp.where(
                position < my_first,
                position,
                jnp.where(position < my_count, MAXT + position - my_first, -1),
            )
            meta_ref[place["goes"] + slot * group_count + d] = goes


def slot_count_of(group_count):
    return (REQ_G * MAXT + group_count - 1) // group_count


def meta_places(group_count):
    table = slot_count_of(group_count) * group_count
    return {
        "first": 0,
        "second": 1,
        "text_first": 2,
        "text_both": 3,
        "star": 4,
        "send": 8,
        "goes": 8 + table,
        "size": 8 + 2 * table,
    }


def mlp_kernel(piece_count, bases, tiles, where_ref, *refs):
    pieces = refs[:piece_count]
    gain_ref, bias_ref, up_bias_ref, up_ref, down_ref = refs[piece_count : piece_count + 5]
    outs = refs[piece_count + 5 : 2 * piece_count + 5]
    cat_ref, normed_ref, hidden_ref, total_ref = refs[2 * piece_count + 5 :]
    index = where_ref[1]
    _, width, tile_rows = pieces[0].shape
    rows = tiles * tile_rows
    channels, hidden_width = up_ref.shape
    up_step = column_step(hidden_width)
    down_step = column_step(channels)

    gain, bias = one_row(gain_ref, channels), one_row(bias_ref, channels)
    up_bias = one_row(up_bias_ref, hidden_width)
    for tile in range(tiles):
        for k, piece in enumerate(pieces):
            start = pl.multiple_of((index ^ k) * width, math.gcd(width, LANES))
            cat_ref[pl.ds(start, width), :] = piece[bases[k] + tile]
        values = cat_ref[...].T.astype(F32)
        average = jnp.sum(values, axis=1, keepdims=True) * (1.0 / channels)
        centered = values - average
        variance = jnp.sum(centered * centered, axis=1, keepdims=True) * (1.0 / channels)
        normed = centered * lax.rsqrt(variance + epsilon)
        normed = normed * gain + bias
        normed_ref[tile * tile_rows : (tile + 1) * tile_rows, :] = normed.astype(BF16)
    for n in range(hidden_width // up_step):
        take = slice(n * up_step, (n + 1) * up_step)
        value = jnp.dot(normed_ref[...], up_ref[:, take], preferred_element_type=F32)
        value = value + up_bias[:, take]
        value = 0.5 * value * (1.0 + lax.erf(value * (1.0 / math.sqrt(2.0))))
        hidden_ref[:, take] = value.astype(BF16)
    for n in range(channels // down_step):
        take = slice(n * down_step, (n + 1) * down_step)
        total_ref[:, take] = jnp.dot(
            hidden_ref[...], down_ref[:, take], preferred_element_type=F32
        )
    whole, tail, extra = tail_plan(rows, width)
    step = extra or ROW_BLOCK
    for part in range(rows // step):
        take = pl.ds(part * step, step)
        blocks = [total_ref[take, j * width : (j + 1) * width] for j in range(piece_count)]
        for out, block in zip(outs, xor_order(blocks, index)):
            block = block.astype(BF16)
            if extra:
                out[take, :] = block[:, :whole]
                out[rows : rows + extra, part * tail : (part + 1) * tail] = block[:, whole:]
            else:
                out[take, :] = block


def encoder_mlp(where, pieces, bases, tiles, ln_gain, ln_bias, w_up, b_up, w_down):
    _, width, tile_rows = pieces[0].shape
    rows = tiles * tile_rows
    count = len(pieces)
    channels, hidden_width = w_up.shape
    shape = sent_shape(rows, width)
    return pl.pallas_call(
        functools.partial(mlp_kernel, count, bases, tiles),
        out_shape=[jax.ShapeDtypeStruct(shape, BF16)] * count,
        in_specs=[SMEM] + [VMEM] * (count + 5),
        out_specs=[VMEM] * count,
        scratch_shapes=[
            pltpu.VMEM((channels, tile_rows), BF16),
            pltpu.VMEM((rows, channels), BF16),
            pltpu.VMEM((rows, hidden_width), BF16),
            pltpu.VMEM((rows, channels), F32),
        ],
        compiler_params=pltpu.CompilerParams(vmem_limit_bytes=44 * MIB),
        cost_estimate=LIGHT,
        name="encoder_mlp",
    )(
        where,
        *pieces,
        lane_rows(ln_gain),
        lane_rows(ln_bias),
        lane_rows(b_up),
        w_up,
        w_down,
    )


def prepare_kernel(
    group_count,
    tiles_local,
    where_ref,
    gain_ref,
    query_ref,
    normed_ref,
    meta_ref,
):
    @pl.when(pl.program_id(0) == 0)
    def _():
        layout_kernel(group_count, tiles_local, where_ref, meta_ref)

    gain = gain_ref[...] * (math.log2(math.e) / math.sqrt(HD))
    for col in range(0, query_ref.shape[1], HD):
        values = query_ref[:, col : col + HD].astype(F32)
        square = jnp.sum(values * values, axis=1, keepdims=True) * (1.0 / HD)
        normed_ref[:, col : col + HD] = (values * lax.rsqrt(square + epsilon) * gain).astype(BF16)


def prepare(where, q_gain, queries, group_count, tiles_local):
    text_rows, width = queries.shape
    step = ROW_BLOCK
    return pl.pallas_call(
        functools.partial(prepare_kernel, group_count, tiles_local),
        out_shape=[
            jax.ShapeDtypeStruct((text_rows, width), BF16),
            jax.ShapeDtypeStruct((meta_places(group_count)["size"],), jnp.int32),
        ],
        grid=(text_rows // step,),
        in_specs=[
            SMEM,
            pl.BlockSpec((1, HD), lambda n: (0, 0)),
            pl.BlockSpec((step, width), lambda n: (n, 0)),
        ],
        out_specs=[pl.BlockSpec((step, width), lambda n: (n, 0)), SMEM],
        compiler_params=pltpu.CompilerParams(vmem_limit_bytes=16 * MIB),
        cost_estimate=LIGHT,
        name="prepare",
    )(where, lane_rows(q_gain), queries)


def tap_kernel(blocks, head_count, dup, staged, where_ref, tap_hbm, weight_hbm, *refs):
    sources, out_ref = refs[:staged], refs[staged]
    targets = refs[staged + 1 : 2 * staged + 1]
    if staged:
        tap_ref, weight_ref, tap_sem, weight_sem, staged_sem = refs[2 * staged + 1 :]
    else:
        tap_ref, (weight_ref, weight_sem) = tap_hbm, refs[1:]
    tiles, _, tile_rows = tap_ref.shape
    block = weight_ref.shape[2]
    mine = lax.div(where_ref[1], jnp.int32(dup))
    taps = [
        pltpu.make_async_copy(tap_hbm.at[n], tap_ref.at[n], tap_sem.at[n])
        for n in range(tiles if staged else 0)
    ]
    weights = []
    for n, (head, k) in enumerate(blocks):
        column = pl.multiple_of(((mine ^ k) * head_count + head) * block, block)
        weights.append(
            pltpu.make_async_copy(
                weight_hbm.at[:, pl.ds(column, block)], weight_ref.at[n], weight_sem.at[n]
            )
        )
    others = [
        pltpu.make_async_copy(source, target, staged_sem.at[n])
        for n, (source, target) in enumerate(zip(sources, targets))
    ]
    for copy in weights[:1] + taps + weights[1:] + others:
        copy.start()
    for n in range(len(blocks)):
        weights[n].wait()
        for tile in range(tiles):
            if n == 0 and staged:
                taps[tile].wait()
            value = lax.dot_general(
                tap_ref[tile],
                weight_ref[n],
                (((0,), (0,)), ((), ())),
                preferred_element_type=F32,
            )
            out_ref[n, tile * tile_rows : (tile + 1) * tile_rows, :] = value.astype(BF16)
    for copy in others:
        copy.wait()


def tap_projection(where, tap_tiles, weights, blocks, head_count, dup, staged):
    tiles, depth, tile_rows = tap_tiles.shape
    block = 2 * HD
    return pl.pallas_call(
        functools.partial(tap_kernel, blocks, head_count, dup, len(staged)),
        out_shape=[jax.ShapeDtypeStruct((len(blocks), tiles * tile_rows, block), BF16)]
        + [jax.ShapeDtypeStruct(w.shape, w.dtype) for w in staged]
        + ([jax.ShapeDtypeStruct(tap_tiles.shape, BF16)] if staged else []),
        in_specs=[SMEM, HBM if staged else VMEM, HBM] + [HBM] * len(staged),
        out_specs=[VMEM] * (1 + len(staged) + bool(staged)),
        scratch_shapes=[pltpu.VMEM((len(blocks), depth, block), BF16)]
        + ([pltpu.SemaphoreType.DMA((tiles,))] if staged else [])
        + [pltpu.SemaphoreType.DMA((len(blocks),))]
        + ([pltpu.SemaphoreType.DMA((len(staged),))] if staged else []),
        compiler_params=pltpu.CompilerParams(vmem_limit_bytes=(42 if staged else 50) * MIB),
        cost_estimate=LIGHT,
        name="tap_projection",
    )(where, tap_tiles, weights, *staged)


def encode(x_ref, bias_ref, term_counts, terms, encoded_ref):
    tiles, width, tile_rows = x_ref.shape
    half_tiles = tiles // len(term_counts)
    whole, tail, extra = tail_plan(half_tiles * tile_rows, width)
    bias = one_row(bias_ref, width)
    for tile in range(tiles):
        half, row = tile // half_tiles, tile % half_tiles * tile_rows
        mine = terms[sum(term_counts[:half]) : sum(term_counts[: half + 1])]

        def summed(part, lanes):
            out = mine[0][part, lanes].astype(F32)
            for term in mine[1:]:
                out = out + term[part, lanes].astype(F32)
            return out

        total = summed(pl.ds(row, tile_rows), slice(None))
        if extra:
            chunks = range(row // extra, (row + tile_rows) // extra)
            rest = [
                summed(pl.ds(half_tiles * tile_rows, extra), slice(c * tail, (c + 1) * tail))
                for c in chunks
            ]
            rest = rest[0] if len(rest) == 1 else jnp.concatenate(rest, axis=0)
            total = jnp.concatenate([total, rest], axis=1)
        total = total + x_ref[tile].T.astype(F32) + bias
        encoded_ref[tile * tile_rows : (tile + 1) * tile_rows, :] = total.astype(BF16)


def kv_kernel(head, head_count, dest_count, dup, taps_at, term_counts, where_ref, *refs):
    weight_ref, refs = refs[0], refs[1:]
    part_count = 1 + max(part for part, _ in taps_at)
    tap_refs, refs = refs[:part_count], refs[part_count:]
    outs = refs[-dest_count - 1 :] if head == 0 else refs[-dest_count:]
    if head == 0:
        encoded_ref = outs[-1]
        encode(refs[0], refs[1], term_counts, refs[2 : 2 + sum(term_counts)], encoded_ref)
    else:
        encoded_ref = refs[0]
    block = 2 * HD
    mine = lax.div(where_ref[1], jnp.int32(dup))
    for k in range(dest_count):
        column = ((mine ^ k) * head_count + head) * block
        weights = weight_ref[:, pl.ds(pl.multiple_of(column, block), block)]
        value = jnp.dot(encoded_ref[...], weights, preferred_element_type=F32)
        part, n = taps_at[k]
        value = value + tap_refs[part][n].astype(F32)
        outs[k][...] = value.astype(BF16)


def kv_projection(where, weights, tap_parts, taps_at, inputs, term_counts, head, head_count, dup):
    tap_parts = tap_parts[: 1 + max(part for part, _ in taps_at)]
    rows, dest_count, block = tap_parts[0].shape[1], len(taps_at), 2 * HD
    outs = [jax.ShapeDtypeStruct((rows, block), BF16)] * dest_count
    if head == 0:
        outs.append(jax.ShapeDtypeStruct((rows, weights.shape[0]), BF16))
    return pl.pallas_call(
        functools.partial(
            kv_kernel, head, head_count, dest_count, dup, tuple(taps_at), term_counts
        ),
        out_shape=outs,
        in_specs=[SMEM] + [VMEM] * (1 + len(tap_parts) + len(inputs)),
        out_specs=[VMEM] * len(outs),
        compiler_params=pltpu.CompilerParams(vmem_limit_bytes=24 * MIB),
        cost_estimate=LIGHT,
        name="kv_projection",
    )(where, weights, *tap_parts, *inputs)


def finish_kernel(term_count, picks, meta_ref, gain_ref, *refs):
    terms = refs[:term_count]
    outs = refs[term_count : term_count + len(picks)]
    done_ref = refs[-1]
    rows = terms[0].shape[0]
    for row in range(0, rows, ROW_BLOCK):
        take = pl.ds(row, ROW_BLOCK)
        total = terms[0][take, :].astype(F32)
        for term in terms[1:]:
            total = total + term[take, :].astype(F32)
        keys = total[:, :HD]
        square = jnp.sum(keys * keys, axis=1, keepdims=True) * (1.0 / HD)
        keys = keys * lax.rsqrt(square + epsilon) * gain_ref[...]
        done_ref[take, :HD] = keys.astype(BF16).T
        done_ref[take, HD:] = (total[:, HD:] * VALUE_SHIFT).astype(BF16)
    for out, places in zip(outs, picks):
        for n, place in enumerate(places):
            start = pl.multiple_of(meta_ref[place] * ROW_BLOCK, ROW_BLOCK)
            out[n] = done_ref[pl.ds(start, ROW_BLOCK), :]


def finish_tiles(meta, k_gain, terms, picks):
    rows, block = terms[0].shape
    return pl.pallas_call(
        functools.partial(finish_kernel, len(terms), picks),
        out_shape=[jax.ShapeDtypeStruct((len(p), ROW_BLOCK, block), BF16) for p in picks],
        in_specs=[SMEM] + [VMEM] * (1 + len(terms)),
        out_specs=[VMEM] * len(picks),
        scratch_shapes=[pltpu.VMEM((rows, block), BF16)],
        compiler_params=pltpu.CompilerParams(vmem_limit_bytes=8 * MIB),
        cost_estimate=LIGHT,
        name="finish_tiles",
    )(meta, lane_rows(k_gain), *terms)


def attend_kernel(group_count, sources, head, has_base, meta_ref, query_ref, *refs):
    tile_refs = refs[: len(sources)]
    out_hbm, out_ref, key_ref, value_ref, out_sem = refs[len(sources) + has_base :]
    place = meta_places(group_count)
    counts = (meta_ref[place["first"]], meta_ref[place["second"]])
    text_first, text_both = meta_ref[place["text_first"]], meta_ref[place["text_both"]]
    span = MAXT * ROW_BLOCK
    text_rows, width = out_ref.shape
    heads = width // HD
    for label in range(REQ_G):
        for tile in range(1, MAXT):

            @pl.when(counts[label] <= tile)
            def _(tile=label * MAXT + tile):
                take = slice(tile * ROW_BLOCK, (tile + 1) * ROW_BLOCK)
                key_ref[:, take] = jnp.zeros((HD, ROW_BLOCK), BF16)
                value_ref[take, :] = jnp.zeros((ROW_BLOCK, 2 * HD), BF16)

    for tile_ref, places in zip(tile_refs, sources):
        for n, slot in enumerate(places):
            if slot is None:
                continue
            goes = meta_ref[place["goes"] + slot]

            @pl.when(goes >= 0)
            def _(tile_ref=tile_ref, n=n, goes=goes):
                take = pl.ds(pl.multiple_of(goes * ROW_BLOCK, ROW_BLOCK), ROW_BLOCK)
                key_ref[:, take] = tile_ref[n, :, :HD]
                value_ref[take, :HD] = tile_ref[n, :, HD:]
                value_ref[take, HD:] = jnp.ones((ROW_BLOCK, HD), BF16)

    copies = []
    for block in range(text_rows // ROW_BLOCK):
        start = block * ROW_BLOCK
        take = pl.ds(start, ROW_BLOCK)
        for label, (low, high) in enumerate(((0, text_first), (text_first, text_both))):
            meets = jnp.maximum(low, start) < jnp.minimum(high, start + ROW_BLOCK)

            def attend(key_rows, label=label, start=start, take=take, low=low, high=high):
                part = pl.ds(label * span, key_rows)
                slots = start + lax.broadcasted_iota(jnp.int32, (ROW_BLOCK, HD), 0)
                owned = (slots >= low) & (slots < high)
                for first in range(0, heads, HEAD_GROUP):
                    group = range(first, min(first + HEAD_GROUP, heads))
                    column = head * width
                    stacked = jnp.concatenate(
                        [
                            query_ref[take, column + h * HD : column + (h + 1) * HD]
                            for h in group
                        ],
                        axis=0,
                    )
                    scores = jnp.dot(stacked, key_ref[:, part], preferred_element_type=F32)
                    weights = jnp.exp2(scores).astype(BF16)
                    sums = jnp.dot(weights, value_ref[part, :], preferred_element_type=F32)
                    result = sums[:, :HD] / sums[:, HD:] * (1.0 / VALUE_SHIFT)
                    for n, h in enumerate(group):
                        lanes = slice(h * HD, (h + 1) * HD)
                        own = result[n * ROW_BLOCK : (n + 1) * ROW_BLOCK]
                        kept = 0.0 if label == 0 else out_ref[take, lanes].astype(F32)
                        out_ref[take, lanes] = jnp.where(owned, own, kept).astype(BF16)

            half = span // 2
            few = counts[label] * ROW_BLOCK <= half

            @pl.when(meets & few)
            def _(attend=attend):
                attend(half)

            @pl.when(meets & jnp.logical_not(few))
            def _(attend=attend):
                attend(span)

            if label == 0:

                @pl.when(jnp.logical_not(meets))
                def _(take=take):
                    out_ref[take, :] = jnp.zeros((ROW_BLOCK, width), BF16)

        copies.append(
            pltpu.make_async_copy(
                out_ref.at[take, :],
                out_hbm.at[take, pl.ds(head * width, width)],
                out_sem.at[block],
            )
        )
        copies[-1].start()
    for copy in copies:
        copy.wait()


def attend_head(group_count, meta, queries, tiles, sources, base, head, head_count):
    rows, width = queries.shape
    head_width = width // head_count
    group_rows = REQ_G * MAXT * ROW_BLOCK
    extra = [] if base is None else [base]
    return pl.pallas_call(
        functools.partial(attend_kernel, group_count, sources, head, len(extra)),
        out_shape=jax.ShapeDtypeStruct((rows, width), BF16),
        in_specs=[SMEM] + [VMEM] * (1 + len(tiles)) + [HBM] * len(extra),
        out_specs=HBM,
        scratch_shapes=[
            pltpu.VMEM((rows, head_width), BF16),
            pltpu.VMEM((HD, group_rows), BF16),
            pltpu.VMEM((group_rows, 2 * HD), BF16),
            pltpu.SemaphoreType.DMA((rows // ROW_BLOCK,)),
        ],
        input_output_aliases={2 + len(tiles): 0} if extra else {},
        compiler_params=pltpu.CompilerParams(vmem_limit_bytes=24 * MIB),
        cost_estimate=LIGHT,
        name="attend_head",
    )(meta, queries, *tiles, *extra)


def add_rounded(a, b):
    return (a.astype(F32) + b.astype(F32)).astype(BF16)


def after(value, *others):
    others = [v for v in others if v is not None]
    return lax.optimization_barrier((value, others))[0]


def scatter_sum(blocks, count, first_bit, earlier=None):
    blocks = dict(enumerate(blocks))
    bits = bits_of(len(blocks))
    for b in range(bits):
        pairs = xor_pairs(count, 1 << (b + first_bit))
        got, sent = {}, None
        for k in sorted((k for k in blocks if (k >> b) & 1), reverse=True):
            sent = blocks[k]
            if b == bits - 1 and earlier is not None:
                sent = after(sent, earlier)
            got[k ^ (1 << b)] = lax.ppermute(sent, "tp", pairs)
        if b == bits - 1:
            return [blocks[0], got[0]], sent
        blocks = {k: add_rounded(blocks[k], got[k]) for k in got}
    return [blocks[0]], blocks[0]


def gather_half(whole, own, first, count, ready):
    bits = bits_of(count)
    pieces = {0: own}
    for b in reversed(range(1, bits)):
        pairs = xor_pairs(count, 1 << b)
        for k in sorted(pieces):
            pieces[k | (1 << b)] = lax.ppermute(pieces[k], "tp", pairs)
    pairs = xor_pairs(count, 1)
    for k in sorted(pieces):
        if k:
            pieces[k | 1] = lax.ppermute(after(pieces[k], ready), "tp", pairs)
    pieces[0], pieces[1] = whole
    bases = tuple(first if k < 2 else 0 for k in range(count))
    return [pieces[k] for k in range(count)], bases


def local(
    x_in,
    taps,
    ln_gain,
    ln_bias,
    w_up,
    b_up,
    w_down,
    b_down,
    kv_w_out,
    kv_w_taps,
    k_gain,
    q_gain,
    queries,
    tiles_per_request,
    owner,
    text_per_request,
):
    group_count = lax.axis_size("grp")
    tp_count = lax.axis_size("tp")
    position = jnp.stack([lax.axis_index("grp"), lax.axis_index("tp")]).astype(jnp.int32)
    where = jnp.concatenate([position, tiles_per_request, owner, text_per_request])
    tiles_local = x_in.shape[0]
    x_tiles = jnp.swapaxes(x_in, 2, 3)[:, 0]
    tap_tiles = jnp.swapaxes(taps, 2, 3)[:, 0]
    head_count = max(1, KVH // tp_count)
    dup = max(1, tp_count // KVH)
    dest_count = tp_count // dup
    place = meta_places(group_count)

    halves = HALVES if tiles_local % HALVES == 0 else 1
    tiles = tiles_local // halves
    own_halves = [x_tiles[:tiles]] + [
        after(x_tiles, where)[h * tiles : (h + 1) * tiles] for h in range(1, halves)
    ]
    whole = [x_tiles, lax.ppermute(x_tiles, "tp", xor_pairs(tp_count, 1))]

    tap_blocks = [(h, k) for h in range(head_count) for k in range(dest_count)]
    early = len(tap_blocks) * TAPS_EARLY // 8
    first_taps, w_up, w_down, tap_tiles = tap_projection(
        where, tap_tiles, kv_w_taps, tap_blocks[:early], head_count, dup, (w_up, w_down)
    )
    mlp_terms = []
    ready, begun = first_taps, where
    for half in range(halves):
        pieces, bases = gather_half(whole, own_halves[half], half * tiles, tp_count, ready)
        mlp_blocks = encoder_mlp(
            begun, pieces, bases, tiles, ln_gain, ln_bias, w_up, b_up, w_down
        )
        terms, sent = scatter_sum(mlp_blocks, tp_count, 0)
        mlp_terms.append(terms)
        ready, begun = mlp_blocks[0], after(where, sent)
    (last_taps,) = tap_projection(
        begun, tap_tiles, kv_w_taps, tap_blocks[early:], head_count, dup, ()
    )
    taps_at = [(0, n) for n in range(early)]
    taps_at += [(1, n) for n in range(len(tap_blocks) - early)]
    kv_blocks = []
    inputs = (x_tiles, lane_rows(b_down), *(term for half in mlp_terms for term in half))
    for head in range(head_count):
        made = kv_projection(
            where,
            kv_w_out,
            (first_taps, last_taps),
            taps_at[head * dest_count : (head + 1) * dest_count],
            inputs,
            tuple(len(half) for half in mlp_terms),
            head,
            head_count,
            dup,
        )
        kv_blocks.append(made[:dest_count])
        if head == 0:
            inputs = (made[-1],)
    kv_terms, arrived = [], None
    for head in range(head_count):
        blocks = kv_blocks[head]
        for b in range(bits_of(dup)):
            pairs = xor_pairs(tp_count, 1 << b)
            blocks = [add_rounded(v, lax.ppermute(v, "tp", pairs)) for v in blocks]
        terms, sent = scatter_sum(blocks, tp_count, bits_of(dup), arrived)
        kv_terms.append(terms)
        if head == 0:
            query_rows, meta = prepare(
                after(where, sent), q_gain, queries, group_count, tiles_local
            )
        arrived = (terms[-1], meta)

    slots = slot_count_of(group_count)
    total_tiles = group_count * tiles_local
    most_other = total_tiles - REQ_G * MAXT - REQ_G * (group_count - 2)
    one_large = group_count == 4 and slots == 2 and most_other <= group_count
    send = place["send"]
    out = None

    def move(value, mask):
        return lax.ppermute(value, "grp", xor_pairs(group_count, mask))

    for head in range(head_count):
        terms = kv_terms[head]
        if one_large:
            star = place["star"]
            order = (0, 2, 3, 1)
            picks = tuple((send + d, star) for d in order)
            made = finish_tiles(meta, k_gain, terms, picks)
            tiles = tuple(move(tile, d) if d else tile for tile, d in zip(made, order))
            sources = tuple((d, group_count + d) for d in order)
        else:
            picks = tuple(
                tuple(send + s * group_count + d for s in range(slots)) for d in range(group_count)
            )
            made = finish_tiles(meta, k_gain, terms, picks)
            tiles = tuple(made[:1]) + tuple(move(made[d], d) for d in range(1, group_count))
            sources = tuple(
                tuple(s * group_count + d for s in range(slots)) for d in range(group_count)
            )
        out = attend_head(
            group_count, meta, query_rows, tiles, sources, out, head, head_count
        )
    return out


def solution(mesh):
    in_specs = (
        P(None, ("rep", "grp"), None, "tp"),
        P(None, ("rep", "grp"), None, "tp"),
        P(),
        P(),
        P(None, "tp"),
        P("tp"),
        P("tp", None),
        P("tp"),
        P("tp", None),
        P("tp", None),
        P(),
        P(),
        P(("rep", "grp"), "tp"),
        P("rep"),
        P("rep"),
        P("rep"),
    )
    out_specs = P(("rep", "grp"), "tp")
    return jax.shard_map(local, mesh=mesh, in_specs=in_specs, out_specs=out_specs, check_vma=False)
```

```python
import functools
import math

import jax
import jax.numpy as jnp
from jax import lax
from jax.experimental import pallas as pl
from jax.experimental.pallas import tpu as pltpu
from jax.sharding import PartitionSpec as P

KVH = 8
HD = 128
MAXT = 4
REQ_G = 2
LANES = 128
ROW_BLOCK = 128
HIDDEN_BLOCK = 256
HEAD_GROUP = 8
HALVES = 2
TAPS_EARLY = 3
VALUE_SHIFT = 2.0**-24
epsilon = 1e-05

F32 = jnp.float32
BF16 = jnp.bfloat16
VMEM = pl.BlockSpec(memory_space=pltpu.VMEM)
HBM = pl.BlockSpec(memory_space=pltpu.HBM)
SMEM = pl.BlockSpec(memory_space=pltpu.SMEM)
MIB = 1024 * 1024
LIGHT = pl.CostEstimate(flops=1024, bytes_accessed=1024, transcendentals=0)


def bits_of(count):
    bits = count.bit_length() - 1
    assert 1 << bits == count
    return bits


def xor_order(blocks, index):
    blocks = list(blocks)
    for b in range(bits_of(len(blocks))):
        swap = ((index >> b) & 1) == 1
        for k in range(len(blocks)):
            if not (k >> b) & 1:
                low, high = blocks[k], blocks[k | (1 << b)]
                blocks[k] = lax.select(swap, high, low)
                blocks[k | (1 << b)] = lax.select(swap, low, high)
    return blocks


def xor_pairs(count, mask):
    return [(i, i ^ mask) for i in range(count)]


def lane_rows(vector):
    return jnp.pad(vector, (0, -vector.shape[0] % LANES)).reshape(-1, LANES)


def one_row(ref, width):
    rows = [ref[n : n + 1, :] for n in range(ref.shape[0])]
    return (rows[0] if len(rows) == 1 else jnp.concatenate(rows, axis=1))[:, :width]


def column_step(width):
    return HIDDEN_BLOCK if width % HIDDEN_BLOCK == 0 else width


def tail_plan(rows, width):
    whole = width // LANES * LANES
    tail = width - whole
    packed = tail > 0 and whole > 0 and whole % tail == 0 and rows * tail % whole == 0
    extra = rows * tail // whole if packed else 0
    packed = packed and extra % 16 == 0 and ROW_BLOCK % extra == 0
    return whole, tail, extra if packed else 0


def sent_shape(rows, width):
    whole, _, extra = tail_plan(rows, width)
    return (rows + extra, whole) if extra else (rows, width)


def layout_kernel(group_count, tiles_local, where_ref, meta_ref):
    group = where_ref[0]
    requests = (where_ref.shape[0] - 2) // 3
    tiles_of, owner_of, text_of = ([where_ref[2 + n * requests + r] for r in range(requests)] for n in range(3))
    zero = jnp.int32(0)
    firsts, counts, offsets, texts_first, texts_both = [], [], [], [], []
    offset = zero
    for p in range(group_count):
        first, count, text_first, text_both, seen = zero, zero, zero, zero, zero
        for r in range(requests):
            mine = owner_of[r] == p
            tiles = jnp.where(mine, tiles_of[r], 0)
            text = jnp.where(mine, text_of[r], 0)
            first = first + jnp.where(seen == 0, tiles, 0)
            text_first = text_first + jnp.where(seen == 0, text, 0)
            count = count + tiles
            text_both = text_both + text
            seen = seen + jnp.where(mine, 1, 0)
        firsts.append(first)
        counts.append(count)
        offsets.append(offset)
        texts_first.append(text_first)
        texts_both.append(text_both)
        offset = offset + count

    def pick(values, index):
        out = values[0]
        for p in range(1, group_count):
            out = jnp.where(index == p, values[p], out)
        return out

    slots = slot_count_of(group_count)
    star, most = zero, counts[0]
    for p in range(1, group_count):
        larger = counts[p] > most
        star = jnp.where(larger, p, star)
        most = jnp.where(larger, counts[p], most)

    def local_tile(offset, slot):
        lane = lax.rem(group - offset + group_count * REQ_G * MAXT * group_count, group_count)
        tile = lax.div(offset + slot * group_count + lane, group_count)
        return jnp.minimum(tile, tiles_local - 1)

    my_first, my_count = pick(firsts, group), pick(counts, group)
    my_offset = pick(offsets, group)
    place = meta_places(group_count)
    meta_ref[place["first"]] = my_first
    meta_ref[place["second"]] = my_count - my_first
    meta_ref[place["text_first"]] = pick(texts_first, group)
    meta_ref[place["text_both"]] = pick(texts_both, group)
    meta_ref[place["star"]] = local_tile(pick(offsets, star), 1)
    for slot in range(slots):
        for d in range(group_count):
            other = group ^ d
            meta_ref[place["send"] + slot * group_count + d] = local_tile(pick(offsets, other), slot)
            lane = lax.rem(other - my_offset + group_count * REQ_G * MAXT * group_count, group_count)
            position = slot * group_count + lane
            goes = jnp.where(
                position < my_first,
                position,
                jnp.where(position < my_count, MAXT + position - my_first, -1),
            )
            meta_ref[place["goes"] + slot * group_count + d] = goes


def slot_count_of(group_count):
    return (REQ_G * MAXT + group_count - 1) // group_count


def meta_places(group_count):
    table = slot_count_of(group_count) * group_count
    return {
        "first": 0,
        "second": 1,
        "text_first": 2,
        "text_both": 3,
        "star": 4,
        "send": 8,
        "goes": 8 + table,
        "size": 8 + 2 * table,
    }


def mlp_kernel(piece_count, base, tiles, where_ref, *refs):
    pieces = refs[:piece_count]
    gain_ref, bias_ref, up_bias_ref, up_ref, down_ref = refs[piece_count : piece_count + 5]
    outs = refs[piece_count + 5 : 2 * piece_count + 5]
    cat_ref, normed_ref, hidden_ref, total_ref = refs[2 * piece_count + 5 :]
    index = where_ref[1]
    _, width, tile_rows = pieces[0].shape
    rows = tiles * tile_rows
    channels, hidden_width = up_ref.shape
    up_step = column_step(hidden_width)
    down_step = column_step(channels)

    gain, bias = one_row(gain_ref, channels), one_row(bias_ref, channels)
    up_bias = one_row(up_bias_ref, hidden_width)
    for tile in range(tiles):
        for k, piece in enumerate(pieces):
            start = pl.multiple_of((index ^ k) * width, math.gcd(width, LANES))
            cat_ref[pl.ds(start, width), :] = piece[base + tile]
        values = cat_ref[...].T.astype(F32)
        average = jnp.sum(values, axis=1, keepdims=True) * (1.0 / channels)
        centered = values - average
        variance = jnp.sum(centered * centered, axis=1, keepdims=True) * (1.0 / channels)
        normed = centered * lax.rsqrt(variance + epsilon)
        normed = normed * gain + bias
        normed_ref[tile * tile_rows : (tile + 1) * tile_rows, :] = normed.astype(BF16)
    for n in range(hidden_width // up_step):
        take = slice(n * up_step, (n + 1) * up_step)
        value = jnp.dot(normed_ref[...], up_ref[:, take], preferred_element_type=F32)
        value = value + up_bias[:, take]
        value = 0.5 * value * (1.0 + lax.erf(value * (1.0 / math.sqrt(2.0))))
        hidden_ref[:, take] = value.astype(BF16)
    for n in range(channels // down_step):
        take = slice(n * down_step, (n + 1) * down_step)
        total_ref[:, take] = jnp.dot(
            hidden_ref[...], down_ref[:, take], preferred_element_type=F32
        )
    whole, tail, extra = tail_plan(rows, width)
    step = extra or ROW_BLOCK
    for part in range(rows // step):
        take = pl.ds(part * step, step)
        blocks = [total_ref[take, j * width : (j + 1) * width] for j in range(piece_count)]
        for out, block in zip(outs, xor_order(blocks, index)):
            block = block.astype(BF16)
            if extra:
                out[take, :] = block[:, :whole]
                out[rows : rows + extra, part * tail : (part + 1) * tail] = block[:, whole:]
            else:
                out[take, :] = block


def encoder_mlp(where, pieces, base, tiles, ln_gain, ln_bias, w_up, b_up, w_down):
    _, width, tile_rows = pieces[0].shape
    rows = tiles * tile_rows
    count = len(pieces)
    channels, hidden_width = w_up.shape
    shape = sent_shape(rows, width)
    return pl.pallas_call(
        functools.partial(mlp_kernel, count, base, tiles),
        out_shape=[jax.ShapeDtypeStruct(shape, BF16)] * count,
        in_specs=[SMEM] + [VMEM] * (count + 5),
        out_specs=[VMEM] * count,
        scratch_shapes=[
            pltpu.VMEM((channels, tile_rows), BF16),
            pltpu.VMEM((rows, channels), BF16),
            pltpu.VMEM((rows, hidden_width), BF16),
            pltpu.VMEM((rows, channels), F32),
        ],
        compiler_params=pltpu.CompilerParams(vmem_limit_bytes=44 * MIB),
        cost_estimate=LIGHT,
        name="encoder_mlp",
    )(
        where,
        *pieces,
        lane_rows(ln_gain),
        lane_rows(ln_bias),
        lane_rows(b_up),
        w_up,
        w_down,
    )


def prepare_kernel(
    group_count,
    tiles_local,
    where_ref,
    gain_ref,
    query_ref,
    normed_ref,
    meta_ref,
):
    @pl.when(pl.program_id(0) == 0)
    def _():
        layout_kernel(group_count, tiles_local, where_ref, meta_ref)

    gain = gain_ref[...] * (math.log2(math.e) / math.sqrt(HD))
    for col in range(0, query_ref.shape[1], HD):
        values = query_ref[:, col : col + HD].astype(F32)
        square = jnp.sum(values * values, axis=1, keepdims=True) * (1.0 / HD)
        normed_ref[:, col : col + HD] = (values * lax.rsqrt(square + epsilon) * gain).astype(BF16)


def prepare(where, q_gain, queries, group_count, tiles_local):
    text_rows, width = queries.shape
    step = ROW_BLOCK
    return pl.pallas_call(
        functools.partial(prepare_kernel, group_count, tiles_local),
        out_shape=[
            jax.ShapeDtypeStruct((text_rows, width), BF16),
            jax.ShapeDtypeStruct((meta_places(group_count)["size"],), jnp.int32),
        ],
        grid=(text_rows // step,),
        in_specs=[
            SMEM,
            pl.BlockSpec((1, HD), lambda n: (0, 0)),
            pl.BlockSpec((step, width), lambda n: (n, 0)),
        ],
        out_specs=[pl.BlockSpec((step, width), lambda n: (n, 0)), SMEM],
        compiler_params=pltpu.CompilerParams(vmem_limit_bytes=16 * MIB),
        cost_estimate=LIGHT,
        name="prepare",
    )(where, lane_rows(q_gain), queries)


def tap_kernel(blocks, head_count, dup, staged, where_ref, tap_hbm, weight_hbm, *refs):
    sources, out_ref = refs[:staged], refs[staged]
    targets = refs[staged + 1 : 2 * staged + 1]
    if staged:
        tap_ref, weight_ref, tap_sem, weight_sem, staged_sem = refs[2 * staged + 1 :]
    else:
        tap_ref, (weight_ref, weight_sem) = tap_hbm, refs[1:]
    tiles, _, tile_rows = tap_ref.shape
    block = weight_ref.shape[2]
    mine = lax.div(where_ref[1], jnp.int32(dup))
    taps = [
        pltpu.make_async_copy(tap_hbm.at[n], tap_ref.at[n], tap_sem.at[n])
        for n in range(tiles if staged else 0)
    ]
    weights = []
    for n, (head, k) in enumerate(blocks):
        column = pl.multiple_of(((mine ^ k) * head_count + head) * block, block)
        weights.append(
            pltpu.make_async_copy(
                weight_hbm.at[:, pl.ds(column, block)], weight_ref.at[n], weight_sem.at[n]
            )
        )
    others = [
        pltpu.make_async_copy(source, target, staged_sem.at[n])
        for n, (source, target) in enumerate(zip(sources, targets))
    ]
    for copy in weights[:1] + taps + weights[1:] + others:
        copy.start()
    for n in range(len(blocks)):
        weights[n].wait()
        for tile in range(tiles):
            if n == 0 and staged:
                taps[tile].wait()
            value = lax.dot_general(
                tap_ref[tile],
                weight_ref[n],
                (((0,), (0,)), ((), ())),
                preferred_element_type=F32,
            )
            out_ref[n, tile * tile_rows : (tile + 1) * tile_rows, :] = value.astype(BF16)
    for copy in others:
        copy.wait()


def tap_projection(where, tap_tiles, weights, blocks, head_count, dup, staged):
    tiles, depth, tile_rows = tap_tiles.shape
    block = 2 * HD
    return pl.pallas_call(
        functools.partial(tap_kernel, blocks, head_count, dup, len(staged)),
        out_shape=[jax.ShapeDtypeStruct((len(blocks), tiles * tile_rows, block), BF16)]
        + [jax.ShapeDtypeStruct(w.shape, w.dtype) for w in staged]
        + ([jax.ShapeDtypeStruct(tap_tiles.shape, BF16)] if staged else []),
        in_specs=[SMEM, HBM if staged else VMEM, HBM] + [HBM] * len(staged),
        out_specs=[VMEM] * (1 + len(staged) + bool(staged)),
        scratch_shapes=[pltpu.VMEM((len(blocks), depth, block), BF16)]
        + ([pltpu.SemaphoreType.DMA((tiles,))] if staged else [])
        + [pltpu.SemaphoreType.DMA((len(blocks),))]
        + ([pltpu.SemaphoreType.DMA((len(staged),))] if staged else []),
        compiler_params=pltpu.CompilerParams(vmem_limit_bytes=(42 if staged else 50) * MIB),
        cost_estimate=LIGHT,
        name="tap_projection",
    )(where, tap_tiles, weights, *staged)


def encode(x_ref, bias_ref, term_counts, terms, encoded_ref):
    tiles, width, tile_rows = x_ref.shape
    half_tiles = tiles // len(term_counts)
    whole, tail, extra = tail_plan(half_tiles * tile_rows, width)
    bias = one_row(bias_ref, width)
    for tile in range(tiles):
        half, row = tile // half_tiles, tile % half_tiles * tile_rows
        mine = terms[sum(term_counts[:half]) : sum(term_counts[: half + 1])]

        def summed(part, lanes):
            out = mine[0][part, lanes].astype(F32)
            for term in mine[1:]:
                out = out + term[part, lanes].astype(F32)
            return out

        total = summed(pl.ds(row, tile_rows), slice(None))
        if extra:
            chunks = range(row // extra, (row + tile_rows) // extra)
            rest = [
                summed(pl.ds(half_tiles * tile_rows, extra), slice(c * tail, (c + 1) * tail))
                for c in chunks
            ]
            rest = rest[0] if len(rest) == 1 else jnp.concatenate(rest, axis=0)
            total = jnp.concatenate([total, rest], axis=1)
        total = total + x_ref[tile].T.astype(F32) + bias
        encoded_ref[tile * tile_rows : (tile + 1) * tile_rows, :] = total.astype(BF16)


def kv_kernel(head, head_count, dest_count, dup, taps_at, term_counts, where_ref, *refs):
    weight_ref, refs = refs[0], refs[1:]
    part_count = 1 + max(part for part, _ in taps_at)
    tap_refs, refs = refs[:part_count], refs[part_count:]
    outs = refs[-dest_count - 1 :] if head == 0 else refs[-dest_count:]
    if head == 0:
        encoded_ref = outs[-1]
        encode(refs[0], refs[1], term_counts, refs[2 : 2 + sum(term_counts)], encoded_ref)
    else:
        encoded_ref = refs[0]
    block = 2 * HD
    mine = lax.div(where_ref[1], jnp.int32(dup))
    for k in range(dest_count):
        column = ((mine ^ k) * head_count + head) * block
        weights = weight_ref[:, pl.ds(pl.multiple_of(column, block), block)]
        value = jnp.dot(encoded_ref[...], weights, preferred_element_type=F32)
        part, n = taps_at[k]
        value = value + tap_refs[part][n].astype(F32)
        outs[k][...] = value.astype(BF16)


def kv_projection(where, weights, tap_parts, taps_at, inputs, term_counts, head, head_count, dup):
    tap_parts = tap_parts[: 1 + max(part for part, _ in taps_at)]
    rows, dest_count, block = tap_parts[0].shape[1], len(taps_at), 2 * HD
    outs = [jax.ShapeDtypeStruct((rows, block), BF16)] * dest_count
    if head == 0:
        outs.append(jax.ShapeDtypeStruct((rows, weights.shape[0]), BF16))
    return pl.pallas_call(
        functools.partial(
            kv_kernel, head, head_count, dest_count, dup, tuple(taps_at), term_counts
        ),
        out_shape=outs,
        in_specs=[SMEM] + [VMEM] * (1 + len(tap_parts) + len(inputs)),
        out_specs=[VMEM] * len(outs),
        compiler_params=pltpu.CompilerParams(vmem_limit_bytes=24 * MIB),
        cost_estimate=LIGHT,
        name="kv_projection",
    )(where, weights, *tap_parts, *inputs)


def finish_kernel(term_count, picks, meta_ref, gain_ref, *refs):
    terms = refs[:term_count]
    outs = refs[term_count : term_count + len(picks)]
    done_ref = refs[-1]
    rows = terms[0].shape[0]
    for row in range(0, rows, ROW_BLOCK):
        take = pl.ds(row, ROW_BLOCK)
        total = terms[0][take, :].astype(F32)
        for term in terms[1:]:
            total = total + term[take, :].astype(F32)
        keys = total[:, :HD]
        square = jnp.sum(keys * keys, axis=1, keepdims=True) * (1.0 / HD)
        keys = keys * lax.rsqrt(square + epsilon) * gain_ref[...]
        done_ref[take, :HD] = keys.astype(BF16).T
        done_ref[take, HD:] = (total[:, HD:] * VALUE_SHIFT).astype(BF16)
    for out, places in zip(outs, picks):
        for n, place in enumerate(places):
            start = pl.multiple_of(meta_ref[place] * ROW_BLOCK, ROW_BLOCK)
            out[n] = done_ref[pl.ds(start, ROW_BLOCK), :]


def finish_tiles(meta, k_gain, terms, picks):
    rows, block = terms[0].shape
    return pl.pallas_call(
        functools.partial(finish_kernel, len(terms), picks),
        out_shape=[jax.ShapeDtypeStruct((len(p), ROW_BLOCK, block), BF16) for p in picks],
        in_specs=[SMEM] + [VMEM] * (1 + len(terms)),
        out_specs=[VMEM] * len(picks),
        scratch_shapes=[pltpu.VMEM((rows, block), BF16)],
        compiler_params=pltpu.CompilerParams(vmem_limit_bytes=8 * MIB),
        cost_estimate=LIGHT,
        name="finish_tiles",
    )(meta, lane_rows(k_gain), *terms)


def attend_kernel(group_count, sources, head, has_base, meta_ref, query_ref, *refs):
    tile_refs = refs[: len(sources)]
    out_hbm, out_ref, key_ref, value_ref, out_sem = refs[len(sources) + has_base :]
    place = meta_places(group_count)
    counts = (meta_ref[place["first"]], meta_ref[place["second"]])
    text_first, text_both = meta_ref[place["text_first"]], meta_ref[place["text_both"]]
    span = MAXT * ROW_BLOCK
    text_rows, width = out_ref.shape
    heads = width // HD
    for label in range(REQ_G):
        for tile in range(1, MAXT):

            @pl.when(counts[label] <= tile)
            def _(tile=label * MAXT + tile):
                take = slice(tile * ROW_BLOCK, (tile + 1) * ROW_BLOCK)
                key_ref[:, take] = jnp.zeros((HD, ROW_BLOCK), BF16)
                value_ref[take, :] = jnp.zeros((ROW_BLOCK, 2 * HD), BF16)

    for tile_ref, places in zip(tile_refs, sources):
        for n, slot in enumerate(places):
            if slot is None:
                continue
            goes = meta_ref[place["goes"] + slot]

            @pl.when(goes >= 0)
            def _(tile_ref=tile_ref, n=n, goes=goes):
                take = pl.ds(pl.multiple_of(goes * ROW_BLOCK, ROW_BLOCK), ROW_BLOCK)
                key_ref[:, take] = tile_ref[n, :, :HD]
                value_ref[take, :HD] = tile_ref[n, :, HD:]
                value_ref[take, HD:] = jnp.ones((ROW_BLOCK, HD), BF16)

    copies = []
    for block in range(text_rows // ROW_BLOCK):
        start = block * ROW_BLOCK
        take = pl.ds(start, ROW_BLOCK)
        for label, (low, high) in enumerate(((0, text_first), (text_first, text_both))):
            meets = jnp.maximum(low, start) < jnp.minimum(high, start + ROW_BLOCK)

            def attend(key_rows, label=label, start=start, take=take, low=low, high=high):
                part = pl.ds(label * span, key_rows)
                slots = start + lax.broadcasted_iota(jnp.int32, (ROW_BLOCK, HD), 0)
                owned = (slots >= low) & (slots < high)
                for first in range(0, heads, HEAD_GROUP):
                    group = range(first, min(first + HEAD_GROUP, heads))
                    column = head * width
                    stacked = jnp.concatenate(
                        [
                            query_ref[take, column + h * HD : column + (h + 1) * HD]
                            for h in group
                        ],
                        axis=0,
                    )
                    scores = jnp.dot(stacked, key_ref[:, part], preferred_element_type=F32)
                    weights = jnp.exp2(scores).astype(BF16)
                    sums = jnp.dot(weights, value_ref[part, :], preferred_element_type=F32)
                    result = sums[:, :HD] / sums[:, HD:] * (1.0 / VALUE_SHIFT)
                    for n, h in enumerate(group):
                        lanes = slice(h * HD, (h + 1) * HD)
                        own = result[n * ROW_BLOCK : (n + 1) * ROW_BLOCK]
                        kept = 0.0 if label == 0 else out_ref[take, lanes].astype(F32)
                        out_ref[take, lanes] = jnp.where(owned, own, kept).astype(BF16)

            half = span // 2
            few = counts[label] * ROW_BLOCK <= half

            @pl.when(meets & few)
            def _(attend=attend):
                attend(half)

            @pl.when(meets & jnp.logical_not(few))
            def _(attend=attend):
                attend(span)

            if label == 0:

                @pl.when(jnp.logical_not(meets))
                def _(take=take):
                    out_ref[take, :] = jnp.zeros((ROW_BLOCK, width), BF16)

        copies.append(
            pltpu.make_async_copy(
                out_ref.at[take, :],
                out_hbm.at[take, pl.ds(head * width, width)],
                out_sem.at[block],
            )
        )
        copies[-1].start()
    for copy in copies:
        copy.wait()


def attend_head(group_count, meta, queries, tiles, sources, base, head, head_count):
    rows, width = queries.shape
    head_width = width // head_count
    group_rows = REQ_G * MAXT * ROW_BLOCK
    extra = [] if base is None else [base]
    return pl.pallas_call(
        functools.partial(attend_kernel, group_count, sources, head, len(extra)),
        out_shape=jax.ShapeDtypeStruct((rows, width), BF16),
        in_specs=[SMEM] + [VMEM] * (1 + len(tiles)) + [HBM] * len(extra),
        out_specs=HBM,
        scratch_shapes=[
            pltpu.VMEM((rows, head_width), BF16),
            pltpu.VMEM((HD, group_rows), BF16),
            pltpu.VMEM((group_rows, 2 * HD), BF16),
            pltpu.SemaphoreType.DMA((rows // ROW_BLOCK,)),
        ],
        input_output_aliases={2 + len(tiles): 0} if extra else {},
        compiler_params=pltpu.CompilerParams(vmem_limit_bytes=24 * MIB),
        cost_estimate=LIGHT,
        name="attend_head",
    )(meta, queries, *tiles, *extra)


def add_rounded(a, b):
    return (a.astype(F32) + b.astype(F32)).astype(BF16)


def after(value, *others):
    others = [v for v in others if v is not None]
    return lax.optimization_barrier((value, others))[0]


def scatter_sum(blocks, count, first_bit, earlier=None):
    blocks = dict(enumerate(blocks))
    bits = bits_of(len(blocks))
    for b in range(bits):
        pairs = xor_pairs(count, 1 << (b + first_bit))
        got, sent = {}, None
        for k in sorted((k for k in blocks if (k >> b) & 1), reverse=True):
            sent = blocks[k]
            if b == bits - 1 and earlier is not None:
                sent = after(sent, earlier)
            got[k ^ (1 << b)] = lax.ppermute(sent, "tp", pairs)
        if b == bits - 1:
            return [blocks[0], got[0]], sent
        blocks = {k: add_rounded(blocks[k], got[k]) for k in got}
    return [blocks[0]], blocks[0]


def gather_pieces(whole, count, ready):
    bits = bits_of(count)
    pieces = {0: whole[0]}
    for b in reversed(range(1, bits)):
        pairs = xor_pairs(count, 1 << b)
        for k in sorted(pieces):
            pieces[k | (1 << b)] = lax.ppermute(pieces[k], "tp", pairs)
    pairs = xor_pairs(count, 1)
    for k in sorted(pieces):
        if k:
            pieces[k | 1] = lax.ppermute(after(pieces[k], ready), "tp", pairs)
    pieces[0], pieces[1] = whole
    return [pieces[k] for k in range(count)]


def local(
    x_in,
    taps,
    ln_gain,
    ln_bias,
    w_up,
    b_up,
    w_down,
    b_down,
    kv_w_out,
    kv_w_taps,
    k_gain,
    q_gain,
    queries,
    tiles_per_request,
    owner,
    text_per_request,
):
    group_count = lax.axis_size("grp")
    tp_count = lax.axis_size("tp")
    position = jnp.stack([lax.axis_index("grp"), lax.axis_index("tp")]).astype(jnp.int32)
    where = jnp.concatenate([position, tiles_per_request, owner, text_per_request])
    tiles_local = x_in.shape[0]
    x_tiles = jnp.swapaxes(x_in, 2, 3)[:, 0]
    tap_tiles = jnp.swapaxes(taps, 2, 3)[:, 0]
    head_count = max(1, KVH // tp_count)
    dup = max(1, tp_count // KVH)
    dest_count = tp_count // dup
    place = meta_places(group_count)

    halves = HALVES if tiles_local % HALVES == 0 else 1
    tiles = tiles_local // halves
    whole = [x_tiles, lax.ppermute(x_tiles, "tp", xor_pairs(tp_count, 1))]

    tap_blocks = [(h, k) for h in range(head_count) for k in range(dest_count)]
    early = len(tap_blocks) * TAPS_EARLY // 8
    first_taps, w_up, w_down, tap_tiles = tap_projection(
        where, tap_tiles, kv_w_taps, tap_blocks[:early], head_count, dup, (w_up, w_down)
    )
    pieces = gather_pieces(whole, tp_count, first_taps)
    mlp_terms, begun = [], where
    for half in range(halves):
        mlp_blocks = encoder_mlp(
            begun, pieces, half * tiles, tiles, ln_gain, ln_bias, w_up, b_up, w_down
        )
        terms, sent = scatter_sum(mlp_blocks, tp_count, 0)
        mlp_terms.append(terms)
        begun = after(where, sent)
    (last_taps,) = tap_projection(
        begun, tap_tiles, kv_w_taps, tap_blocks[early:], head_count, dup, ()
    )
    taps_at = [(0, n) for n in range(early)]
    taps_at += [(1, n) for n in range(len(tap_blocks) - early)]
    kv_blocks = []
    inputs = (x_tiles, lane_rows(b_down), *(term for half in mlp_terms for term in half))
    for head in range(head_count):
        made = kv_projection(
            where,
            kv_w_out,
            (first_taps, last_taps),
            taps_at[head * dest_count : (head + 1) * dest_count],
            inputs,
            tuple(len(half) for half in mlp_terms),
            head,
            head_count,
            dup,
        )
        kv_blocks.append(made[:dest_count])
        if head == 0:
            inputs = (made[-1],)
    kv_terms, arrived = [], None
    for head in range(head_count):
        blocks = kv_blocks[head]
        for b in range(bits_of(dup)):
            pairs = xor_pairs(tp_count, 1 << b)
            blocks = [add_rounded(v, lax.ppermute(v, "tp", pairs)) for v in blocks]
        terms, sent = scatter_sum(blocks, tp_count, bits_of(dup), arrived)
        kv_terms.append(terms)
        if head == 0:
            query_rows, meta = prepare(
                after(where, sent), q_gain, queries, group_count, tiles_local
            )
        arrived = (terms[-1], meta)

    slots = slot_count_of(group_count)
    total_tiles = group_count * tiles_local
    most_other = total_tiles - REQ_G * MAXT - REQ_G * (group_count - 2)
    one_large = group_count == 4 and slots == 2 and most_other <= group_count
    send = place["send"]
    out = None

    def move(value, mask):
        return lax.ppermute(value, "grp", xor_pairs(group_count, mask))

    for head in range(head_count):
        terms = kv_terms[head]
        if one_large:
            star = place["star"]
            order = (0, 2, 3, 1)
            picks = tuple((send + d, star) for d in order)
            made = finish_tiles(meta, k_gain, terms, picks)
            tiles = tuple(move(tile, d) if d else tile for tile, d in zip(made, order))
            sources = tuple((d, group_count + d) for d in order)
        else:
            picks = tuple(
                tuple(send + s * group_count + d for s in range(slots)) for d in range(group_count)
            )
            made = finish_tiles(meta, k_gain, terms, picks)
            tiles = tuple(made[:1]) + tuple(move(made[d], d) for d in range(1, group_count))
            sources = tuple(
                tuple(s * group_count + d for s in range(slots)) for d in range(group_count)
            )
        out = attend_head(
            group_count, meta, query_rows, tiles, sources, out, head, head_count
        )
    return out


def solution(mesh):
    in_specs = (
        P(None, ("rep", "grp"), None, "tp"),
        P(None, ("rep", "grp"), None, "tp"),
        P(),
        P(),
        P(None, "tp"),
        P("tp"),
        P("tp", None),
        P("tp"),
        P("tp", None),
        P("tp", None),
        P(),
        P(),
        P(("rep", "grp"), "tp"),
        P("rep"),
        P("rep"),
        P("rep"),
    )
    out_specs = P(("rep", "grp"), "tp")
    return jax.shard_map(local, mesh=mesh, in_specs=in_specs, out_specs=out_specs, check_vma=False)
```

```python
import functools
import math

import jax
import jax.numpy as jnp
from jax import lax
from jax.experimental import pallas as pl
from jax.experimental.pallas import tpu as pltpu
from jax.sharding import PartitionSpec as P

KVH = 8
HD = 128
MAXT = 4
REQ_G = 2
LANES = 128
ROW_BLOCK = 128
HIDDEN_BLOCK = 256
HEAD_GROUP = 8
HALVES = 2
TAPS_EARLY = 4
VALUE_SHIFT = 2.0**-24
epsilon = 1e-05

F32 = jnp.float32
BF16 = jnp.bfloat16
VMEM = pl.BlockSpec(memory_space=pltpu.VMEM)
HBM = pl.BlockSpec(memory_space=pltpu.HBM)
SMEM = pl.BlockSpec(memory_space=pltpu.SMEM)
MIB = 1024 * 1024
LIGHT = pl.CostEstimate(flops=1024, bytes_accessed=1024, transcendentals=0)


def bits_of(count):
    bits = count.bit_length() - 1
    assert 1 << bits == count
    return bits


def xor_order(blocks, index):
    blocks = list(blocks)
    for b in range(bits_of(len(blocks))):
        swap = ((index >> b) & 1) == 1
        for k in range(len(blocks)):
            if not (k >> b) & 1:
                low, high = blocks[k], blocks[k | (1 << b)]
                blocks[k] = lax.select(swap, high, low)
                blocks[k | (1 << b)] = lax.select(swap, low, high)
    return blocks


def xor_pairs(count, mask):
    return [(i, i ^ mask) for i in range(count)]


def lane_rows(vector):
    return jnp.pad(vector, (0, -vector.shape[0] % LANES)).reshape(-1, LANES)


def one_row(ref, width):
    rows = [ref[n : n + 1, :] for n in range(ref.shape[0])]
    return (rows[0] if len(rows) == 1 else jnp.concatenate(rows, axis=1))[:, :width]


def column_step(width):
    return HIDDEN_BLOCK if width % HIDDEN_BLOCK == 0 else width


def tail_plan(rows, width):
    whole = width // LANES * LANES
    tail = width - whole
    packed = tail > 0 and whole > 0 and whole % tail == 0 and rows * tail % whole == 0
    extra = rows * tail // whole if packed else 0
    packed = packed and extra % 16 == 0 and ROW_BLOCK % extra == 0
    return whole, tail, extra if packed else 0


def sent_shape(rows, width):
    whole, _, extra = tail_plan(rows, width)
    return (rows + extra, whole) if extra else (rows, width)


def layout_kernel(group_count, tiles_local, where_ref, meta_ref):
    group = where_ref[0]
    requests = (where_ref.shape[0] - 2) // 3
    tiles_of, owner_of, text_of = ([where_ref[2 + n * requests + r] for r in range(requests)] for n in range(3))
    zero = jnp.int32(0)
    firsts, counts, offsets, texts_first, texts_both = [], [], [], [], []
    offset = zero
    for p in range(group_count):
        first, count, text_first, text_both, seen = zero, zero, zero, zero, zero
        for r in range(requests):
            mine = owner_of[r] == p
            tiles = jnp.where(mine, tiles_of[r], 0)
            text = jnp.where(mine, text_of[r], 0)
            first = first + jnp.where(seen == 0, tiles, 0)
            text_first = text_first + jnp.where(seen == 0, text, 0)
            count = count + tiles
            text_both = text_both + text
            seen = seen + jnp.where(mine, 1, 0)
        firsts.append(first)
        counts.append(count)
        offsets.append(offset)
        texts_first.append(text_first)
        texts_both.append(text_both)
        offset = offset + count

    def pick(values, index):
        out = values[0]
        for p in range(1, group_count):
            out = jnp.where(index == p, values[p], out)
        return out

    slots = slot_count_of(group_count)
    star, most = zero, counts[0]
    for p in range(1, group_count):
        larger = counts[p] > most
        star = jnp.where(larger, p, star)
        most = jnp.where(larger, counts[p], most)

    def local_tile(offset, slot):
        lane = lax.rem(group - offset + group_count * REQ_G * MAXT * group_count, group_count)
        tile = lax.div(offset + slot * group_count + lane, group_count)
        return jnp.minimum(tile, tiles_local - 1)

    my_first, my_count = pick(firsts, group), pick(counts, group)
    my_offset = pick(offsets, group)
    place = meta_places(group_count)
    meta_ref[place["first"]] = my_first
    meta_ref[place["second"]] = my_count - my_first
    meta_ref[place["text_first"]] = pick(texts_first, group)
    meta_ref[place["text_both"]] = pick(texts_both, group)
    meta_ref[place["star"]] = local_tile(pick(offsets, star), 1)
    for slot in range(slots):
        for d in range(group_count):
            other = group ^ d
            meta_ref[place["send"] + slot * group_count + d] = local_tile(pick(offsets, other), slot)
            lane = lax.rem(other - my_offset + group_count * REQ_G * MAXT * group_count, group_count)
            position = slot * group_count + lane
            goes = jnp.where(
                position < my_first,
                position,
                jnp.where(position < my_count, MAXT + position - my_first, -1),
            )
            meta_ref[place["goes"] + slot * group_count + d] = goes


def slot_count_of(group_count):
    return (REQ_G * MAXT + group_count - 1) // group_count


def meta_places(group_count):
    table = slot_count_of(group_count) * group_count
    return {
        "first": 0,
        "second": 1,
        "text_first": 2,
        "text_both": 3,
        "star": 4,
        "send": 8,
        "goes": 8 + table,
        "size": 8 + 2 * table,
    }


def mlp_kernel(piece_count, base, tiles, where_ref, *refs):
    pieces = refs[:piece_count]
    gain_ref, bias_ref, up_bias_ref, up_ref, down_ref = refs[piece_count : piece_count + 5]
    outs = refs[piece_count + 5 : 2 * piece_count + 5]
    cat_ref, normed_ref, hidden_ref, total_ref = refs[2 * piece_count + 5 :]
    index = where_ref[1]
    _, width, tile_rows = pieces[0].shape
    rows = tiles * tile_rows
    channels, hidden_width = up_ref.shape
    up_step = column_step(hidden_width)
    down_step = column_step(channels)

    gain, bias = one_row(gain_ref, channels), one_row(bias_ref, channels)
    up_bias = one_row(up_bias_ref, hidden_width)
    for tile in range(tiles):
        for k, piece in enumerate(pieces):
            start = pl.multiple_of((index ^ k) * width, math.gcd(width, LANES))
            cat_ref[pl.ds(start, width), :] = piece[base + tile]
        values = cat_ref[...].T.astype(F32)
        average = jnp.sum(values, axis=1, keepdims=True) * (1.0 / channels)
        centered = values - average
        variance = jnp.sum(centered * centered, axis=1, keepdims=True) * (1.0 / channels)
        normed = centered * lax.rsqrt(variance + epsilon)
        normed = normed * gain + bias
        normed_ref[tile * tile_rows : (tile + 1) * tile_rows, :] = normed.astype(BF16)
    for n in range(hidden_width // up_step):
        take = slice(n * up_step, (n + 1) * up_step)
        value = jnp.dot(normed_ref[...], up_ref[:, take], preferred_element_type=F32)
        value = value + up_bias[:, take]
        value = 0.5 * value * (1.0 + lax.erf(value * (1.0 / math.sqrt(2.0))))
        hidden_ref[:, take] = value.astype(BF16)
    for n in range(channels // down_step):
        take = slice(n * down_step, (n + 1) * down_step)
        total_ref[:, take] = jnp.dot(
            hidden_ref[...], down_ref[:, take], preferred_element_type=F32
        )
    whole, tail, extra = tail_plan(rows, width)
    step = extra or ROW_BLOCK
    for part in range(rows // step):
        take = pl.ds(part * step, step)
        blocks = [total_ref[take, j * width : (j + 1) * width] for j in range(piece_count)]
        for out, block in zip(outs, xor_order(blocks, index)):
            block = block.astype(BF16)
            if extra:
                out[take, :] = block[:, :whole]
                out[rows : rows + extra, part * tail : (part + 1) * tail] = block[:, whole:]
            else:
                out[take, :] = block


def encoder_mlp(where, pieces, base, tiles, ln_gain, ln_bias, w_up, b_up, w_down):
    _, width, tile_rows = pieces[0].shape
    rows = tiles * tile_rows
    count = len(pieces)
    channels, hidden_width = w_up.shape
    shape = sent_shape(rows, width)
    return pl.pallas_call(
        functools.partial(mlp_kernel, count, base, tiles),
        out_shape=[jax.ShapeDtypeStruct(shape, BF16)] * count,
        in_specs=[SMEM] + [VMEM] * (count + 5),
        out_specs=[VMEM] * count,
        scratch_shapes=[
            pltpu.VMEM((channels, tile_rows), BF16),
            pltpu.VMEM((rows, channels), BF16),
            pltpu.VMEM((rows, hidden_width), BF16),
            pltpu.VMEM((rows, channels), F32),
        ],
        compiler_params=pltpu.CompilerParams(vmem_limit_bytes=44 * MIB),
        cost_estimate=LIGHT,
        name="encoder_mlp",
    )(
        where,
        *pieces,
        lane_rows(ln_gain),
        lane_rows(ln_bias),
        lane_rows(b_up),
        w_up,
        w_down,
    )


def prepare_kernel(
    group_count,
    tiles_local,
    where_ref,
    gain_ref,
    query_ref,
    normed_ref,
    meta_ref,
):
    @pl.when(pl.program_id(0) == 0)
    def _():
        layout_kernel(group_count, tiles_local, where_ref, meta_ref)

    gain = gain_ref[...] * (math.log2(math.e) / math.sqrt(HD))
    for col in range(0, query_ref.shape[1], HD):
        values = query_ref[:, col : col + HD].astype(F32)
        square = jnp.sum(values * values, axis=1, keepdims=True) * (1.0 / HD)
        normed_ref[:, col : col + HD] = (values * lax.rsqrt(square + epsilon) * gain).astype(BF16)


def prepare(where, q_gain, queries, group_count, tiles_local):
    text_rows, width = queries.shape
    step = ROW_BLOCK
    return pl.pallas_call(
        functools.partial(prepare_kernel, group_count, tiles_local),
        out_shape=[
            jax.ShapeDtypeStruct((text_rows, width), BF16),
            jax.ShapeDtypeStruct((meta_places(group_count)["size"],), jnp.int32),
        ],
        grid=(text_rows // step,),
        in_specs=[
            SMEM,
            pl.BlockSpec((1, HD), lambda n: (0, 0)),
            pl.BlockSpec((step, width), lambda n: (n, 0)),
        ],
        out_specs=[pl.BlockSpec((step, width), lambda n: (n, 0)), SMEM],
        compiler_params=pltpu.CompilerParams(vmem_limit_bytes=16 * MIB),
        cost_estimate=LIGHT,
        name="prepare",
    )(where, lane_rows(q_gain), queries)


def tap_kernel(blocks, head_count, dup, staged, where_ref, tap_hbm, weight_hbm, *refs):
    sources, out_ref = refs[:staged], refs[staged]
    targets = refs[staged + 1 : 2 * staged + 1]
    if staged:
        tap_ref, weight_ref, tap_sem, weight_sem, staged_sem = refs[2 * staged + 1 :]
    else:
        tap_ref, (weight_ref, weight_sem) = tap_hbm, refs[1:]
    tiles, _, tile_rows = tap_ref.shape
    block = weight_ref.shape[2]
    mine = lax.div(where_ref[1], jnp.int32(dup))
    taps = [
        pltpu.make_async_copy(tap_hbm.at[n], tap_ref.at[n], tap_sem.at[n])
        for n in range(tiles if staged else 0)
    ]
    weights = []
    for n, (head, k) in enumerate(blocks):
        column = pl.multiple_of(((mine ^ k) * head_count + head) * block, block)
        weights.append(
            pltpu.make_async_copy(
                weight_hbm.at[:, pl.ds(column, block)], weight_ref.at[n], weight_sem.at[n]
            )
        )
    others = [
        pltpu.make_async_copy(source, target, staged_sem.at[n])
        for n, (source, target) in enumerate(zip(sources, targets))
    ]
    for copy in weights[:1] + taps + weights[1:] + others:
        copy.start()
    for n in range(len(blocks)):
        weights[n].wait()
        for tile in range(tiles):
            if n == 0 and staged:
                taps[tile].wait()
            value = lax.dot_general(
                tap_ref[tile],
                weight_ref[n],
                (((0,), (0,)), ((), ())),
                preferred_element_type=F32,
            )
            out_ref[n, tile * tile_rows : (tile + 1) * tile_rows, :] = value.astype(BF16)
    for copy in others:
        copy.wait()


def tap_projection(where, tap_tiles, weights, blocks, head_count, dup, staged):
    tiles, depth, tile_rows = tap_tiles.shape
    block = 2 * HD
    return pl.pallas_call(
        functools.partial(tap_kernel, blocks, head_count, dup, len(staged)),
        out_shape=[jax.ShapeDtypeStruct((len(blocks), tiles * tile_rows, block), BF16)]
        + [jax.ShapeDtypeStruct(w.shape, w.dtype) for w in staged]
        + ([jax.ShapeDtypeStruct(tap_tiles.shape, BF16)] if staged else []),
        in_specs=[SMEM, HBM if staged else VMEM, HBM] + [HBM] * len(staged),
        out_specs=[VMEM] * (1 + len(staged) + bool(staged)),
        scratch_shapes=[pltpu.VMEM((len(blocks), depth, block), BF16)]
        + ([pltpu.SemaphoreType.DMA((tiles,))] if staged else [])
        + [pltpu.SemaphoreType.DMA((len(blocks),))]
        + ([pltpu.SemaphoreType.DMA((len(staged),))] if staged else []),
        compiler_params=pltpu.CompilerParams(vmem_limit_bytes=(42 if staged else 50) * MIB),
        cost_estimate=LIGHT,
        name="tap_projection",
    )(where, tap_tiles, weights, *staged)


def encode(x_ref, bias_ref, term_counts, terms, encoded_ref):
    tiles, width, tile_rows = x_ref.shape
    half_tiles = tiles // len(term_counts)
    whole, tail, extra = tail_plan(half_tiles * tile_rows, width)
    bias = one_row(bias_ref, width)
    for tile in range(tiles):
        half, row = tile // half_tiles, tile % half_tiles * tile_rows
        mine = terms[sum(term_counts[:half]) : sum(term_counts[: half + 1])]

        def summed(part, lanes):
            out = mine[0][part, lanes].astype(F32)
            for term in mine[1:]:
                out = out + term[part, lanes].astype(F32)
            return out

        total = summed(pl.ds(row, tile_rows), slice(None))
        if extra:
            chunks = range(row // extra, (row + tile_rows) // extra)
            rest = [
                summed(pl.ds(half_tiles * tile_rows, extra), slice(c * tail, (c + 1) * tail))
                for c in chunks
            ]
            rest = rest[0] if len(rest) == 1 else jnp.concatenate(rest, axis=0)
            total = jnp.concatenate([total, rest], axis=1)
        total = total + x_ref[tile].T.astype(F32) + bias
        encoded_ref[tile * tile_rows : (tile + 1) * tile_rows, :] = total.astype(BF16)


def kv_kernel(head, head_count, dest_count, dup, taps_at, term_counts, where_ref, *refs):
    weight_ref, refs = refs[0], refs[1:]
    part_count = 1 + max(part for part, _ in taps_at)
    tap_refs, refs = refs[:part_count], refs[part_count:]
    outs = refs[-dest_count - 1 :] if head == 0 else refs[-dest_count:]
    if head == 0:
        encoded_ref = outs[-1]
        encode(refs[0], refs[1], term_counts, refs[2 : 2 + sum(term_counts)], encoded_ref)
    else:
        encoded_ref = refs[0]
    block = 2 * HD
    mine = lax.div(where_ref[1], jnp.int32(dup))
    for k in range(dest_count):
        column = ((mine ^ k) * head_count + head) * block
        weights = weight_ref[:, pl.ds(pl.multiple_of(column, block), block)]
        value = jnp.dot(encoded_ref[...], weights, preferred_element_type=F32)
        part, n = taps_at[k]
        value = value + tap_refs[part][n].astype(F32)
        outs[k][...] = value.astype(BF16)


def kv_projection(where, weights, tap_parts, taps_at, inputs, term_counts, head, head_count, dup):
    tap_parts = tap_parts[: 1 + max(part for part, _ in taps_at)]
    rows, dest_count, block = tap_parts[0].shape[1], len(taps_at), 2 * HD
    outs = [jax.ShapeDtypeStruct((rows, block), BF16)] * dest_count
    if head == 0:
        outs.append(jax.ShapeDtypeStruct((rows, weights.shape[0]), BF16))
    return pl.pallas_call(
        functools.partial(
            kv_kernel, head, head_count, dest_count, dup, tuple(taps_at), term_counts
        ),
        out_shape=outs,
        in_specs=[SMEM] + [VMEM] * (1 + len(tap_parts) + len(inputs)),
        out_specs=[VMEM] * len(outs),
        compiler_params=pltpu.CompilerParams(vmem_limit_bytes=24 * MIB),
        cost_estimate=LIGHT,
        name="kv_projection",
    )(where, weights, *tap_parts, *inputs)


def finish_kernel(term_count, picks, meta_ref, gain_ref, *refs):
    terms = refs[:term_count]
    outs = refs[term_count : term_count + len(picks)]
    done_ref = refs[-1]
    rows = terms[0].shape[0]
    for row in range(0, rows, ROW_BLOCK):
        take = pl.ds(row, ROW_BLOCK)
        total = terms[0][take, :].astype(F32)
        for term in terms[1:]:
            total = total + term[take, :].astype(F32)
        keys = total[:, :HD]
        square = jnp.sum(keys * keys, axis=1, keepdims=True) * (1.0 / HD)
        keys = keys * lax.rsqrt(square + epsilon) * gain_ref[...]
        done_ref[take, :HD] = keys.astype(BF16).T
        done_ref[take, HD:] = (total[:, HD:] * VALUE_SHIFT).astype(BF16)
    for out, places in zip(outs, picks):
        for n, place in enumerate(places):
            start = pl.multiple_of(meta_ref[place] * ROW_BLOCK, ROW_BLOCK)
            out[n] = done_ref[pl.ds(start, ROW_BLOCK), :]


def finish_tiles(meta, k_gain, terms, picks):
    rows, block = terms[0].shape
    return pl.pallas_call(
        functools.partial(finish_kernel, len(terms), picks),
        out_shape=[jax.ShapeDtypeStruct((len(p), ROW_BLOCK, block), BF16) for p in picks],
        in_specs=[SMEM] + [VMEM] * (1 + len(terms)),
        out_specs=[VMEM] * len(picks),
        scratch_shapes=[pltpu.VMEM((rows, block), BF16)],
        compiler_params=pltpu.CompilerParams(vmem_limit_bytes=8 * MIB),
        cost_estimate=LIGHT,
        name="finish_tiles",
    )(meta, lane_rows(k_gain), *terms)


def attend_kernel(group_count, sources, head, has_base, meta_ref, query_ref, *refs):
    tile_refs = refs[: len(sources)]
    out_hbm, out_ref, key_ref, value_ref, out_sem = refs[len(sources) + has_base :]
    place = meta_places(group_count)
    counts = (meta_ref[place["first"]], meta_ref[place["second"]])
    text_first, text_both = meta_ref[place["text_first"]], meta_ref[place["text_both"]]
    span = MAXT * ROW_BLOCK
    text_rows, width = out_ref.shape
    heads = width // HD
    for label in range(REQ_G):
        for tile in range(1, MAXT):

            @pl.when(counts[label] <= tile)
            def _(tile=label * MAXT + tile):
                take = slice(tile * ROW_BLOCK, (tile + 1) * ROW_BLOCK)
                key_ref[:, take] = jnp.zeros((HD, ROW_BLOCK), BF16)
                value_ref[take, :] = jnp.zeros((ROW_BLOCK, 2 * HD), BF16)

    for tile_ref, places in zip(tile_refs, sources):
        for n, slot in enumerate(places):
            if slot is None:
                continue
            goes = meta_ref[place["goes"] + slot]

            @pl.when(goes >= 0)
            def _(tile_ref=tile_ref, n=n, goes=goes):
                take = pl.ds(pl.multiple_of(goes * ROW_BLOCK, ROW_BLOCK), ROW_BLOCK)
                key_ref[:, take] = tile_ref[n, :, :HD]
                value_ref[take, :HD] = tile_ref[n, :, HD:]
                value_ref[take, HD:] = jnp.ones((ROW_BLOCK, HD), BF16)

    copies = []
    for block in range(text_rows // ROW_BLOCK):
        start = block * ROW_BLOCK
        take = pl.ds(start, ROW_BLOCK)
        for label, (low, high) in enumerate(((0, text_first), (text_first, text_both))):
            meets = jnp.maximum(low, start) < jnp.minimum(high, start + ROW_BLOCK)

            def attend(key_rows, label=label, start=start, take=take, low=low, high=high):
                part = pl.ds(label * span, key_rows)
                slots = start + lax.broadcasted_iota(jnp.int32, (ROW_BLOCK, HD), 0)
                owned = (slots >= low) & (slots < high)
                for first in range(0, heads, HEAD_GROUP):
                    group = range(first, min(first + HEAD_GROUP, heads))
                    column = head * width
                    stacked = jnp.concatenate(
                        [
                            query_ref[take, column + h * HD : column + (h + 1) * HD]
                            for h in group
                        ],
                        axis=0,
                    )
                    scores = jnp.dot(stacked, key_ref[:, part], preferred_element_type=F32)
                    weights = jnp.exp2(scores).astype(BF16)
                    sums = jnp.dot(weights, value_ref[part, :], preferred_element_type=F32)
                    result = sums[:, :HD] / sums[:, HD:] * (1.0 / VALUE_SHIFT)
                    for n, h in enumerate(group):
                        lanes = slice(h * HD, (h + 1) * HD)
                        own = result[n * ROW_BLOCK : (n + 1) * ROW_BLOCK]
                        kept = 0.0 if label == 0 else out_ref[take, lanes].astype(F32)
                        out_ref[take, lanes] = jnp.where(owned, own, kept).astype(BF16)

            half = span // 2
            few = counts[label] * ROW_BLOCK <= half

            @pl.when(meets & few)
            def _(attend=attend):
                attend(half)

            @pl.when(meets & jnp.logical_not(few))
            def _(attend=attend):
                attend(span)

            if label == 0:

                @pl.when(jnp.logical_not(meets))
                def _(take=take):
                    out_ref[take, :] = jnp.zeros((ROW_BLOCK, width), BF16)

        copies.append(
            pltpu.make_async_copy(
                out_ref.at[take, :],
                out_hbm.at[take, pl.ds(head * width, width)],
                out_sem.at[block],
            )
        )
        copies[-1].start()
    for copy in copies:
        copy.wait()


def attend_head(group_count, meta, queries, tiles, sources, base, head, head_count):
    rows, width = queries.shape
    head_width = width // head_count
    group_rows = REQ_G * MAXT * ROW_BLOCK
    extra = [] if base is None else [base]
    return pl.pallas_call(
        functools.partial(attend_kernel, group_count, sources, head, len(extra)),
        out_shape=jax.ShapeDtypeStruct((rows, width), BF16),
        in_specs=[SMEM] + [VMEM] * (1 + len(tiles)) + [HBM] * len(extra),
        out_specs=HBM,
        scratch_shapes=[
            pltpu.VMEM((rows, head_width), BF16),
            pltpu.VMEM((HD, group_rows), BF16),
            pltpu.VMEM((group_rows, 2 * HD), BF16),
            pltpu.SemaphoreType.DMA((rows // ROW_BLOCK,)),
        ],
        input_output_aliases={2 + len(tiles): 0} if extra else {},
        compiler_params=pltpu.CompilerParams(vmem_limit_bytes=24 * MIB),
        cost_estimate=LIGHT,
        name="attend_head",
    )(meta, queries, *tiles, *extra)


def add_rounded(a, b):
    return (a.astype(F32) + b.astype(F32)).astype(BF16)


def after(value, *others):
    others = [v for v in others if v is not None]
    return lax.optimization_barrier((value, others))[0]


def scatter_sum(blocks, count, first_bit, earlier=None):
    blocks = dict(enumerate(blocks))
    bits = bits_of(len(blocks))
    for b in range(bits):
        pairs = xor_pairs(count, 1 << (b + first_bit))
        got, sent = {}, None
        for k in sorted((k for k in blocks if (k >> b) & 1), reverse=True):
            sent = blocks[k]
            if b == bits - 1 and earlier is not None:
                sent = after(sent, earlier)
            got[k ^ (1 << b)] = lax.ppermute(sent, "tp", pairs)
        if b == bits - 1:
            return [blocks[0], got[0]], sent
        blocks = {k: add_rounded(blocks[k], got[k]) for k in got}
    return [blocks[0]], blocks[0]


def gather_pieces(whole, count, ready):
    bits = bits_of(count)
    pieces = {0: whole[0]}
    for b in reversed(range(1, bits)):
        pairs = xor_pairs(count, 1 << b)
        for k in sorted(pieces):
            pieces[k | (1 << b)] = lax.ppermute(pieces[k], "tp", pairs)
    pairs = xor_pairs(count, 1)
    for k in sorted(pieces):
        if k:
            pieces[k | 1] = lax.ppermute(after(pieces[k], ready), "tp", pairs)
    pieces[0], pieces[1] = whole
    return [pieces[k] for k in range(count)]


def local(
    x_in,
    taps,
    ln_gain,
    ln_bias,
    w_up,
    b_up,
    w_down,
    b_down,
    kv_w_out,
    kv_w_taps,
    k_gain,
    q_gain,
    queries,
    tiles_per_request,
    owner,
    text_per_request,
):
    group_count = lax.axis_size("grp")
    tp_count = lax.axis_size("tp")
    position = jnp.stack([lax.axis_index("grp"), lax.axis_index("tp")]).astype(jnp.int32)
    where = jnp.concatenate([position, tiles_per_request, owner, text_per_request])
    tiles_local = x_in.shape[0]
    x_tiles = jnp.swapaxes(x_in, 2, 3)[:, 0]
    tap_tiles = jnp.swapaxes(taps, 2, 3)[:, 0]
    head_count = max(1, KVH // tp_count)
    dup = max(1, tp_count // KVH)
    dest_count = tp_count // dup
    place = meta_places(group_count)

    halves = HALVES if tiles_local % HALVES == 0 else 1
    tiles = tiles_local // halves
    whole = [x_tiles, lax.ppermute(x_tiles, "tp", xor_pairs(tp_count, 1))]

    tap_blocks = [(h, k) for h in range(head_count) for k in range(dest_count)]
    early = len(tap_blocks) * TAPS_EARLY // 8
    first_taps, w_up, w_down, tap_tiles = tap_projection(
        where, tap_tiles, kv_w_taps, tap_blocks[:early], head_count, dup, (w_up, w_down)
    )
    pieces = gather_pieces(whole, tp_count, first_taps)
    mlp_terms, begun = [], where
    for half in range(halves):
        mlp_blocks = encoder_mlp(
            begun, pieces, half * tiles, tiles, ln_gain, ln_bias, w_up, b_up, w_down
        )
        terms, sent = scatter_sum(mlp_blocks, tp_count, 0)
        mlp_terms.append(terms)
        begun = after(where, sent)
    (last_taps,) = tap_projection(
        begun, tap_tiles, kv_w_taps, tap_blocks[early:], head_count, dup, ()
    )
    taps_at = [(0, n) for n in range(early)]
    taps_at += [(1, n) for n in range(len(tap_blocks) - early)]
    kv_blocks = []
    inputs = (x_tiles, lane_rows(b_down), *(term for half in mlp_terms for term in half))
    for head in range(head_count):
        made = kv_projection(
            where,
            kv_w_out,
            (first_taps, last_taps),
            taps_at[head * dest_count : (head + 1) * dest_count],
            inputs,
            tuple(len(half) for half in mlp_terms),
            head,
            head_count,
            dup,
        )
        kv_blocks.append(made[:dest_count])
        if head == 0:
            inputs = (made[-1],)
    kv_terms, arrived = [], None
    for head in range(head_count):
        blocks = kv_blocks[head]
        for b in range(bits_of(dup)):
            pairs = xor_pairs(tp_count, 1 << b)
            blocks = [add_rounded(v, lax.ppermute(v, "tp", pairs)) for v in blocks]
        terms, sent = scatter_sum(blocks, tp_count, bits_of(dup), arrived)
        kv_terms.append(terms)
        if head == 0:
            query_rows, meta = prepare(
                after(where, sent), q_gain, queries, group_count, tiles_local
            )
        arrived = (terms[-1], meta)

    slots = slot_count_of(group_count)
    total_tiles = group_count * tiles_local
    most_other = total_tiles - REQ_G * MAXT - REQ_G * (group_count - 2)
    one_large = group_count == 4 and slots == 2 and most_other <= group_count
    send = place["send"]
    out = None

    def move(value, mask):
        return lax.ppermute(value, "grp", xor_pairs(group_count, mask))

    for head in range(head_count):
        terms = kv_terms[head]
        if one_large:
            star = place["star"]
            order = (0, 2, 3, 1)
            picks = tuple((send + d, star) for d in order)
            made = finish_tiles(meta, k_gain, terms, picks)
            tiles = tuple(move(tile, d) if d else tile for tile, d in zip(made, order))
            sources = tuple((d, group_count + d) for d in order)
        else:
            picks = tuple(
                tuple(send + s * group_count + d for s in range(slots)) for d in range(group_count)
            )
            made = finish_tiles(meta, k_gain, terms, picks)
            tiles = tuple(made[:1]) + tuple(move(made[d], d) for d in range(1, group_count))
            sources = tuple(
                tuple(s * group_count + d for s in range(slots)) for d in range(group_count)
            )
        out = attend_head(
            group_count, meta, query_rows, tiles, sources, out, head, head_count
        )
    return out


def solution(mesh):
    in_specs = (
        P(None, ("rep", "grp"), None, "tp"),
        P(None, ("rep", "grp"), None, "tp"),
        P(),
        P(),
        P(None, "tp"),
        P("tp"),
        P("tp", None),
        P("tp"),
        P("tp", None),
        P("tp", None),
        P(),
        P(),
        P(("rep", "grp"), "tp"),
        P("rep"),
        P("rep"),
        P("rep"),
    )
    out_specs = P(("rep", "grp"), "tp")
    return jax.shard_map(local, mesh=mesh, in_specs=in_specs, out_specs=out_specs, check_vma=False)
```

```python
import functools
import math

import jax
import jax.numpy as jnp
from jax import lax
from jax.experimental import pallas as pl
from jax.experimental.pallas import tpu as pltpu
from jax.sharding import PartitionSpec as P

KVH = 8
HD = 128
MAXT = 4
REQ_G = 2
LANES = 128
ROW_BLOCK = 128
HIDDEN_BLOCK = 256
HEAD_GROUP = 8
HALVES = 1
TAPS_EARLY = 3
VALUE_SHIFT = 2.0**-24
epsilon = 1e-05

F32 = jnp.float32
BF16 = jnp.bfloat16
VMEM = pl.BlockSpec(memory_space=pltpu.VMEM)
HBM = pl.BlockSpec(memory_space=pltpu.HBM)
SMEM = pl.BlockSpec(memory_space=pltpu.SMEM)
MIB = 1024 * 1024
LIGHT = pl.CostEstimate(flops=1024, bytes_accessed=1024, transcendentals=0)


def bits_of(count):
    bits = count.bit_length() - 1
    assert 1 << bits == count
    return bits


def xor_order(blocks, index):
    blocks = list(blocks)
    for b in range(bits_of(len(blocks))):
        swap = ((index >> b) & 1) == 1
        for k in range(len(blocks)):
            if not (k >> b) & 1:
                low, high = blocks[k], blocks[k | (1 << b)]
                blocks[k] = lax.select(swap, high, low)
                blocks[k | (1 << b)] = lax.select(swap, low, high)
    return blocks


def xor_pairs(count, mask):
    return [(i, i ^ mask) for i in range(count)]


def lane_rows(vector):
    return jnp.pad(vector, (0, -vector.shape[0] % LANES)).reshape(-1, LANES)


def one_row(ref, width):
    rows = [ref[n : n + 1, :] for n in range(ref.shape[0])]
    return (rows[0] if len(rows) == 1 else jnp.concatenate(rows, axis=1))[:, :width]


def column_step(width):
    return HIDDEN_BLOCK if width % HIDDEN_BLOCK == 0 else width


def tail_plan(rows, width):
    whole = width // LANES * LANES
    tail = width - whole
    packed = tail > 0 and whole > 0 and whole % tail == 0 and rows * tail % whole == 0
    extra = rows * tail // whole if packed else 0
    packed = packed and extra % 16 == 0 and ROW_BLOCK % extra == 0
    return whole, tail, extra if packed else 0


def sent_shape(rows, width):
    whole, _, extra = tail_plan(rows, width)
    return (rows + extra, whole) if extra else (rows, width)


def layout_kernel(group_count, tiles_local, where_ref, meta_ref):
    group = where_ref[0]
    requests = (where_ref.shape[0] - 2) // 3
    tiles_of, owner_of, text_of = ([where_ref[2 + n * requests + r] for r in range(requests)] for n in range(3))
    zero = jnp.int32(0)
    firsts, counts, offsets, texts_first, texts_both = [], [], [], [], []
    offset = zero
    for p in range(group_count):
        first, count, text_first, text_both, seen = zero, zero, zero, zero, zero
        for r in range(requests):
            mine = owner_of[r] == p
            tiles = jnp.where(mine, tiles_of[r], 0)
            text = jnp.where(mine, text_of[r], 0)
            first = first + jnp.where(seen == 0, tiles, 0)
            text_first = text_first + jnp.where(seen == 0, text, 0)
            count = count + tiles
            text_both = text_both + text
            seen = seen + jnp.where(mine, 1, 0)
        firsts.append(first)
        counts.append(count)
        offsets.append(offset)
        texts_first.append(text_first)
        texts_both.append(text_both)
        offset = offset + count

    def pick(values, index):
        out = values[0]
        for p in range(1, group_count):
            out = jnp.where(index == p, values[p], out)
        return out

    slots = slot_count_of(group_count)
    star, most = zero, counts[0]
    for p in range(1, group_count):
        larger = counts[p] > most
        star = jnp.where(larger, p, star)
        most = jnp.where(larger, counts[p], most)

    def local_tile(offset, slot):
        lane = lax.rem(group - offset + group_count * REQ_G * MAXT * group_count, group_count)
        tile = lax.div(offset + slot * group_count + lane, group_count)
        return jnp.minimum(tile, tiles_local - 1)

    my_first, my_count = pick(firsts, group), pick(counts, group)
    my_offset = pick(offsets, group)
    place = meta_places(group_count)
    meta_ref[place["first"]] = my_first
    meta_ref[place["second"]] = my_count - my_first
    meta_ref[place["text_first"]] = pick(texts_first, group)
    meta_ref[place["text_both"]] = pick(texts_both, group)
    meta_ref[place["star"]] = local_tile(pick(offsets, star), 1)
    for slot in range(slots):
        for d in range(group_count):
            other = group ^ d
            meta_ref[place["send"] + slot * group_count + d] = local_tile(pick(offsets, other), slot)
            lane = lax.rem(other - my_offset + group_count * REQ_G * MAXT * group_count, group_count)
            position = slot * group_count + lane
            goes = jnp.where(
                position < my_first,
                position,
                jnp.where(position < my_count, MAXT + position - my_first, -1),
            )
            meta_ref[place["goes"] + slot * group_count + d] = goes


def slot_count_of(group_count):
    return (REQ_G * MAXT + group_count - 1) // group_count


def meta_places(group_count):
    table = slot_count_of(group_count) * group_count
    return {
        "first": 0,
        "second": 1,
        "text_first": 2,
        "text_both": 3,
        "star": 4,
        "send": 8,
        "goes": 8 + table,
        "size": 8 + 2 * table,
    }


def mlp_kernel(piece_count, bases, tiles, where_ref, *refs):
    pieces = refs[:piece_count]
    gain_ref, bias_ref, up_bias_ref, up_ref, down_ref = refs[piece_count : piece_count + 5]
    outs = refs[piece_count + 5 : 2 * piece_count + 5]
    cat_ref, normed_ref, hidden_ref, total_ref = refs[2 * piece_count + 5 :]
    index = where_ref[1]
    _, width, tile_rows = pieces[0].shape
    rows = tiles * tile_rows
    channels, hidden_width = up_ref.shape
    up_step = column_step(hidden_width)
    down_step = column_step(channels)

    gain, bias = one_row(gain_ref, channels), one_row(bias_ref, channels)
    up_bias = one_row(up_bias_ref, hidden_width)
    for tile in range(tiles):
        for k, piece in enumerate(pieces):
            start = pl.multiple_of((index ^ k) * width, math.gcd(width, LANES))
            cat_ref[pl.ds(start, width), :] = piece[bases[k] + tile]
        values = cat_ref[...].T.astype(F32)
        average = jnp.sum(values, axis=1, keepdims=True) * (1.0 / channels)
        centered = values - average
        variance = jnp.sum(centered * centered, axis=1, keepdims=True) * (1.0 / channels)
        normed = centered * lax.rsqrt(variance + epsilon)
        normed = normed * gain + bias
        normed_ref[tile * tile_rows : (tile + 1) * tile_rows, :] = normed.astype(BF16)
    for n in range(hidden_width // up_step):
        take = slice(n * up_step, (n + 1) * up_step)
        value = jnp.dot(normed_ref[...], up_ref[:, take], preferred_element_type=F32)
        value = value + up_bias[:, take]
        value = 0.5 * value * (1.0 + lax.erf(value * (1.0 / math.sqrt(2.0))))
        hidden_ref[:, take] = value.astype(BF16)
    for n in range(channels // down_step):
        take = slice(n * down_step, (n + 1) * down_step)
        total_ref[:, take] = jnp.dot(
            hidden_ref[...], down_ref[:, take], preferred_element_type=F32
        )
    whole, tail, extra = tail_plan(rows, width)
    step = extra or ROW_BLOCK
    for part in range(rows // step):
        take = pl.ds(part * step, step)
        blocks = [total_ref[take, j * width : (j + 1) * width] for j in range(piece_count)]
        for out, block in zip(outs, xor_order(blocks, index)):
            block = block.astype(BF16)
            if extra:
                out[take, :] = block[:, :whole]
                out[rows : rows + extra, part * tail : (part + 1) * tail] = block[:, whole:]
            else:
                out[take, :] = block


def encoder_mlp(where, pieces, bases, tiles, ln_gain, ln_bias, w_up, b_up, w_down):
    _, width, tile_rows = pieces[0].shape
    rows = tiles * tile_rows
    count = len(pieces)
    channels, hidden_width = w_up.shape
    shape = sent_shape(rows, width)
    return pl.pallas_call(
        functools.partial(mlp_kernel, count, bases, tiles),
        out_shape=[jax.ShapeDtypeStruct(shape, BF16)] * count,
        in_specs=[SMEM] + [VMEM] * (count + 5),
        out_specs=[VMEM] * count,
        scratch_shapes=[
            pltpu.VMEM((channels, tile_rows), BF16),
            pltpu.VMEM((rows, channels), BF16),
            pltpu.VMEM((rows, hidden_width), BF16),
            pltpu.VMEM((rows, channels), F32),
        ],
        compiler_params=pltpu.CompilerParams(vmem_limit_bytes=44 * MIB),
        cost_estimate=LIGHT,
        name="encoder_mlp",
    )(
        where,
        *pieces,
        lane_rows(ln_gain),
        lane_rows(ln_bias),
        lane_rows(b_up),
        w_up,
        w_down,
    )


def prepare_kernel(
    group_count,
    tiles_local,
    where_ref,
    gain_ref,
    query_ref,
    normed_ref,
    meta_ref,
):
    @pl.when(pl.program_id(0) == 0)
    def _():
        layout_kernel(group_count, tiles_local, where_ref, meta_ref)

    gain = gain_ref[...] * (math.log2(math.e) / math.sqrt(HD))
    for col in range(0, query_ref.shape[1], HD):
        values = query_ref[:, col : col + HD].astype(F32)
        square = jnp.sum(values * values, axis=1, keepdims=True) * (1.0 / HD)
        normed_ref[:, col : col + HD] = (values * lax.rsqrt(square + epsilon) * gain).astype(BF16)


def prepare(where, q_gain, queries, group_count, tiles_local):
    text_rows, width = queries.shape
    step = ROW_BLOCK
    return pl.pallas_call(
        functools.partial(prepare_kernel, group_count, tiles_local),
        out_shape=[
            jax.ShapeDtypeStruct((text_rows, width), BF16),
            jax.ShapeDtypeStruct((meta_places(group_count)["size"],), jnp.int32),
        ],
        grid=(text_rows // step,),
        in_specs=[
            SMEM,
            pl.BlockSpec((1, HD), lambda n: (0, 0)),
            pl.BlockSpec((step, width), lambda n: (n, 0)),
        ],
        out_specs=[pl.BlockSpec((step, width), lambda n: (n, 0)), SMEM],
        compiler_params=pltpu.CompilerParams(vmem_limit_bytes=16 * MIB),
        cost_estimate=LIGHT,
        name="prepare",
    )(where, lane_rows(q_gain), queries)


def tap_kernel(blocks, head_count, dup, staged, where_ref, tap_hbm, weight_hbm, *refs):
    sources, out_ref = refs[:staged], refs[staged]
    targets = refs[staged + 1 : 2 * staged + 1]
    if staged:
        tap_ref, weight_ref, tap_sem, weight_sem, staged_sem = refs[2 * staged + 1 :]
    else:
        tap_ref, (weight_ref, weight_sem) = tap_hbm, refs[1:]
    tiles, _, tile_rows = tap_ref.shape
    block = weight_ref.shape[2]
    mine = lax.div(where_ref[1], jnp.int32(dup))
    taps = [
        pltpu.make_async_copy(tap_hbm.at[n], tap_ref.at[n], tap_sem.at[n])
        for n in range(tiles if staged else 0)
    ]
    weights = []
    for n, (head, k) in enumerate(blocks):
        column = pl.multiple_of(((mine ^ k) * head_count + head) * block, block)
        weights.append(
            pltpu.make_async_copy(
                weight_hbm.at[:, pl.ds(column, block)], weight_ref.at[n], weight_sem.at[n]
            )
        )
    others = [
        pltpu.make_async_copy(source, target, staged_sem.at[n])
        for n, (source, target) in enumerate(zip(sources, targets))
    ]
    for copy in weights[:1] + taps + weights[1:] + others:
        copy.start()
    for n in range(len(blocks)):
        weights[n].wait()
        for tile in range(tiles):
            if n == 0 and staged:
                taps[tile].wait()
            value = lax.dot_general(
                tap_ref[tile],
                weight_ref[n],
                (((0,), (0,)), ((), ())),
                preferred_element_type=F32,
            )
            out_ref[n, tile * tile_rows : (tile + 1) * tile_rows, :] = value.astype(BF16)
    for copy in others:
        copy.wait()


def tap_projection(where, tap_tiles, weights, blocks, head_count, dup, staged):
    tiles, depth, tile_rows = tap_tiles.shape
    block = 2 * HD
    return pl.pallas_call(
        functools.partial(tap_kernel, blocks, head_count, dup, len(staged)),
        out_shape=[jax.ShapeDtypeStruct((len(blocks), tiles * tile_rows, block), BF16)]
        + [jax.ShapeDtypeStruct(w.shape, w.dtype) for w in staged]
        + ([jax.ShapeDtypeStruct(tap_tiles.shape, BF16)] if staged else []),
        in_specs=[SMEM, HBM if staged else VMEM, HBM] + [HBM] * len(staged),
        out_specs=[VMEM] * (1 + len(staged) + bool(staged)),
        scratch_shapes=[pltpu.VMEM((len(blocks), depth, block), BF16)]
        + ([pltpu.SemaphoreType.DMA((tiles,))] if staged else [])
        + [pltpu.SemaphoreType.DMA((len(blocks),))]
        + ([pltpu.SemaphoreType.DMA((len(staged),))] if staged else []),
        compiler_params=pltpu.CompilerParams(vmem_limit_bytes=(42 if staged else 50) * MIB),
        cost_estimate=LIGHT,
        name="tap_projection",
    )(where, tap_tiles, weights, *staged)


def encode(x_ref, bias_ref, term_counts, terms, encoded_ref):
    tiles, width, tile_rows = x_ref.shape
    half_tiles = tiles // len(term_counts)
    whole, tail, extra = tail_plan(half_tiles * tile_rows, width)
    bias = one_row(bias_ref, width)
    for tile in range(tiles):
        half, row = tile // half_tiles, tile % half_tiles * tile_rows
        mine = terms[sum(term_counts[:half]) : sum(term_counts[: half + 1])]

        def summed(part, lanes):
            out = mine[0][part, lanes].astype(F32)
            for term in mine[1:]:
                out = out + term[part, lanes].astype(F32)
            return out

        total = summed(pl.ds(row, tile_rows), slice(None))
        if extra:
            chunks = range(row // extra, (row + tile_rows) // extra)
            rest = [
                summed(pl.ds(half_tiles * tile_rows, extra), slice(c * tail, (c + 1) * tail))
                for c in chunks
            ]
            rest = rest[0] if len(rest) == 1 else jnp.concatenate(rest, axis=0)
            total = jnp.concatenate([total, rest], axis=1)
        total = total + x_ref[tile].T.astype(F32) + bias
        encoded_ref[tile * tile_rows : (tile + 1) * tile_rows, :] = total.astype(BF16)


def kv_kernel(head, head_count, dest_count, dup, taps_at, term_counts, where_ref, *refs):
    weight_ref, refs = refs[0], refs[1:]
    part_count = 1 + max(part for part, _ in taps_at)
    tap_refs, refs = refs[:part_count], refs[part_count:]
    outs = refs[-dest_count - 1 :] if head == 0 else refs[-dest_count:]
    if head == 0:
        encoded_ref = outs[-1]
        encode(refs[0], refs[1], term_counts, refs[2 : 2 + sum(term_counts)], encoded_ref)
    else:
        encoded_ref = refs[0]
    block = 2 * HD
    mine = lax.div(where_ref[1], jnp.int32(dup))
    for k in range(dest_count):
        column = ((mine ^ k) * head_count + head) * block
        weights = weight_ref[:, pl.ds(pl.multiple_of(column, block), block)]
        value = jnp.dot(encoded_ref[...], weights, preferred_element_type=F32)
        part, n = taps_at[k]
        value = value + tap_refs[part][n].astype(F32)
        outs[k][...] = value.astype(BF16)


def kv_projection(where, weights, tap_parts, taps_at, inputs, term_counts, head, head_count, dup):
    tap_parts = tap_parts[: 1 + max(part for part, _ in taps_at)]
    rows, dest_count, block = tap_parts[0].shape[1], len(taps_at), 2 * HD
    outs = [jax.ShapeDtypeStruct((rows, block), BF16)] * dest_count
    if head == 0:
        outs.append(jax.ShapeDtypeStruct((rows, weights.shape[0]), BF16))
    return pl.pallas_call(
        functools.partial(
            kv_kernel, head, head_count, dest_count, dup, tuple(taps_at), term_counts
        ),
        out_shape=outs,
        in_specs=[SMEM] + [VMEM] * (1 + len(tap_parts) + len(inputs)),
        out_specs=[VMEM] * len(outs),
        compiler_params=pltpu.CompilerParams(vmem_limit_bytes=24 * MIB),
        cost_estimate=LIGHT,
        name="kv_projection",
    )(where, weights, *tap_parts, *inputs)


def finish_kernel(term_count, picks, meta_ref, gain_ref, *refs):
    terms = refs[:term_count]
    outs = refs[term_count : term_count + len(picks)]
    done_ref = refs[-1]
    rows = terms[0].shape[0]
    for row in range(0, rows, ROW_BLOCK):
        take = pl.ds(row, ROW_BLOCK)
        total = terms[0][take, :].astype(F32)
        for term in terms[1:]:
            total = total + term[take, :].astype(F32)
        keys = total[:, :HD]
        square = jnp.sum(keys * keys, axis=1, keepdims=True) * (1.0 / HD)
        keys = keys * lax.rsqrt(square + epsilon) * gain_ref[...]
        done_ref[take, :HD] = keys.astype(BF16).T
        done_ref[take, HD:] = (total[:, HD:] * VALUE_SHIFT).astype(BF16)
    for out, places in zip(outs, picks):
        for n, place in enumerate(places):
            start = pl.multiple_of(meta_ref[place] * ROW_BLOCK, ROW_BLOCK)
            out[n] = done_ref[pl.ds(start, ROW_BLOCK), :]


def finish_tiles(meta, k_gain, terms, picks):
    rows, block = terms[0].shape
    return pl.pallas_call(
        functools.partial(finish_kernel, len(terms), picks),
        out_shape=[jax.ShapeDtypeStruct((len(p), ROW_BLOCK, block), BF16) for p in picks],
        in_specs=[SMEM] + [VMEM] * (1 + len(terms)),
        out_specs=[VMEM] * len(picks),
        scratch_shapes=[pltpu.VMEM((rows, block), BF16)],
        compiler_params=pltpu.CompilerParams(vmem_limit_bytes=8 * MIB),
        cost_estimate=LIGHT,
        name="finish_tiles",
    )(meta, lane_rows(k_gain), *terms)


def attend_kernel(group_count, sources, head, has_base, meta_ref, query_ref, *refs):
    tile_refs = refs[: len(sources)]
    out_hbm, out_ref, key_ref, value_ref, out_sem = refs[len(sources) + has_base :]
    place = meta_places(group_count)
    counts = (meta_ref[place["first"]], meta_ref[place["second"]])
    text_first, text_both = meta_ref[place["text_first"]], meta_ref[place["text_both"]]
    span = MAXT * ROW_BLOCK
    text_rows, width = out_ref.shape
    heads = width // HD
    for label in range(REQ_G):
        for tile in range(1, MAXT):

            @pl.when(counts[label] <= tile)
            def _(tile=label * MAXT + tile):
                take = slice(tile * ROW_BLOCK, (tile + 1) * ROW_BLOCK)
                key_ref[:, take] = jnp.zeros((HD, ROW_BLOCK), BF16)
                value_ref[take, :] = jnp.zeros((ROW_BLOCK, 2 * HD), BF16)

    for tile_ref, places in zip(tile_refs, sources):
        for n, slot in enumerate(places):
            if slot is None:
                continue
            goes = meta_ref[place["goes"] + slot]

            @pl.when(goes >= 0)
            def _(tile_ref=tile_ref, n=n, goes=goes):
                take = pl.ds(pl.multiple_of(goes * ROW_BLOCK, ROW_BLOCK), ROW_BLOCK)
                key_ref[:, take] = tile_ref[n, :, :HD]
                value_ref[take, :HD] = tile_ref[n, :, HD:]
                value_ref[take, HD:] = jnp.ones((ROW_BLOCK, HD), BF16)

    copies = []
    for block in range(text_rows // ROW_BLOCK):
        start = block * ROW_BLOCK
        take = pl.ds(start, ROW_BLOCK)
        for label, (low, high) in enumerate(((0, text_first), (text_first, text_both))):
            meets = jnp.maximum(low, start) < jnp.minimum(high, start + ROW_BLOCK)

            def attend(key_rows, label=label, start=start, take=take, low=low, high=high):
                part = pl.ds(label * span, key_rows)
                slots = start + lax.broadcasted_iota(jnp.int32, (ROW_BLOCK, HD), 0)
                owned = (slots >= low) & (slots < high)
                for first in range(0, heads, HEAD_GROUP):
                    group = range(first, min(first + HEAD_GROUP, heads))
                    column = head * width
                    stacked = jnp.concatenate(
                        [
                            query_ref[take, column + h * HD : column + (h + 1) * HD]
                            for h in group
                        ],
                        axis=0,
                    )
                    scores = jnp.dot(stacked, key_ref[:, part], preferred_element_type=F32)
                    weights = jnp.exp2(scores).astype(BF16)
                    sums = jnp.dot(weights, value_ref[part, :], preferred_element_type=F32)
                    result = sums[:, :HD] / sums[:, HD:] * (1.0 / VALUE_SHIFT)
                    for n, h in enumerate(group):
                        lanes = slice(h * HD, (h + 1) * HD)
                        own = result[n * ROW_BLOCK : (n + 1) * ROW_BLOCK]
                        kept = 0.0 if label == 0 else out_ref[take, lanes].astype(F32)
                        out_ref[take, lanes] = jnp.where(owned, own, kept).astype(BF16)

            half = span // 2
            few = counts[label] * ROW_BLOCK <= half

            @pl.when(meets & few)
            def _(attend=attend):
                attend(half)

            @pl.when(meets & jnp.logical_not(few))
            def _(attend=attend):
                attend(span)

            if label == 0:

                @pl.when(jnp.logical_not(meets))
                def _(take=take):
                    out_ref[take, :] = jnp.zeros((ROW_BLOCK, width), BF16)

        copies.append(
            pltpu.make_async_copy(
                out_ref.at[take, :],
                out_hbm.at[take, pl.ds(head * width, width)],
                out_sem.at[block],
            )
        )
        copies[-1].start()
    for copy in copies:
        copy.wait()


def attend_head(group_count, meta, queries, tiles, sources, base, head, head_count):
    rows, width = queries.shape
    head_width = width // head_count
    group_rows = REQ_G * MAXT * ROW_BLOCK
    extra = [] if base is None else [base]
    return pl.pallas_call(
        functools.partial(attend_kernel, group_count, sources, head, len(extra)),
        out_shape=jax.ShapeDtypeStruct((rows, width), BF16),
        in_specs=[SMEM] + [VMEM] * (1 + len(tiles)) + [HBM] * len(extra),
        out_specs=HBM,
        scratch_shapes=[
            pltpu.VMEM((rows, head_width), BF16),
            pltpu.VMEM((HD, group_rows), BF16),
            pltpu.VMEM((group_rows, 2 * HD), BF16),
            pltpu.SemaphoreType.DMA((rows // ROW_BLOCK,)),
        ],
        input_output_aliases={2 + len(tiles): 0} if extra else {},
        compiler_params=pltpu.CompilerParams(vmem_limit_bytes=24 * MIB),
        cost_estimate=LIGHT,
        name="attend_head",
    )(meta, queries, *tiles, *extra)


def add_rounded(a, b):
    return (a.astype(F32) + b.astype(F32)).astype(BF16)


def after(value, *others):
    others = [v for v in others if v is not None]
    return lax.optimization_barrier((value, others))[0]


def scatter_sum(blocks, count, first_bit, earlier=None):
    blocks = dict(enumerate(blocks))
    bits = bits_of(len(blocks))
    for b in range(bits):
        pairs = xor_pairs(count, 1 << (b + first_bit))
        got, sent = {}, None
        for k in sorted((k for k in blocks if (k >> b) & 1), reverse=True):
            sent = blocks[k]
            if b == bits - 1 and earlier is not None:
                sent = after(sent, earlier)
            got[k ^ (1 << b)] = lax.ppermute(sent, "tp", pairs)
        if b == bits - 1:
            return [blocks[0], got[0]], sent
        blocks = {k: add_rounded(blocks[k], got[k]) for k in got}
    return [blocks[0]], blocks[0]


def gather_half(whole, own, first, count, ready):
    bits = bits_of(count)
    pieces = {0: own}
    for b in reversed(range(1, bits)):
        pairs = xor_pairs(count, 1 << b)
        for k in sorted(pieces):
            pieces[k | (1 << b)] = lax.ppermute(pieces[k], "tp", pairs)
    pairs = xor_pairs(count, 1)
    for k in sorted(pieces):
        if k:
            pieces[k | 1] = lax.ppermute(after(pieces[k], ready), "tp", pairs)
    pieces[0], pieces[1] = whole
    bases = tuple(first if k < 2 else 0 for k in range(count))
    return [pieces[k] for k in range(count)], bases


def local(
    x_in,
    taps,
    ln_gain,
    ln_bias,
    w_up,
    b_up,
    w_down,
    b_down,
    kv_w_out,
    kv_w_taps,
    k_gain,
    q_gain,
    queries,
    tiles_per_request,
    owner,
    text_per_request,
):
    group_count = lax.axis_size("grp")
    tp_count = lax.axis_size("tp")
    position = jnp.stack([lax.axis_index("grp"), lax.axis_index("tp")]).astype(jnp.int32)
    where = jnp.concatenate([position, tiles_per_request, owner, text_per_request])
    tiles_local = x_in.shape[0]
    x_tiles = jnp.swapaxes(x_in, 2, 3)[:, 0]
    tap_tiles = jnp.swapaxes(taps, 2, 3)[:, 0]
    head_count = max(1, KVH // tp_count)
    dup = max(1, tp_count // KVH)
    dest_count = tp_count // dup
    place = meta_places(group_count)

    halves = HALVES if tiles_local % HALVES == 0 else 1
    tiles = tiles_local // halves
    own_halves = [x_tiles[:tiles]] + [
        after(x_tiles, where)[h * tiles : (h + 1) * tiles] for h in range(1, halves)
    ]
    whole = [x_tiles, lax.ppermute(x_tiles, "tp", xor_pairs(tp_count, 1))]

    tap_blocks = [(h, k) for h in range(head_count) for k in range(dest_count)]
    early = len(tap_blocks) * TAPS_EARLY // 8
    first_taps, w_up, w_down, tap_tiles = tap_projection(
        where, tap_tiles, kv_w_taps, tap_blocks[:early], head_count, dup, (w_up, w_down)
    )
    mlp_terms = []
    ready, begun = first_taps, where
    for half in range(halves):
        pieces, bases = gather_half(whole, own_halves[half], half * tiles, tp_count, ready)
        mlp_blocks = encoder_mlp(
            begun, pieces, bases, tiles, ln_gain, ln_bias, w_up, b_up, w_down
        )
        terms, sent = scatter_sum(mlp_blocks, tp_count, 0)
        mlp_terms.append(terms)
        ready, begun = mlp_blocks[0], after(where, sent)
    (last_taps,) = tap_projection(
        begun, tap_tiles, kv_w_taps, tap_blocks[early:], head_count, dup, ()
    )
    taps_at = [(0, n) for n in range(early)]
    taps_at += [(1, n) for n in range(len(tap_blocks) - early)]
    kv_blocks = []
    inputs = (x_tiles, lane_rows(b_down), *(term for half in mlp_terms for term in half))
    for head in range(head_count):
        made = kv_projection(
            where,
            kv_w_out,
            (first_taps, last_taps),
            taps_at[head * dest_count : (head + 1) * dest_count],
            inputs,
            tuple(len(half) for half in mlp_terms),
            head,
            head_count,
            dup,
        )
        kv_blocks.append(made[:dest_count])
        if head == 0:
            inputs = (made[-1],)
    kv_terms, arrived = [], None
    for head in range(head_count):
        blocks = kv_blocks[head]
        for b in range(bits_of(dup)):
            pairs = xor_pairs(tp_count, 1 << b)
            blocks = [add_rounded(v, lax.ppermute(v, "tp", pairs)) for v in blocks]
        terms, sent = scatter_sum(blocks, tp_count, bits_of(dup), arrived)
        kv_terms.append(terms)
        if head == 0:
            query_rows, meta = prepare(
                after(where, sent), q_gain, queries, group_count, tiles_local
            )
        arrived = (terms[-1], meta)

    slots = slot_count_of(group_count)
    total_tiles = group_count * tiles_local
    most_other = total_tiles - REQ_G * MAXT - REQ_G * (group_count - 2)
    one_large = group_count == 4 and slots == 2 and most_other <= group_count
    send = place["send"]
    out = None

    def move(value, mask):
        return lax.ppermute(value, "grp", xor_pairs(group_count, mask))

    for head in range(head_count):
        terms = kv_terms[head]
        if one_large:
            star = place["star"]
            direct = head == head_count - 1
            picks = ((send, star), (send + 2, star))
            picks += ((send + 3, star) if direct else (send + 3,), (send + 1, star))
            own, middle, far, near = finish_tiles(meta, k_gain, terms, picks)
            middle_got, far_got, near_got = move(middle, 2), move(far, 3), move(near, 1)
            tiles = (own, middle_got, far_got, near_got)
            sources = ((0, 4), (2, 6), (3, 7) if direct else (3,), (1, 5))
            if not direct:
                tiles += (move(after(middle_got[1:], far_got), 1),)
                sources += ((7,),)
        else:
            picks = tuple(
                tuple(send + s * group_count + d for s in range(slots)) for d in range(group_count)
            )
            made = finish_tiles(meta, k_gain, terms, picks)
            tiles = tuple(made[:1]) + tuple(move(made[d], d) for d in range(1, group_count))
            sources = tuple(
                tuple(s * group_count + d for s in range(slots)) for d in range(group_count)
            )
        out = attend_head(
            group_count, meta, query_rows, tiles, sources, out, head, head_count
        )
    return out


def solution(mesh):
    in_specs = (
        P(None, ("rep", "grp"), None, "tp"),
        P(None, ("rep", "grp"), None, "tp"),
        P(),
        P(),
        P(None, "tp"),
        P("tp"),
        P("tp", None),
        P("tp"),
        P("tp", None),
        P("tp", None),
        P(),
        P(),
        P(("rep", "grp"), "tp"),
        P("rep"),
        P("rep"),
        P("rep"),
    )
    out_specs = P(("rep", "grp"), "tp")
    return jax.shard_map(local, mesh=mesh, in_specs=in_specs, out_specs=out_specs, check_vma=False)
```

```python
import functools
import math

import jax
import jax.numpy as jnp
from jax import lax
from jax.experimental import pallas as pl
from jax.experimental.pallas import tpu as pltpu
from jax.sharding import PartitionSpec as P

KVH = 8
HD = 128
MAXT = 4
REQ_G = 2
LANES = 128
ROW_BLOCK = 128
HIDDEN_BLOCK = 256
HEAD_GROUP = 8
HALVES = 2
TAPS_EARLY = 4
VALUE_SHIFT = 2.0**-24
epsilon = 1e-05

F32 = jnp.float32
BF16 = jnp.bfloat16
VMEM = pl.BlockSpec(memory_space=pltpu.VMEM)
HBM = pl.BlockSpec(memory_space=pltpu.HBM)
SMEM = pl.BlockSpec(memory_space=pltpu.SMEM)
MIB = 1024 * 1024
LIGHT = pl.CostEstimate(flops=1024, bytes_accessed=1024, transcendentals=0)


def bits_of(count):
    bits = count.bit_length() - 1
    assert 1 << bits == count
    return bits


def xor_order(blocks, index):
    blocks = list(blocks)
    for b in range(bits_of(len(blocks))):
        swap = ((index >> b) & 1) == 1
        for k in range(len(blocks)):
            if not (k >> b) & 1:
                low, high = blocks[k], blocks[k | (1 << b)]
                blocks[k] = lax.select(swap, high, low)
                blocks[k | (1 << b)] = lax.select(swap, low, high)
    return blocks


def xor_pairs(count, mask):
    return [(i, i ^ mask) for i in range(count)]


def lane_rows(vector):
    return jnp.pad(vector, (0, -vector.shape[0] % LANES)).reshape(-1, LANES)


def one_row(ref, width):
    rows = [ref[n : n + 1, :] for n in range(ref.shape[0])]
    return (rows[0] if len(rows) == 1 else jnp.concatenate(rows, axis=1))[:, :width]


def column_step(width):
    return HIDDEN_BLOCK if width % HIDDEN_BLOCK == 0 else width


def tail_plan(rows, width):
    whole = width // LANES * LANES
    tail = width - whole
    packed = tail > 0 and whole > 0 and whole % tail == 0 and rows * tail % whole == 0
    extra = rows * tail // whole if packed else 0
    packed = packed and extra % 16 == 0 and ROW_BLOCK % extra == 0
    return whole, tail, extra if packed else 0


def sent_shape(rows, width):
    whole, _, extra = tail_plan(rows, width)
    return (rows + extra, whole) if extra else (rows, width)


def layout_kernel(group_count, tiles_local, where_ref, meta_ref):
    group = where_ref[0]
    requests = (where_ref.shape[0] - 2) // 3
    tiles_of, owner_of, text_of = ([where_ref[2 + n * requests + r] for r in range(requests)] for n in range(3))
    zero = jnp.int32(0)
    firsts, counts, offsets, texts_first, texts_both = [], [], [], [], []
    offset = zero
    for p in range(group_count):
        first, count, text_first, text_both, seen = zero, zero, zero, zero, zero
        for r in range(requests):
            mine = owner_of[r] == p
            tiles = jnp.where(mine, tiles_of[r], 0)
            text = jnp.where(mine, text_of[r], 0)
            first = first + jnp.where(seen == 0, tiles, 0)
            text_first = text_first + jnp.where(seen == 0, text, 0)
            count = count + tiles
            text_both = text_both + text
            seen = seen + jnp.where(mine, 1, 0)
        firsts.append(first)
        counts.append(count)
        offsets.append(offset)
        texts_first.append(text_first)
        texts_both.append(text_both)
        offset = offset + count

    def pick(values, index):
        out = values[0]
        for p in range(1, group_count):
            out = jnp.where(index == p, values[p], out)
        return out

    slots = slot_count_of(group_count)
    star, most = zero, counts[0]
    for p in range(1, group_count):
        larger = counts[p] > most
        star = jnp.where(larger, p, star)
        most = jnp.where(larger, counts[p], most)

    def local_tile(offset, slot):
        lane = lax.rem(group - offset + group_count * REQ_G * MAXT * group_count, group_count)
        tile = lax.div(offset + slot * group_count + lane, group_count)
        return jnp.minimum(tile, tiles_local - 1)

    my_first, my_count = pick(firsts, group), pick(counts, group)
    my_offset = pick(offsets, group)
    place = meta_places(group_count)
    meta_ref[place["first"]] = my_first
    meta_ref[place["second"]] = my_count - my_first
    meta_ref[place["text_first"]] = pick(texts_first, group)
    meta_ref[place["text_both"]] = pick(texts_both, group)
    meta_ref[place["star"]] = local_tile(pick(offsets, star), 1)
    for slot in range(slots):
        for d in range(group_count):
            other = group ^ d
            meta_ref[place["send"] + slot * group_count + d] = local_tile(pick(offsets, other), slot)
            lane = lax.rem(other - my_offset + group_count * REQ_G * MAXT * group_count, group_count)
            position = slot * group_count + lane
            goes = jnp.where(
                position < my_first,
                position,
                jnp.where(position < my_count, MAXT + position - my_first, -1),
            )
            meta_ref[place["goes"] + slot * group_count + d] = goes


def slot_count_of(group_count):
    return (REQ_G * MAXT + group_count - 1) // group_count


def meta_places(group_count):
    table = slot_count_of(group_count) * group_count
    return {
        "first": 0,
        "second": 1,
        "text_first": 2,
        "text_both": 3,
        "star": 4,
        "send": 8,
        "goes": 8 + table,
        "size": 8 + 2 * table,
    }


def mlp_kernel(piece_count, base, tiles, where_ref, *refs):
    pieces = refs[:piece_count]
    gain_ref, bias_ref, up_bias_ref, up_ref, down_ref = refs[piece_count : piece_count + 5]
    outs = refs[piece_count + 5 : 2 * piece_count + 5]
    cat_ref, normed_ref, hidden_ref, total_ref = refs[2 * piece_count + 5 :]
    index = where_ref[1]
    _, width, tile_rows = pieces[0].shape
    rows = tiles * tile_rows
    channels, hidden_width = up_ref.shape
    up_step = column_step(hidden_width)
    down_step = column_step(channels)

    gain, bias = one_row(gain_ref, channels), one_row(bias_ref, channels)
    up_bias = one_row(up_bias_ref, hidden_width)
    for tile in range(tiles):
        for k, piece in enumerate(pieces):
            start = pl.multiple_of((index ^ k) * width, math.gcd(width, LANES))
            cat_ref[pl.ds(start, width), :] = piece[base + tile]
        values = cat_ref[...].T.astype(F32)
        average = jnp.sum(values, axis=1, keepdims=True) * (1.0 / channels)
        centered = values - average
        variance = jnp.sum(centered * centered, axis=1, keepdims=True) * (1.0 / channels)
        normed = centered * lax.rsqrt(variance + epsilon)
        normed = normed * gain + bias
        normed_ref[tile * tile_rows : (tile + 1) * tile_rows, :] = normed.astype(BF16)
    for n in range(hidden_width // up_step):
        take = slice(n * up_step, (n + 1) * up_step)
        value = jnp.dot(normed_ref[...], up_ref[:, take], preferred_element_type=F32)
        value = value + up_bias[:, take]
        value = 0.5 * value * (1.0 + lax.erf(value * (1.0 / math.sqrt(2.0))))
        hidden_ref[:, take] = value.astype(BF16)
    for n in range(channels // down_step):
        take = slice(n * down_step, (n + 1) * down_step)
        total_ref[:, take] = jnp.dot(
            hidden_ref[...], down_ref[:, take], preferred_element_type=F32
        )
    whole, tail, extra = tail_plan(rows, width)
    step = extra or ROW_BLOCK
    for part in range(rows // step):
        take = pl.ds(part * step, step)
        blocks = [total_ref[take, j * width : (j + 1) * width] for j in range(piece_count)]
        for out, block in zip(outs, xor_order(blocks, index)):
            block = block.astype(BF16)
            if extra:
                out[take, :] = block[:, :whole]
                out[rows : rows + extra, part * tail : (part + 1) * tail] = block[:, whole:]
            else:
                out[take, :] = block


def encoder_mlp(where, pieces, base, tiles, ln_gain, ln_bias, w_up, b_up, w_down):
    _, width, tile_rows = pieces[0].shape
    rows = tiles * tile_rows
    count = len(pieces)
    channels, hidden_width = w_up.shape
    shape = sent_shape(rows, width)
    return pl.pallas_call(
        functools.partial(mlp_kernel, count, base, tiles),
        out_shape=[jax.ShapeDtypeStruct(shape, BF16)] * count,
        in_specs=[SMEM] + [VMEM] * (count + 5),
        out_specs=[VMEM] * count,
        scratch_shapes=[
            pltpu.VMEM((channels, tile_rows), BF16),
            pltpu.VMEM((rows, channels), BF16),
            pltpu.VMEM((rows, hidden_width), BF16),
            pltpu.VMEM((rows, channels), F32),
        ],
        compiler_params=pltpu.CompilerParams(vmem_limit_bytes=44 * MIB),
        cost_estimate=LIGHT,
        name="encoder_mlp",
    )(
        where,
        *pieces,
        lane_rows(ln_gain),
        lane_rows(ln_bias),
        lane_rows(b_up),
        w_up,
        w_down,
    )


def prepare_kernel(
    group_count,
    tiles_local,
    where_ref,
    gain_ref,
    query_ref,
    normed_ref,
    meta_ref,
):
    @pl.when(pl.program_id(0) == 0)
    def _():
        layout_kernel(group_count, tiles_local, where_ref, meta_ref)

    gain = gain_ref[...] * (math.log2(math.e) / math.sqrt(HD))
    for col in range(0, query_ref.shape[1], HD):
        values = query_ref[:, col : col + HD].astype(F32)
        square = jnp.sum(values * values, axis=1, keepdims=True) * (1.0 / HD)
        normed_ref[:, col : col + HD] = (values * lax.rsqrt(square + epsilon) * gain).astype(BF16)


def prepare(where, q_gain, queries, group_count, tiles_local):
    text_rows, width = queries.shape
    step = ROW_BLOCK
    return pl.pallas_call(
        functools.partial(prepare_kernel, group_count, tiles_local),
        out_shape=[
            jax.ShapeDtypeStruct((text_rows, width), BF16),
            jax.ShapeDtypeStruct((meta_places(group_count)["size"],), jnp.int32),
        ],
        grid=(text_rows // step,),
        in_specs=[
            SMEM,
            pl.BlockSpec((1, HD), lambda n: (0, 0)),
            pl.BlockSpec((step, width), lambda n: (n, 0)),
        ],
        out_specs=[pl.BlockSpec((step, width), lambda n: (n, 0)), SMEM],
        compiler_params=pltpu.CompilerParams(vmem_limit_bytes=16 * MIB),
        cost_estimate=LIGHT,
        name="prepare",
    )(where, lane_rows(q_gain), queries)


def tap_kernel(blocks, head_count, dup, staged, where_ref, tap_hbm, weight_hbm, *refs):
    sources, out_ref = refs[:staged], refs[staged]
    targets = refs[staged + 1 : 2 * staged + 1]
    if staged:
        tap_ref, weight_ref, tap_sem, weight_sem, staged_sem = refs[2 * staged + 1 :]
    else:
        tap_ref, (weight_ref, weight_sem) = tap_hbm, refs[1:]
    tiles, _, tile_rows = tap_ref.shape
    block = weight_ref.shape[2]
    mine = lax.div(where_ref[1], jnp.int32(dup))
    taps = [
        pltpu.make_async_copy(tap_hbm.at[n], tap_ref.at[n], tap_sem.at[n])
        for n in range(tiles if staged else 0)
    ]
    weights = []
    for n, (head, k) in enumerate(blocks):
        column = pl.multiple_of(((mine ^ k) * head_count + head) * block, block)
        weights.append(
            pltpu.make_async_copy(
                weight_hbm.at[:, pl.ds(column, block)], weight_ref.at[n], weight_sem.at[n]
            )
        )
    others = [
        pltpu.make_async_copy(source, target, staged_sem.at[n])
        for n, (source, target) in enumerate(zip(sources, targets))
    ]
    for copy in weights[:1] + taps + weights[1:] + others:
        copy.start()
    for n in range(len(blocks)):
        weights[n].wait()
        for tile in range(tiles):
            if n == 0 and staged:
                taps[tile].wait()
            value = lax.dot_general(
                tap_ref[tile],
                weight_ref[n],
                (((0,), (0,)), ((), ())),
                preferred_element_type=F32,
            )
            out_ref[n, tile * tile_rows : (tile + 1) * tile_rows, :] = value.astype(BF16)
    for copy in others:
        copy.wait()


def tap_projection(where, tap_tiles, weights, blocks, head_count, dup, staged):
    tiles, depth, tile_rows = tap_tiles.shape
    block = 2 * HD
    return pl.pallas_call(
        functools.partial(tap_kernel, blocks, head_count, dup, len(staged)),
        out_shape=[jax.ShapeDtypeStruct((len(blocks), tiles * tile_rows, block), BF16)]
        + [jax.ShapeDtypeStruct(w.shape, w.dtype) for w in staged]
        + ([jax.ShapeDtypeStruct(tap_tiles.shape, BF16)] if staged else []),
        in_specs=[SMEM, HBM if staged else VMEM, HBM] + [HBM] * len(staged),
        out_specs=[VMEM] * (1 + len(staged) + bool(staged)),
        scratch_shapes=[pltpu.VMEM((len(blocks), depth, block), BF16)]
        + ([pltpu.SemaphoreType.DMA((tiles,))] if staged else [])
        + [pltpu.SemaphoreType.DMA((len(blocks),))]
        + ([pltpu.SemaphoreType.DMA((len(staged),))] if staged else []),
        compiler_params=pltpu.CompilerParams(vmem_limit_bytes=(42 if staged else 50) * MIB),
        cost_estimate=LIGHT,
        name="tap_projection",
    )(where, tap_tiles, weights, *staged)


def encode(x_ref, bias_ref, term_counts, terms, encoded_ref):
    tiles, width, tile_rows = x_ref.shape
    half_tiles = tiles // len(term_counts)
    whole, tail, extra = tail_plan(half_tiles * tile_rows, width)
    bias = one_row(bias_ref, width)
    for tile in range(tiles):
        half, row = tile // half_tiles, tile % half_tiles * tile_rows
        mine = terms[sum(term_counts[:half]) : sum(term_counts[: half + 1])]

        def summed(part, lanes):
            out = mine[0][part, lanes].astype(F32)
            for term in mine[1:]:
                out = out + term[part, lanes].astype(F32)
            return out

        total = summed(pl.ds(row, tile_rows), slice(None))
        if extra:
            chunks = range(row // extra, (row + tile_rows) // extra)
            rest = [
                summed(pl.ds(half_tiles * tile_rows, extra), slice(c * tail, (c + 1) * tail))
                for c in chunks
            ]
            rest = rest[0] if len(rest) == 1 else jnp.concatenate(rest, axis=0)
            total = jnp.concatenate([total, rest], axis=1)
        total = total + x_ref[tile].T.astype(F32) + bias
        encoded_ref[tile * tile_rows : (tile + 1) * tile_rows, :] = total.astype(BF16)


def kv_kernel(head, head_count, dest_count, dup, taps_at, term_counts, where_ref, *refs):
    weight_ref, refs = refs[0], refs[1:]
    part_count = 1 + max(part for part, _ in taps_at)
    tap_refs, refs = refs[:part_count], refs[part_count:]
    outs = refs[-dest_count - 1 :] if head == 0 else refs[-dest_count:]
    if head == 0:
        encoded_ref = outs[-1]
        encode(refs[0], refs[1], term_counts, refs[2 : 2 + sum(term_counts)], encoded_ref)
    else:
        encoded_ref = refs[0]
    block = 2 * HD
    mine = lax.div(where_ref[1], jnp.int32(dup))
    for k in range(dest_count):
        column = ((mine ^ k) * head_count + head) * block
        weights = weight_ref[:, pl.ds(pl.multiple_of(column, block), block)]
        value = jnp.dot(encoded_ref[...], weights, preferred_element_type=F32)
        part, n = taps_at[k]
        value = value + tap_refs[part][n].astype(F32)
        outs[k][...] = value.astype(BF16)


def kv_projection(where, weights, tap_parts, taps_at, inputs, term_counts, head, head_count, dup):
    tap_parts = tap_parts[: 1 + max(part for part, _ in taps_at)]
    rows, dest_count, block = tap_parts[0].shape[1], len(taps_at), 2 * HD
    outs = [jax.ShapeDtypeStruct((rows, block), BF16)] * dest_count
    if head == 0:
        outs.append(jax.ShapeDtypeStruct((rows, weights.shape[0]), BF16))
    return pl.pallas_call(
        functools.partial(
            kv_kernel, head, head_count, dest_count, dup, tuple(taps_at), term_counts
        ),
        out_shape=outs,
        in_specs=[SMEM] + [VMEM] * (1 + len(tap_parts) + len(inputs)),
        out_specs=[VMEM] * len(outs),
        compiler_params=pltpu.CompilerParams(vmem_limit_bytes=24 * MIB),
        cost_estimate=LIGHT,
        name="kv_projection",
    )(where, weights, *tap_parts, *inputs)


def finish_kernel(term_count, picks, meta_ref, gain_ref, *refs):
    terms = refs[:term_count]
    outs = refs[term_count : term_count + len(picks)]
    done_ref = refs[-1]
    rows = terms[0].shape[0]
    for row in range(0, rows, ROW_BLOCK):
        take = pl.ds(row, ROW_BLOCK)
        total = terms[0][take, :].astype(F32)
        for term in terms[1:]:
            total = total + term[take, :].astype(F32)
        keys = total[:, :HD]
        square = jnp.sum(keys * keys, axis=1, keepdims=True) * (1.0 / HD)
        keys = keys * lax.rsqrt(square + epsilon) * gain_ref[...]
        done_ref[take, :HD] = keys.astype(BF16).T
        done_ref[take, HD:] = (total[:, HD:] * VALUE_SHIFT).astype(BF16)
    for out, places in zip(outs, picks):
        for n, place in enumerate(places):
            start = pl.multiple_of(meta_ref[place] * ROW_BLOCK, ROW_BLOCK)
            out[n] = done_ref[pl.ds(start, ROW_BLOCK), :]


def finish_tiles(meta, k_gain, terms, picks):
    rows, block = terms[0].shape
    return pl.pallas_call(
        functools.partial(finish_kernel, len(terms), picks),
        out_shape=[jax.ShapeDtypeStruct((len(p), ROW_BLOCK, block), BF16) for p in picks],
        in_specs=[SMEM] + [VMEM] * (1 + len(terms)),
        out_specs=[VMEM] * len(picks),
        scratch_shapes=[pltpu.VMEM((rows, block), BF16)],
        compiler_params=pltpu.CompilerParams(vmem_limit_bytes=8 * MIB),
        cost_estimate=LIGHT,
        name="finish_tiles",
    )(meta, lane_rows(k_gain), *terms)


def attend_kernel(group_count, sources, head, has_base, meta_ref, query_ref, *refs):
    tile_refs = refs[: len(sources)]
    out_hbm, out_ref, key_ref, value_ref, out_sem = refs[len(sources) + has_base :]
    place = meta_places(group_count)
    counts = (meta_ref[place["first"]], meta_ref[place["second"]])
    text_first, text_both = meta_ref[place["text_first"]], meta_ref[place["text_both"]]
    span = MAXT * ROW_BLOCK
    text_rows, width = out_ref.shape
    heads = width // HD
    for label in range(REQ_G):
        for tile in range(1, MAXT):

            @pl.when(counts[label] <= tile)
            def _(tile=label * MAXT + tile):
                take = slice(tile * ROW_BLOCK, (tile + 1) * ROW_BLOCK)
                key_ref[:, take] = jnp.zeros((HD, ROW_BLOCK), BF16)
                value_ref[take, :] = jnp.zeros((ROW_BLOCK, 2 * HD), BF16)

    for tile_ref, places in zip(tile_refs, sources):
        for n, slot in enumerate(places):
            if slot is None:
                continue
            goes = meta_ref[place["goes"] + slot]

            @pl.when(goes >= 0)
            def _(tile_ref=tile_ref, n=n, goes=goes):
                take = pl.ds(pl.multiple_of(goes * ROW_BLOCK, ROW_BLOCK), ROW_BLOCK)
                key_ref[:, take] = tile_ref[n, :, :HD]
                value_ref[take, :HD] = tile_ref[n, :, HD:]
                value_ref[take, HD:] = jnp.ones((ROW_BLOCK, HD), BF16)

    copies = []
    for block in range(text_rows // ROW_BLOCK):
        start = block * ROW_BLOCK
        take = pl.ds(start, ROW_BLOCK)
        for label, (low, high) in enumerate(((0, text_first), (text_first, text_both))):
            meets = jnp.maximum(low, start) < jnp.minimum(high, start + ROW_BLOCK)

            def attend(key_rows, label=label, start=start, take=take, low=low, high=high):
                part = pl.ds(label * span, key_rows)
                slots = start + lax.broadcasted_iota(jnp.int32, (ROW_BLOCK, HD), 0)
                owned = (slots >= low) & (slots < high)
                for first in range(0, heads, HEAD_GROUP):
                    group = range(first, min(first + HEAD_GROUP, heads))
                    column = head * width
                    stacked = jnp.concatenate(
                        [
                            query_ref[take, column + h * HD : column + (h + 1) * HD]
                            for h in group
                        ],
                        axis=0,
                    )
                    scores = jnp.dot(stacked, key_ref[:, part], preferred_element_type=F32)
                    weights = jnp.exp2(scores).astype(BF16)
                    sums = jnp.dot(weights, value_ref[part, :], preferred_element_type=F32)
                    result = sums[:, :HD] / sums[:, HD:] * (1.0 / VALUE_SHIFT)
                    for n, h in enumerate(group):
                        lanes = slice(h * HD, (h + 1) * HD)
                        own = result[n * ROW_BLOCK : (n + 1) * ROW_BLOCK]
                        kept = 0.0 if label == 0 else out_ref[take, lanes].astype(F32)
                        out_ref[take, lanes] = jnp.where(owned, own, kept).astype(BF16)

            half = span // 2
            few = counts[label] * ROW_BLOCK <= half

            @pl.when(meets & few)
            def _(attend=attend):
                attend(half)

            @pl.when(meets & jnp.logical_not(few))
            def _(attend=attend):
                attend(span)

            if label == 0:

                @pl.when(jnp.logical_not(meets))
                def _(take=take):
                    out_ref[take, :] = jnp.zeros((ROW_BLOCK, width), BF16)

        copies.append(
            pltpu.make_async_copy(
                out_ref.at[take, :],
                out_hbm.at[take, pl.ds(head * width, width)],
                out_sem.at[block],
            )
        )
        copies[-1].start()
    for copy in copies:
        copy.wait()


def attend_head(group_count, meta, queries, tiles, sources, base, head, head_count):
    rows, width = queries.shape
    head_width = width // head_count
    group_rows = REQ_G * MAXT * ROW_BLOCK
    extra = [] if base is None else [base]
    return pl.pallas_call(
        functools.partial(attend_kernel, group_count, sources, head, len(extra)),
        out_shape=jax.ShapeDtypeStruct((rows, width), BF16),
        in_specs=[SMEM] + [VMEM] * (1 + len(tiles)) + [HBM] * len(extra),
        out_specs=HBM,
        scratch_shapes=[
            pltpu.VMEM((rows, head_width), BF16),
            pltpu.VMEM((HD, group_rows), BF16),
            pltpu.VMEM((group_rows, 2 * HD), BF16),
            pltpu.SemaphoreType.DMA((rows // ROW_BLOCK,)),
        ],
        input_output_aliases={2 + len(tiles): 0} if extra else {},
        compiler_params=pltpu.CompilerParams(vmem_limit_bytes=24 * MIB),
        cost_estimate=LIGHT,
        name="attend_head",
    )(meta, queries, *tiles, *extra)


def add_rounded(a, b):
    return (a.astype(F32) + b.astype(F32)).astype(BF16)


def after(value, *others):
    others = [v for v in others if v is not None]
    return lax.optimization_barrier((value, others))[0]


def scatter_sum(blocks, count, first_bit, earlier=None):
    blocks = dict(enumerate(blocks))
    bits = bits_of(len(blocks))
    for b in range(bits):
        pairs = xor_pairs(count, 1 << (b + first_bit))
        got, sent = {}, None
        for k in sorted((k for k in blocks if (k >> b) & 1), reverse=True):
            sent = blocks[k]
            if b == bits - 1 and earlier is not None:
                sent = after(sent, earlier)
            got[k ^ (1 << b)] = lax.ppermute(sent, "tp", pairs)
        if b == bits - 1:
            return [blocks[0], got[0]], sent
        blocks = {k: add_rounded(blocks[k], got[k]) for k in got}
    return [blocks[0]], blocks[0]


def gather_pieces(whole, count, ready):
    bits = bits_of(count)
    pieces = {0: whole[0]}
    for b in reversed(range(1, bits)):
        pairs = xor_pairs(count, 1 << b)
        for k in sorted(pieces):
            pieces[k | (1 << b)] = lax.ppermute(pieces[k], "tp", pairs)
    pairs = xor_pairs(count, 1)
    for k in sorted(pieces):
        if k:
            pieces[k | 1] = lax.ppermute(after(pieces[k], ready), "tp", pairs)
    pieces[0], pieces[1] = whole
    return [pieces[k] for k in range(count)]


def local(
    x_in,
    taps,
    ln_gain,
    ln_bias,
    w_up,
    b_up,
    w_down,
    b_down,
    kv_w_out,
    kv_w_taps,
    k_gain,
    q_gain,
    queries,
    tiles_per_request,
    owner,
    text_per_request,
):
    group_count = lax.axis_size("grp")
    tp_count = lax.axis_size("tp")
    position = jnp.stack([lax.axis_index("grp"), lax.axis_index("tp")]).astype(jnp.int32)
    where = jnp.concatenate([position, tiles_per_request, owner, text_per_request])
    tiles_local = x_in.shape[0]
    x_tiles = jnp.swapaxes(x_in, 2, 3)[:, 0]
    tap_tiles = jnp.swapaxes(taps, 2, 3)[:, 0]
    head_count = max(1, KVH // tp_count)
    dup = max(1, tp_count // KVH)
    dest_count = tp_count // dup
    place = meta_places(group_count)

    halves = HALVES if tiles_local % HALVES == 0 else 1
    tiles = tiles_local // halves
    whole = [x_tiles, lax.ppermute(x_tiles, "tp", xor_pairs(tp_count, 1))]

    tap_blocks = [(h, k) for h in range(head_count) for k in range(dest_count)]
    early = len(tap_blocks) * TAPS_EARLY // 8
    first_taps, w_up, w_down, tap_tiles = tap_projection(
        where, tap_tiles, kv_w_taps, tap_blocks[:early], head_count, dup, (w_up, w_down)
    )
    pieces = gather_pieces(whole, tp_count, first_taps)
    mlp_terms, begun = [], where
    for half in range(halves):
        mlp_blocks = encoder_mlp(
            begun, pieces, half * tiles, tiles, ln_gain, ln_bias, w_up, b_up, w_down
        )
        terms, sent = scatter_sum(mlp_blocks, tp_count, 0)
        mlp_terms.append(terms)
        begun = after(where, sent)
    (last_taps,) = tap_projection(
        begun, tap_tiles, kv_w_taps, tap_blocks[early:], head_count, dup, ()
    )
    taps_at = [(0, n) for n in range(early)]
    taps_at += [(1, n) for n in range(len(tap_blocks) - early)]
    kv_blocks = []
    inputs = (x_tiles, lane_rows(b_down), *(term for half in mlp_terms for term in half))
    for head in range(head_count):
        made = kv_projection(
            after(where, last_taps),
            kv_w_out,
            (first_taps, last_taps),
            taps_at[head * dest_count : (head + 1) * dest_count],
            inputs,
            tuple(len(half) for half in mlp_terms),
            head,
            head_count,
            dup,
        )
        kv_blocks.append(made[:dest_count])
        if head == 0:
            inputs = (made[-1],)
    kv_terms, arrived = [], None
    for head in range(head_count):
        blocks = kv_blocks[head]
        for b in range(bits_of(dup)):
            pairs = xor_pairs(tp_count, 1 << b)
            blocks = [add_rounded(v, lax.ppermute(v, "tp", pairs)) for v in blocks]
        terms, sent = scatter_sum(blocks, tp_count, bits_of(dup), arrived)
        kv_terms.append(terms)
        if head == 0:
            query_rows, meta = prepare(
                after(where, sent), q_gain, queries, group_count, tiles_local
            )
        arrived = (terms[-1], meta)

    slots = slot_count_of(group_count)
    total_tiles = group_count * tiles_local
    most_other = total_tiles - REQ_G * MAXT - REQ_G * (group_count - 2)
    one_large = group_count == 4 and slots == 2 and most_other <= group_count
    send = place["send"]
    out = None

    def move(value, mask):
        return lax.ppermute(value, "grp", xor_pairs(group_count, mask))

    for head in range(head_count):
        terms = kv_terms[head]
        if one_large:
            star = place["star"]
            order = (0, 2, 3, 1)
            picks = tuple((send + d, star) for d in order)
            made = finish_tiles(meta, k_gain, terms, picks)
            tiles = tuple(move(tile, d) if d else tile for tile, d in zip(made, order))
            sources = tuple((d, group_count + d) for d in order)
        else:
            picks = tuple(
                tuple(send + s * group_count + d for s in range(slots)) for d in range(group_count)
            )
            made = finish_tiles(meta, k_gain, terms, picks)
            tiles = tuple(made[:1]) + tuple(move(made[d], d) for d in range(1, group_count))
            sources = tuple(
                tuple(s * group_count + d for s in range(slots)) for d in range(group_count)
            )
        out = attend_head(
            group_count, meta, query_rows, tiles, sources, out, head, head_count
        )
    return out


def solution(mesh):
    in_specs = (
        P(None, ("rep", "grp"), None, "tp"),
        P(None, ("rep", "grp"), None, "tp"),
        P(),
        P(),
        P(None, "tp"),
        P("tp"),
        P("tp", None),
        P("tp"),
        P("tp", None),
        P("tp", None),
        P(),
        P(),
        P(("rep", "grp"), "tp"),
        P("rep"),
        P("rep"),
        P("rep"),
    )
    out_specs = P(("rep", "grp"), "tp")
    return jax.shard_map(local, mesh=mesh, in_specs=in_specs, out_specs=out_specs, check_vma=False)
```
